32 devices in a mesh: head: 2 (over y), blk: 16 (over z, x, core).
Axes of the slice: x: 2, y: 2, z: 4, core: 2. Of those that a mesh axis runs over, the one named last changes fastest.
Arguments:
- block_input: bfloat16 [2, 4096, 1024], P(None, ('blk', 'head')), may hold values from -6 to 6
- qkv_weight: bfloat16 [1024, 3072], P(('blk', 'head')), may hold values from -0.1875 to 0.1875
- q_bias: bfloat16 [1024], P(('blk', 'head')), may hold values from -3 to 3
- v_bias: bfloat16 [1024], P(('blk', 'head')), may hold values from -0.3125 to 0.3125
- out_weight: bfloat16 [1024, 1024], P(('blk', 'head')), may hold values from -3 to 3
- out_bias: bfloat16 [1024], P(('blk', 'head')), may hold values from -3 to 3
- norm1_gain: bfloat16 [1024], P(('blk', 'head')), may hold values from 0.099609375 to 1.8984375
- norm1_shift: bfloat16 [1024], P(('blk', 'head')), may hold values from -3 to 3
- norm2_gain: bfloat16 [1024], P(('blk', 'head')), may hold values from 0.099609375 to 1.8984375
- norm2_shift: bfloat16 [1024], P(('blk', 'head')), may hold values from -3 to 3
- fc_weight: bfloat16 [1024, 4096], P(('blk', 'head')), may hold values from -0.1875 to 0.1875
- fc_bias: bfloat16 [4096], P(('blk', 'head')), may hold values from -3 to 3
- proj_weight: bfloat16 [4096, 1024], P(('blk', 'head')), may hold values from -0.09375 to 0.09375
- proj_bias: bfloat16 [1024], P(('blk', 'head')), may hold values from -3 to 3
- out_grad: bfloat16 [2, 4096, 1024], P(None, ('blk', 'head')), may hold values from -6 to 6
- dealt: int32 [2, 4096], replicated, may hold values from 0 to 4095, as said below
- lengths: int32 [2, 2], replicated, may hold values from 1024 to 3072, as said below
Outputs:
- block_output: bfloat16 [2, 4096, 1024], P(None, ('blk', 'head'))
- input_grad: bfloat16 [2, 4096, 1024], P(None, ('blk', 'head'))
- grad_qkv_weight: float32 [1024, 3072], P(('blk', 'head'))
- grad_q_bias: float32 [1024], P(('blk', 'head'))
- grad_v_bias: float32 [1024], P(('blk', 'head'))
- grad_out_weight: float32 [1024, 1024], P(('blk', 'head'))
- grad_out_bias: float32 [1024], P(('blk', 'head'))
- grad_norm1_gain: float32 [1024], P(('blk', 'head'))
- grad_norm1_shift: float32 [1024], P(('blk', 'head'))
- grad_norm2_gain: float32 [1024], P(('blk', 'head'))
- grad_norm2_shift: float32 [1024], P(('blk', 'head'))
- grad_fc_weight: float32 [1024, 4096], P(('blk', 'head'))
- grad_fc_bias: float32 [4096], P(('blk', 'head'))
- grad_proj_weight: float32 [4096, 1024], P(('blk', 'head'))
- grad_proj_bias: float32 [1024], P(('blk', 'head'))
The draws below stay inside these ranges and needn't reach their ends.
Inputs may be any that keep to these rules, and one draw needn't show every extreme that they name: `dealt`: row b is a permutation of 0 to 4095: entry j is the packed position of the j-th stored token. Cut the packed order into 64 runs of 64 positions; each consecutive group of 128 stored tokens is run t followed by run 2 * 32 - 1 - t, each ascending, for a t of its own. Row b gives the lengths of micro-batch b's two sequences in packed order (the first holds the positions below lengths[b, 0]); they add up to 4096.
All inputs are finite; a program needn't handle non-finite values.
Results may differ from the reference program's by a relative error of at most 0.024.
Values may be sent and summed in bfloat16 or wider, within the bound.
No kernel may reach another device: no remote copies, remote signals or barrier semaphores. Data moves between devices by JAX's collectives and lax.ppermute only.
A program may use at most 384 MiB of HBM per device.

```python
import jax
import jax.numpy as jnp
from jax import lax

D = 1024
H = 16
DH = 64
FF = 4096
TOK_DEV = 128
MB = 2
MINLEN = 1024
TOKENS = 4096


def draw_dealt(key, part):
    key = jax.random.fold_in(key, 11)
    device_count = TOKENS // TOK_DEV
    half_block = TOK_DEV // 2
    offsets = jnp.arange(half_block, dtype=jnp.int32)

    def deal_one(subkey):
        ordering = jax.random.permutation(subkey, device_count).astype(jnp.int32)
        first_run = ordering[:, None] * half_block + offsets[None, :]
        second_run = (2 * device_count - 1 - ordering)[:, None] * half_block + offsets[None, :]
        return jnp.concatenate([first_run, second_run], axis=1).reshape(TOKENS)
    return jax.vmap(deal_one)(jax.random.split(key, MB)).astype(jnp.int32)


def draw_lengths(key, part):
    key = jax.random.fold_in(key, 23)
    short_key, side_key = jax.random.split(key)
    shorter = jax.random.randint(short_key, (MB,), MINLEN, TOKENS // 2 + 1)
    shorter = jnp.where(jnp.arange(MB) == 0, MINLEN, shorter).astype(jnp.int32)
    longer = TOKENS - shorter
    flipped = jax.random.randint(side_key, (MB,), 0, 2)
    leading = jnp.where(flipped == 1, shorter, longer)
    return jnp.stack([leading, TOKENS - leading], axis=1).astype(jnp.int32)


def steps_of(key, dims, shards, smallest, high):
    def one(position, parts):
        draws = jax.random.uniform(jax.random.fold_in(jax.random.fold_in(key, 6), position), (parts,), jnp.float32, smallest / len(shards), high / len(shards))
        return jnp.repeat(jnp.exp(draws), dims[position] // parts).reshape((-1,) + (1,) * (len(dims) - position - 1))

    level = one(*shards[0])
    for cut in shards[1:]:
        level = level * one(*cut)
    return level


def noise(rng, dims, spread, reach, pieces=(), kind=jnp.bfloat16):
    drawn = spread * jax.random.normal(rng, dims, jnp.float32)
    if pieces:
        drawn = drawn * steps_of(rng, dims, pieces, -0.22, 0.18)
    return jnp.clip(drawn, -reach, reach).astype(kind)


def setup_inputs(seed: int = 0) -> dict:
    seeds = jax.random.split(jax.random.key(seed), 18)
    block_input = noise(seeds[0], (MB, TOKENS, D), 1.0, 6.0, ((1, 32),))
    qkv_weight = noise(seeds[1], (D, 3 * D), D ** -0.5, 0.1875, ((0, 32),))
    q_bias = noise(seeds[2], (D,), 0.5, 3.0, ((0, 32),))
    v_bias = noise(seeds[3], (D,), 0.05, 0.3125, ((0, 32),))
    out_weight = noise(seeds[4], (D, D), (max(1, D * 16 // TOKENS)) ** -0.5, 3.0, ((0, 32),))
    out_bias = noise(seeds[5], (D,), 0.5, 3.0, ((0, 32),))
    norm1_gain = jnp.clip(1.0 + 0.18 * jax.random.normal(seeds[6], (D,), jnp.float32), 0.099609375, 1.8984375).astype(jnp.bfloat16)
    norm1_shift = noise(seeds[7], (D,), 0.5, 3.0, ((0, 32),))
    norm2_gain = jnp.clip(1.0 + 0.18 * jax.random.normal(seeds[8], (D,), jnp.float32), 0.099609375, 1.8984375).astype(jnp.bfloat16)
    norm2_shift = noise(seeds[9], (D,), 0.5, 3.0, ((0, 32),))
    fc_weight = noise(seeds[10], (D, FF), D ** -0.5, 0.1875, ((0, 32),))
    fc_bias = noise(seeds[11], (FF,), 0.5, 3.0, ((0, 32),))
    proj_weight = noise(seeds[12], (FF, D), FF ** -0.5, 0.09375, ((0, 32),))
    proj_bias = noise(seeds[13], (D,), 0.5, 3.0, ((0, 32),))
    out_grad = noise(seeds[14], (MB, TOKENS, D), 1.0, 6.0, ((1, 32),))
    dealt = draw_dealt(jax.random.fold_in(seeds[17], 71), 0)
    lengths = draw_lengths(jax.random.fold_in(seeds[17], 71), 0)
    return {"block_input": block_input, "qkv_weight": qkv_weight, "q_bias": q_bias, "v_bias": v_bias, "out_weight": out_weight, "out_bias": out_bias, "norm1_gain": norm1_gain, "norm1_shift": norm1_shift, "norm2_gain": norm2_gain, "norm2_shift": norm2_shift, "fc_weight": fc_weight, "fc_bias": fc_bias, "proj_weight": proj_weight, "proj_bias": proj_bias, "out_grad": out_grad, "dealt": dealt, "lengths": lengths}


@jax.custom_vjp
def low(v):
    return lax.optimization_barrier(v.astype(jnp.bfloat16)).astype(jnp.float32)

@jax.custom_vjp
def low_back(v):
    return v

def low_keep(v):
    return (low(v), None)

def low_pass(kept, grad):
    return (grad,)

def back_keep(v):
    return (v, None)

def back_low(kept, grad):
    return (low(grad),)
low.defvjp(low_keep, low_pass)
low_back.defvjp(back_keep, back_low)

def layer_norm(values, gain, shift):
    centred = values - lax.optimization_barrier(jnp.mean(values, axis=-1, keepdims=True))
    scaled = centred * lax.rsqrt(lax.optimization_barrier(jnp.mean(centred * centred, axis=-1, keepdims=True)) + 1e-05)
    return scaled * gain + shift

def gelu_tanh(values):
    inner = 0.7978845608028654 * (values + 0.044715 * values * values * values)
    return 0.5 * values * (1.0 + jnp.tanh(inner))

def attention(queries, keys, values, positions, boundary):
    scale = DH ** (-0.5)
    span = min(256, TOKENS)
    blocks = TOKENS // span
    key_side = (positions >= boundary).astype(jnp.int32)

    def one_block(query_block, query_pos):
        query_side = (query_pos >= boundary).astype(jnp.int32)
        visible = (query_side[:, None] == key_side[None, :]) & (positions[None, :] <= query_pos[:, None])
        scores = jnp.einsum('qhd,khd->hqk', query_block, keys, precision=lax.Precision.HIGHEST) * scale
        scores = low_back(jnp.where(visible[None], scores, -1000000000.0))
        shifted = scores - lax.optimization_barrier(jnp.max(scores, axis=-1, keepdims=True))
        expo = jnp.exp(shifted)
        probs = low(expo / lax.optimization_barrier(jnp.sum(expo, axis=-1, keepdims=True)))
        return jnp.einsum('hqk,khd->qhd', probs, values, precision=lax.Precision.HIGHEST)
    checked = jax.checkpoint(one_block)

    def mapped(item):
        return checked(item[0], item[1])
    outputs = lax.map(mapped, (queries.reshape(blocks, span, H, DH), positions.reshape(blocks, span)))
    return outputs.reshape(TOKENS, D)

def block_forward(inputs, qkv_weight, q_bias, v_bias, out_weight, out_bias, norm1_gain, norm1_shift, norm2_gain, norm2_shift, fc_weight, fc_bias, proj_weight, proj_bias, positions, boundary):
    act1 = low(layer_norm(inputs, norm1_gain, norm1_shift))
    mixed = jnp.dot(act1, qkv_weight, precision=lax.Precision.HIGHEST)
    queries = low_back(low(mixed[:, :D] + q_bias))
    keys = low_back(low(mixed[:, D:2 * D]))
    values = low_back(low(mixed[:, 2 * D:] + v_bias))
    attended = attention(queries.reshape(TOKENS, H, DH), keys.reshape(TOKENS, H, DH), values.reshape(TOKENS, H, DH), positions, boundary)
    attended = low_back(low(attended))
    resid = inputs + low_back(jnp.dot(attended, out_weight, precision=lax.Precision.HIGHEST) + out_bias)
    act2 = low(layer_norm(resid, norm2_gain, norm2_shift))
    pre = low_back(jnp.dot(act2, fc_weight, precision=lax.Precision.HIGHEST) + fc_bias)
    hidden = low(gelu_tanh(pre))
    return resid + jnp.dot(hidden, proj_weight, precision=lax.Precision.HIGHEST) + proj_bias

def reference(block_input, qkv_weight, q_bias, v_bias, out_weight, out_bias, norm1_gain, norm1_shift, norm2_gain, norm2_shift, fc_weight, fc_bias, proj_weight, proj_bias, out_grad, dealt, lengths):
    params = tuple((item.astype(jnp.float32) for item in (qkv_weight, q_bias, v_bias, out_weight, out_bias, norm1_gain, norm1_shift, norm2_gain, norm2_shift, fc_weight, fc_bias, proj_weight, proj_bias)))
    totals = [jnp.zeros(item.shape, jnp.float32) for item in params]
    outputs = []
    input_grads = []
    for micro in range(MB):
        positions = dealt[micro]
        boundary = lengths[micro, 0]

        def run_block(inputs, *weights):
            return block_forward(inputs, *weights, positions, boundary)
        result, pullback = jax.vjp(run_block, block_input[micro].astype(jnp.float32), *params)
        grads = pullback(out_grad[micro].astype(jnp.float32))
        outputs.append(result.astype(jnp.bfloat16))
        input_grads.append(grads[0].astype(jnp.bfloat16))
        totals = [total + grad for total, grad in zip(totals, grads[1:])]
    return (jnp.stack(outputs), jnp.stack(input_grads), totals[0], totals[1], totals[2], totals[3], totals[4], totals[5], totals[6], totals[7], totals[8], totals[9], totals[10], totals[11], totals[12])
```

```python
import functools
import math

import jax
import jax.numpy as jnp
from jax import lax
from jax.experimental import pallas as pl
from jax.experimental.pallas import tpu as pltpu
from jax.sharding import Mesh
from jax.sharding import PartitionSpec as P

DH = 64


def gelu_tanh(values):
    inner = 0.7978845608028654 * (values + 0.044715 * values * values * values)
    return 0.5 * values * (1.0 + jnp.tanh(inner))


def normalize(values):
    centred = values - jnp.mean(values, axis=-1, keepdims=True)
    inverse = lax.rsqrt(jnp.mean(centred * centred, axis=-1, keepdims=True) + 1e-05)
    return (centred * inverse, inverse)


def norm_back(grad_normed, normed, inverse):
    return inverse * (
        grad_normed
        - jnp.mean(grad_normed, axis=-1, keepdims=True)
        - normed * jnp.mean(grad_normed * normed, axis=-1, keepdims=True)
    )


def product(left, right):
    return jnp.dot(left, right, preferred_element_type=jnp.float32)


def product_tn(left, right):
    return lax.dot_general(
        left, right, (((0,), (0,)), ((), ())), preferred_element_type=jnp.float32
    )


def product_nt(left, right):
    return lax.dot_general(
        left, right, (((1,), (1,)), ((), ())), preferred_element_type=jnp.float32
    )


def visible_pairs(query_pos, key_pos, boundary):
    same_side = (query_pos[:, None] >= boundary) == (key_pos[None, :] >= boundary)
    return same_side & (key_pos[None, :] <= query_pos[:, None])


def forward_tile(current, queries3, keys3, values3, visible, scale):
    running, total, accum = current
    scores = jnp.einsum("qhd,khd->hqk", queries3, keys3, preferred_element_type=jnp.float32) * scale
    scores = jnp.where(visible[None], scores, -1000000000.0)
    highest = jnp.maximum(running, jnp.max(scores, axis=-1))
    weights = jnp.where(visible[None], jnp.exp(scores - highest[..., None]), 0.0)
    factor = jnp.exp(running - highest)
    total = total * factor + jnp.sum(weights, axis=-1)
    accum = accum * factor[..., None] + jnp.einsum(
        "hqk,khd->hqd", weights.astype(jnp.bfloat16), values3, preferred_element_type=jnp.float32
    )
    return (highest, total, accum)


def general_forward(query_parts, pos_parts, positions, boundary, keys_group, values_group, key_span):
    heads_local, head_size = (query_parts[0].shape[1], query_parts[0].shape[2])
    scale = head_size ** (-0.5)

    def fold_keys(state, pieces, start):
        key_rows, value_rows = pieces
        count_rows = key_rows.shape[0]
        block_rows = math.gcd(count_rows, key_span)
        block_count = count_rows // block_rows

        def one_step(index, inner):
            offset = index * block_rows
            keys3 = lax.dynamic_slice_in_dim(key_rows, offset, block_rows).reshape(
                block_rows, heads_local, head_size
            )
            values3 = lax.dynamic_slice_in_dim(value_rows, offset, block_rows).reshape(
                block_rows, heads_local, head_size
            )
            key_pos = lax.dynamic_slice_in_dim(positions, offset, block_rows)
            part_queries = query_parts[0]
            visible = visible_pairs(pos_parts[0], key_pos, boundary)
            current = inner[0]
            result = forward_tile(current, part_queries, keys3, values3, visible, scale)
            updated = [result]
            return tuple(updated)

        return lax.fori_loop(0, block_count, one_step, state)

    initial = tuple(
        (
            (
                jnp.full((heads_local, part.shape[0]), -1000000000.0, jnp.float32),
                jnp.zeros((heads_local, part.shape[0]), jnp.float32),
                jnp.zeros((heads_local, part.shape[0], head_size), jnp.float32),
            )
            for part in query_parts
        )
    )
    return fold_keys(
        initial,
        (
            lax.all_gather(keys_group, "blk", axis=0, tiled=True),
            lax.all_gather(values_group, "blk", axis=0, tiled=True),
        ),
        jnp.int32(0),
    )


def backward_tile(current, queries3, grad3, log_total, delta, keys3, values3, visible, scale):
    grad_query, term = current
    scores = jnp.einsum("qhd,khd->hqk", queries3, keys3, preferred_element_type=jnp.float32) * scale
    scores = jnp.where(visible[None], scores, -1000000000.0)
    exact = jnp.where(visible[None], jnp.exp(scores - log_total[..., None]), 0.0)
    grad_probs = jnp.einsum("qhd,khd->hqk", grad3, values3, preferred_element_type=jnp.float32)
    grad_scores = (exact * (grad_probs - delta[..., None])).astype(jnp.bfloat16)
    grad_query = (
        grad_query
        + jnp.einsum("hqk,khd->hqd", grad_scores, keys3, preferred_element_type=jnp.float32) * scale
    )
    rounded = exact.astype(jnp.bfloat16)
    grad_values = jnp.einsum("hqk,qhd->khd", rounded, grad3, preferred_element_type=jnp.float32)
    grad_keys = (
        jnp.einsum("hqk,qhd->khd", grad_scores, queries3, preferred_element_type=jnp.float32)
        * scale
    )
    rows = keys3.shape[0]
    term = jnp.stack([grad_keys.reshape(rows, -1), grad_values.reshape(rows, -1)], axis=1)
    return (grad_query, term)


def general_backward(
    query_parts,
    grad_parts,
    total_parts,
    delta_parts,
    pos_parts,
    positions,
    boundary,
    keys_group,
    values_group,
    key_span,
    buffer_rows,
):
    heads_local, head_size = (query_parts[0].shape[1], query_parts[0].shape[2])
    scale = head_size ** (-0.5)

    def fold_keys(state, pieces, start):
        key_rows, value_rows = pieces
        count_rows = key_rows.shape[0]
        block_rows = math.gcd(count_rows, key_span)
        block_count = count_rows // block_rows

        def one_step(index, inner):
            offset = index * block_rows
            keys3 = lax.dynamic_slice_in_dim(key_rows, offset, block_rows).reshape(
                block_rows, heads_local, head_size
            )
            values3 = lax.dynamic_slice_in_dim(value_rows, offset, block_rows).reshape(
                block_rows, heads_local, head_size
            )
            key_pos = lax.dynamic_slice_in_dim(positions, offset, block_rows)
            grads_now, buffer = inner
            term = jnp.zeros((block_rows, 2, heads_local * head_size), jnp.float32)
            part_queries = query_parts[0]
            part_grads = grad_parts[0]
            part_total = total_parts[0]
            part_delta = delta_parts[0]
            visible = visible_pairs(pos_parts[0], key_pos, boundary)
            current = (grads_now[0], term)
            result = backward_tile(
                current,
                part_queries,
                part_grads,
                part_total,
                part_delta,
                keys3,
                values3,
                visible,
                scale,
            )
            updated = [result[0]]
            term = result[1]
            buffer = lax.dynamic_update_slice(buffer, term, (offset, 0, 0))
            return (tuple(updated), buffer)

        return lax.fori_loop(0, block_count, one_step, state)

    grads_init = tuple(
        (jnp.zeros((heads_local, part.shape[0], head_size), jnp.float32) for part in query_parts)
    )
    initial = (grads_init, jnp.zeros((buffer_rows, 2, heads_local * head_size), jnp.float32))
    return fold_keys(
        initial,
        (
            lax.all_gather(keys_group, "blk", axis=0, tiled=True),
            lax.all_gather(values_group, "blk", axis=0, tiled=True),
        ),
        jnp.int32(0),
    )


def general_body(
    block_input,
    qkv_weight,
    q_bias,
    v_bias,
    out_weight,
    out_bias,
    norm1_gain,
    norm1_shift,
    norm2_gain,
    norm2_shift,
    fc_weight,
    fc_bias,
    proj_weight,
    proj_bias,
    out_grad,
    dealt,
    lengths,
):
    micro_count, local_rows, width = block_input.shape
    head_devices = lax.axis_size("head")
    blk_devices = lax.axis_size("blk")
    group = local_rows * head_devices
    blk_index = lax.axis_index("blk")
    head_size = DH
    key_span = 1024
    part_count = group // group
    shards = (
        qkv_weight,
        q_bias,
        v_bias,
        out_weight,
        out_bias,
        norm1_gain,
        norm1_shift,
        norm2_gain,
        norm2_shift,
        fc_weight,
        fc_bias,
        proj_weight,
        proj_bias,
    )
    totals = [
        jnp.zeros((shard.shape[0] * blk_devices * head_devices,) + shard.shape[1:], jnp.float32)
        for shard in shards
    ]
    outputs = []
    input_grads = []
    for micro_index in range(micro_count):
        whole = (
            lax.all_gather(shards[0], ("blk", "head"), axis=0, tiled=True),
            lax.all_gather(shards[1], ("blk", "head"), axis=0, tiled=True),
            lax.all_gather(shards[2], ("blk", "head"), axis=0, tiled=True),
            lax.all_gather(shards[3], ("blk", "head"), axis=0, tiled=True),
            lax.all_gather(shards[4], ("blk", "head"), axis=0, tiled=True),
            lax.all_gather(shards[5], ("blk", "head"), axis=0, tiled=True),
            lax.all_gather(shards[6], ("blk", "head"), axis=0, tiled=True),
            lax.all_gather(shards[7], ("blk", "head"), axis=0, tiled=True),
            lax.all_gather(shards[8], ("blk", "head"), axis=0, tiled=True),
            lax.all_gather(shards[9], ("blk", "head"), axis=0, tiled=True),
            lax.all_gather(shards[10], ("blk", "head"), axis=0, tiled=True),
            lax.all_gather(shards[11], ("blk", "head"), axis=0, tiled=True),
            lax.all_gather(shards[12], ("blk", "head"), axis=0, tiled=True),
        )
        (
            w_qkv,
            b_query,
            b_value,
            w_out,
            b_out,
            gain_one,
            shift_one,
            gain_two,
            shift_two,
            w_fc,
            b_fc,
            w_proj,
            b_proj,
        ) = whole
        b_query = b_query.astype(jnp.float32)
        b_value = b_value.astype(jnp.float32)
        b_out = b_out.astype(jnp.float32)
        gain_one = gain_one.astype(jnp.float32)
        shift_one = shift_one.astype(jnp.float32)
        gain_two = gain_two.astype(jnp.float32)
        shift_two = shift_two.astype(jnp.float32)
        b_fc = b_fc.astype(jnp.float32)
        b_proj = b_proj.astype(jnp.float32)
        positions = dealt[micro_index]
        boundary = lengths[micro_index, 0]
        query_pos = lax.dynamic_slice_in_dim(positions, blk_index * group, group)
        inputs = block_input[micro_index].astype(jnp.float32)
        normed_one, inverse_one = normalize(inputs)
        act_one = (normed_one * gain_one + shift_one).astype(jnp.bfloat16)
        mixed = product(act_one, w_qkv)
        queries = (mixed[:, :width] + b_query).astype(jnp.bfloat16)
        keys = mixed[:, width : 2 * width].astype(jnp.bfloat16)
        values = (mixed[:, 2 * width :] + b_value).astype(jnp.bfloat16)
        heads_in = lax.all_to_all(
            jnp.stack([queries, keys, values], axis=1),
            "head",
            split_axis=2,
            concat_axis=0,
            tiled=True,
        )
        local_width = heads_in.shape[2]
        heads_local = local_width // head_size
        queries3 = heads_in[:, 0].reshape(group, heads_local, head_size)
        keys_group = heads_in[:, 1]
        values_group = heads_in[:, 2]
        query_parts = tuple((queries3 for index in range(part_count)))
        pos_parts = tuple((query_pos for index in range(part_count)))
        states = general_forward(
            query_parts, pos_parts, positions, boundary, keys_group, values_group, key_span
        )
        running = jnp.concatenate([state[0] for state in states], axis=1)
        total = jnp.concatenate([state[1] for state in states], axis=1)
        accum = jnp.concatenate([state[2] for state in states], axis=1)
        log_total = running + jnp.log(total)
        attn_heads = (
            (accum / total[..., None])
            .transpose(1, 0, 2)
            .reshape(group, local_width)
            .astype(jnp.bfloat16)
        )
        attended = lax.all_to_all(attn_heads, "head", split_axis=0, concat_axis=1, tiled=True)
        resid = inputs + product(attended, w_out) + b_out
        normed_two, inverse_two = normalize(resid)
        act_two = (normed_two * gain_two + shift_two).astype(jnp.bfloat16)
        pre = product(act_two, w_fc) + b_fc
        hidden = gelu_tanh(pre).astype(jnp.bfloat16)
        outputs.append((resid + product(hidden, w_proj) + b_proj).astype(jnp.bfloat16))
        cotangent = out_grad[micro_index]
        grad_proj_w = product_tn(hidden, cotangent)
        grad_proj_b = jnp.sum(cotangent.astype(jnp.float32), axis=0)
        grad_hidden = product_nt(cotangent, w_proj)
        grad_pre = jax.vjp(gelu_tanh, pre)[1](grad_hidden)[0].astype(jnp.bfloat16)
        grad_fc_w = product_tn(act_two, grad_pre)
        grad_fc_b = jnp.sum(grad_pre.astype(jnp.float32), axis=0)
        grad_act_two = product_nt(grad_pre, w_fc)
        grad_gain_two = jnp.sum(grad_act_two * normed_two, axis=0)
        grad_shift_two = jnp.sum(grad_act_two, axis=0)
        grad_resid = cotangent.astype(jnp.float32) + norm_back(
            grad_act_two * gain_two, normed_two, inverse_two
        )
        grad_branch = grad_resid.astype(jnp.bfloat16)
        grad_out_w = product_tn(attended, grad_branch)
        grad_out_b = jnp.sum(grad_branch.astype(jnp.float32), axis=0)
        grad_attn = product_nt(grad_branch, w_out).astype(jnp.bfloat16)
        grad_heads = lax.all_to_all(grad_attn, "head", split_axis=1, concat_axis=0, tiled=True)
        grad3 = grad_heads.reshape(group, heads_local, head_size)
        attn3 = attn_heads.reshape(group, heads_local, head_size)
        delta = jnp.sum(grad3.astype(jnp.float32) * attn3.astype(jnp.float32), axis=-1).T
        grad_parts = tuple((grad3 for index in range(part_count)))
        total_parts = tuple((log_total for index in range(part_count)))
        delta_parts = tuple((delta for index in range(part_count)))
        query_grads, buffer = general_backward(
            query_parts,
            grad_parts,
            total_parts,
            delta_parts,
            pos_parts,
            positions,
            boundary,
            keys_group,
            values_group,
            key_span,
            group * blk_devices,
        )
        kv_sums = lax.psum_scatter(buffer, "blk", scatter_dimension=0, tiled=True)
        grad_k_heads = kv_sums[:, 0].astype(jnp.bfloat16)
        grad_v_heads = kv_sums[:, 1].astype(jnp.bfloat16)
        grad_query = jnp.concatenate(list(query_grads), axis=1)
        grad_q_heads = (
            grad_query.transpose(1, 0, 2).reshape(group, local_width).astype(jnp.bfloat16)
        )
        grads_heads = jnp.stack([grad_q_heads, grad_k_heads, grad_v_heads], axis=1)
        back_tokens = lax.all_to_all(grads_heads, "head", split_axis=0, concat_axis=2, tiled=True)
        grad_mixed = back_tokens.reshape(local_rows, 3 * width)
        grad_qkv_w = product_tn(act_one, grad_mixed)
        grad_q_b = jnp.sum(back_tokens[:, 0].astype(jnp.float32), axis=0)
        grad_v_b = jnp.sum(back_tokens[:, 2].astype(jnp.float32), axis=0)
        grad_act_one = product_nt(grad_mixed, w_qkv)
        grad_gain_one = jnp.sum(grad_act_one * normed_one, axis=0)
        grad_shift_one = jnp.sum(grad_act_one, axis=0)
        input_grads.append(
            (grad_resid + norm_back(grad_act_one * gain_one, normed_one, inverse_one)).astype(
                jnp.bfloat16
            )
        )
        terms = (
            grad_qkv_w,
            grad_q_b,
            grad_v_b,
            grad_out_w,
            grad_out_b,
            grad_gain_one,
            grad_shift_one,
            grad_gain_two,
            grad_shift_two,
            grad_fc_w,
            grad_fc_b,
            grad_proj_w,
            grad_proj_b,
        )
        totals = [running_sum + term for running_sum, term in zip(totals, terms)]
    final = (
        lax.psum_scatter(totals[0], ("blk", "head"), scatter_dimension=0, tiled=True),
        lax.psum_scatter(totals[1], ("blk", "head"), scatter_dimension=0, tiled=True),
        lax.psum_scatter(totals[2], ("blk", "head"), scatter_dimension=0, tiled=True),
        lax.psum_scatter(totals[3], ("blk", "head"), scatter_dimension=0, tiled=True),
        lax.psum_scatter(totals[4], ("blk", "head"), scatter_dimension=0, tiled=True),
        lax.psum_scatter(totals[5], ("blk", "head"), scatter_dimension=0, tiled=True),
        lax.psum_scatter(totals[6], ("blk", "head"), scatter_dimension=0, tiled=True),
        lax.psum_scatter(totals[7], ("blk", "head"), scatter_dimension=0, tiled=True),
        lax.psum_scatter(totals[8], ("blk", "head"), scatter_dimension=0, tiled=True),
        lax.psum_scatter(totals[9], ("blk", "head"), scatter_dimension=0, tiled=True),
        lax.psum_scatter(totals[10], ("blk", "head"), scatter_dimension=0, tiled=True),
        lax.psum_scatter(totals[11], ("blk", "head"), scatter_dimension=0, tiled=True),
        lax.psum_scatter(totals[12], ("blk", "head"), scatter_dimension=0, tiled=True),
    )
    return (
        jnp.stack(outputs),
        jnp.stack(input_grads),
        final[0],
        final[1],
        final[2],
        final[3],
        final[4],
        final[5],
        final[6],
        final[7],
        final[8],
        final[9],
        final[10],
        final[11],
        final[12],
    )


RUN = 64
BLOCK = 512
NEG = -1000000000.0
VM = pltpu.VMEM
SM = pltpu.SMEM


def dot_nt(left, right):
    return lax.dot_general(left, right, (((1,), (1,)), ((), ())), preferred_element_type=jnp.float32)


def dot_nn(left, right):
    return lax.dot_general(left, right, (((1,), (0,)), ((), ())), preferred_element_type=jnp.float32)


def rows_at(index, size):
    return pl.ds(pl.multiple_of(index * size, size), size)


def first_block(start, bound):
    return jnp.where(start >= bound, bound // BLOCK, 0)


def forward_kernel(head_size, bound_ref, inloc, outloc, qkv, out, qs, ks, vs, attn_t, lse, vt, mixed):
    tokens = qkv.shape[0]
    runs = tokens // RUN
    scale = head_size ** (-0.5)
    bound = bound_ref[0]

    @pl.loop(0, runs)
    def _(run):
        rows = qkv[rows_at(inloc[run], RUN), :]
        here = rows_at(run, RUN)
        qs[here, :] = (rows[:, :head_size].astype(jnp.float32) * scale).astype(jnp.bfloat16)
        ks[here, :] = rows[:, head_size : 2 * head_size]
        vs[here, :] = rows[:, 2 * head_size :]

    @pl.loop(0, tokens // BLOCK)
    def _(block):
        here = rows_at(block, BLOCK)
        vt[:, here] = vs[here, :].astype(jnp.float32).T.astype(jnp.bfloat16)

    @pl.loop(0, tokens // BLOCK)
    def _(block):
        start = block * BLOCK
        here = rows_at(block, BLOCK)
        queries = qs[here, :]
        query_pos = start + lax.broadcasted_iota(jnp.int32, (1, BLOCK), 1)
        floor = jnp.where(query_pos >= bound, bound, 0)

        def scores_of(index, diagonal):
            keys = ks[rows_at(index, BLOCK), :]
            scores = dot_nt(keys, queries)
            key_pos = index * BLOCK + lax.broadcasted_iota(jnp.int32, (BLOCK, BLOCK), 0)
            visible = key_pos >= floor
            if diagonal:
                visible = visible & (key_pos <= query_pos)
            return jnp.where(visible, scores, NEG)

        scores = scores_of(block, True)
        highest = jnp.max(scores, axis=0, keepdims=True)
        weights = jnp.exp(scores - highest)
        total = jnp.sum(weights, axis=0, keepdims=True)
        accum = dot_nn(vt[:, here], weights.astype(jnp.bfloat16))

        def step(index, state):
            highest, total, accum = state
            scores = scores_of(index, False)
            higher = jnp.maximum(highest, jnp.max(scores, axis=0, keepdims=True))
            weights = jnp.exp(scores - higher)
            factor = jnp.exp(highest - higher)
            total = total * factor + jnp.sum(weights, axis=0, keepdims=True)
            accum = accum * factor + dot_nn(vt[:, rows_at(index, BLOCK)], weights.astype(jnp.bfloat16))
            return higher, total, accum

        highest, total, accum = lax.fori_loop(first_block(start, bound), block, step, (highest, total, accum))
        result = accum / total
        attn_t[:, here] = result.astype(jnp.bfloat16)
        lse[:, here] = highest + jnp.log(total)
        result = result.T.astype(jnp.bfloat16)
        for part in range(BLOCK // RUN):
            mixed[rows_at(outloc[block * (BLOCK // RUN) + part], RUN), :] = result[part * RUN : (part + 1) * RUN]

    chips, _, span = out.shape

    @pl.loop(0, chips)
    def _(chip):
        out[chip] = mixed[rows_at(chip, span), :].astype(jnp.float32).T.astype(jnp.bfloat16)


def attend_forward(bound, inloc, outloc, qkv, chips, head_size):
    tokens = qkv.shape[0]
    bf16 = jnp.bfloat16
    pairs = tokens * (tokens // 2)
    return pl.pallas_call(
        functools.partial(forward_kernel, head_size),
        out_shape=(
            jax.ShapeDtypeStruct((chips, head_size, tokens // chips), bf16),
            jax.ShapeDtypeStruct((tokens, head_size), bf16),
            jax.ShapeDtypeStruct((tokens, head_size), bf16),
            jax.ShapeDtypeStruct((tokens, head_size), bf16),
            jax.ShapeDtypeStruct((head_size, tokens), bf16),
            jax.ShapeDtypeStruct((1, tokens), jnp.float32),
        ),
        in_specs=[pl.BlockSpec(memory_space=SM)] * 3 + [pl.BlockSpec(memory_space=VM)],
        out_specs=[pl.BlockSpec(memory_space=VM)] * 6,
        scratch_shapes=[VM((head_size, tokens), bf16), VM((tokens, head_size), bf16)],
        compiler_params=pltpu.CompilerParams(vmem_limit_bytes=40 * 1024 * 1024),
        cost_estimate=pl.CostEstimate(flops=4 * 4 * pairs * head_size, bytes_accessed=tokens * 2048, transcendentals=pairs),
        name="attend_forward",
    )(bound, inloc, outloc, qkv)


def backward_kernel(
    head_size, bound_ref, inloc, outloc, grad_t, qs, ks, vs, attn_t, lse, slot_out, send_out, grads, kt, dk, dv, mixed, wide, moved
):
    tokens = qs.shape[0]
    runs = tokens // RUN
    scale = head_size ** (-0.5)
    bound = bound_ref[0]
    chips, _, span = grad_t.shape

    @pl.loop(0, chips)
    def _(chip):
        mixed[rows_at(chip, span), :] = grad_t[chip].astype(jnp.float32).T.astype(jnp.bfloat16)

    @pl.loop(0, runs)
    def _(run):
        grads[rows_at(run, RUN), :] = mixed[rows_at(outloc[run], RUN), :]

    @pl.loop(0, tokens // BLOCK)
    def _(block):
        here = rows_at(block, BLOCK)
        kt[:, here] = ks[here, :].astype(jnp.float32).T.astype(jnp.bfloat16)

    @pl.loop(0, tokens // BLOCK)
    def _(block):
        start = block * BLOCK
        here = rows_at(block, BLOCK)
        queries = qs[here, :]
        grad = grads[here, :]
        log_total = lse[:, here]
        delta = jnp.sum(grad.astype(jnp.float32).T * attn_t[:, here].astype(jnp.float32), axis=0, keepdims=True)
        query_pos = start + lax.broadcasted_iota(jnp.int32, (1, BLOCK), 1)
        floor = jnp.where(query_pos >= bound, bound, 0)

        def one(index, diagonal):
            there = rows_at(index, BLOCK)
            scores = dot_nt(ks[there, :], queries)
            key_pos = index * BLOCK + lax.broadcasted_iota(jnp.int32, (BLOCK, BLOCK), 0)
            visible = key_pos >= floor
            if diagonal:
                visible = visible & (key_pos <= query_pos)
            probs = jnp.where(visible, jnp.exp(scores - log_total), 0.0)
            grad_probs = dot_nt(vs[there, :], grad)
            grad_scores = (probs * (grad_probs - delta)).astype(jnp.bfloat16)
            return (
                dot_nn(probs.astype(jnp.bfloat16), grad),
                dot_nn(grad_scores, queries),
                dot_nn(kt[:, there], grad_scores),
                there,
            )

        grad_v, grad_k, grad_q, there = one(block, True)
        dv[there, :] = grad_v
        dk[there, :] = grad_k

        def step(index, grad_q):
            grad_v, grad_k, term, there = one(index, False)
            dv[there, :] += grad_v
            dk[there, :] += grad_k
            return grad_q + term

        grad_q = lax.fori_loop(first_block(start, bound), block, step, grad_q)
        wide[here, :head_size] = (grad_q.T * scale).astype(jnp.bfloat16)

    wide[:, head_size : 2 * head_size] = dk[...].astype(jnp.bfloat16)
    wide[:, 2 * head_size :] = dv[...].astype(jnp.bfloat16)

    @pl.loop(0, runs)
    def _(run):
        slot_out[rows_at(inloc[run], RUN), :] = wide[rows_at(run, RUN), :]

    @pl.loop(0, runs)
    def _(run):
        moved[rows_at(outloc[run], RUN), :] = wide[rows_at(run, RUN), :]

    @pl.loop(0, chips)
    def _(chip):
        send_out[chip] = moved[rows_at(chip, span), :].astype(jnp.float32).T.astype(jnp.bfloat16)


def attend_backward(bound, inloc, outloc, grad_t, qs, ks, vs, attn_t, lse):
    tokens, head_size = qs.shape
    chips = grad_t.shape[0]
    bf16 = jnp.bfloat16
    pairs = tokens * (tokens // 2)
    return pl.pallas_call(
        functools.partial(backward_kernel, head_size),
        out_shape=(
            jax.ShapeDtypeStruct((tokens, 3 * head_size), bf16),
            jax.ShapeDtypeStruct((chips, 3 * head_size, tokens // chips), bf16),
        ),
        in_specs=[pl.BlockSpec(memory_space=SM)] * 3 + [pl.BlockSpec(memory_space=VM)] * 6,
        out_specs=[pl.BlockSpec(memory_space=VM)] * 2,
        scratch_shapes=[
            VM((tokens, head_size), bf16),
            VM((head_size, tokens), bf16),
            VM((tokens, head_size), jnp.float32),
            VM((tokens, head_size), jnp.float32),
            VM((tokens, head_size), bf16),
            VM((tokens, 3 * head_size), bf16),
            VM((tokens, 3 * head_size), bf16),
        ],
        compiler_params=pltpu.CompilerParams(vmem_limit_bytes=48 * 1024 * 1024),
        cost_estimate=pl.CostEstimate(flops=4 * 10 * pairs * head_size, bytes_accessed=tokens * 4096, transcendentals=pairs),
        name="attend_backward",
    )(bound, inloc, outloc, grad_t, qs, ks, vs, attn_t, lse)


PAIR = [(0, 1), (1, 0)]


def swap(values, axis):
    return lax.ppermute(values, axis, PAIR)


def in_order(mine, other, index, axis):
    first = jnp.where(index == 0, mine, other)
    second = jnp.where(index == 0, other, mine)
    return jnp.stack([first, second], axis=axis)


def shifted(values, count):
    return [
        lax.ppermute(values, "z", [(i, (i + step) % count) for i in range(count)]) for step in range(1, count)
    ]


def split_float(values):
    high = values.astype(jnp.bfloat16)
    low = (values - high.astype(jnp.float32)).astype(jnp.bfloat16)
    return high, low


def run_table(order, pair_start):
    pairs = order.shape[0]
    runs = jnp.arange(2 * pairs, dtype=jnp.int32)[:, None]
    low = jnp.where(runs == order[None, :], pair_start[None, :], 0)
    high = jnp.where(runs == 2 * pairs - 1 - order[None, :], pair_start[None, :] + 1, 0)
    return jnp.sum(low + high, axis=1).astype(jnp.int32)


def fast_body(
    block_input,
    qkv_weight,
    q_bias,
    v_bias,
    out_weight,
    out_bias,
    norm1_gain,
    norm1_shift,
    norm2_gain,
    norm2_shift,
    fc_weight,
    fc_bias,
    proj_weight,
    proj_bias,
    out_grad,
    dealt,
    lengths,
):
    f32, bf16 = jnp.float32, jnp.bfloat16
    micro, rows, width = block_input.shape
    nz, nx = lax.axis_size("z"), lax.axis_size("x")
    iz, ix, ic, iy = (lax.axis_index(name) for name in ("z", "x", "core", "head"))
    zx = nz * nx
    every, chips = ("z", "x", "core", "head"), ("z", "x", "head")
    devices, chip_count = 4 * zx, 2 * zx
    heads = 2 * zx
    local = heads * DH // 2
    share = qkv_weight.shape[0]
    hidden_share = proj_weight.shape[0]
    hidden_half = hidden_share * chip_count

    inputs = block_input.astype(f32)
    normed_one, inverse_one = normalize(inputs)
    n1 = normed_one.astype(bf16)
    gain_one = norm1_gain.astype(f32)
    shift_one = norm1_shift.astype(f32)
    raw_qkv = qkv_weight.astype(f32)
    scaled_qkv = (raw_qkv * gain_one[:, None]).astype(bf16)
    device = ((iz * nx + ix) * 2 + ic) * 2 + iy
    offset = jnp.sum(raw_qkv * shift_one[:, None], axis=0)
    zero = jnp.zeros((width,), f32)
    place = device * share
    offset = offset + jnp.concatenate(
        [
            lax.dynamic_update_slice(zero, q_bias.astype(f32), (place,)),
            zero,
            lax.dynamic_update_slice(zero, v_bias.astype(f32), (place,)),
        ]
    )
    high, low = split_float(offset)
    to_heads = jnp.concatenate([scaled_qkv, high[None], low[None], jnp.zeros((6, 3 * width), bf16)], axis=0)
    to_heads = to_heads.reshape(share + 8, 3, heads, DH).transpose(2, 0, 1, 3).reshape(heads, 1, share + 8, 3 * DH)
    to_heads = jnp.broadcast_to(to_heads, (heads, 2, share + 8, 3 * DH)).reshape(devices, share + 8, 3 * DH)
    head_rows = lax.all_to_all(to_heads, every, split_axis=0, concat_axis=0, tiled=True)
    head_weight = head_rows[:, :share].reshape(width, 3 * DH)
    head_offset = jnp.sum(head_rows[:, share : share + 2].astype(f32), axis=(0, 1))

    near = lax.dynamic_index_in_dim(n1, iy, 0, keepdims=False)
    far = swap(lax.dynamic_index_in_dim(n1, 1 - iy, 0, keepdims=False), "head")
    a_z = jnp.stack([near] + shifted(near, nz))
    a_x = swap(a_z, "x")
    b_x = jnp.stack([far, swap(far, "x")])
    b_z = [b_x] + shifted(b_x, nz)
    pieces, owners = [], []

    def add(piece, dz, dx, dy):
        pieces.append(piece.reshape(-1, width))
        owners.append((dz, dx, dy))

    def add_all(flip):
        pick = (lambda v: swap(v, "core")) if flip else (lambda v: v)
        core = 1 - ic if flip else ic
        for dx, part in enumerate((a_z, a_x)):
            pieces.append(pick(part).reshape(-1, width))
            owners.extend((dz, dx, core, 0) for dz in range(nz))
        for dz, part in enumerate(b_z):
            pieces.append(pick(part).reshape(-1, width))
            owners.extend((dz, dx, core, 1) for dx in range(nx))

    add_all(False)
    add_all(True)
    slot_device = jnp.stack(
        [
            (((iz - dz) % nz * nx + (ix + dx) % nx) * 2 + core) * 2 + (iy + dy) % 2
            for dz, dx, core, dy in owners
        ]
    ).astype(jnp.int32)
    my_dealt = lax.dynamic_index_in_dim(dealt, iy, 0, keepdims=False)
    order = my_dealt.reshape(devices, rows)[:, 0] // RUN
    slot_of = jnp.sum(
        jnp.where(jnp.arange(devices)[:, None] == slot_device[None, :], jnp.arange(devices)[None, :], 0), axis=1
    )
    inloc = run_table(order, (slot_of * 2).astype(jnp.int32))
    ids = jnp.arange(devices, dtype=jnp.int32)
    id_y, id_c, id_zx = ids % 2, ids // 2 % 2, ids // 4
    send_pair = (id_zx * 2 + id_y) * 2 + (id_c ^ ic)
    outloc = run_table(order, (send_pair * 2).astype(jnp.int32))
    bound = lax.dynamic_index_in_dim(lengths, iy, 0, keepdims=False)[:1]

    fc_parts = fc_weight.reshape(share, zx, 2, 2, hidden_share)

    def core_columns(values, index):
        return lax.dynamic_index_in_dim(values, index, 2, keepdims=False)

    fc_mine = core_columns(fc_parts, ic).reshape(share, hidden_half)
    fc_other = swap(core_columns(fc_parts, 1 - ic).reshape(share, hidden_half), "core")
    fc_pair = in_order(fc_mine, fc_other, ic, 0).reshape(2 * share, hidden_half)
    small = jnp.stack([norm2_gain, norm2_shift, out_bias, proj_bias])
    small_pair = in_order(small, swap(small, "core"), ic, 0).reshape(8 * share)
    small_row = jnp.concatenate(
        [small_pair, fc_bias, jnp.zeros((8 * width - 8 * share - hidden_share,), bf16)]
    ).reshape(8, width)
    folds = hidden_half // width
    fc_folded = fc_pair.reshape(2 * share, folds, width).transpose(1, 0, 2).reshape(-1, width)
    packed = jnp.concatenate([out_weight, proj_weight, fc_folded, small_row], axis=0)
    gathered = lax.all_gather(packed, chips, axis=0)
    out_rows = share
    proj_rows = hidden_share
    fc_rows = 2 * share * folds
    w_out = gathered[:, :out_rows].reshape(local, width)
    w_proj = gathered[:, out_rows : out_rows + proj_rows].reshape(hidden_half, width)
    w_fc = gathered[:, out_rows + proj_rows : out_rows + proj_rows + fc_rows]
    w_fc = w_fc.reshape(zx, 2, folds, 2, share, width).transpose(0, 3, 1, 4, 2, 5).reshape(width, hidden_half)
    smalls = gathered[:, out_rows + proj_rows + fc_rows :].reshape(chip_count, 8 * width)
    vectors = smalls[:, : 8 * share].astype(f32).reshape(zx, 2, 2, 4, share)
    vectors = vectors.transpose(3, 0, 2, 1, 4).reshape(4, width)
    gain_two, shift_two, b_out, b_proj = vectors[0], vectors[1], vectors[2], vectors[3]
    b_fc = smalls[:, 8 * share : 8 * share + hidden_share].astype(f32).reshape(hidden_half)

    qkv_parts = scaled_qkv.reshape(share, 3, zx, 2, DH).transpose(0, 2, 1, 3, 4)

    def core_heads(index):
        return lax.dynamic_index_in_dim(qkv_parts, index, 3, keepdims=False).reshape(share, 3 * local)

    qkv_pair = in_order(core_heads(ic), swap(core_heads(1 - ic), "core"), ic, 0)
    packed_qkv, gathered, head_rows = lax.optimization_barrier((qkv_pair, gathered, head_rows))
    w_qkv = lax.all_gather(packed_qkv, chips, axis=0)
    w_qkv = w_qkv.reshape(zx, 2, 2, share, 3 * local).transpose(0, 2, 1, 3, 4).reshape(width, 3 * local)

    mixed = [(product(piece, head_weight) + head_offset).astype(bf16) for piece in pieces]
    slots = jnp.concatenate(mixed, axis=0)
    attn_send, queries, keys, values, attn_t, lse = attend_forward(bound, inloc, outloc, slots, chip_count, DH)

    x_all = jnp.stack([block_input, swap(block_input, "core")]).reshape(-1, width)
    g_all = jnp.stack([out_grad, swap(out_grad, "core")]).reshape(-1, width)
    own = micro * rows
    grad_hidden = product_nt(g_all, w_proj)

    attn_got = lax.all_to_all(attn_send, chips, split_axis=0, concat_axis=0, tiled=True)
    attn_in = attn_got.reshape(zx, 2, DH, 2, rows).transpose(0, 2, 3, 1, 4).reshape(local, 2 * own)

    def share_sum(part):
        sent = part.astype(bf16)
        first = swap(sent[own:], "core")
        second = swap(sent[:own], "core")
        return part + jnp.concatenate([first, second], axis=0).astype(f32)

    resid = x_all.astype(f32) + share_sum(product_tn(attn_in, w_out)) + b_out
    normed_two, inverse_two = normalize(resid)
    act_two = (normed_two * gain_two + shift_two).astype(bf16)
    pre = product(act_two, w_fc) + b_fc
    hidden, gelu_back = jax.vjp(gelu_tanh, pre)
    hidden = hidden.astype(bf16)
    projected = product(hidden, w_proj)
    project_other = swap(projected[own:].astype(bf16), "core")
    output = (resid[:own] + projected[:own] + project_other.astype(f32) + b_proj).astype(bf16)

    grad_pre = gelu_back(grad_hidden)[0].astype(bf16)
    grad_proj_w = product_tn(hidden, g_all).astype(bf16)
    grad_fc_w = product_tn(act_two, grad_pre).astype(bf16)
    grad_fc_b = jnp.sum(grad_pre.astype(f32), axis=0)
    grad_proj_b = jnp.sum(g_all.astype(f32), axis=0)
    grad_act_two = share_sum(product_nt(grad_pre, w_fc))
    grad_gain_two = jnp.sum(grad_act_two * normed_two, axis=0)
    grad_shift_two = jnp.sum(grad_act_two, axis=0)
    grad_resid = g_all.astype(f32) + norm_back(grad_act_two * gain_two, normed_two, inverse_two)
    grad_branch = grad_resid.astype(bf16)
    grad_out_b = jnp.sum(grad_branch.astype(f32), axis=0)
    grad_out_w = product(attn_in, grad_branch).astype(bf16)
    grad_attn = product_nt(w_out, grad_branch).astype(bf16)

    sums = jnp.stack([grad_gain_two, grad_shift_two, grad_out_b, grad_proj_b]).reshape(4, zx, 2, 2, share)
    sums = lax.dynamic_index_in_dim(sums, ic, 2, keepdims=False).transpose(1, 2, 0, 3).reshape(chip_count, 4 * share)
    sums = jnp.concatenate([sums, grad_fc_b.reshape(chip_count, hidden_share)], axis=1)
    high, low = split_float(sums)
    extra = jnp.stack([high, low], axis=1)
    extra = jnp.pad(extra, ((0, 0), (0, 6), (0, 2 * rows - extra.shape[2])))
    grad_send = grad_attn.reshape(zx, DH, 2, 2, rows).transpose(0, 3, 1, 2, 4).reshape(chip_count, DH, 2 * rows)
    grad_got = lax.all_to_all(
        jnp.concatenate([grad_send, extra], axis=1), chips, split_axis=0, concat_axis=0, tiled=True
    )
    grad_heads = grad_got[:, :DH]
    vector_sums = jnp.sum(grad_got[:, DH : DH + 2].astype(f32), axis=(0, 1))
    final_vectors = vector_sums[: 4 * share].reshape(4, share)
    final_fc_b = vector_sums[4 * share : 4 * share + hidden_share]

    final_proj_w = lax.psum_scatter(grad_proj_w, chips, scatter_dimension=0, tiled=True).astype(f32)
    fc_terms = grad_fc_w.reshape(zx, 2, 2, share, hidden_half).transpose(0, 2, 1, 3, 4).reshape(width, hidden_half)
    fc_sum = lax.psum_scatter(fc_terms, chips, scatter_dimension=0, tiled=True).reshape(2, share, hidden_half)
    final_out_w = lax.psum_scatter(grad_out_w, chips, scatter_dimension=0, tiled=True).astype(f32)
    fc_keep = lax.dynamic_index_in_dim(fc_sum, ic, 0, keepdims=False)
    fc_give = swap(lax.dynamic_index_in_dim(fc_sum, 1 - ic, 0, keepdims=False), "core")
    final_fc_w = in_order(
        fc_keep.reshape(share, zx, 2, hidden_share), fc_give.reshape(share, zx, 2, hidden_share), ic, 2
    )
    final_fc_w = final_fc_w.reshape(share, 2 * hidden_half).astype(f32)

    slot_grads, send_grads = attend_backward(
        bound, inloc, outloc, grad_heads, queries, keys, values, attn_t, lse
    )
    grads_got = lax.all_to_all(send_grads, chips, split_axis=0, concat_axis=0, tiled=True)

    count = 0
    raw_term = jnp.zeros((width, 3 * DH), f32)
    for piece in pieces:
        raw_term = raw_term + product_tn(piece, slot_grads[count : count + piece.shape[0]])
        count += piece.shape[0]
    column_sums = jnp.sum(slot_grads.astype(f32), axis=0)
    high, low = split_float(column_sums)
    tail = jnp.concatenate([high[None], low[None], jnp.zeros((6, 3 * DH), bf16)], axis=0)
    raw_send = jnp.concatenate(
        [
            raw_term.astype(bf16).reshape(devices, share, 3 * DH),
            jnp.broadcast_to(tail[None], (devices, 8, 3 * DH)),
        ],
        axis=1,
    )
    raw_got = lax.all_to_all(raw_send, every, split_axis=0, concat_axis=0, tiled=True)
    raw_sum = jnp.sum(raw_got.reshape(heads, 2, share + 8, 3 * DH).astype(f32), axis=1)
    raw_grad = raw_sum[:, :share].reshape(heads, share, 3, DH).transpose(1, 2, 0, 3).reshape(share, 3 * width)
    all_sums = (raw_sum[:, share] + raw_sum[:, share + 1]).reshape(heads, 3, DH).transpose(1, 0, 2)
    all_sums = all_sums.reshape(3 * width)
    final_qkv_w = raw_grad * gain_one[:, None] + shift_one[:, None] * all_sums[None, :]
    final_gain_one = jnp.sum(raw_grad * raw_qkv, axis=1)
    final_shift_one = jnp.sum(raw_qkv * all_sums[None, :], axis=1)
    final_q_b = lax.dynamic_slice(all_sums, (place,), (share,))
    final_v_b = lax.dynamic_slice(all_sums, (2 * width + place,), (share,))

    grads_in = grads_got.reshape(zx, 2, 3 * DH, 2, rows).transpose(0, 2, 3, 1, 4).reshape(3 * local, 2 * own)
    back = lax.dot_general(grads_in, w_qkv, (((0,), (1,)), ((), ())), preferred_element_type=f32)
    back_own = back[:own] + swap(back[own:].astype(bf16), "core").astype(f32)
    back_own = back_own.reshape(micro, rows, width)
    input_grad = grad_resid[:own].reshape(micro, rows, width) + norm_back(back_own, normed_one, inverse_one)

    return (
        output.reshape(micro, rows, width),
        input_grad.astype(bf16),
        final_qkv_w,
        final_q_b,
        final_v_b,
        final_out_w,
        final_vectors[2],
        final_gain_one,
        final_shift_one,
        final_vectors[0],
        final_vectors[1],
        final_fc_w,
        final_fc_b,
        final_proj_w,
        final_vectors[3],
    )


def specs(names):
    rows, vector, tokens = P(names, None), P(names), P(None, names, None)
    weights = (rows, vector, vector, rows, vector, vector, vector, vector, vector, rows, vector, rows, vector)
    return (tokens, *weights, tokens, P(), P()), (tokens, tokens, *weights)


def solution(mesh):
    sizes = dict(mesh.shape)
    if sizes["head"] == 2 and sizes["blk"] == 16:
        fine = Mesh(mesh.devices.reshape(2, 4, 2, 2), ("head", "z", "x", "core"))
        given, made = specs(("z", "x", "core", "head"))
        return jax.shard_map(fast_body, mesh=fine, in_specs=given, out_specs=made, check_vma=False)
    given, made = specs(("blk", "head"))
    return jax.shard_map(general_body, mesh=mesh, in_specs=given, out_specs=made, check_vma=False)
```

```python
import functools
import math

import jax
import jax.numpy as jnp
from jax import lax
from jax.experimental import pallas as pl
from jax.experimental.pallas import tpu as pltpu
from jax.sharding import Mesh
from jax.sharding import PartitionSpec as P

DH = 64


def gelu_tanh(values):
    inner = 0.7978845608028654 * (values + 0.044715 * values * values * values)
    return 0.5 * values * (1.0 + jnp.tanh(inner))


def normalize(values):
    centred = values - jnp.mean(values, axis=-1, keepdims=True)
    inverse = lax.rsqrt(jnp.mean(centred * centred, axis=-1, keepdims=True) + 1e-05)
    return (centred * inverse, inverse)


def norm_back(grad_normed, normed, inverse):
    return inverse * (
        grad_normed
        - jnp.mean(grad_normed, axis=-1, keepdims=True)
        - normed * jnp.mean(grad_normed * normed, axis=-1, keepdims=True)
    )


def product(left, right):
    return jnp.dot(left, right, preferred_element_type=jnp.float32)


def product_tn(left, right):
    return lax.dot_general(
        left, right, (((0,), (0,)), ((), ())), preferred_element_type=jnp.float32
    )


def product_nt(left, right):
    return lax.dot_general(
        left, right, (((1,), (1,)), ((), ())), preferred_element_type=jnp.float32
    )


def visible_pairs(query_pos, key_pos, boundary):
    same_side = (query_pos[:, None] >= boundary) == (key_pos[None, :] >= boundary)
    return same_side & (key_pos[None, :] <= query_pos[:, None])


def forward_tile(current, queries3, keys3, values3, visible, scale):
    running, total, accum = current
    scores = jnp.einsum("qhd,khd->hqk", queries3, keys3, preferred_element_type=jnp.float32) * scale
    scores = jnp.where(visible[None], scores, -1000000000.0)
    highest = jnp.maximum(running, jnp.max(scores, axis=-1))
    weights = jnp.where(visible[None], jnp.exp(scores - highest[..., None]), 0.0)
    factor = jnp.exp(running - highest)
    total = total * factor + jnp.sum(weights, axis=-1)
    accum = accum * factor[..., None] + jnp.einsum(
        "hqk,khd->hqd", weights.astype(jnp.bfloat16), values3, preferred_element_type=jnp.float32
    )
    return (highest, total, accum)


def general_forward(query_parts, pos_parts, positions, boundary, keys_group, values_group, key_span):
    heads_local, head_size = (query_parts[0].shape[1], query_parts[0].shape[2])
    scale = head_size ** (-0.5)

    def fold_keys(state, pieces, start):
        key_rows, value_rows = pieces
        count_rows = key_rows.shape[0]
        block_rows = math.gcd(count_rows, key_span)
        block_count = count_rows // block_rows

        def one_step(index, inner):
            offset = index * block_rows
            keys3 = lax.dynamic_slice_in_dim(key_rows, offset, block_rows).reshape(
                block_rows, heads_local, head_size
            )
            values3 = lax.dynamic_slice_in_dim(value_rows, offset, block_rows).reshape(
                block_rows, heads_local, head_size
            )
            key_pos = lax.dynamic_slice_in_dim(positions, offset, block_rows)
            part_queries = query_parts[0]
            visible = visible_pairs(pos_parts[0], key_pos, boundary)
            current = inner[0]
            result = forward_tile(current, part_queries, keys3, values3, visible, scale)
            updated = [result]
            return tuple(updated)

        return lax.fori_loop(0, block_count, one_step, state)

    initial = tuple(
        (
            (
                jnp.full((heads_local, part.shape[0]), -1000000000.0, jnp.float32),
                jnp.zeros((heads_local, part.shape[0]), jnp.float32),
                jnp.zeros((heads_local, part.shape[0], head_size), jnp.float32),
            )
            for part in query_parts
        )
    )
    return fold_keys(
        initial,
        (
            lax.all_gather(keys_group, "blk", axis=0, tiled=True),
            lax.all_gather(values_group, "blk", axis=0, tiled=True),
        ),
        jnp.int32(0),
    )


def backward_tile(current, queries3, grad3, log_total, delta, keys3, values3, visible, scale):
    grad_query, term = current
    scores = jnp.einsum("qhd,khd->hqk", queries3, keys3, preferred_element_type=jnp.float32) * scale
    scores = jnp.where(visible[None], scores, -1000000000.0)
    exact = jnp.where(visible[None], jnp.exp(scores - log_total[..., None]), 0.0)
    grad_probs = jnp.einsum("qhd,khd->hqk", grad3, values3, preferred_element_type=jnp.float32)
    grad_scores = (exact * (grad_probs - delta[..., None])).astype(jnp.bfloat16)
    grad_query = (
        grad_query
        + jnp.einsum("hqk,khd->hqd", grad_scores, keys3, preferred_element_type=jnp.float32) * scale
    )
    rounded = exact.astype(jnp.bfloat16)
    grad_values = jnp.einsum("hqk,qhd->khd", rounded, grad3, preferred_element_type=jnp.float32)
    grad_keys = (
        jnp.einsum("hqk,qhd->khd", grad_scores, queries3, preferred_element_type=jnp.float32)
        * scale
    )
    rows = keys3.shape[0]
    term = jnp.stack([grad_keys.reshape(rows, -1), grad_values.reshape(rows, -1)], axis=1)
    return (grad_query, term)


def general_backward(
    query_parts,
    grad_parts,
    total_parts,
    delta_parts,
    pos_parts,
    positions,
    boundary,
    keys_group,
    values_group,
    key_span,
    buffer_rows,
):
    heads_local, head_size = (query_parts[0].shape[1], query_parts[0].shape[2])
    scale = head_size ** (-0.5)

    def fold_keys(state, pieces, start):
        key_rows, value_rows = pieces
        count_rows = key_rows.shape[0]
        block_rows = math.gcd(count_rows, key_span)
        block_count = count_rows // block_rows

        def one_step(index, inner):
            offset = index * block_rows
            keys3 = lax.dynamic_slice_in_dim(key_rows, offset, block_rows).reshape(
                block_rows, heads_local, head_size
            )
            values3 = lax.dynamic_slice_in_dim(value_rows, offset, block_rows).reshape(
                block_rows, heads_local, head_size
            )
            key_pos = lax.dynamic_slice_in_dim(positions, offset, block_rows)
            grads_now, buffer = inner
            term = jnp.zeros((block_rows, 2, heads_local * head_size), jnp.float32)
            part_queries = query_parts[0]
            part_grads = grad_parts[0]
            part_total = total_parts[0]
            part_delta = delta_parts[0]
            visible = visible_pairs(pos_parts[0], key_pos, boundary)
            current = (grads_now[0], term)
            result = backward_tile(
                current,
                part_queries,
                part_grads,
                part_total,
                part_delta,
                keys3,
                values3,
                visible,
                scale,
            )
            updated = [result[0]]
            term = result[1]
            buffer = lax.dynamic_update_slice(buffer, term, (offset, 0, 0))
            return (tuple(updated), buffer)

        return lax.fori_loop(0, block_count, one_step, state)

    grads_init = tuple(
        (jnp.zeros((heads_local, part.shape[0], head_size), jnp.float32) for part in query_parts)
    )
    initial = (grads_init, jnp.zeros((buffer_rows, 2, heads_local * head_size), jnp.float32))
    return fold_keys(
        initial,
        (
            lax.all_gather(keys_group, "blk", axis=0, tiled=True),
            lax.all_gather(values_group, "blk", axis=0, tiled=True),
        ),
        jnp.int32(0),
    )


def general_body(
    block_input,
    qkv_weight,
    q_bias,
    v_bias,
    out_weight,
    out_bias,
    norm1_gain,
    norm1_shift,
    norm2_gain,
    norm2_shift,
    fc_weight,
    fc_bias,
    proj_weight,
    proj_bias,
    out_grad,
    dealt,
    lengths,
):
    micro_count, local_rows, width = block_input.shape
    head_devices = lax.axis_size("head")
    blk_devices = lax.axis_size("blk")
    group = local_rows * head_devices
    blk_index = lax.axis_index("blk")
    head_size = DH
    key_span = 1024
    part_count = group // group
    shards = (
        qkv_weight,
        q_bias,
        v_bias,
        out_weight,
        out_bias,
        norm1_gain,
        norm1_shift,
        norm2_gain,
        norm2_shift,
        fc_weight,
        fc_bias,
        proj_weight,
        proj_bias,
    )
    totals = [
        jnp.zeros((shard.shape[0] * blk_devices * head_devices,) + shard.shape[1:], jnp.float32)
        for shard in shards
    ]
    outputs = []
    input_grads = []
    for micro_index in range(micro_count):
        whole = (
            lax.all_gather(shards[0], ("blk", "head"), axis=0, tiled=True),
            lax.all_gather(shards[1], ("blk", "head"), axis=0, tiled=True),
            lax.all_gather(shards[2], ("blk", "head"), axis=0, tiled=True),
            lax.all_gather(shards[3], ("blk", "head"), axis=0, tiled=True),
            lax.all_gather(shards[4], ("blk", "head"), axis=0, tiled=True),
            lax.all_gather(shards[5], ("blk", "head"), axis=0, tiled=True),
            lax.all_gather(shards[6], ("blk", "head"), axis=0, tiled=True),
            lax.all_gather(shards[7], ("blk", "head"), axis=0, tiled=True),
            lax.all_gather(shards[8], ("blk", "head"), axis=0, tiled=True),
            lax.all_gather(shards[9], ("blk", "head"), axis=0, tiled=True),
            lax.all_gather(shards[10], ("blk", "head"), axis=0, tiled=True),
            lax.all_gather(shards[11], ("blk", "head"), axis=0, tiled=True),
            lax.all_gather(shards[12], ("blk", "head"), axis=0, tiled=True),
        )
        (
            w_qkv,
            b_query,
            b_value,
            w_out,
            b_out,
            gain_one,
            shift_one,
            gain_two,
            shift_two,
            w_fc,
            b_fc,
            w_proj,
            b_proj,
        ) = whole
        b_query = b_query.astype(jnp.float32)
        b_value = b_value.astype(jnp.float32)
        b_out = b_out.astype(jnp.float32)
        gain_one = gain_one.astype(jnp.float32)
        shift_one = shift_one.astype(jnp.float32)
        gain_two = gain_two.astype(jnp.float32)
        shift_two = shift_two.astype(jnp.float32)
        b_fc = b_fc.astype(jnp.float32)
        b_proj = b_proj.astype(jnp.float32)
        positions = dealt[micro_index]
        boundary = lengths[micro_index, 0]
        query_pos = lax.dynamic_slice_in_dim(positions, blk_index * group, group)
        inputs = block_input[micro_index].astype(jnp.float32)
        normed_one, inverse_one = normalize(inputs)
        act_one = (normed_one * gain_one + shift_one).astype(jnp.bfloat16)
        mixed = product(act_one, w_qkv)
        queries = (mixed[:, :width] + b_query).astype(jnp.bfloat16)
        keys = mixed[:, width : 2 * width].astype(jnp.bfloat16)
        values = (mixed[:, 2 * width :] + b_value).astype(jnp.bfloat16)
        heads_in = lax.all_to_all(
            jnp.stack([queries, keys, values], axis=1),
            "head",
            split_axis=2,
            concat_axis=0,
            tiled=True,
        )
        local_width = heads_in.shape[2]
        heads_local = local_width // head_size
        queries3 = heads_in[:, 0].reshape(group, heads_local, head_size)
        keys_group = heads_in[:, 1]
        values_group = heads_in[:, 2]
        query_parts = tuple((queries3 for index in range(part_count)))
        pos_parts = tuple((query_pos for index in range(part_count)))
        states = general_forward(
            query_parts, pos_parts, positions, boundary, keys_group, values_group, key_span
        )
        running = jnp.concatenate([state[0] for state in states], axis=1)
        total = jnp.concatenate([state[1] for state in states], axis=1)
        accum = jnp.concatenate([state[2] for state in states], axis=1)
        log_total = running + jnp.log(total)
        attn_heads = (
            (accum / total[..., None])
            .transpose(1, 0, 2)
            .reshape(group, local_width)
            .astype(jnp.bfloat16)
        )
        attended = lax.all_to_all(attn_heads, "head", split_axis=0, concat_axis=1, tiled=True)
        resid = inputs + product(attended, w_out) + b_out
        normed_two, inverse_two = normalize(resid)
        act_two = (normed_two * gain_two + shift_two).astype(jnp.bfloat16)
        pre = product(act_two, w_fc) + b_fc
        hidden = gelu_tanh(pre).astype(jnp.bfloat16)
        outputs.append((resid + product(hidden, w_proj) + b_proj).astype(jnp.bfloat16))
        cotangent = out_grad[micro_index]
        grad_proj_w = product_tn(hidden, cotangent)
        grad_proj_b = jnp.sum(cotangent.astype(jnp.float32), axis=0)
        grad_hidden = product_nt(cotangent, w_proj)
        grad_pre = jax.vjp(gelu_tanh, pre)[1](grad_hidden)[0].astype(jnp.bfloat16)
        grad_fc_w = product_tn(act_two, grad_pre)
        grad_fc_b = jnp.sum(grad_pre.astype(jnp.float32), axis=0)
        grad_act_two = product_nt(grad_pre, w_fc)
        grad_gain_two = jnp.sum(grad_act_two * normed_two, axis=0)
        grad_shift_two = jnp.sum(grad_act_two, axis=0)
        grad_resid = cotangent.astype(jnp.float32) + norm_back(
            grad_act_two * gain_two, normed_two, inverse_two
        )
        grad_branch = grad_resid.astype(jnp.bfloat16)
        grad_out_w = product_tn(attended, grad_branch)
        grad_out_b = jnp.sum(grad_branch.astype(jnp.float32), axis=0)
        grad_attn = product_nt(grad_branch, w_out).astype(jnp.bfloat16)
        grad_heads = lax.all_to_all(grad_attn, "head", split_axis=1, concat_axis=0, tiled=True)
        grad3 = grad_heads.reshape(group, heads_local, head_size)
        attn3 = attn_heads.reshape(group, heads_local, head_size)
        delta = jnp.sum(grad3.astype(jnp.float32) * attn3.astype(jnp.float32), axis=-1).T
        grad_parts = tuple((grad3 for index in range(part_count)))
        total_parts = tuple((log_total for index in range(part_count)))
        delta_parts = tuple((delta for index in range(part_count)))
        query_grads, buffer = general_backward(
            query_parts,
            grad_parts,
            total_parts,
            delta_parts,
            pos_parts,
            positions,
            boundary,
            keys_group,
            values_group,
            key_span,
            group * blk_devices,
        )
        kv_sums = lax.psum_scatter(buffer, "blk", scatter_dimension=0, tiled=True)
        grad_k_heads = kv_sums[:, 0].astype(jnp.bfloat16)
        grad_v_heads = kv_sums[:, 1].astype(jnp.bfloat16)
        grad_query = jnp.concatenate(list(query_grads), axis=1)
        grad_q_heads = (
            grad_query.transpose(1, 0, 2).reshape(group, local_width).astype(jnp.bfloat16)
        )
        grads_heads = jnp.stack([grad_q_heads, grad_k_heads, grad_v_heads], axis=1)
        back_tokens = lax.all_to_all(grads_heads, "head", split_axis=0, concat_axis=2, tiled=True)
        grad_mixed = back_tokens.reshape(local_rows, 3 * width)
        grad_qkv_w = product_tn(act_one, grad_mixed)
        grad_q_b = jnp.sum(back_tokens[:, 0].astype(jnp.float32), axis=0)
        grad_v_b = jnp.sum(back_tokens[:, 2].astype(jnp.float32), axis=0)
        grad_act_one = product_nt(grad_mixed, w_qkv)
        grad_gain_one = jnp.sum(grad_act_one * normed_one, axis=0)
        grad_shift_one = jnp.sum(grad_act_one, axis=0)
        input_grads.append(
            (grad_resid + norm_back(grad_act_one * gain_one, normed_one, inverse_one)).astype(
                jnp.bfloat16
            )
        )
        terms = (
            grad_qkv_w,
            grad_q_b,
            grad_v_b,
            grad_out_w,
            grad_out_b,
            grad_gain_one,
            grad_shift_one,
            grad_gain_two,
            grad_shift_two,
            grad_fc_w,
            grad_fc_b,
            grad_proj_w,
            grad_proj_b,
        )
        totals = [running_sum + term for running_sum, term in zip(totals, terms)]
    final = (
        lax.psum_scatter(totals[0], ("blk", "head"), scatter_dimension=0, tiled=True),
        lax.psum_scatter(totals[1], ("blk", "head"), scatter_dimension=0, tiled=True),
        lax.psum_scatter(totals[2], ("blk", "head"), scatter_dimension=0, tiled=True),
        lax.psum_scatter(totals[3], ("blk", "head"), scatter_dimension=0, tiled=True),
        lax.psum_scatter(totals[4], ("blk", "head"), scatter_dimension=0, tiled=True),
        lax.psum_scatter(totals[5], ("blk", "head"), scatter_dimension=0, tiled=True),
        lax.psum_scatter(totals[6], ("blk", "head"), scatter_dimension=0, tiled=True),
        lax.psum_scatter(totals[7], ("blk", "head"), scatter_dimension=0, tiled=True),
        lax.psum_scatter(totals[8], ("blk", "head"), scatter_dimension=0, tiled=True),
        lax.psum_scatter(totals[9], ("blk", "head"), scatter_dimension=0, tiled=True),
        lax.psum_scatter(totals[10], ("blk", "head"), scatter_dimension=0, tiled=True),
        lax.psum_scatter(totals[11], ("blk", "head"), scatter_dimension=0, tiled=True),
        lax.psum_scatter(totals[12], ("blk", "head"), scatter_dimension=0, tiled=True),
    )
    return (
        jnp.stack(outputs),
        jnp.stack(input_grads),
        final[0],
        final[1],
        final[2],
        final[3],
        final[4],
        final[5],
        final[6],
        final[7],
        final[8],
        final[9],
        final[10],
        final[11],
        final[12],
    )


RUN = 64
BLOCK = 512
NEG = -1000000000.0
VM = pltpu.VMEM
SM = pltpu.SMEM


def dot_nt(left, right):
    return lax.dot_general(left, right, (((1,), (1,)), ((), ())), preferred_element_type=jnp.float32)


def dot_nn(left, right):
    return lax.dot_general(left, right, (((1,), (0,)), ((), ())), preferred_element_type=jnp.float32)


def rows_at(index, size):
    return pl.ds(pl.multiple_of(index * size, size), size)


def first_block(start, bound):
    return jnp.where(start >= bound, bound // BLOCK, 0)


def forward_kernel(head_size, bound_ref, inloc, outloc, qkv, out, qs, ks, vs, attn_t, lse, vt, mixed):
    tokens = qkv.shape[0]
    runs = tokens // RUN
    scale = head_size ** (-0.5)
    bound = bound_ref[0]

    @pl.loop(0, runs)
    def _(run):
        rows = qkv[rows_at(inloc[run], RUN), :]
        here = rows_at(run, RUN)
        qs[here, :] = (rows[:, :head_size].astype(jnp.float32) * scale).astype(jnp.bfloat16)
        ks[here, :] = rows[:, head_size : 2 * head_size]
        vs[here, :] = rows[:, 2 * head_size :]

    @pl.loop(0, tokens // BLOCK)
    def _(block):
        here = rows_at(block, BLOCK)
        vt[:, here] = vs[here, :].astype(jnp.float32).T.astype(jnp.bfloat16)

    @pl.loop(0, tokens // BLOCK)
    def _(block):
        start = block * BLOCK
        here = rows_at(block, BLOCK)
        queries = qs[here, :]
        query_pos = start + lax.broadcasted_iota(jnp.int32, (1, BLOCK), 1)
        floor = jnp.where(query_pos >= bound, bound, 0)

        def scores_of(index, diagonal):
            keys = ks[rows_at(index, BLOCK), :]
            scores = dot_nt(keys, queries)
            key_pos = index * BLOCK + lax.broadcasted_iota(jnp.int32, (BLOCK, BLOCK), 0)
            visible = key_pos >= floor
            if diagonal:
                visible = visible & (key_pos <= query_pos)
            return jnp.where(visible, scores, NEG)

        scores = scores_of(block, True)
        highest = jnp.max(scores, axis=0, keepdims=True)
        weights = jnp.exp(scores - highest)
        total = jnp.sum(weights, axis=0, keepdims=True)
        accum = dot_nn(vt[:, here], weights.astype(jnp.bfloat16))

        def step(index, state):
            highest, total, accum = state
            scores = scores_of(index, False)
            higher = jnp.maximum(highest, jnp.max(scores, axis=0, keepdims=True))
            weights = jnp.exp(scores - higher)
            factor = jnp.exp(highest - higher)
            total = total * factor + jnp.sum(weights, axis=0, keepdims=True)
            accum = accum * factor + dot_nn(vt[:, rows_at(index, BLOCK)], weights.astype(jnp.bfloat16))
            return higher, total, accum

        highest, total, accum = lax.fori_loop(first_block(start, bound), block, step, (highest, total, accum))
        result = accum / total
        attn_t[:, here] = result.astype(jnp.bfloat16)
        lse[:, here] = highest + jnp.log(total)
        result = result.T.astype(jnp.bfloat16)
        for part in range(BLOCK // RUN):
            mixed[rows_at(outloc[block * (BLOCK // RUN) + part], RUN), :] = result[part * RUN : (part + 1) * RUN]

    chips, _, span = out.shape

    @pl.loop(0, chips)
    def _(chip):
        out[chip] = mixed[rows_at(chip, span), :].astype(jnp.float32).T.astype(jnp.bfloat16)


def attend_forward(bound, inloc, outloc, qkv, chips, head_size):
    tokens = qkv.shape[0]
    bf16 = jnp.bfloat16
    pairs = tokens * (tokens // 2)
    return pl.pallas_call(
        functools.partial(forward_kernel, head_size),
        out_shape=(
            jax.ShapeDtypeStruct((chips, head_size, tokens // chips), bf16),
            jax.ShapeDtypeStruct((tokens, head_size), bf16),
            jax.ShapeDtypeStruct((tokens, head_size), bf16),
            jax.ShapeDtypeStruct((tokens, head_size), bf16),
            jax.ShapeDtypeStruct((head_size, tokens), bf16),
            jax.ShapeDtypeStruct((1, tokens), jnp.float32),
        ),
        in_specs=[pl.BlockSpec(memory_space=SM)] * 3 + [pl.BlockSpec(memory_space=VM)],
        out_specs=[pl.BlockSpec(memory_space=VM)] * 6,
        scratch_shapes=[VM((head_size, tokens), bf16), VM((tokens, head_size), bf16)],
        compiler_params=pltpu.CompilerParams(vmem_limit_bytes=40 * 1024 * 1024),
        cost_estimate=pl.CostEstimate(flops=4 * 4 * pairs * head_size, bytes_accessed=tokens * 2048, transcendentals=pairs),
        name="attend_forward",
    )(bound, inloc, outloc, qkv)


def backward_kernel(
    head_size, bound_ref, inloc, outloc, grad_t, qs, ks, vs, attn_t, lse, slot_out, send_out, grads, kt, dk, dv, mixed, wide, moved
):
    tokens = qs.shape[0]
    runs = tokens // RUN
    scale = head_size ** (-0.5)
    bound = bound_ref[0]
    chips, _, span = grad_t.shape

    @pl.loop(0, chips)
    def _(chip):
        mixed[rows_at(chip, span), :] = grad_t[chip].astype(jnp.float32).T.astype(jnp.bfloat16)

    @pl.loop(0, runs)
    def _(run):
        grads[rows_at(run, RUN), :] = mixed[rows_at(outloc[run], RUN), :]

    @pl.loop(0, tokens // BLOCK)
    def _(block):
        here = rows_at(block, BLOCK)
        kt[:, here] = ks[here, :].astype(jnp.float32).T.astype(jnp.bfloat16)

    @pl.loop(0, tokens // BLOCK)
    def _(block):
        start = block * BLOCK
        here = rows_at(block, BLOCK)
        queries = qs[here, :]
        grad = grads[here, :]
        log_total = lse[:, here]
        delta = jnp.sum(grad.astype(jnp.float32).T * attn_t[:, here].astype(jnp.float32), axis=0, keepdims=True)
        query_pos = start + lax.broadcasted_iota(jnp.int32, (1, BLOCK), 1)
        floor = jnp.where(query_pos >= bound, bound, 0)

        def one(index, diagonal):
            there = rows_at(index, BLOCK)
            scores = dot_nt(ks[there, :], queries)
            key_pos = index * BLOCK + lax.broadcasted_iota(jnp.int32, (BLOCK, BLOCK), 0)
            visible = key_pos >= floor
            if diagonal:
                visible = visible & (key_pos <= query_pos)
            probs = jnp.where(visible, jnp.exp(scores - log_total), 0.0)
            grad_probs = dot_nt(vs[there, :], grad)
            grad_scores = (probs * (grad_probs - delta)).astype(jnp.bfloat16)
            return (
                dot_nn(probs.astype(jnp.bfloat16), grad),
                dot_nn(grad_scores, queries),
                dot_nn(kt[:, there], grad_scores),
                there,
            )

        grad_v, grad_k, grad_q, there = one(block, True)
        dv[there, :] = grad_v
        dk[there, :] = grad_k

        def step(index, grad_q):
            grad_v, grad_k, term, there = one(index, False)
            dv[there, :] += grad_v
            dk[there, :] += grad_k
            return grad_q + term

        grad_q = lax.fori_loop(first_block(start, bound), block, step, grad_q)
        wide[here, :head_size] = (grad_q.T * scale).astype(jnp.bfloat16)

    wide[:, head_size : 2 * head_size] = dk[...].astype(jnp.bfloat16)
    wide[:, 2 * head_size :] = dv[...].astype(jnp.bfloat16)

    @pl.loop(0, runs)
    def _(run):
        slot_out[rows_at(inloc[run], RUN), :] = wide[rows_at(run, RUN), :]

    @pl.loop(0, runs)
    def _(run):
        moved[rows_at(outloc[run], RUN), :] = wide[rows_at(run, RUN), :]

    @pl.loop(0, chips)
    def _(chip):
        send_out[chip] = moved[rows_at(chip, span), :].astype(jnp.float32).T.astype(jnp.bfloat16)


def attend_backward(bound, inloc, outloc, grad_t, qs, ks, vs, attn_t, lse):
    tokens, head_size = qs.shape
    chips = grad_t.shape[0]
    bf16 = jnp.bfloat16
    pairs = tokens * (tokens // 2)
    return pl.pallas_call(
        functools.partial(backward_kernel, head_size),
        out_shape=(
            jax.ShapeDtypeStruct((tokens, 3 * head_size), bf16),
            jax.ShapeDtypeStruct((chips, 3 * head_size, tokens // chips), bf16),
        ),
        in_specs=[pl.BlockSpec(memory_space=SM)] * 3 + [pl.BlockSpec(memory_space=VM)] * 6,
        out_specs=[pl.BlockSpec(memory_space=VM)] * 2,
        scratch_shapes=[
            VM((tokens, head_size), bf16),
            VM((head_size, tokens), bf16),
            VM((tokens, head_size), jnp.float32),
            VM((tokens, head_size), jnp.float32),
            VM((tokens, head_size), bf16),
            VM((tokens, 3 * head_size), bf16),
            VM((tokens, 3 * head_size), bf16),
        ],
        compiler_params=pltpu.CompilerParams(vmem_limit_bytes=48 * 1024 * 1024),
        cost_estimate=pl.CostEstimate(flops=4 * 10 * pairs * head_size, bytes_accessed=tokens * 4096, transcendentals=pairs),
        name="attend_backward",
    )(bound, inloc, outloc, grad_t, qs, ks, vs, attn_t, lse)


HALF_STEP = 512


def gelu_pair(values):
    cubic = values * values
    inner = 0.7978845608028654 * values * (1.0 + 0.044715 * cubic)
    bent = jnp.tanh(inner)
    slope = 0.7978845608028654 * (1.0 + 0.134145 * cubic)
    half = 0.5 * (1.0 + bent)
    return values * half, half + 0.5 * values * (1.0 - bent * bent) * slope


def load_rows(table, pieces, targets, sem, wait):
    slot = 0
    for piece in pieces:
        count = piece.shape[0]

        @pl.loop(0, count)
        def _(index, piece=piece, slot=slot):
            chip = table[0, slot + index]
            for rows, target in targets(chip):
                copy = pltpu.make_async_copy(piece.at[index, rows], target, sem)
                if wait:
                    copy.wait()
                else:
                    copy.start()

        slot += count


def project_kernel(count, table, got, *refs):
    pieces, (part_out, sent, attn_in, w_out, sem) = refs[:count], refs[count:]
    chips, size, span = got.shape
    share = w_out.shape[0] // chips
    rows = span // 2

    def targets(chip):
        return [(pl.ds(0, share), w_out.at[rows_at(chip, share)])]

    load_rows(table, pieces, targets, sem, False)
    for chip in range(chips):
        micro, head = divmod(chip, chips // 2)
        for rel in range(2):
            column = (rel * 2 + micro) * rows
            attn_in[head * size : (head + 1) * size, column : column + rows] = got[chip, :, rel * rows : (rel + 1) * rows]
    load_rows(table, pieces, targets, sem, True)
    left = attn_in[...].astype(jnp.float32).T.astype(jnp.bfloat16)
    part = dot_nn(left, w_out[...])
    part_out[...] = part
    sent[...] = part.astype(jnp.bfloat16)


def project(table, got, pieces, share):
    chips, size, span = got.shape
    width = pieces[0].shape[2]
    tokens = 2 * span
    bf16 = jnp.bfloat16
    return pl.pallas_call(
        functools.partial(project_kernel, len(pieces)),
        out_shape=(
            jax.ShapeDtypeStruct((tokens, width), jnp.float32),
            jax.ShapeDtypeStruct((tokens, width), bf16),
            jax.ShapeDtypeStruct((chips // 2 * size, tokens), bf16),
        ),
        in_specs=[pl.BlockSpec(memory_space=SM), pl.BlockSpec(memory_space=VM)]
        + [pl.BlockSpec(memory_space=pl.ANY)] * len(pieces),
        out_specs=[pl.BlockSpec(memory_space=VM)] * 3,
        scratch_shapes=[VM((chips * share, width), bf16), pltpu.SemaphoreType.DMA],
        compiler_params=pltpu.CompilerParams(vmem_limit_bytes=24 * 1024 * 1024),
        cost_estimate=pl.CostEstimate(
            flops=2 * tokens * chips * share * width, bytes_accessed=8 * tokens * width, transcendentals=0
        ),
        name="project",
    )(table, got, *pieces)


def middle_kernel(count, share, table, x_a, x_b, g_a, g_b, part, got_a, got_b, vectors, fc_bias, *refs):
    pieces = refs[:count]
    (resid, base, other, grad_act, grad_sent, fc_sums, terms) = refs[count : count + 7]
    (w_fc, w_proj, g_all, act, act_t, rest, proj_buf, fc_buf, load_sem, proj_sem, fc_sem) = refs[count + 7 :]
    f32, bf16 = jnp.float32, jnp.bfloat16
    tokens, width = part.shape
    own = tokens // 2
    hidden = w_proj.shape[0]
    chips = terms.shape[0]
    each = hidden // chips
    folds = hidden // width
    fc_row = share + each

    def targets(chip):
        wanted = [(pl.ds(share, each), w_proj.at[rows_at(chip, each)])]
        for fold in range(folds):
            for core in range(2):
                first = fc_row + (fold * 2 + core) * share
                place = ((chip // 2) * 2 + core) * 2 + chip % 2
                wanted.append(
                    (pl.ds(first, share), w_fc.at[rows_at(place, share), pl.ds(fold * width, width)])
                )
        return wanted

    load_rows(table, pieces, targets, load_sem, False)
    for half, (x_in, g_in, arrived) in enumerate(((x_a, g_a, got_a), (x_b, g_b, got_b))):
        here = slice(half * own, (half + 1) * own)
        g_all[here, :] = g_in[...]
        value = x_in[...].astype(f32) + part[here, :] + arrived[...].astype(f32) + vectors[2:3, :]
        resid[here, :] = value
        centred = value - jnp.mean(value, axis=-1, keepdims=True)
        inverse = lax.rsqrt(jnp.mean(centred * centred, axis=-1, keepdims=True) + 1e-05)
        rounded = (centred * inverse * vectors[0:1, :] + vectors[1:2, :]).astype(bf16)
        act[here, :] = rounded
        act_t[:, here] = rounded.astype(f32).T.astype(bf16)
    base[...] = resid[:own, :] + vectors[3:4, :]
    load_rows(table, pieces, targets, load_sem, True)

    per_step = HALF_STEP // each

    def copies(step, slot):
        made = []
        for index in range(per_step):
            made.append(
                pltpu.make_async_copy(
                    proj_buf.at[slot, pl.ds(index * each, each)],
                    terms.at[table[1, step * per_step + index], pl.ds(0, each)],
                    proj_sem.at[slot],
                )
            )
        fold = step // (width // HALF_STEP)
        column = pl.multiple_of(step % (width // HALF_STEP) * HALF_STEP, HALF_STEP)
        for chip in range(chips):
            for core in range(2):
                place = ((chip // 2) * 2 + core) * 2 + chip % 2
                made.append(
                    pltpu.make_async_copy(
                        fc_buf.at[slot, pl.ds(place * share, share)],
                        terms.at[
                            table[1, chip],
                            pl.ds(pl.multiple_of(each + share + (fold * 2 + core) * share, 16), share),
                            pl.ds(column, HALF_STEP),
                        ],
                        fc_sem.at[slot],
                    )
                )
        return made

    steps = hidden // HALF_STEP

    @pl.loop(0, steps)
    def _(step):
        slot = step % 2
        columns = pl.ds(pl.multiple_of(step * HALF_STEP, HALF_STEP), HALF_STEP)
        rows = rows_at(step, HALF_STEP)

        @pl.when(step >= 2)
        def _():
            for copy in copies(step - 2, slot):
                copy.wait()

        grads = g_all[...]
        value, slope = gelu_pair(dot_nn(act[...], w_fc[:, columns]) + fc_bias[:, columns])
        value = value.astype(bf16)
        proj_buf[slot] = dot_nn(value.astype(f32).T.astype(bf16), grads).astype(bf16)
        grad_pre = (dot_nt(grads, w_proj[rows, :]) * slope).astype(bf16)
        fc_sums[:, columns] = jnp.sum(grad_pre.astype(f32), axis=0, keepdims=True)
        fc_buf[slot] = dot_nn(act_t[...], grad_pre).astype(bf16)
        for copy in copies(step, slot):
            copy.start()
        projected = dot_nn(value, w_proj[rows, :])
        back = dot_nt(grad_pre, w_fc[:, columns])
        base[...] += projected[:own]

        @pl.when(step == 0)
        def _():
            grad_act[...] = back
            rest[...] = projected[own:]

        @pl.when(step > 0)
        def _():
            grad_act[...] += back
            rest[...] += projected[own:]

    other[...] = rest[...].astype(bf16)
    grad_sent[...] = grad_act[...].astype(bf16)
    for step in range(steps - 2, steps):
        for copy in copies(step, step % 2):
            copy.wait()


def middle(table, x_a, x_b, g_a, g_b, part, got_a, got_b, vectors, fc_bias, pieces, share):
    tokens, width = part.shape
    f32, bf16 = jnp.float32, jnp.bfloat16
    hidden = fc_bias.shape[1]
    chips = table.shape[1]
    each = hidden // chips
    rows = share + each + 2 * share * (hidden // width)
    shape = jax.ShapeDtypeStruct
    return pl.pallas_call(
        functools.partial(middle_kernel, len(pieces), share),
        out_shape=(
            shape((tokens, width), f32),
            shape((tokens // 2, width), f32),
            shape((tokens // 2, width), bf16),
            shape((tokens, width), f32),
            shape((tokens, width), bf16),
            shape((1, hidden), f32),
            shape((chips, rows, width), bf16),
        ),
        in_specs=[pl.BlockSpec(memory_space=SM)]
        + [pl.BlockSpec(memory_space=VM)] * 9
        + [pl.BlockSpec(memory_space=pl.ANY)] * len(pieces),
        out_specs=[pl.BlockSpec(memory_space=VM)] * 6 + [pl.BlockSpec(memory_space=pl.ANY)],
        scratch_shapes=[
            VM((width, hidden), bf16),
            VM((hidden, width), bf16),
            VM((tokens, width), bf16),
            VM((tokens, width), bf16),
            VM((width, tokens), bf16),
            VM((tokens // 2, width), f32),
            VM((2, HALF_STEP, width), bf16),
            VM((2, width, HALF_STEP), bf16),
            pltpu.SemaphoreType.DMA,
            pltpu.SemaphoreType.DMA((2,)),
            pltpu.SemaphoreType.DMA((2,)),
        ],
        compiler_params=pltpu.CompilerParams(vmem_limit_bytes=56 * 1024 * 1024),
        cost_estimate=pl.CostEstimate(
            flops=12 * tokens * width * hidden, bytes_accessed=8 * width * hidden, transcendentals=tokens * hidden
        ),
        name="middle",
    )(table, x_a, x_b, g_a, g_b, part, got_a, got_b, vectors, fc_bias, *pieces)


def branch_kernel(count, share, row, table, resid, g_a, g_b, part, got_a, got_b, vectors, fc_sums, attn_in, *refs):
    pieces = refs[:count]
    given, grad_resid, sent, terms, w_out, branch, products, load_sem, sem = refs[count:]
    f32, bf16 = jnp.float32, jnp.bfloat16
    tokens, width = resid.shape
    own = tokens // 2
    chips, size, span = sent.shape
    size -= 8
    rows = span // 2

    def targets(chip):
        return [(pl.ds(0, share), w_out.at[rows_at(chip, share)])]

    load_rows(table, pieces, targets, load_sem, False)
    gain_sum = jnp.zeros((1, width), f32)
    shift_sum = jnp.zeros((1, width), f32)
    bias_sum = jnp.zeros((1, width), f32)
    proj_sum = jnp.zeros((1, width), f32)
    for half, (g_in, arrived) in enumerate(((g_a, got_a), (g_b, got_b))):
        here = slice(half * own, (half + 1) * own)
        value = resid[here, :]
        centred = value - jnp.mean(value, axis=-1, keepdims=True)
        inverse = lax.rsqrt(jnp.mean(centred * centred, axis=-1, keepdims=True) + 1e-05)
        normed = centred * inverse
        grad = part[here, :] + arrived[...].astype(f32)
        gain_sum += jnp.sum(grad * normed, axis=0, keepdims=True)
        shift_sum += jnp.sum(grad, axis=0, keepdims=True)
        scaled = grad * vectors[0:1, :]
        given_grad = g_in[...].astype(f32)
        total = given_grad + inverse * (
            scaled
            - jnp.mean(scaled, axis=-1, keepdims=True)
            - normed * jnp.mean(scaled * normed, axis=-1, keepdims=True)
        )
        rounded = total.astype(bf16)
        bias_sum += jnp.sum(rounded.astype(f32), axis=0, keepdims=True)
        proj_sum += jnp.sum(given_grad, axis=0, keepdims=True)
        branch[here, :] = rounded
        if half == 0:
            grad_resid[...] = total
    load_rows(table, pieces, targets, load_sem, True)
    grads = dot_nt(w_out[...], branch[...]).astype(bf16)
    group = width // (chips // 2)
    sums = jnp.concatenate([gain_sum, shift_sum, bias_sum, proj_sum], axis=0)
    each = fc_sums.shape[1] // chips
    for chip in range(chips):
        micro, head = divmod(chip, chips // 2)
        for rel in range(2):
            column = (rel * 2 + micro) * rows
            sent[chip, :size, rel * rows : (rel + 1) * rows] = grads[
                head * size : (head + 1) * size, column : column + rows
            ]
        first = chip // 2 * group
        tail = jnp.concatenate(
            [
                sums[:, first : first + group],
                fc_sums[:, chip * each : (chip + 1) * each],
                jnp.zeros((3, group), f32),
            ],
            axis=0,
        )
        high = tail.astype(bf16)
        low = (tail - high.astype(f32)).astype(bf16)
        sent[chip, size:, :] = jnp.concatenate([high, low], axis=1)
    products[...] = dot_nn(attn_in[...], branch[...]).astype(bf16)

    @pl.loop(0, chips)
    def _(chip):
        pltpu.make_async_copy(products.at[rows_at(chip, share)], terms.at[table[1, chip], pl.ds(row, share)], sem).start()

    @pl.loop(0, chips)
    def _(chip):
        pltpu.make_async_copy(products.at[rows_at(chip, share)], terms.at[table[1, chip], pl.ds(row, share)], sem).wait()


def branch_back(table, resid, g_a, g_b, part, got_a, got_b, vectors, fc_sums, attn_in, pieces, terms, share, row, span):
    tokens, width = resid.shape
    f32, bf16 = jnp.float32, jnp.bfloat16
    chips = table.shape[1]
    size = attn_in.shape[0] // (chips // 2)
    shape = jax.ShapeDtypeStruct
    inputs = 10 + len(pieces)
    return pl.pallas_call(
        functools.partial(branch_kernel, len(pieces), share, row),
        out_shape=(
            shape((tokens // 2, width), f32),
            shape((chips, size + 8, span), bf16),
            shape(terms.shape, bf16),
        ),
        in_specs=[pl.BlockSpec(memory_space=SM)]
        + [pl.BlockSpec(memory_space=VM)] * 9
        + [pl.BlockSpec(memory_space=pl.ANY)] * (len(pieces) + 1),
        out_specs=[pl.BlockSpec(memory_space=VM)] * 2 + [pl.BlockSpec(memory_space=pl.ANY)],
        scratch_shapes=[
            VM((chips * share, width), bf16),
            VM((tokens, width), bf16),
            VM((chips * share, width), bf16),
            pltpu.SemaphoreType.DMA,
            pltpu.SemaphoreType.DMA,
        ],
        input_output_aliases={inputs: 2},
        compiler_params=pltpu.CompilerParams(vmem_limit_bytes=40 * 1024 * 1024),
        cost_estimate=pl.CostEstimate(
            flops=4 * tokens * chips * share * width, bytes_accessed=16 * tokens * width, transcendentals=0
        ),
        name="branch_back",
    )(table, resid, g_a, g_b, part, got_a, got_b, vectors, fc_sums, attn_in, *pieces, terms)


def finish_kernel(count, share, table, got, *refs):
    pieces, (kept, sent, weight, grads, sem) = refs[:count], refs[count:]
    chips, size, span = got.shape
    rows = span // 2
    own = kept.shape[0]

    def targets(chip):
        wanted = []
        for core in range(2):
            place = ((chip // 2) * 2 + core) * 2 + chip % 2
            wanted.append((pl.ds(core * share, share), weight.at[rows_at(place, share)]))
        return wanted

    load_rows(table, pieces, targets, sem, False)
    for chip in range(chips):
        micro, head = divmod(chip, chips // 2)
        for rel in range(2):
            column = (rel * 2 + micro) * rows
            grads[head * size : (head + 1) * size, column : column + rows] = got[chip, :, rel * rows : (rel + 1) * rows]
    load_rows(table, pieces, targets, sem, True)
    back = dot_nn(weight[...], grads[...])
    kept[...] = back[:, :own].T
    sent[...] = back[:, own:].T.astype(jnp.bfloat16)


def finish(table, got, pieces, share):
    chips, size, span = got.shape
    depth = pieces[0].shape[2]
    width = chips * 2 * share
    bf16 = jnp.bfloat16
    return pl.pallas_call(
        functools.partial(finish_kernel, len(pieces), share),
        out_shape=(
            jax.ShapeDtypeStruct((span, width), jnp.float32),
            jax.ShapeDtypeStruct((span, width), bf16),
        ),
        in_specs=[pl.BlockSpec(memory_space=SM), pl.BlockSpec(memory_space=VM)]
        + [pl.BlockSpec(memory_space=pl.ANY)] * len(pieces),
        out_specs=[pl.BlockSpec(memory_space=VM)] * 2,
        scratch_shapes=[VM((width, depth), bf16), VM((depth, 2 * span), bf16), pltpu.SemaphoreType.DMA],
        compiler_params=pltpu.CompilerParams(vmem_limit_bytes=32 * 1024 * 1024),
        cost_estimate=pl.CostEstimate(
            flops=4 * span * width * depth, bytes_accessed=2 * width * depth + 8 * span * width, transcendentals=0
        ),
        name="finish",
    )(table, got, *pieces)


PAIR = [(0, 1), (1, 0)]
NEAR = [(0, 1), (1, 0), (2, 3), (3, 2)]
FAR = [(0, 2), (2, 0), (1, 3), (3, 1)]


def swap(values, axis, pairs=PAIR):
    return lax.ppermute(values, axis, pairs)


def in_order(mine, other, index, axis):
    first = jnp.where(index == 0, mine, other)
    second = jnp.where(index == 0, other, mine)
    return jnp.stack([first, second], axis=axis)


def split_float(values):
    high = values.astype(jnp.bfloat16)
    low = (values - high.astype(jnp.float32)).astype(jnp.bfloat16)
    return high, low


def run_table(order, pair_start):
    pairs = order.shape[0]
    runs = jnp.arange(2 * pairs, dtype=jnp.int32)[:, None]
    low = jnp.where(runs == order[None, :], pair_start[None, :], 0)
    high = jnp.where(runs == 2 * pairs - 1 - order[None, :], pair_start[None, :] + 1, 0)
    return jnp.sum(low + high, axis=1).astype(jnp.int32)


def ring_order(count):
    half = [(z, (z + step) % 2) for z in range(count) for step in range(2)]
    up = [(z * 2) * 2 + y for z, y in half]
    down = [(z * 2 + 1) * 2 + y for z, y in reversed(half)]
    return up + down


def fast_body(
    block_input,
    qkv_weight,
    q_bias,
    v_bias,
    out_weight,
    out_bias,
    norm1_gain,
    norm1_shift,
    norm2_gain,
    norm2_shift,
    fc_weight,
    fc_bias,
    proj_weight,
    proj_bias,
    out_grad,
    dealt,
    lengths,
):
    f32, bf16 = jnp.float32, jnp.bfloat16
    micro, rows, width = block_input.shape
    nz, nx = lax.axis_size("z"), lax.axis_size("x")
    iz, ix, ic, iy = (lax.axis_index(name) for name in ("z", "x", "core", "head"))
    zx = nz * nx
    every, chips = ("z", "x", "core", "head"), ("z", "x", "head")
    devices, chip_count = 4 * zx, 2 * zx
    heads = 2 * zx
    local = heads * DH // 2
    share = qkv_weight.shape[0]
    hidden_share = proj_weight.shape[0]
    hidden_half = hidden_share * chip_count

    inputs = block_input.astype(f32)
    normed_one, inverse_one = normalize(inputs)
    n1 = normed_one.astype(bf16)
    gain_one = norm1_gain.astype(f32)
    shift_one = norm1_shift.astype(f32)
    raw_qkv = qkv_weight.astype(f32)
    scaled_qkv = (raw_qkv * gain_one[:, None]).astype(bf16)
    device = ((iz * nx + ix) * 2 + ic) * 2 + iy
    offset = jnp.sum(raw_qkv * shift_one[:, None], axis=0)
    zero = jnp.zeros((width,), f32)
    place = device * share
    offset = offset + jnp.concatenate(
        [
            lax.dynamic_update_slice(zero, q_bias.astype(f32), (place,)),
            zero,
            lax.dynamic_update_slice(zero, v_bias.astype(f32), (place,)),
        ]
    )
    high, low = split_float(offset)
    to_heads = jnp.concatenate([scaled_qkv, high[None], low[None], jnp.zeros((6, 3 * width), bf16)], axis=0)
    to_heads = to_heads.reshape(share + 8, 3, zx // 2, 2, 2, DH).transpose(2, 4, 3, 0, 1, 5)
    to_heads = to_heads.reshape(1, heads, share + 8, 3 * DH)
    to_heads = jnp.broadcast_to(to_heads, (2, heads, share + 8, 3 * DH)).reshape(devices, share + 8, 3 * DH)
    head_rows = lax.all_to_all(to_heads, every, split_axis=0, concat_axis=0, tiled=True)
    head_weight = head_rows[:, :share].reshape(width, 3 * DH)
    head_offset = jnp.sum(head_rows[:, share : share + 2].astype(f32), axis=(0, 1))

    mine = iz // 2
    near = lax.dynamic_index_in_dim(n1, mine, 0, keepdims=False)
    far = swap(lax.dynamic_index_in_dim(n1, 1 - mine, 0, keepdims=False), "z", FAR)
    near = jnp.stack([near, swap(near, "x")])
    near = jnp.stack([near, swap(near, "z", NEAR)])
    far = jnp.stack([far, swap(far, "head")])
    far = jnp.stack([far, swap(far, "z", NEAR)])
    parts = [near, swap(near, "head"), far, swap(far, "x")]
    pieces, owners = [], []

    def add_all(flip):
        core = 1 - ic if flip else ic
        for index, part in enumerate(parts):
            pieces.append((swap(part, "core") if flip else part).reshape(-1, width))
            for dz in range(2):
                for step in range(2):
                    dx, dy = (step, index) if index < 2 else (index - 2, step)
                    z = iz ^ dz if index < 2 else iz ^ dz ^ 2
                    owners.append((z, ix ^ dx, core, iy ^ dy))

    add_all(False)
    add_all(True)
    slot_device = jnp.stack([((z * nx + x) * 2 + core) * 2 + y for z, x, core, y in owners]).astype(jnp.int32)
    my_dealt = lax.dynamic_index_in_dim(dealt, mine, 0, keepdims=False)
    order = my_dealt.reshape(devices, rows)[:, 0] // RUN
    slot_of = jnp.sum(
        jnp.where(jnp.arange(devices)[:, None] == slot_device[None, :], jnp.arange(devices)[None, :], 0), axis=1
    )
    inloc = run_table(order, (slot_of * 2).astype(jnp.int32))
    ids = jnp.arange(devices, dtype=jnp.int32)
    id_y, id_c, id_zx = ids % 2, ids // 2 % 2, ids // 4
    send_pair = (id_zx * 2 + id_y) * 2 + (id_c ^ ic)
    outloc = run_table(order, (send_pair * 2).astype(jnp.int32))
    bound = lax.dynamic_index_in_dim(lengths, mine, 0, keepdims=False)[:1]

    fc_parts = fc_weight.reshape(share, zx, 2, 2, hidden_share)

    def core_columns(values, index):
        return lax.dynamic_index_in_dim(values, index, 2, keepdims=False)

    fc_mine = core_columns(fc_parts, ic).reshape(share, hidden_half)
    fc_other = swap(core_columns(fc_parts, 1 - ic).reshape(share, hidden_half), "core")
    fc_pair = in_order(fc_mine, fc_other, ic, 0).reshape(2 * share, hidden_half)
    small = jnp.stack([norm2_gain, norm2_shift, out_bias, proj_bias])
    small_pair = in_order(small, swap(small, "core"), ic, 0).reshape(8 * share)
    small_row = jnp.concatenate(
        [small_pair, fc_bias, jnp.zeros((8 * width - 8 * share - hidden_share,), bf16)]
    ).reshape(8, width)
    folds = hidden_half // width
    fc_folded = fc_pair.reshape(2 * share, folds, width).transpose(1, 0, 2).reshape(-1, width)
    packed = jnp.concatenate([out_weight, proj_weight, fc_folded, small_row], axis=0)
    ring = ring_order(nz)
    places = [ring.index(chip) for chip in range(chip_count)]
    table = jnp.array([ring, places], jnp.int32)
    gathered = lax.all_gather(packed, chips, axis=0, axis_index_groups=[ring])
    out_rows = share
    proj_rows = hidden_share
    fc_rows = 2 * share * folds

    qkv_parts = scaled_qkv.reshape(share, 3, zx, 2, DH).transpose(0, 2, 1, 3, 4)

    def core_heads(index):
        return lax.dynamic_index_in_dim(qkv_parts, index, 3, keepdims=False).reshape(share, 3 * local)

    qkv_pair = in_order(core_heads(ic), swap(core_heads(1 - ic), "core"), ic, 0)

    mixed = [(product(piece, head_weight) + head_offset).astype(bf16) for piece in pieces]
    slots = jnp.concatenate(mixed, axis=0)
    attn_send, queries, keys, values, attn_t, lse = attend_forward(bound, inloc, outloc, slots, chip_count, DH)

    x_a, x_b = block_input.reshape(-1, width), swap(block_input, "core").reshape(-1, width)
    g_a, g_b = out_grad.reshape(-1, width), swap(out_grad, "core").reshape(-1, width)
    own = micro * rows
    attn_got = lax.all_to_all(attn_send, chips, split_axis=0, concat_axis=0, tiled=True)
    gathered, qkv_pair, _ = lax.optimization_barrier((gathered, qkv_pair, lse))
    qkv_pair = qkv_pair.reshape(2 * share, 3 * local)
    w_qkv = lax.all_gather(qkv_pair, chips, axis=0, axis_index_groups=[ring])
    smalls = gathered[:, out_rows + proj_rows + fc_rows :].reshape(chip_count, 8 * width)
    smalls = jnp.stack([smalls[place] for place in places])
    vectors = smalls[:, : 8 * share].astype(f32).reshape(zx, 2, 2, 4, share)
    vectors = jnp.pad(vectors.transpose(3, 0, 2, 1, 4).reshape(4, width), ((0, 4), (0, 0)))
    b_fc = smalls[:, 8 * share : 8 * share + hidden_share].astype(f32).reshape(1, hidden_half)
    part, sent, attn_in = project(table, attn_got, [gathered], share)
    resid, base, project_other, grad_part, sent_back, fc_sums, terms = middle(
        table, x_a, x_b, g_a, g_b, part, swap(sent[own:], "core"), swap(sent[:own], "core"), vectors, b_fc, [gathered], share
    )
    grad_resid, grad_send, terms = branch_back(
        table,
        resid,
        g_a,
        g_b,
        grad_part,
        swap(sent_back[own:], "core"),
        swap(sent_back[:own], "core"),
        vectors,
        fc_sums,
        attn_in,
        [gathered],
        terms,
        share,
        proj_rows,
        2 * rows,
    )
    output = (base + swap(project_other, "core").astype(f32)).astype(bf16)

    grad_got = lax.all_to_all(grad_send, chips, split_axis=0, concat_axis=0, tiled=True)
    grad_heads = grad_got[:, :DH]
    vector_sums = jnp.sum(grad_got[:, DH:].astype(f32), axis=0)
    vector_sums = vector_sums[:, :rows] + vector_sums[:, rows:]
    final_vectors = lax.dynamic_slice(vector_sums, (0, (ic * 2 + iy) * share), (4, share))
    final_fc_b = vector_sums[4]

    summed = lax.psum_scatter(terms, chips, scatter_dimension=0, tiled=True, axis_index_groups=[ring])[0]
    final_proj_w = summed[:proj_rows].astype(f32)
    slot_grads, send_grads = attend_backward(
        bound, inloc, outloc, grad_heads, queries, keys, values, attn_t, lse
    )
    grads_got = lax.all_to_all(send_grads, chips, split_axis=0, concat_axis=0, tiled=True)

    count = 0
    raw_term = jnp.zeros((width, 3 * DH), f32)
    for piece in pieces:
        raw_term = raw_term + product_tn(piece, slot_grads[count : count + piece.shape[0]])
        count += piece.shape[0]
    column_sums = jnp.sum(slot_grads.astype(f32), axis=0)
    high, low = split_float(column_sums)
    tail = jnp.concatenate([high[None], low[None], jnp.zeros((6, 3 * DH), bf16)], axis=0)
    raw_rows = raw_term.astype(bf16).reshape(zx, 2, 2, share, 3 * DH).transpose(0, 2, 1, 3, 4)
    raw_send = jnp.concatenate(
        [
            raw_rows.reshape(chip_count, 2 * share, 3 * DH),
            jnp.broadcast_to(tail[None], (chip_count, 8, 3 * DH)),
        ],
        axis=1,
    )
    raw_send, grads_got = lax.optimization_barrier((raw_send, grads_got))
    final_out_w = summed[proj_rows : proj_rows + out_rows].astype(f32)
    fc_sum = summed[proj_rows + out_rows :].reshape(folds, 2, share, width)
    fc_keep = lax.dynamic_index_in_dim(fc_sum, ic, 1, keepdims=False)
    fc_give = swap(lax.dynamic_index_in_dim(fc_sum, 1 - ic, 1, keepdims=False), "core")

    def by_owner(values):
        return values.transpose(1, 0, 2).reshape(share, zx, 2, hidden_share)

    final_fc_w = in_order(by_owner(fc_keep), by_owner(fc_give), ic, 2).reshape(share, 2 * hidden_half).astype(f32)
    raw_got = lax.all_to_all(raw_send, chips, split_axis=0, concat_axis=0, tiled=True)
    raw_sum = jnp.sum(raw_got.reshape(2, zx, 2 * share + 8, 3 * DH).astype(f32), axis=0)
    raw_parts = raw_sum[:, : 2 * share].reshape(zx, 2, share, 3 * DH)
    sums_mine = raw_sum[:, 2 * share : 2 * share + 1] + raw_sum[:, 2 * share + 1 : 2 * share + 2]
    raw_keep = jnp.concatenate([lax.dynamic_index_in_dim(raw_parts, ic, 1, keepdims=False), sums_mine], axis=1)
    raw_give = jnp.concatenate([lax.dynamic_index_in_dim(raw_parts, 1 - ic, 1, keepdims=False), sums_mine], axis=1)
    raw_all = in_order(raw_keep, swap(raw_give, "core"), ic, 1).reshape(heads, share + 1, 3, DH)
    raw_all = raw_all.transpose(1, 2, 0, 3).reshape(share + 1, 3 * width)
    raw_grad, all_sums = raw_all[:share], raw_all[share]
    final_qkv_w = raw_grad * gain_one[:, None] + shift_one[:, None] * all_sums[None, :]
    final_gain_one = jnp.sum(raw_grad * raw_qkv, axis=1)
    final_shift_one = jnp.sum(raw_qkv * all_sums[None, :], axis=1)
    final_q_b = lax.dynamic_slice(all_sums, (place,), (share,))
    final_v_b = lax.dynamic_slice(all_sums, (2 * width + place,), (share,))

    back_own, back_other = finish(table, grads_got, [w_qkv], share)
    back_own = back_own + swap(back_other, "core").astype(f32)
    back_own = back_own.reshape(micro, rows, width)
    input_grad = grad_resid.reshape(micro, rows, width) + norm_back(back_own, normed_one, inverse_one)

    return (
        output.reshape(micro, rows, width),
        input_grad.astype(bf16),
        final_qkv_w,
        final_q_b,
        final_v_b,
        final_out_w,
        final_vectors[2],
        final_gain_one,
        final_shift_one,
        final_vectors[0],
        final_vectors[1],
        final_fc_w,
        final_fc_b,
        final_proj_w,
        final_vectors[3],
    )


def specs(names):
    rows, vector, tokens = P(names, None), P(names), P(None, names, None)
    weights = (rows, vector, vector, rows, vector, vector, vector, vector, vector, rows, vector, rows, vector)
    return (tokens, *weights, tokens, P(), P()), (tokens, tokens, *weights)


def solution(mesh):
    sizes = dict(mesh.shape)
    if sizes["head"] == 2 and sizes["blk"] == 16:
        fine = Mesh(mesh.devices.reshape(2, 4, 2, 2), ("head", "z", "x", "core"))
        given, made = specs(("z", "x", "core", "head"))
        return jax.shard_map(fast_body, mesh=fine, in_specs=given, out_specs=made, check_vma=False)
    given, made = specs(("blk", "head"))
    return jax.shard_map(general_body, mesh=mesh, in_specs=given, out_specs=made, check_vma=False)
```

```python
import functools
import math

import jax
import jax.numpy as jnp
from jax import lax
from jax.experimental import pallas as pl
from jax.experimental.pallas import tpu as pltpu
from jax.sharding import Mesh
from jax.sharding import PartitionSpec as P

DH = 64


def gelu_tanh(values):
    inner = 0.7978845608028654 * (values + 0.044715 * values * values * values)
    return 0.5 * values * (1.0 + jnp.tanh(inner))


def normalize(values):
    centred = values - jnp.mean(values, axis=-1, keepdims=True)
    inverse = lax.rsqrt(jnp.mean(centred * centred, axis=-1, keepdims=True) + 1e-05)
    return (centred * inverse, inverse)


def norm_back(grad_normed, normed, inverse):
    return inverse * (
        grad_normed
        - jnp.mean(grad_normed, axis=-1, keepdims=True)
        - normed * jnp.mean(grad_normed * normed, axis=-1, keepdims=True)
    )


def product(left, right):
    return jnp.dot(left, right, preferred_element_type=jnp.float32)


def product_tn(left, right):
    return lax.dot_general(
        left, right, (((0,), (0,)), ((), ())), preferred_element_type=jnp.float32
    )


def product_nt(left, right):
    return lax.dot_general(
        left, right, (((1,), (1,)), ((), ())), preferred_element_type=jnp.float32
    )


def visible_pairs(query_pos, key_pos, boundary):
    same_side = (query_pos[:, None] >= boundary) == (key_pos[None, :] >= boundary)
    return same_side & (key_pos[None, :] <= query_pos[:, None])


def forward_tile(current, queries3, keys3, values3, visible, scale):
    running, total, accum = current
    scores = jnp.einsum("qhd,khd->hqk", queries3, keys3, preferred_element_type=jnp.float32) * scale
    scores = jnp.where(visible[None], scores, -1000000000.0)
    highest = jnp.maximum(running, jnp.max(scores, axis=-1))
    weights = jnp.where(visible[None], jnp.exp(scores - highest[..., None]), 0.0)
    factor = jnp.exp(running - highest)
    total = total * factor + jnp.sum(weights, axis=-1)
    accum = accum * factor[..., None] + jnp.einsum(
        "hqk,khd->hqd", weights.astype(jnp.bfloat16), values3, preferred_element_type=jnp.float32
    )
    return (highest, total, accum)


def general_forward(query_parts, pos_parts, positions, boundary, keys_group, values_group, key_span):
    heads_local, head_size = (query_parts[0].shape[1], query_parts[0].shape[2])
    scale = head_size ** (-0.5)

    def fold_keys(state, pieces, start):
        key_rows, value_rows = pieces
        count_rows = key_rows.shape[0]
        block_rows = math.gcd(count_rows, key_span)
        block_count = count_rows // block_rows

        def one_step(index, inner):
            offset = index * block_rows
            keys3 = lax.dynamic_slice_in_dim(key_rows, offset, block_rows).reshape(
                block_rows, heads_local, head_size
            )
            values3 = lax.dynamic_slice_in_dim(value_rows, offset, block_rows).reshape(
                block_rows, heads_local, head_size
            )
            key_pos = lax.dynamic_slice_in_dim(positions, offset, block_rows)
            part_queries = query_parts[0]
            visible = visible_pairs(pos_parts[0], key_pos, boundary)
            current = inner[0]
            result = forward_tile(current, part_queries, keys3, values3, visible, scale)
            updated = [result]
            return tuple(updated)

        return lax.fori_loop(0, block_count, one_step, state)

    initial = tuple(
        (
            (
                jnp.full((heads_local, part.shape[0]), -1000000000.0, jnp.float32),
                jnp.zeros((heads_local, part.shape[0]), jnp.float32),
                jnp.zeros((heads_local, part.shape[0], head_size), jnp.float32),
            )
            for part in query_parts
        )
    )
    return fold_keys(
        initial,
        (
            lax.all_gather(keys_group, "blk", axis=0, tiled=True),
            lax.all_gather(values_group, "blk", axis=0, tiled=True),
        ),
        jnp.int32(0),
    )


def backward_tile(current, queries3, grad3, log_total, delta, keys3, values3, visible, scale):
    grad_query, term = current
    scores = jnp.einsum("qhd,khd->hqk", queries3, keys3, preferred_element_type=jnp.float32) * scale
    scores = jnp.where(visible[None], scores, -1000000000.0)
    exact = jnp.where(visible[None], jnp.exp(scores - log_total[..., None]), 0.0)
    grad_probs = jnp.einsum("qhd,khd->hqk", grad3, values3, preferred_element_type=jnp.float32)
    grad_scores = (exact * (grad_probs - delta[..., None])).astype(jnp.bfloat16)
    grad_query = (
        grad_query
        + jnp.einsum("hqk,khd->hqd", grad_scores, keys3, preferred_element_type=jnp.float32) * scale
    )
    rounded = exact.astype(jnp.bfloat16)
    grad_values = jnp.einsum("hqk,qhd->khd", rounded, grad3, preferred_element_type=jnp.float32)
    grad_keys = (
        jnp.einsum("hqk,qhd->khd", grad_scores, queries3, preferred_element_type=jnp.float32)
        * scale
    )
    rows = keys3.shape[0]
    term = jnp.stack([grad_keys.reshape(rows, -1), grad_values.reshape(rows, -1)], axis=1)
    return (grad_query, term)


def general_backward(
    query_parts,
    grad_parts,
    total_parts,
    delta_parts,
    pos_parts,
    positions,
    boundary,
    keys_group,
    values_group,
    key_span,
    buffer_rows,
):
    heads_local, head_size = (query_parts[0].shape[1], query_parts[0].shape[2])
    scale = head_size ** (-0.5)

    def fold_keys(state, pieces, start):
        key_rows, value_rows = pieces
        count_rows = key_rows.shape[0]
        block_rows = math.gcd(count_rows, key_span)
        block_count = count_rows // block_rows

        def one_step(index, inner):
            offset = index * block_rows
            keys3 = lax.dynamic_slice_in_dim(key_rows, offset, block_rows).reshape(
                block_rows, heads_local, head_size
            )
            values3 = lax.dynamic_slice_in_dim(value_rows, offset, block_rows).reshape(
                block_rows, heads_local, head_size
            )
            key_pos = lax.dynamic_slice_in_dim(positions, offset, block_rows)
            grads_now, buffer = inner
            term = jnp.zeros((block_rows, 2, heads_local * head_size), jnp.float32)
            part_queries = query_parts[0]
            part_grads = grad_parts[0]
            part_total = total_parts[0]
            part_delta = delta_parts[0]
            visible = visible_pairs(pos_parts[0], key_pos, boundary)
            current = (grads_now[0], term)
            result = backward_tile(
                current,
                part_queries,
                part_grads,
                part_total,
                part_delta,
                keys3,
                values3,
                visible,
                scale,
            )
            updated = [result[0]]
            term = result[1]
            buffer = lax.dynamic_update_slice(buffer, term, (offset, 0, 0))
            return (tuple(updated), buffer)

        return lax.fori_loop(0, block_count, one_step, state)

    grads_init = tuple(
        (jnp.zeros((heads_local, part.shape[0], head_size), jnp.float32) for part in query_parts)
    )
    initial = (grads_init, jnp.zeros((buffer_rows, 2, heads_local * head_size), jnp.float32))
    return fold_keys(
        initial,
        (
            lax.all_gather(keys_group, "blk", axis=0, tiled=True),
            lax.all_gather(values_group, "blk", axis=0, tiled=True),
        ),
        jnp.int32(0),
    )


def general_body(
    block_input,
    qkv_weight,
    q_bias,
    v_bias,
    out_weight,
    out_bias,
    norm1_gain,
    norm1_shift,
    norm2_gain,
    norm2_shift,
    fc_weight,
    fc_bias,
    proj_weight,
    proj_bias,
    out_grad,
    dealt,
    lengths,
):
    micro_count, local_rows, width = block_input.shape
    head_devices = lax.axis_size("head")
    blk_devices = lax.axis_size("blk")
    group = local_rows * head_devices
    blk_index = lax.axis_index("blk")
    head_size = DH
    key_span = 1024
    part_count = group // group
    shards = (
        qkv_weight,
        q_bias,
        v_bias,
        out_weight,
        out_bias,
        norm1_gain,
        norm1_shift,
        norm2_gain,
        norm2_shift,
        fc_weight,
        fc_bias,
        proj_weight,
        proj_bias,
    )
    totals = [
        jnp.zeros((shard.shape[0] * blk_devices * head_devices,) + shard.shape[1:], jnp.float32)
        for shard in shards
    ]
    outputs = []
    input_grads = []
    for micro_index in range(micro_count):
        whole = (
            lax.all_gather(shards[0], ("blk", "head"), axis=0, tiled=True),
            lax.all_gather(shards[1], ("blk", "head"), axis=0, tiled=True),
            lax.all_gather(shards[2], ("blk", "head"), axis=0, tiled=True),
            lax.all_gather(shards[3], ("blk", "head"), axis=0, tiled=True),
            lax.all_gather(shards[4], ("blk", "head"), axis=0, tiled=True),
            lax.all_gather(shards[5], ("blk", "head"), axis=0, tiled=True),
            lax.all_gather(shards[6], ("blk", "head"), axis=0, tiled=True),
            lax.all_gather(shards[7], ("blk", "head"), axis=0, tiled=True),
            lax.all_gather(shards[8], ("blk", "head"), axis=0, tiled=True),
            lax.all_gather(shards[9], ("blk", "head"), axis=0, tiled=True),
            lax.all_gather(shards[10], ("blk", "head"), axis=0, tiled=True),
            lax.all_gather(shards[11], ("blk", "head"), axis=0, tiled=True),
            lax.all_gather(shards[12], ("blk", "head"), axis=0, tiled=True),
        )
        (
            w_qkv,
            b_query,
            b_value,
            w_out,
            b_out,
            gain_one,
            shift_one,
            gain_two,
            shift_two,
            w_fc,
            b_fc,
            w_proj,
            b_proj,
        ) = whole
        b_query = b_query.astype(jnp.float32)
        b_value = b_value.astype(jnp.float32)
        b_out = b_out.astype(jnp.float32)
        gain_one = gain_one.astype(jnp.float32)
        shift_one = shift_one.astype(jnp.float32)
        gain_two = gain_two.astype(jnp.float32)
        shift_two = shift_two.astype(jnp.float32)
        b_fc = b_fc.astype(jnp.float32)
        b_proj = b_proj.astype(jnp.float32)
        positions = dealt[micro_index]
        boundary = lengths[micro_index, 0]
        query_pos = lax.dynamic_slice_in_dim(positions, blk_index * group, group)
        inputs = block_input[micro_index].astype(jnp.float32)
        normed_one, inverse_one = normalize(inputs)
        act_one = (normed_one * gain_one + shift_one).astype(jnp.bfloat16)
        mixed = product(act_one, w_qkv)
        queries = (mixed[:, :width] + b_query).astype(jnp.bfloat16)
        keys = mixed[:, width : 2 * width].astype(jnp.bfloat16)
        values = (mixed[:, 2 * width :] + b_value).astype(jnp.bfloat16)
        heads_in = lax.all_to_all(
            jnp.stack([queries, keys, values], axis=1),
            "head",
            split_axis=2,
            concat_axis=0,
            tiled=True,
        )
        local_width = heads_in.shape[2]
        heads_local = local_width // head_size
        queries3 = heads_in[:, 0].reshape(group, heads_local, head_size)
        keys_group = heads_in[:, 1]
        values_group = heads_in[:, 2]
        query_parts = tuple((queries3 for index in range(part_count)))
        pos_parts = tuple((query_pos for index in range(part_count)))
        states = general_forward(
            query_parts, pos_parts, positions, boundary, keys_group, values_group, key_span
        )
        running = jnp.concatenate([state[0] for state in states], axis=1)
        total = jnp.concatenate([state[1] for state in states], axis=1)
        accum = jnp.concatenate([state[2] for state in states], axis=1)
        log_total = running + jnp.log(total)
        attn_heads = (
            (accum / total[..., None])
            .transpose(1, 0, 2)
            .reshape(group, local_width)
            .astype(jnp.bfloat16)
        )
        attended = lax.all_to_all(attn_heads, "head", split_axis=0, concat_axis=1, tiled=True)
        resid = inputs + product(attended, w_out) + b_out
        normed_two, inverse_two = normalize(resid)
        act_two = (normed_two * gain_two + shift_two).astype(jnp.bfloat16)
        pre = product(act_two, w_fc) + b_fc
        hidden = gelu_tanh(pre).astype(jnp.bfloat16)
        outputs.append((resid + product(hidden, w_proj) + b_proj).astype(jnp.bfloat16))
        cotangent = out_grad[micro_index]
        grad_proj_w = product_tn(hidden, cotangent)
        grad_proj_b = jnp.sum(cotangent.astype(jnp.float32), axis=0)
        grad_hidden = product_nt(cotangent, w_proj)
        grad_pre = jax.vjp(gelu_tanh, pre)[1](grad_hidden)[0].astype(jnp.bfloat16)
        grad_fc_w = product_tn(act_two, grad_pre)
        grad_fc_b = jnp.sum(grad_pre.astype(jnp.float32), axis=0)
        grad_act_two = product_nt(grad_pre, w_fc)
        grad_gain_two = jnp.sum(grad_act_two * normed_two, axis=0)
        grad_shift_two = jnp.sum(grad_act_two, axis=0)
        grad_resid = cotangent.astype(jnp.float32) + norm_back(
            grad_act_two * gain_two, normed_two, inverse_two
        )
        grad_branch = grad_resid.astype(jnp.bfloat16)
        grad_out_w = product_tn(attended, grad_branch)
        grad_out_b = jnp.sum(grad_branch.astype(jnp.float32), axis=0)
        grad_attn = product_nt(grad_branch, w_out).astype(jnp.bfloat16)
        grad_heads = lax.all_to_all(grad_attn, "head", split_axis=1, concat_axis=0, tiled=True)
        grad3 = grad_heads.reshape(group, heads_local, head_size)
        attn3 = attn_heads.reshape(group, heads_local, head_size)
        delta = jnp.sum(grad3.astype(jnp.float32) * attn3.astype(jnp.float32), axis=-1).T
        grad_parts = tuple((grad3 for index in range(part_count)))
        total_parts = tuple((log_total for index in range(part_count)))
        delta_parts = tuple((delta for index in range(part_count)))
        query_grads, buffer = general_backward(
            query_parts,
            grad_parts,
            total_parts,
            delta_parts,
            pos_parts,
            positions,
            boundary,
            keys_group,
            values_group,
            key_span,
            group * blk_devices,
        )
        kv_sums = lax.psum_scatter(buffer, "blk", scatter_dimension=0, tiled=True)
        grad_k_heads = kv_sums[:, 0].astype(jnp.bfloat16)
        grad_v_heads = kv_sums[:, 1].astype(jnp.bfloat16)
        grad_query = jnp.concatenate(list(query_grads), axis=1)
        grad_q_heads = (
            grad_query.transpose(1, 0, 2).reshape(group, local_width).astype(jnp.bfloat16)
        )
        grads_heads = jnp.stack([grad_q_heads, grad_k_heads, grad_v_heads], axis=1)
        back_tokens = lax.all_to_all(grads_heads, "head", split_axis=0, concat_axis=2, tiled=True)
        grad_mixed = back_tokens.reshape(local_rows, 3 * width)
        grad_qkv_w = product_tn(act_one, grad_mixed)
        grad_q_b = jnp.sum(back_tokens[:, 0].astype(jnp.float32), axis=0)
        grad_v_b = jnp.sum(back_tokens[:, 2].astype(jnp.float32), axis=0)
        grad_act_one = product_nt(grad_mixed, w_qkv)
        grad_gain_one = jnp.sum(grad_act_one * normed_one, axis=0)
        grad_shift_one = jnp.sum(grad_act_one, axis=0)
        input_grads.append(
            (grad_resid + norm_back(grad_act_one * gain_one, normed_one, inverse_one)).astype(
                jnp.bfloat16
            )
        )
        terms = (
            grad_qkv_w,
            grad_q_b,
            grad_v_b,
            grad_out_w,
            grad_out_b,
            grad_gain_one,
            grad_shift_one,
            grad_gain_two,
            grad_shift_two,
            grad_fc_w,
            grad_fc_b,
            grad_proj_w,
            grad_proj_b,
        )
        totals = [running_sum + term for running_sum, term in zip(totals, terms)]
    final = (
        lax.psum_scatter(totals[0], ("blk", "head"), scatter_dimension=0, tiled=True),
        lax.psum_scatter(totals[1], ("blk", "head"), scatter_dimension=0, tiled=True),
        lax.psum_scatter(totals[2], ("blk", "head"), scatter_dimension=0, tiled=True),
        lax.psum_scatter(totals[3], ("blk", "head"), scatter_dimension=0, tiled=True),
        lax.psum_scatter(totals[4], ("blk", "head"), scatter_dimension=0, tiled=True),
        lax.psum_scatter(totals[5], ("blk", "head"), scatter_dimension=0, tiled=True),
        lax.psum_scatter(totals[6], ("blk", "head"), scatter_dimension=0, tiled=True),
        lax.psum_scatter(totals[7], ("blk", "head"), scatter_dimension=0, tiled=True),
        lax.psum_scatter(totals[8], ("blk", "head"), scatter_dimension=0, tiled=True),
        lax.psum_scatter(totals[9], ("blk", "head"), scatter_dimension=0, tiled=True),
        lax.psum_scatter(totals[10], ("blk", "head"), scatter_dimension=0, tiled=True),
        lax.psum_scatter(totals[11], ("blk", "head"), scatter_dimension=0, tiled=True),
        lax.psum_scatter(totals[12], ("blk", "head"), scatter_dimension=0, tiled=True),
    )
    return (
        jnp.stack(outputs),
        jnp.stack(input_grads),
        final[0],
        final[1],
        final[2],
        final[3],
        final[4],
        final[5],
        final[6],
        final[7],
        final[8],
        final[9],
        final[10],
        final[11],
        final[12],
    )


RUN = 64
BLOCK = 512
NEG = -1000000000.0
VM = pltpu.VMEM
SM = pltpu.SMEM


def dot_nt(left, right):
    return lax.dot_general(left, right, (((1,), (1,)), ((), ())), preferred_element_type=jnp.float32)


def dot_nn(left, right):
    return lax.dot_general(left, right, (((1,), (0,)), ((), ())), preferred_element_type=jnp.float32)


def rows_at(index, size):
    return pl.ds(pl.multiple_of(index * size, size), size)


def first_block(start, bound):
    return jnp.where(start >= bound, bound // BLOCK, 0)


def forward_kernel(head_size, bound_ref, inloc, outloc, qkv, out, qs, ks, vs, attn_t, lse, vt, mixed):
    tokens = qkv.shape[0]
    runs = tokens // RUN
    scale = head_size ** (-0.5)
    bound = bound_ref[0]

    @pl.loop(0, runs)
    def _(run):
        rows = qkv[rows_at(inloc[run], RUN), :]
        here = rows_at(run, RUN)
        qs[here, :] = (rows[:, :head_size].astype(jnp.float32) * scale).astype(jnp.bfloat16)
        ks[here, :] = rows[:, head_size : 2 * head_size]
        vs[here, :] = rows[:, 2 * head_size :]

    @pl.loop(0, tokens // BLOCK)
    def _(block):
        here = rows_at(block, BLOCK)
        vt[:, here] = vs[here, :].astype(jnp.float32).T.astype(jnp.bfloat16)

    @pl.loop(0, tokens // BLOCK)
    def _(block):
        start = block * BLOCK
        here = rows_at(block, BLOCK)
        queries = qs[here, :]
        query_pos = start + lax.broadcasted_iota(jnp.int32, (1, BLOCK), 1)
        floor = jnp.where(query_pos >= bound, bound, 0)

        def scores_of(index, diagonal):
            keys = ks[rows_at(index, BLOCK), :]
            scores = dot_nt(keys, queries)
            key_pos = index * BLOCK + lax.broadcasted_iota(jnp.int32, (BLOCK, BLOCK), 0)
            visible = key_pos >= floor
            if diagonal:
                visible = visible & (key_pos <= query_pos)
            return jnp.where(visible, scores, NEG)

        scores = scores_of(block, True)
        highest = jnp.max(scores, axis=0, keepdims=True)
        weights = jnp.exp(scores - highest)
        total = jnp.sum(weights, axis=0, keepdims=True)
        accum = dot_nn(vt[:, here], weights.astype(jnp.bfloat16))

        def step(index, state):
            highest, total, accum = state
            scores = scores_of(index, False)
            higher = jnp.maximum(highest, jnp.max(scores, axis=0, keepdims=True))
            weights = jnp.exp(scores - higher)
            factor = jnp.exp(highest - higher)
            total = total * factor + jnp.sum(weights, axis=0, keepdims=True)
            accum = accum * factor + dot_nn(vt[:, rows_at(index, BLOCK)], weights.astype(jnp.bfloat16))
            return higher, total, accum

        highest, total, accum = lax.fori_loop(first_block(start, bound), block, step, (highest, total, accum))
        result = accum / total
        attn_t[:, here] = result.astype(jnp.bfloat16)
        lse[:, here] = highest + jnp.log(total)
        result = result.T.astype(jnp.bfloat16)
        for part in range(BLOCK // RUN):
            mixed[rows_at(outloc[block * (BLOCK // RUN) + part], RUN), :] = result[part * RUN : (part + 1) * RUN]

    chips, _, span = out.shape

    @pl.loop(0, chips)
    def _(chip):
        out[chip] = mixed[rows_at(chip, span), :].astype(jnp.float32).T.astype(jnp.bfloat16)


def attend_forward(bound, inloc, outloc, qkv, chips, head_size):
    tokens = qkv.shape[0]
    bf16 = jnp.bfloat16
    pairs = tokens * (tokens // 2)
    return pl.pallas_call(
        functools.partial(forward_kernel, head_size),
        out_shape=(
            jax.ShapeDtypeStruct((chips, head_size, tokens // chips), bf16),
            jax.ShapeDtypeStruct((tokens, head_size), bf16),
            jax.ShapeDtypeStruct((tokens, head_size), bf16),
            jax.ShapeDtypeStruct((tokens, head_size), bf16),
            jax.ShapeDtypeStruct((head_size, tokens), bf16),
            jax.ShapeDtypeStruct((1, tokens), jnp.float32),
        ),
        in_specs=[pl.BlockSpec(memory_space=SM)] * 3 + [pl.BlockSpec(memory_space=VM)],
        out_specs=[pl.BlockSpec(memory_space=VM)] * 6,
        scratch_shapes=[VM((head_size, tokens), bf16), VM((tokens, head_size), bf16)],
        compiler_params=pltpu.CompilerParams(vmem_limit_bytes=40 * 1024 * 1024),
        cost_estimate=pl.CostEstimate(flops=4 * 4 * pairs * head_size, bytes_accessed=tokens * 2048, transcendentals=pairs),
        name="attend_forward",
    )(bound, inloc, outloc, qkv)


def backward_kernel(
    head_size, bound_ref, inloc, outloc, grad_t, qs, ks, vs, attn_t, lse, slot_out, send_out, grads, kt, dk, dv, mixed, wide, moved
):
    tokens = qs.shape[0]
    runs = tokens // RUN
    scale = head_size ** (-0.5)
    bound = bound_ref[0]
    chips, _, span = grad_t.shape

    @pl.loop(0, chips)
    def _(chip):
        mixed[rows_at(chip, span), :] = grad_t[chip].astype(jnp.float32).T.astype(jnp.bfloat16)

    @pl.loop(0, runs)
    def _(run):
        grads[rows_at(run, RUN), :] = mixed[rows_at(outloc[run], RUN), :]

    @pl.loop(0, tokens // BLOCK)
    def _(block):
        here = rows_at(block, BLOCK)
        kt[:, here] = ks[here, :].astype(jnp.float32).T.astype(jnp.bfloat16)

    @pl.loop(0, tokens // BLOCK)
    def _(block):
        start = block * BLOCK
        here = rows_at(block, BLOCK)
        queries = qs[here, :]
        grad = grads[here, :]
        log_total = lse[:, here]
        delta = jnp.sum(grad.astype(jnp.float32).T * attn_t[:, here].astype(jnp.float32), axis=0, keepdims=True)
        query_pos = start + lax.broadcasted_iota(jnp.int32, (1, BLOCK), 1)
        floor = jnp.where(query_pos >= bound, bound, 0)

        def one(index, diagonal):
            there = rows_at(index, BLOCK)
            scores = dot_nt(ks[there, :], queries)
            key_pos = index * BLOCK + lax.broadcasted_iota(jnp.int32, (BLOCK, BLOCK), 0)
            visible = key_pos >= floor
            if diagonal:
                visible = visible & (key_pos <= query_pos)
            probs = jnp.where(visible, jnp.exp(scores - log_total), 0.0)
            grad_probs = dot_nt(vs[there, :], grad)
            grad_scores = (probs * (grad_probs - delta)).astype(jnp.bfloat16)
            return (
                dot_nn(probs.astype(jnp.bfloat16), grad),
                dot_nn(grad_scores, queries),
                dot_nn(kt[:, there], grad_scores),
                there,
            )

        grad_v, grad_k, grad_q, there = one(block, True)
        dv[there, :] = grad_v
        dk[there, :] = grad_k

        def step(index, grad_q):
            grad_v, grad_k, term, there = one(index, False)
            dv[there, :] += grad_v
            dk[there, :] += grad_k
            return grad_q + term

        grad_q = lax.fori_loop(first_block(start, bound), block, step, grad_q)
        wide[here, :head_size] = (grad_q.T * scale).astype(jnp.bfloat16)

    wide[:, head_size : 2 * head_size] = dk[...].astype(jnp.bfloat16)
    wide[:, 2 * head_size :] = dv[...].astype(jnp.bfloat16)

    @pl.loop(0, runs)
    def _(run):
        slot_out[rows_at(inloc[run], RUN), :] = wide[rows_at(run, RUN), :]

    @pl.loop(0, runs)
    def _(run):
        moved[rows_at(outloc[run], RUN), :] = wide[rows_at(run, RUN), :]

    @pl.loop(0, chips)
    def _(chip):
        send_out[chip] = moved[rows_at(chip, span), :].astype(jnp.float32).T.astype(jnp.bfloat16)


def attend_backward(bound, inloc, outloc, grad_t, qs, ks, vs, attn_t, lse):
    tokens, head_size = qs.shape
    chips = grad_t.shape[0]
    bf16 = jnp.bfloat16
    pairs = tokens * (tokens // 2)
    return pl.pallas_call(
        functools.partial(backward_kernel, head_size),
        out_shape=(
            jax.ShapeDtypeStruct((tokens, 3 * head_size), bf16),
            jax.ShapeDtypeStruct((chips, 3 * head_size, tokens // chips), bf16),
        ),
        in_specs=[pl.BlockSpec(memory_space=SM)] * 3 + [pl.BlockSpec(memory_space=VM)] * 6,
        out_specs=[pl.BlockSpec(memory_space=VM)] * 2,
        scratch_shapes=[
            VM((tokens, head_size), bf16),
            VM((head_size, tokens), bf16),
            VM((tokens, head_size), jnp.float32),
            VM((tokens, head_size), jnp.float32),
            VM((tokens, head_size), bf16),
            VM((tokens, 3 * head_size), bf16),
            VM((tokens, 3 * head_size), bf16),
        ],
        compiler_params=pltpu.CompilerParams(vmem_limit_bytes=48 * 1024 * 1024),
        cost_estimate=pl.CostEstimate(flops=4 * 10 * pairs * head_size, bytes_accessed=tokens * 4096, transcendentals=pairs),
        name="attend_backward",
    )(bound, inloc, outloc, grad_t, qs, ks, vs, attn_t, lse)


HALF_STEP = 512


def gelu_pair(values):
    cubic = values * values
    inner = 0.7978845608028654 * values * (1.0 + 0.044715 * cubic)
    bent = jnp.tanh(inner)
    slope = 0.7978845608028654 * (1.0 + 0.134145 * cubic)
    half = 0.5 * (1.0 + bent)
    return values * half, half + 0.5 * values * (1.0 - bent * bent) * slope


def load_rows(table, pieces, targets, sem, wait):
    slot = 0
    for piece in pieces:
        count = piece.shape[0]

        @pl.loop(0, count)
        def _(index, piece=piece, slot=slot):
            chip = table[0, slot + index]
            for rows, target in targets(chip):
                copy = pltpu.make_async_copy(piece.at[index, rows], target, sem)
                if wait:
                    copy.wait()
                else:
                    copy.start()

        slot += count


def project_kernel(count, table, got, *refs):
    pieces, (part_out, sent, attn_in, w_out, sem) = refs[:count], refs[count:]
    chips, size, span = got.shape
    share = w_out.shape[0] // chips
    rows = span // 2

    def targets(chip):
        return [(pl.ds(0, share), w_out.at[rows_at(chip, share)])]

    load_rows(table, pieces, targets, sem, False)
    for chip in range(chips):
        micro, head = divmod(chip, chips // 2)
        for rel in range(2):
            column = (rel * 2 + micro) * rows
            attn_in[head * size : (head + 1) * size, column : column + rows] = got[chip, :, rel * rows : (rel + 1) * rows]
    load_rows(table, pieces, targets, sem, True)
    left = attn_in[...].astype(jnp.float32).T.astype(jnp.bfloat16)
    part = dot_nn(left, w_out[...])
    part_out[...] = part
    sent[...] = part.astype(jnp.bfloat16)


def project(table, got, pieces, share):
    chips, size, span = got.shape
    width = pieces[0].shape[2]
    tokens = 2 * span
    bf16 = jnp.bfloat16
    return pl.pallas_call(
        functools.partial(project_kernel, len(pieces)),
        out_shape=(
            jax.ShapeDtypeStruct((tokens, width), jnp.float32),
            jax.ShapeDtypeStruct((tokens, width), bf16),
            jax.ShapeDtypeStruct((chips // 2 * size, tokens), bf16),
        ),
        in_specs=[pl.BlockSpec(memory_space=SM), pl.BlockSpec(memory_space=VM)]
        + [pl.BlockSpec(memory_space=pl.ANY)] * len(pieces),
        out_specs=[pl.BlockSpec(memory_space=VM)] * 3,
        scratch_shapes=[VM((chips * share, width), bf16), pltpu.SemaphoreType.DMA],
        compiler_params=pltpu.CompilerParams(vmem_limit_bytes=24 * 1024 * 1024),
        cost_estimate=pl.CostEstimate(
            flops=2 * tokens * chips * share * width, bytes_accessed=8 * tokens * width, transcendentals=0
        ),
        name="project",
    )(table, got, *pieces)


def middle_kernel(count, share, table, x_a, x_b, g_a, g_b, part, got_a, got_b, *refs):
    pieces = refs[:count]
    (resid, base, other, grad_act, grad_sent, fc_sums, vectors, terms) = refs[count : count + 8]
    (smalls, fc_bias, w_fc, w_proj, g_all, act, act_t, rest, proj_buf, fc_buf, small_sem, load_sem, proj_sem, fc_sem) = refs[count + 8 :]
    f32, bf16 = jnp.float32, jnp.bfloat16
    tokens, width = part.shape
    own = tokens // 2
    hidden = w_proj.shape[0]
    chips = terms.shape[0]
    each = hidden // chips
    folds = hidden // width
    fc_row = share + each

    def targets(chip):
        wanted = [(pl.ds(share, each), w_proj.at[rows_at(chip, each)])]
        for fold in range(folds):
            for core in range(2):
                first = fc_row + (fold * 2 + core) * share
                place = ((chip // 2) * 2 + core) * 2 + chip % 2
                wanted.append(
                    (pl.ds(first, share), w_fc.at[rows_at(place, share), pl.ds(fold * width, width)])
                )
        return wanted

    def small_targets(chip):
        return [(pl.ds(pieces[0].shape[1] - 16, 16), smalls.at[chip])]

    load_rows(table, pieces, small_targets, small_sem, False)
    load_rows(table, pieces, targets, load_sem, False)
    load_rows(table, pieces, small_targets, small_sem, True)
    small_sum = jnp.sum(smalls[...].astype(f32), axis=0)
    vectors[...] = small_sum[:8]
    for fold in range(folds):
        fc_bias[:, fold * width : (fold + 1) * width] = small_sum[8 + fold : 9 + fold]
    for half, (x_in, g_in, arrived) in enumerate(((x_a, g_a, got_a), (x_b, g_b, got_b))):
        here = slice(half * own, (half + 1) * own)
        g_all[here, :] = g_in[...]
        value = x_in[...].astype(f32) + part[here, :] + arrived[...].astype(f32) + vectors[2:3, :]
        resid[here, :] = value
        centred = value - jnp.mean(value, axis=-1, keepdims=True)
        inverse = lax.rsqrt(jnp.mean(centred * centred, axis=-1, keepdims=True) + 1e-05)
        rounded = (centred * inverse * vectors[0:1, :] + vectors[1:2, :]).astype(bf16)
        act[here, :] = rounded
        act_t[:, here] = rounded.astype(f32).T.astype(bf16)
    base[...] = resid[:own, :] + vectors[3:4, :]
    load_rows(table, pieces, targets, load_sem, True)

    per_step = HALF_STEP // each

    def copies(step, slot):
        made = []
        for index in range(per_step):
            made.append(
                pltpu.make_async_copy(
                    proj_buf.at[slot, pl.ds(index * each, each)],
                    terms.at[table[1, step * per_step + index], pl.ds(0, each)],
                    proj_sem.at[slot],
                )
            )
        fold = step // (width // HALF_STEP)
        column = pl.multiple_of(step % (width // HALF_STEP) * HALF_STEP, HALF_STEP)
        for chip in range(chips):
            for core in range(2):
                place = ((chip // 2) * 2 + core) * 2 + chip % 2
                made.append(
                    pltpu.make_async_copy(
                        fc_buf.at[slot, pl.ds(place * share, share)],
                        terms.at[
                            table[1, chip],
                            pl.ds(pl.multiple_of(each + share + (fold * 2 + core) * share, 16), share),
                            pl.ds(column, HALF_STEP),
                        ],
                        fc_sem.at[slot],
                    )
                )
        return made

    steps = hidden // HALF_STEP

    @pl.loop(0, steps)
    def _(step):
        slot = step % 2
        columns = pl.ds(pl.multiple_of(step * HALF_STEP, HALF_STEP), HALF_STEP)
        rows = rows_at(step, HALF_STEP)

        @pl.when(step >= 2)
        def _():
            for copy in copies(step - 2, slot):
                copy.wait()

        grads = g_all[...]
        value, slope = gelu_pair(dot_nn(act[...], w_fc[:, columns]) + fc_bias[:, columns])
        value = value.astype(bf16)
        proj_buf[slot] = dot_nn(value.astype(f32).T.astype(bf16), grads).astype(bf16)
        grad_pre = (dot_nt(grads, w_proj[rows, :]) * slope).astype(bf16)
        fc_sums[:, columns] = jnp.sum(grad_pre.astype(f32), axis=0, keepdims=True)
        fc_buf[slot] = dot_nn(act_t[...], grad_pre).astype(bf16)
        for copy in copies(step, slot):
            copy.start()
        projected = dot_nn(value, w_proj[rows, :])
        back = dot_nt(grad_pre, w_fc[:, columns])
        base[...] += projected[:own]

        @pl.when(step == 0)
        def _():
            grad_act[...] = back
            rest[...] = projected[own:]

        @pl.when(step > 0)
        def _():
            grad_act[...] += back
            rest[...] += projected[own:]

    other[...] = rest[...].astype(bf16)
    grad_sent[...] = grad_act[...].astype(bf16)
    for step in range(steps - 2, steps):
        for copy in copies(step, step % 2):
            copy.wait()


def middle(table, x_a, x_b, g_a, g_b, part, got_a, got_b, pieces, share, hidden):
    tokens, width = part.shape
    f32, bf16 = jnp.float32, jnp.bfloat16
    chips = table.shape[1]
    each = hidden // chips
    rows = share + each + 2 * share * (hidden // width)
    shape = jax.ShapeDtypeStruct
    return pl.pallas_call(
        functools.partial(middle_kernel, len(pieces), share),
        out_shape=(
            shape((tokens, width), f32),
            shape((tokens // 2, width), f32),
            shape((tokens // 2, width), bf16),
            shape((tokens, width), f32),
            shape((tokens, width), bf16),
            shape((1, hidden), f32),
            shape((8, width), f32),
            shape((chips, rows, width), bf16),
        ),
        in_specs=[pl.BlockSpec(memory_space=SM)]
        + [pl.BlockSpec(memory_space=VM)] * 7
        + [pl.BlockSpec(memory_space=pl.ANY)] * len(pieces),
        out_specs=[pl.BlockSpec(memory_space=VM)] * 7 + [pl.BlockSpec(memory_space=pl.ANY)],
        scratch_shapes=[
            VM((chips, 16, width), bf16),
            VM((1, hidden), f32),
            VM((width, hidden), bf16),
            VM((hidden, width), bf16),
            VM((tokens, width), bf16),
            VM((tokens, width), bf16),
            VM((width, tokens), bf16),
            VM((tokens // 2, width), f32),
            VM((2, HALF_STEP, width), bf16),
            VM((2, width, HALF_STEP), bf16),
            pltpu.SemaphoreType.DMA,
            pltpu.SemaphoreType.DMA,
            pltpu.SemaphoreType.DMA((2,)),
            pltpu.SemaphoreType.DMA((2,)),
        ],
        compiler_params=pltpu.CompilerParams(vmem_limit_bytes=56 * 1024 * 1024),
        cost_estimate=pl.CostEstimate(
            flops=12 * tokens * width * hidden, bytes_accessed=8 * width * hidden, transcendentals=tokens * hidden
        ),
        name="middle",
    )(table, x_a, x_b, g_a, g_b, part, got_a, got_b, *pieces)


def branch_kernel(count, share, row, table, resid, g_a, g_b, part, got_a, got_b, vectors, fc_sums, attn_in, *refs):
    pieces = refs[:count]
    given, grad_resid, sent, terms, w_out, branch, products, load_sem, sem = refs[count:]
    f32, bf16 = jnp.float32, jnp.bfloat16
    tokens, width = resid.shape
    own = tokens // 2
    chips, size, span = sent.shape
    size -= 8
    rows = span // 2

    def targets(chip):
        return [(pl.ds(0, share), w_out.at[rows_at(chip, share)])]

    load_rows(table, pieces, targets, load_sem, False)
    gain_sum = jnp.zeros((1, width), f32)
    shift_sum = jnp.zeros((1, width), f32)
    bias_sum = jnp.zeros((1, width), f32)
    proj_sum = jnp.zeros((1, width), f32)
    for half, (g_in, arrived) in enumerate(((g_a, got_a), (g_b, got_b))):
        here = slice(half * own, (half + 1) * own)
        value = resid[here, :]
        centred = value - jnp.mean(value, axis=-1, keepdims=True)
        inverse = lax.rsqrt(jnp.mean(centred * centred, axis=-1, keepdims=True) + 1e-05)
        normed = centred * inverse
        grad = part[here, :] + arrived[...].astype(f32)
        gain_sum += jnp.sum(grad * normed, axis=0, keepdims=True)
        shift_sum += jnp.sum(grad, axis=0, keepdims=True)
        scaled = grad * vectors[0:1, :]
        given_grad = g_in[...].astype(f32)
        total = given_grad + inverse * (
            scaled
            - jnp.mean(scaled, axis=-1, keepdims=True)
            - normed * jnp.mean(scaled * normed, axis=-1, keepdims=True)
        )
        rounded = total.astype(bf16)
        bias_sum += jnp.sum(rounded.astype(f32), axis=0, keepdims=True)
        proj_sum += jnp.sum(given_grad, axis=0, keepdims=True)
        branch[here, :] = rounded
        if half == 0:
            grad_resid[...] = total
    load_rows(table, pieces, targets, load_sem, True)
    grads = dot_nt(w_out[...], branch[...]).astype(bf16)
    group = width // (chips // 2)
    sums = jnp.concatenate([gain_sum, shift_sum, bias_sum, proj_sum], axis=0)
    each = fc_sums.shape[1] // chips
    for chip in range(chips):
        micro, head = divmod(chip, chips // 2)
        for rel in range(2):
            column = (rel * 2 + micro) * rows
            sent[chip, :size, rel * rows : (rel + 1) * rows] = grads[
                head * size : (head + 1) * size, column : column + rows
            ]
        first = chip // 2 * group
        tail = jnp.concatenate(
            [
                sums[:, first : first + group],
                fc_sums[:, chip * each : (chip + 1) * each],
                jnp.zeros((3, group), f32),
            ],
            axis=0,
        )
        high = tail.astype(bf16)
        low = (tail - high.astype(f32)).astype(bf16)
        sent[chip, size:, :] = jnp.concatenate([high, low], axis=1)
    products[...] = dot_nn(attn_in[...], branch[...]).astype(bf16)

    @pl.loop(0, chips)
    def _(chip):
        pltpu.make_async_copy(products.at[rows_at(chip, share)], terms.at[table[1, chip], pl.ds(row, share)], sem).start()

    @pl.loop(0, chips)
    def _(chip):
        pltpu.make_async_copy(products.at[rows_at(chip, share)], terms.at[table[1, chip], pl.ds(row, share)], sem).wait()


def branch_back(table, resid, g_a, g_b, part, got_a, got_b, vectors, fc_sums, attn_in, pieces, terms, share, row, span):
    tokens, width = resid.shape
    f32, bf16 = jnp.float32, jnp.bfloat16
    chips = table.shape[1]
    size = attn_in.shape[0] // (chips // 2)
    shape = jax.ShapeDtypeStruct
    inputs = 10 + len(pieces)
    return pl.pallas_call(
        functools.partial(branch_kernel, len(pieces), share, row),
        out_shape=(
            shape((tokens // 2, width), f32),
            shape((chips, size + 8, span), bf16),
            shape(terms.shape, bf16),
        ),
        in_specs=[pl.BlockSpec(memory_space=SM)]
        + [pl.BlockSpec(memory_space=VM)] * 9
        + [pl.BlockSpec(memory_space=pl.ANY)] * (len(pieces) + 1),
        out_specs=[pl.BlockSpec(memory_space=VM)] * 2 + [pl.BlockSpec(memory_space=pl.ANY)],
        scratch_shapes=[
            VM((chips * share, width), bf16),
            VM((tokens, width), bf16),
            VM((chips * share, width), bf16),
            pltpu.SemaphoreType.DMA,
            pltpu.SemaphoreType.DMA,
        ],
        input_output_aliases={inputs: 2},
        compiler_params=pltpu.CompilerParams(vmem_limit_bytes=40 * 1024 * 1024),
        cost_estimate=pl.CostEstimate(
            flops=4 * tokens * chips * share * width, bytes_accessed=16 * tokens * width, transcendentals=0
        ),
        name="branch_back",
    )(table, resid, g_a, g_b, part, got_a, got_b, vectors, fc_sums, attn_in, *pieces, terms)


def finish_kernel(count, share, table, got, *refs):
    pieces, (kept, sent, weight, grads, sem) = refs[:count], refs[count:]
    chips, size, span = got.shape
    rows = span // 2
    own = kept.shape[0]

    def targets(chip):
        wanted = []
        for core in range(2):
            place = ((chip // 2) * 2 + core) * 2 + chip % 2
            wanted.append((pl.ds(core * share, share), weight.at[rows_at(place, share)]))
        return wanted

    load_rows(table, pieces, targets, sem, False)
    for chip in range(chips):
        micro, head = divmod(chip, chips // 2)
        for rel in range(2):
            column = (rel * 2 + micro) * rows
            grads[head * size : (head + 1) * size, column : column + rows] = got[chip, :, rel * rows : (rel + 1) * rows]
    load_rows(table, pieces, targets, sem, True)
    back = dot_nn(weight[...], grads[...])
    kept[...] = back[:, :own].T
    sent[...] = back[:, own:].T.astype(jnp.bfloat16)


def finish(table, got, pieces, share):
    chips, size, span = got.shape
    depth = pieces[0].shape[2]
    width = chips * 2 * share
    bf16 = jnp.bfloat16
    return pl.pallas_call(
        functools.partial(finish_kernel, len(pieces), share),
        out_shape=(
            jax.ShapeDtypeStruct((span, width), jnp.float32),
            jax.ShapeDtypeStruct((span, width), bf16),
        ),
        in_specs=[pl.BlockSpec(memory_space=SM), pl.BlockSpec(memory_space=VM)]
        + [pl.BlockSpec(memory_space=pl.ANY)] * len(pieces),
        out_specs=[pl.BlockSpec(memory_space=VM)] * 2,
        scratch_shapes=[VM((width, depth), bf16), VM((depth, 2 * span), bf16), pltpu.SemaphoreType.DMA],
        compiler_params=pltpu.CompilerParams(vmem_limit_bytes=32 * 1024 * 1024),
        cost_estimate=pl.CostEstimate(
            flops=4 * span * width * depth, bytes_accessed=2 * width * depth + 8 * span * width, transcendentals=0
        ),
        name="finish",
    )(table, got, *pieces)


PAIR = [(0, 1), (1, 0)]
NEAR = [(0, 1), (1, 0), (2, 3), (3, 2)]
FAR = [(0, 2), (2, 0), (1, 3), (3, 1)]


def swap(values, axis, pairs=PAIR):
    return lax.ppermute(values, axis, pairs)


def in_order(mine, other, index, axis):
    first = jnp.where(index == 0, mine, other)
    second = jnp.where(index == 0, other, mine)
    return jnp.stack([first, second], axis=axis)


def split_float(values):
    high = values.astype(jnp.bfloat16)
    low = (values - high.astype(jnp.float32)).astype(jnp.bfloat16)
    return high, low


def run_table(order, pair_start):
    pairs = order.shape[0]
    runs = jnp.arange(2 * pairs, dtype=jnp.int32)[:, None]
    low = jnp.where(runs == order[None, :], pair_start[None, :], 0)
    high = jnp.where(runs == 2 * pairs - 1 - order[None, :], pair_start[None, :] + 1, 0)
    return jnp.sum(low + high, axis=1).astype(jnp.int32)


def ring_order(count):
    half = [(z, (z + step) % 2) for z in range(count) for step in range(2)]
    up = [(z * 2) * 2 + y for z, y in half]
    down = [(z * 2 + 1) * 2 + y for z, y in reversed(half)]
    return up + down


def fast_body(
    block_input,
    qkv_weight,
    q_bias,
    v_bias,
    out_weight,
    out_bias,
    norm1_gain,
    norm1_shift,
    norm2_gain,
    norm2_shift,
    fc_weight,
    fc_bias,
    proj_weight,
    proj_bias,
    out_grad,
    dealt,
    lengths,
):
    f32, bf16 = jnp.float32, jnp.bfloat16
    micro, rows, width = block_input.shape
    nz, nx = lax.axis_size("z"), lax.axis_size("x")
    iz, ix, ic, iy = (lax.axis_index(name) for name in ("z", "x", "core", "head"))
    zx = nz * nx
    every, chips = ("z", "x", "core", "head"), ("z", "x", "head")
    devices, chip_count = 4 * zx, 2 * zx
    heads = 2 * zx
    local = heads * DH // 2
    share = qkv_weight.shape[0]
    hidden_share = proj_weight.shape[0]
    hidden_half = hidden_share * chip_count

    inputs = block_input.astype(f32)
    normed_one, inverse_one = normalize(inputs)
    n1 = normed_one.astype(bf16)
    n1, qkv_weight, fc_weight, norm1_gain, norm2_gain = lax.optimization_barrier(
        (n1, qkv_weight, fc_weight, norm1_gain, norm2_gain)
    )
    gain_one = norm1_gain.astype(f32)
    shift_one = norm1_shift.astype(f32)
    raw_qkv = qkv_weight.astype(f32)
    scaled_qkv = (raw_qkv * gain_one[:, None]).astype(bf16)
    device = ((iz * nx + ix) * 2 + ic) * 2 + iy
    offset = jnp.sum(raw_qkv * shift_one[:, None], axis=0)
    zero = jnp.zeros((width,), f32)
    place = device * share
    offset = offset + jnp.concatenate(
        [
            lax.dynamic_update_slice(zero, q_bias.astype(f32), (place,)),
            zero,
            lax.dynamic_update_slice(zero, v_bias.astype(f32), (place,)),
        ]
    )
    high, low = split_float(offset)
    to_heads = jnp.concatenate([scaled_qkv, high[None], low[None], jnp.zeros((6, 3 * width), bf16)], axis=0)
    to_heads = to_heads.reshape(share + 8, 3, zx // 2, 2, 2, DH).transpose(2, 4, 3, 0, 1, 5)
    to_heads = to_heads.reshape(1, heads, share + 8, 3 * DH)
    to_heads = jnp.broadcast_to(to_heads, (2, heads, share + 8, 3 * DH)).reshape(devices, share + 8, 3 * DH)
    head_rows = lax.all_to_all(to_heads, every, split_axis=0, concat_axis=0, tiled=True)
    head_weight = head_rows[:, :share].reshape(width, 3 * DH)
    head_offset = jnp.sum(head_rows[:, share : share + 2].astype(f32), axis=(0, 1))

    mine = iz // 2
    near = lax.dynamic_index_in_dim(n1, mine, 0, keepdims=False)
    far = swap(lax.dynamic_index_in_dim(n1, 1 - mine, 0, keepdims=False), "z", FAR)
    near_x = swap(near, "x")
    far, near_x = lax.optimization_barrier((far, near_x))
    near = jnp.stack([near, near_x])
    near_z, far_y = swap(near, "z", NEAR), swap(far, "head")
    near_z, far_y = lax.optimization_barrier((near_z, far_y))
    near, far = jnp.stack([near, near_z]), jnp.stack([far, far_y])
    near_y, far_z = swap(near, "head"), swap(far, "z", NEAR)
    far = jnp.stack([far, far_z])
    parts = [near, near_y, far, swap(far, "x")]
    pieces, owners = [], []

    def add_all(flip):
        core = 1 - ic if flip else ic
        for index, part in enumerate(parts):
            pieces.append((swap(part, "core") if flip else part).reshape(-1, width))
            for dz in range(2):
                for step in range(2):
                    dx, dy = (step, index) if index < 2 else (index - 2, step)
                    owners.append((iz ^ dz ^ (index // 2 * 2), ix ^ dx, core, iy ^ dy))

    add_all(False)
    add_all(True)
    slot_device = jnp.stack([((z * nx + x) * 2 + core) * 2 + y for z, x, core, y in owners]).astype(jnp.int32)
    my_dealt = lax.dynamic_index_in_dim(dealt, mine, 0, keepdims=False)
    order = my_dealt.reshape(devices, rows)[:, 0] // RUN
    slot_of = jnp.sum(
        jnp.where(jnp.arange(devices)[:, None] == slot_device[None, :], jnp.arange(devices)[None, :], 0), axis=1
    )
    inloc = run_table(order, (slot_of * 2).astype(jnp.int32))
    ids = jnp.arange(devices, dtype=jnp.int32)
    id_y, id_c, id_zx = ids % 2, ids // 2 % 2, ids // 4
    send_pair = (id_zx * 2 + id_y) * 2 + (id_c ^ ic)
    outloc = run_table(order, (send_pair * 2).astype(jnp.int32))
    bound = lax.dynamic_index_in_dim(lengths, mine, 0, keepdims=False)[:1]

    fc_parts = fc_weight.reshape(share, zx, 2, 2, hidden_share)

    def core_columns(values, index):
        return lax.dynamic_index_in_dim(values, index, 2, keepdims=False)

    fc_mine = core_columns(fc_parts, ic).reshape(share, hidden_half)
    fc_other = swap(core_columns(fc_parts, 1 - ic).reshape(share, hidden_half), "core")
    fc_pair = in_order(fc_mine, fc_other, ic, 0).reshape(2 * share, hidden_half)
    small = jnp.stack([norm2_gain, norm2_shift, out_bias, proj_bias])
    small_rows = jnp.zeros((16, width), bf16)
    small_rows = lax.dynamic_update_slice(small_rows, small, (0, place))
    other_place = (((iz * nx + ix) * 2 + 1 - ic) * 2 + iy) * share
    small_rows = lax.dynamic_update_slice(small_rows, swap(small, "core"), (0, other_place))
    fc_place = ((iz * nx + ix) * 2 + iy) * hidden_share
    small_rows = lax.dynamic_update_slice(small_rows, fc_bias[None], (8 + fc_place // width, fc_place % width))
    folds = hidden_half // width
    fc_folded = fc_pair.reshape(2 * share, folds, width).transpose(1, 0, 2).reshape(-1, width)
    packed = jnp.concatenate([out_weight, proj_weight, fc_folded, small_rows], axis=0)
    ring = ring_order(nz)
    places = [ring.index(chip) for chip in range(chip_count)]
    table = jnp.array([ring, places], jnp.int32)
    gathered = lax.all_gather(packed, chips, axis=0, axis_index_groups=[ring])
    out_rows = share
    proj_rows = hidden_share
    fc_rows = 2 * share * folds

    qkv_parts = scaled_qkv.reshape(share, 3, zx, 2, DH).transpose(0, 2, 1, 3, 4)

    def core_heads(index):
        return lax.dynamic_index_in_dim(qkv_parts, index, 3, keepdims=False).reshape(share, 3 * local)

    qkv_pair = in_order(core_heads(ic), swap(core_heads(1 - ic), "core"), ic, 0)

    mixed = [(product(piece, head_weight) + head_offset).astype(bf16) for piece in pieces]
    slots = jnp.concatenate(mixed, axis=0)
    attn_send, queries, keys, values, attn_t, lse = attend_forward(bound, inloc, outloc, slots, chip_count, DH)

    x_a, x_b = block_input.reshape(-1, width), swap(block_input, "core").reshape(-1, width)
    g_a, g_b = out_grad.reshape(-1, width), swap(out_grad, "core").reshape(-1, width)
    own = micro * rows
    attn_got = lax.all_to_all(attn_send, chips, split_axis=0, concat_axis=0, tiled=True)
    qkv_pair, attn_got = lax.optimization_barrier((qkv_pair, attn_got))
    qkv_pair = qkv_pair.reshape(2 * share, 3 * local)
    w_qkv = lax.all_gather(qkv_pair, chips, axis=0, axis_index_groups=[ring])
    part, sent, attn_in = project(table, attn_got, [gathered], share)
    resid, base, project_other, grad_part, sent_back, fc_sums, vectors, terms = middle(
        table, x_a, x_b, g_a, g_b, part, swap(sent[own:], "core"), swap(sent[:own], "core"), [gathered], share, hidden_half
    )
    grad_resid, grad_send, terms = branch_back(
        table,
        resid,
        g_a,
        g_b,
        grad_part,
        swap(sent_back[own:], "core"),
        swap(sent_back[:own], "core"),
        vectors,
        fc_sums,
        attn_in,
        [gathered],
        terms,
        share,
        proj_rows,
        2 * rows,
    )
    output = (base + swap(project_other, "core").astype(f32)).astype(bf16)

    grad_got = lax.all_to_all(grad_send, chips, split_axis=0, concat_axis=0, tiled=True)
    grad_heads = grad_got[:, :DH]
    vector_sums = jnp.sum(grad_got[:, DH:].astype(f32), axis=0)
    vector_sums = vector_sums[:, :rows] + vector_sums[:, rows:]
    final_vectors = lax.dynamic_slice(vector_sums, (0, (ic * 2 + iy) * share), (4, share))
    final_fc_b = vector_sums[4]

    summed = lax.psum_scatter(terms, chips, scatter_dimension=0, tiled=True, axis_index_groups=[ring])[0]
    final_proj_w = summed[:proj_rows].astype(f32)
    slot_grads, send_grads = attend_backward(
        bound, inloc, outloc, grad_heads, queries, keys, values, attn_t, lse
    )
    grads_got = lax.all_to_all(send_grads, chips, split_axis=0, concat_axis=0, tiled=True)

    count = 0
    raw_term = jnp.zeros((width, 3 * DH), f32)
    for piece in pieces:
        raw_term = raw_term + product_tn(piece, slot_grads[count : count + piece.shape[0]])
        count += piece.shape[0]
    column_sums = jnp.sum(slot_grads.astype(f32), axis=0)
    high, low = split_float(column_sums)
    tail = jnp.concatenate([high[None], low[None], jnp.zeros((6, 3 * DH), bf16)], axis=0)
    raw_rows = raw_term.astype(bf16).reshape(zx, 2, 2, share, 3 * DH).transpose(0, 2, 1, 3, 4)
    raw_send = jnp.concatenate(
        [
            raw_rows.reshape(chip_count, 2 * share, 3 * DH),
            jnp.broadcast_to(tail[None], (chip_count, 8, 3 * DH)),
        ],
        axis=1,
    )
    back_own, back_other = finish(table, grads_got, [w_qkv], share)
    raw_send, back_other = lax.optimization_barrier((raw_send, back_other))
    final_out_w = summed[proj_rows : proj_rows + out_rows].astype(f32)
    fc_sum = summed[proj_rows + out_rows :].reshape(folds, 2, share, width)
    fc_keep = lax.dynamic_index_in_dim(fc_sum, ic, 1, keepdims=False)
    fc_give = swap(lax.dynamic_index_in_dim(fc_sum, 1 - ic, 1, keepdims=False), "core")

    def by_owner(values):
        return values.transpose(1, 0, 2).reshape(share, zx, 2, hidden_share)

    final_fc_w = in_order(by_owner(fc_keep), by_owner(fc_give), ic, 2).reshape(share, 2 * hidden_half).astype(f32)
    raw_got = lax.all_to_all(raw_send, chips, split_axis=0, concat_axis=0, tiled=True)
    raw_sum = jnp.sum(raw_got.reshape(2, zx, 2 * share + 8, 3 * DH).astype(f32), axis=0)
    raw_parts = raw_sum[:, : 2 * share].reshape(zx, 2, share, 3 * DH)
    sums_mine = raw_sum[:, 2 * share : 2 * share + 1] + raw_sum[:, 2 * share + 1 : 2 * share + 2]
    raw_keep = jnp.concatenate([lax.dynamic_index_in_dim(raw_parts, ic, 1, keepdims=False), sums_mine], axis=1)
    raw_give = jnp.concatenate([lax.dynamic_index_in_dim(raw_parts, 1 - ic, 1, keepdims=False), sums_mine], axis=1)
    raw_all = in_order(raw_keep, swap(raw_give, "core"), ic, 1).reshape(heads, share + 1, 3, DH)
    raw_all = raw_all.transpose(1, 2, 0, 3).reshape(share + 1, 3 * width)
    raw_grad, all_sums = raw_all[:share], raw_all[share]
    final_qkv_w = raw_grad * gain_one[:, None] + shift_one[:, None] * all_sums[None, :]
    final_gain_one = jnp.sum(raw_grad * raw_qkv, axis=1)
    final_shift_one = jnp.sum(raw_qkv * all_sums[None, :], axis=1)
    final_q_b = lax.dynamic_slice(all_sums, (place,), (share,))
    final_v_b = lax.dynamic_slice(all_sums, (2 * width + place,), (share,))

    back_own = back_own + swap(back_other, "core").astype(f32)
    back_own = back_own.reshape(micro, rows, width)
    input_grad = grad_resid.reshape(micro, rows, width) + norm_back(back_own, normed_one, inverse_one)

    return (
        output.reshape(micro, rows, width),
        input_grad.astype(bf16),
        final_qkv_w,
        final_q_b,
        final_v_b,
        final_out_w,
        final_vectors[2],
        final_gain_one,
        final_shift_one,
        final_vectors[0],
        final_vectors[1],
        final_fc_w,
        final_fc_b,
        final_proj_w,
        final_vectors[3],
    )


def specs(names):
    rows, vector, tokens = P(names, None), P(names), P(None, names, None)
    weights = (rows, vector, vector, rows, vector, vector, vector, vector, vector, rows, vector, rows, vector)
    return (tokens, *weights, tokens, P(), P()), (tokens, tokens, *weights)


def solution(mesh):
    sizes = dict(mesh.shape)
    if sizes["head"] == 2 and sizes["blk"] == 16:
        fine = Mesh(mesh.devices.reshape(2, 4, 2, 2), ("head", "z", "x", "core"))
        given, made = specs(("z", "x", "core", "head"))
        return jax.shard_map(fast_body, mesh=fine, in_specs=given, out_specs=made, check_vma=False)
    given, made = specs(("blk", "head"))
    return jax.shard_map(general_body, mesh=mesh, in_specs=given, out_specs=made, check_vma=False)
```

```python
import functools
import math

import jax
import jax.numpy as jnp
from jax import lax
from jax.experimental import pallas as pl
from jax.experimental.pallas import tpu as pltpu
from jax.sharding import Mesh
from jax.sharding import PartitionSpec as P

DH = 64


def gelu_tanh(values):
    inner = 0.7978845608028654 * (values + 0.044715 * values * values * values)
    return 0.5 * values * (1.0 + jnp.tanh(inner))


def normalize(values):
    centred = values - jnp.mean(values, axis=-1, keepdims=True)
    inverse = lax.rsqrt(jnp.mean(centred * centred, axis=-1, keepdims=True) + 1e-05)
    return (centred * inverse, inverse)


def norm_back(grad_normed, normed, inverse):
    return inverse * (
        grad_normed
        - jnp.mean(grad_normed, axis=-1, keepdims=True)
        - normed * jnp.mean(grad_normed * normed, axis=-1, keepdims=True)
    )


def product(left, right):
    return jnp.dot(left, right, preferred_element_type=jnp.float32)


def product_tn(left, right):
    return lax.dot_general(
        left, right, (((0,), (0,)), ((), ())), preferred_element_type=jnp.float32
    )


def product_nt(left, right):
    return lax.dot_general(
        left, right, (((1,), (1,)), ((), ())), preferred_element_type=jnp.float32
    )


def visible_pairs(query_pos, key_pos, boundary):
    same_side = (query_pos[:, None] >= boundary) == (key_pos[None, :] >= boundary)
    return same_side & (key_pos[None, :] <= query_pos[:, None])


def forward_tile(current, queries3, keys3, values3, visible, scale):
    running, total, accum = current
    scores = jnp.einsum("qhd,khd->hqk", queries3, keys3, preferred_element_type=jnp.float32) * scale
    scores = jnp.where(visible[None], scores, -1000000000.0)
    highest = jnp.maximum(running, jnp.max(scores, axis=-1))
    weights = jnp.where(visible[None], jnp.exp(scores - highest[..., None]), 0.0)
    factor = jnp.exp(running - highest)
    total = total * factor + jnp.sum(weights, axis=-1)
    accum = accum * factor[..., None] + jnp.einsum(
        "hqk,khd->hqd", weights.astype(jnp.bfloat16), values3, preferred_element_type=jnp.float32
    )
    return (highest, total, accum)


def general_forward(query_parts, pos_parts, positions, boundary, keys_group, values_group, key_span):
    heads_local, head_size = (query_parts[0].shape[1], query_parts[0].shape[2])
    scale = head_size ** (-0.5)

    def fold_keys(state, pieces, start):
        key_rows, value_rows = pieces
        count_rows = key_rows.shape[0]
        block_rows = math.gcd(count_rows, key_span)
        block_count = count_rows // block_rows

        def one_step(index, inner):
            offset = index * block_rows
            keys3 = lax.dynamic_slice_in_dim(key_rows, offset, block_rows).reshape(
                block_rows, heads_local, head_size
            )
            values3 = lax.dynamic_slice_in_dim(value_rows, offset, block_rows).reshape(
                block_rows, heads_local, head_size
            )
            key_pos = lax.dynamic_slice_in_dim(positions, offset, block_rows)
            part_queries = query_parts[0]
            visible = visible_pairs(pos_parts[0], key_pos, boundary)
            current = inner[0]
            result = forward_tile(current, part_queries, keys3, values3, visible, scale)
            updated = [result]
            return tuple(updated)

        return lax.fori_loop(0, block_count, one_step, state)

    initial = tuple(
        (
            (
                jnp.full((heads_local, part.shape[0]), -1000000000.0, jnp.float32),
                jnp.zeros((heads_local, part.shape[0]), jnp.float32),
                jnp.zeros((heads_local, part.shape[0], head_size), jnp.float32),
            )
            for part in query_parts
        )
    )
    return fold_keys(
        initial,
        (
            lax.all_gather(keys_group, "blk", axis=0, tiled=True),
            lax.all_gather(values_group, "blk", axis=0, tiled=True),
        ),
        jnp.int32(0),
    )


def backward_tile(current, queries3, grad3, log_total, delta, keys3, values3, visible, scale):
    grad_query, term = current
    scores = jnp.einsum("qhd,khd->hqk", queries3, keys3, preferred_element_type=jnp.float32) * scale
    scores = jnp.where(visible[None], scores, -1000000000.0)
    exact = jnp.where(visible[None], jnp.exp(scores - log_total[..., None]), 0.0)
    grad_probs = jnp.einsum("qhd,khd->hqk", grad3, values3, preferred_element_type=jnp.float32)
    grad_scores = (exact * (grad_probs - delta[..., None])).astype(jnp.bfloat16)
    grad_query = (
        grad_query
        + jnp.einsum("hqk,khd->hqd", grad_scores, keys3, preferred_element_type=jnp.float32) * scale
    )
    rounded = exact.astype(jnp.bfloat16)
    grad_values = jnp.einsum("hqk,qhd->khd", rounded, grad3, preferred_element_type=jnp.float32)
    grad_keys = (
        jnp.einsum("hqk,qhd->khd", grad_scores, queries3, preferred_element_type=jnp.float32)
        * scale
    )
    rows = keys3.shape[0]
    term = jnp.stack([grad_keys.reshape(rows, -1), grad_values.reshape(rows, -1)], axis=1)
    return (grad_query, term)


def general_backward(
    query_parts,
    grad_parts,
    total_parts,
    delta_parts,
    pos_parts,
    positions,
    boundary,
    keys_group,
    values_group,
    key_span,
    buffer_rows,
):
    heads_local, head_size = (query_parts[0].shape[1], query_parts[0].shape[2])
    scale = head_size ** (-0.5)

    def fold_keys(state, pieces, start):
        key_rows, value_rows = pieces
        count_rows = key_rows.shape[0]
        block_rows = math.gcd(count_rows, key_span)
        block_count = count_rows // block_rows

        def one_step(index, inner):
            offset = index * block_rows
            keys3 = lax.dynamic_slice_in_dim(key_rows, offset, block_rows).reshape(
                block_rows, heads_local, head_size
            )
            values3 = lax.dynamic_slice_in_dim(value_rows, offset, block_rows).reshape(
                block_rows, heads_local, head_size
            )
            key_pos = lax.dynamic_slice_in_dim(positions, offset, block_rows)
            grads_now, buffer = inner
            term = jnp.zeros((block_rows, 2, heads_local * head_size), jnp.float32)
            part_queries = query_parts[0]
            part_grads = grad_parts[0]
            part_total = total_parts[0]
            part_delta = delta_parts[0]
            visible = visible_pairs(pos_parts[0], key_pos, boundary)
            current = (grads_now[0], term)
            result = backward_tile(
                current,
                part_queries,
                part_grads,
                part_total,
                part_delta,
                keys3,
                values3,
                visible,
                scale,
            )
            updated = [result[0]]
            term = result[1]
            buffer = lax.dynamic_update_slice(buffer, term, (offset, 0, 0))
            return (tuple(updated), buffer)

        return lax.fori_loop(0, block_count, one_step, state)

    grads_init = tuple(
        (jnp.zeros((heads_local, part.shape[0], head_size), jnp.float32) for part in query_parts)
    )
    initial = (grads_init, jnp.zeros((buffer_rows, 2, heads_local * head_size), jnp.float32))
    return fold_keys(
        initial,
        (
            lax.all_gather(keys_group, "blk", axis=0, tiled=True),
            lax.all_gather(values_group, "blk", axis=0, tiled=True),
        ),
        jnp.int32(0),
    )


def general_body(
    block_input,
    qkv_weight,
    q_bias,
    v_bias,
    out_weight,
    out_bias,
    norm1_gain,
    norm1_shift,
    norm2_gain,
    norm2_shift,
    fc_weight,
    fc_bias,
    proj_weight,
    proj_bias,
    out_grad,
    dealt,
    lengths,
):
    micro_count, local_rows, width = block_input.shape
    head_devices = lax.axis_size("head")
    blk_devices = lax.axis_size("blk")
    group = local_rows * head_devices
    blk_index = lax.axis_index("blk")
    head_size = DH
    key_span = 1024
    part_count = group // group
    shards = (
        qkv_weight,
        q_bias,
        v_bias,
        out_weight,
        out_bias,
        norm1_gain,
        norm1_shift,
        norm2_gain,
        norm2_shift,
        fc_weight,
        fc_bias,
        proj_weight,
        proj_bias,
    )
    totals = [
        jnp.zeros((shard.shape[0] * blk_devices * head_devices,) + shard.shape[1:], jnp.float32)
        for shard in shards
    ]
    outputs = []
    input_grads = []
    for micro_index in range(micro_count):
        whole = (
            lax.all_gather(shards[0], ("blk", "head"), axis=0, tiled=True),
            lax.all_gather(shards[1], ("blk", "head"), axis=0, tiled=True),
            lax.all_gather(shards[2], ("blk", "head"), axis=0, tiled=True),
            lax.all_gather(shards[3], ("blk", "head"), axis=0, tiled=True),
            lax.all_gather(shards[4], ("blk", "head"), axis=0, tiled=True),
            lax.all_gather(shards[5], ("blk", "head"), axis=0, tiled=True),
            lax.all_gather(shards[6], ("blk", "head"), axis=0, tiled=True),
            lax.all_gather(shards[7], ("blk", "head"), axis=0, tiled=True),
            lax.all_gather(shards[8], ("blk", "head"), axis=0, tiled=True),
            lax.all_gather(shards[9], ("blk", "head"), axis=0, tiled=True),
            lax.all_gather(shards[10], ("blk", "head"), axis=0, tiled=True),
            lax.all_gather(shards[11], ("blk", "head"), axis=0, tiled=True),
            lax.all_gather(shards[12], ("blk", "head"), axis=0, tiled=True),
        )
        (
            w_qkv,
            b_query,
            b_value,
            w_out,
            b_out,
            gain_one,
            shift_one,
            gain_two,
            shift_two,
            w_fc,
            b_fc,
            w_proj,
            b_proj,
        ) = whole
        b_query = b_query.astype(jnp.float32)
        b_value = b_value.astype(jnp.float32)
        b_out = b_out.astype(jnp.float32)
        gain_one = gain_one.astype(jnp.float32)
        shift_one = shift_one.astype(jnp.float32)
        gain_two = gain_two.astype(jnp.float32)
        shift_two = shift_two.astype(jnp.float32)
        b_fc = b_fc.astype(jnp.float32)
        b_proj = b_proj.astype(jnp.float32)
        positions = dealt[micro_index]
        boundary = lengths[micro_index, 0]
        query_pos = lax.dynamic_slice_in_dim(positions, blk_index * group, group)
        inputs = block_input[micro_index].astype(jnp.float32)
        normed_one, inverse_one = normalize(inputs)
        act_one = (normed_one * gain_one + shift_one).astype(jnp.bfloat16)
        mixed = product(act_one, w_qkv)
        queries = (mixed[:, :width] + b_query).astype(jnp.bfloat16)
        keys = mixed[:, width : 2 * width].astype(jnp.bfloat16)
        values = (mixed[:, 2 * width :] + b_value).astype(jnp.bfloat16)
        heads_in = lax.all_to_all(
            jnp.stack([queries, keys, values], axis=1),
            "head",
            split_axis=2,
            concat_axis=0,
            tiled=True,
        )
        local_width = heads_in.shape[2]
        heads_local = local_width // head_size
        queries3 = heads_in[:, 0].reshape(group, heads_local, head_size)
        keys_group = heads_in[:, 1]
        values_group = heads_in[:, 2]
        query_parts = tuple((queries3 for index in range(part_count)))
        pos_parts = tuple((query_pos for index in range(part_count)))
        states = general_forward(
            query_parts, pos_parts, positions, boundary, keys_group, values_group, key_span
        )
        running = jnp.concatenate([state[0] for state in states], axis=1)
        total = jnp.concatenate([state[1] for state in states], axis=1)
        accum = jnp.concatenate([state[2] for state in states], axis=1)
        log_total = running + jnp.log(total)
        attn_heads = (
            (accum / total[..., None])
            .transpose(1, 0, 2)
            .reshape(group, local_width)
            .astype(jnp.bfloat16)
        )
        attended = lax.all_to_all(attn_heads, "head", split_axis=0, concat_axis=1, tiled=True)
        resid = inputs + product(attended, w_out) + b_out
        normed_two, inverse_two = normalize(resid)
        act_two = (normed_two * gain_two + shift_two).astype(jnp.bfloat16)
        pre = product(act_two, w_fc) + b_fc
        hidden = gelu_tanh(pre).astype(jnp.bfloat16)
        outputs.append((resid + product(hidden, w_proj) + b_proj).astype(jnp.bfloat16))
        cotangent = out_grad[micro_index]
        grad_proj_w = product_tn(hidden, cotangent)
        grad_proj_b = jnp.sum(cotangent.astype(jnp.float32), axis=0)
        grad_hidden = product_nt(cotangent, w_proj)
        grad_pre = jax.vjp(gelu_tanh, pre)[1](grad_hidden)[0].astype(jnp.bfloat16)
        grad_fc_w = product_tn(act_two, grad_pre)
        grad_fc_b = jnp.sum(grad_pre.astype(jnp.float32), axis=0)
        grad_act_two = product_nt(grad_pre, w_fc)
        grad_gain_two = jnp.sum(grad_act_two * normed_two, axis=0)
        grad_shift_two = jnp.sum(grad_act_two, axis=0)
        grad_resid = cotangent.astype(jnp.float32) + norm_back(
            grad_act_two * gain_two, normed_two, inverse_two
        )
        grad_branch = grad_resid.astype(jnp.bfloat16)
        grad_out_w = product_tn(attended, grad_branch)
        grad_out_b = jnp.sum(grad_branch.astype(jnp.float32), axis=0)
        grad_attn = product_nt(grad_branch, w_out).astype(jnp.bfloat16)
        grad_heads = lax.all_to_all(grad_attn, "head", split_axis=1, concat_axis=0, tiled=True)
        grad3 = grad_heads.reshape(group, heads_local, head_size)
        attn3 = attn_heads.reshape(group, heads_local, head_size)
        delta = jnp.sum(grad3.astype(jnp.float32) * attn3.astype(jnp.float32), axis=-1).T
        grad_parts = tuple((grad3 for index in range(part_count)))
        total_parts = tuple((log_total for index in range(part_count)))
        delta_parts = tuple((delta for index in range(part_count)))
        query_grads, buffer = general_backward(
            query_parts,
            grad_parts,
            total_parts,
            delta_parts,
            pos_parts,
            positions,
            boundary,
            keys_group,
            values_group,
            key_span,
            group * blk_devices,
        )
        kv_sums = lax.psum_scatter(buffer, "blk", scatter_dimension=0, tiled=True)
        grad_k_heads = kv_sums[:, 0].astype(jnp.bfloat16)
        grad_v_heads = kv_sums[:, 1].astype(jnp.bfloat16)
        grad_query = jnp.concatenate(list(query_grads), axis=1)
        grad_q_heads = (
            grad_query.transpose(1, 0, 2).reshape(group, local_width).astype(jnp.bfloat16)
        )
        grads_heads = jnp.stack([grad_q_heads, grad_k_heads, grad_v_heads], axis=1)
        back_tokens = lax.all_to_all(grads_heads, "head", split_axis=0, concat_axis=2, tiled=True)
        grad_mixed = back_tokens.reshape(local_rows, 3 * width)
        grad_qkv_w = product_tn(act_one, grad_mixed)
        grad_q_b = jnp.sum(back_tokens[:, 0].astype(jnp.float32), axis=0)
        grad_v_b = jnp.sum(back_tokens[:, 2].astype(jnp.float32), axis=0)
        grad_act_one = product_nt(grad_mixed, w_qkv)
        grad_gain_one = jnp.sum(grad_act_one * normed_one, axis=0)
        grad_shift_one = jnp.sum(grad_act_one, axis=0)
        input_grads.append(
            (grad_resid + norm_back(grad_act_one * gain_one, normed_one, inverse_one)).astype(
                jnp.bfloat16
            )
        )
        terms = (
            grad_qkv_w,
            grad_q_b,
            grad_v_b,
            grad_out_w,
            grad_out_b,
            grad_gain_one,
            grad_shift_one,
            grad_gain_two,
            grad_shift_two,
            grad_fc_w,
            grad_fc_b,
            grad_proj_w,
            grad_proj_b,
        )
        totals = [running_sum + term for running_sum, term in zip(totals, terms)]
    final = (
        lax.psum_scatter(totals[0], ("blk", "head"), scatter_dimension=0, tiled=True),
        lax.psum_scatter(totals[1], ("blk", "head"), scatter_dimension=0, tiled=True),
        lax.psum_scatter(totals[2], ("blk", "head"), scatter_dimension=0, tiled=True),
        lax.psum_scatter(totals[3], ("blk", "head"), scatter_dimension=0, tiled=True),
        lax.psum_scatter(totals[4], ("blk", "head"), scatter_dimension=0, tiled=True),
        lax.psum_scatter(totals[5], ("blk", "head"), scatter_dimension=0, tiled=True),
        lax.psum_scatter(totals[6], ("blk", "head"), scatter_dimension=0, tiled=True),
        lax.psum_scatter(totals[7], ("blk", "head"), scatter_dimension=0, tiled=True),
        lax.psum_scatter(totals[8], ("blk", "head"), scatter_dimension=0, tiled=True),
        lax.psum_scatter(totals[9], ("blk", "head"), scatter_dimension=0, tiled=True),
        lax.psum_scatter(totals[10], ("blk", "head"), scatter_dimension=0, tiled=True),
        lax.psum_scatter(totals[11], ("blk", "head"), scatter_dimension=0, tiled=True),
        lax.psum_scatter(totals[12], ("blk", "head"), scatter_dimension=0, tiled=True),
    )
    return (
        jnp.stack(outputs),
        jnp.stack(input_grads),
        final[0],
        final[1],
        final[2],
        final[3],
        final[4],
        final[5],
        final[6],
        final[7],
        final[8],
        final[9],
        final[10],
        final[11],
        final[12],
    )


RUN = 64
BLOCK = 512
NEG = -1000000000.0
VM = pltpu.VMEM
SM = pltpu.SMEM


def dot_nt(left, right):
    return lax.dot_general(left, right, (((1,), (1,)), ((), ())), preferred_element_type=jnp.float32)


def dot_nn(left, right):
    return lax.dot_general(left, right, (((1,), (0,)), ((), ())), preferred_element_type=jnp.float32)


def rows_at(index, size):
    return pl.ds(pl.multiple_of(index * size, size), size)


def first_block(start, bound):
    return jnp.where(start >= bound, bound // BLOCK, 0)


def forward_kernel(head_size, bound_ref, inloc, outloc, qkv, out, qs, ks, vs, attn_t, lse, vt, mixed):
    tokens = qkv.shape[0]
    runs = tokens // RUN
    scale = head_size ** (-0.5)
    bound = bound_ref[0]

    @pl.loop(0, runs)
    def _(run):
        rows = qkv[rows_at(inloc[run], RUN), :]
        here = rows_at(run, RUN)
        qs[here, :] = (rows[:, :head_size].astype(jnp.float32) * scale).astype(jnp.bfloat16)
        ks[here, :] = rows[:, head_size : 2 * head_size]
        vs[here, :] = rows[:, 2 * head_size :]

    @pl.loop(0, tokens // BLOCK)
    def _(block):
        here = rows_at(block, BLOCK)
        vt[:, here] = vs[here, :].astype(jnp.float32).T.astype(jnp.bfloat16)

    @pl.loop(0, tokens // BLOCK)
    def _(block):
        start = block * BLOCK
        here = rows_at(block, BLOCK)
        queries = qs[here, :]
        query_pos = start + lax.broadcasted_iota(jnp.int32, (1, BLOCK), 1)
        floor = jnp.where(query_pos >= bound, bound, 0)

        def scores_of(index, diagonal):
            keys = ks[rows_at(index, BLOCK), :]
            scores = dot_nt(keys, queries)
            key_pos = index * BLOCK + lax.broadcasted_iota(jnp.int32, (BLOCK, BLOCK), 0)
            visible = key_pos >= floor
            if diagonal:
                visible = visible & (key_pos <= query_pos)
            return jnp.where(visible, scores, NEG)

        scores = scores_of(block, True)
        highest = jnp.max(scores, axis=0, keepdims=True)
        weights = jnp.exp(scores - highest)
        total = jnp.sum(weights, axis=0, keepdims=True)
        accum = dot_nn(vt[:, here], weights.astype(jnp.bfloat16))

        def step(index, state):
            highest, total, accum = state
            scores = scores_of(index, False)
            higher = jnp.maximum(highest, jnp.max(scores, axis=0, keepdims=True))
            weights = jnp.exp(scores - higher)
            factor = jnp.exp(highest - higher)
            total = total * factor + jnp.sum(weights, axis=0, keepdims=True)
            accum = accum * factor + dot_nn(vt[:, rows_at(index, BLOCK)], weights.astype(jnp.bfloat16))
            return higher, total, accum

        highest, total, accum = lax.fori_loop(first_block(start, bound), block, step, (highest, total, accum))
        result = accum / total
        attn_t[:, here] = result.astype(jnp.bfloat16)
        lse[:, here] = highest + jnp.log(total)
        result = result.T.astype(jnp.bfloat16)
        for part in range(BLOCK // RUN):
            mixed[rows_at(outloc[block * (BLOCK // RUN) + part], RUN), :] = result[part * RUN : (part + 1) * RUN]

    chips, _, span = out.shape

    @pl.loop(0, chips)
    def _(chip):
        out[chip] = mixed[rows_at(chip, span), :].astype(jnp.float32).T.astype(jnp.bfloat16)


def attend_forward(bound, inloc, outloc, qkv, chips, head_size):
    tokens = qkv.shape[0]
    bf16 = jnp.bfloat16
    pairs = tokens * (tokens // 2)
    return pl.pallas_call(
        functools.partial(forward_kernel, head_size),
        out_shape=(
            jax.ShapeDtypeStruct((chips, head_size, tokens // chips), bf16),
            jax.ShapeDtypeStruct((tokens, head_size), bf16),
            jax.ShapeDtypeStruct((tokens, head_size), bf16),
            jax.ShapeDtypeStruct((tokens, head_size), bf16),
            jax.ShapeDtypeStruct((head_size, tokens), bf16),
            jax.ShapeDtypeStruct((1, tokens), jnp.float32),
        ),
        in_specs=[pl.BlockSpec(memory_space=SM)] * 3 + [pl.BlockSpec(memory_space=VM)],
        out_specs=[pl.BlockSpec(memory_space=VM)] * 6,
        scratch_shapes=[VM((head_size, tokens), bf16), VM((tokens, head_size), bf16)],
        compiler_params=pltpu.CompilerParams(vmem_limit_bytes=40 * 1024 * 1024),
        cost_estimate=pl.CostEstimate(flops=4 * 4 * pairs * head_size, bytes_accessed=tokens * 2048, transcendentals=pairs),
        name="attend_forward",
    )(bound, inloc, outloc, qkv)


def backward_kernel(
    head_size, count, share, bound_ref, inloc, outloc, grad_t, qs, ks, vs, attn_t, lse, *refs
):
    pieces = refs[:count]
    send_out, normed, raw, grads, kt, dk, dv, mixed, wide, moved, sem = refs[count:]
    tokens = qs.shape[0]
    runs = tokens // RUN
    scale = head_size ** (-0.5)
    bound = bound_ref[0]
    chips, _, span = grad_t.shape
    copies, filled = [], 0
    for piece in pieces:
        copies.append(pltpu.make_async_copy(piece, normed.at[pl.ds(filled, piece.shape[0])], sem))
        filled += piece.shape[0]
    for copy in copies:
        copy.start()

    @pl.loop(0, chips)
    def _(chip):
        mixed[rows_at(chip, span), :] = grad_t[chip, :head_size, :].astype(jnp.float32).T.astype(jnp.bfloat16)

    @pl.loop(0, runs)
    def _(run):
        grads[rows_at(run, RUN), :] = mixed[rows_at(outloc[run], RUN), :]

    @pl.loop(0, tokens // BLOCK)
    def _(block):
        here = rows_at(block, BLOCK)
        kt[:, here] = ks[here, :].astype(jnp.float32).T.astype(jnp.bfloat16)

    @pl.loop(0, tokens // BLOCK)
    def _(block):
        start = block * BLOCK
        here = rows_at(block, BLOCK)
        queries = qs[here, :]
        grad = grads[here, :]
        log_total = lse[:, here]
        delta = jnp.sum(grad.astype(jnp.float32).T * attn_t[:, here].astype(jnp.float32), axis=0, keepdims=True)
        query_pos = start + lax.broadcasted_iota(jnp.int32, (1, BLOCK), 1)
        floor = jnp.where(query_pos >= bound, bound, 0)

        def one(index, diagonal):
            there = rows_at(index, BLOCK)
            scores = dot_nt(ks[there, :], queries)
            key_pos = index * BLOCK + lax.broadcasted_iota(jnp.int32, (BLOCK, BLOCK), 0)
            visible = key_pos >= floor
            if diagonal:
                visible = visible & (key_pos <= query_pos)
            probs = jnp.where(visible, jnp.exp(scores - log_total), 0.0)
            grad_probs = dot_nt(vs[there, :], grad)
            grad_scores = (probs * (grad_probs - delta)).astype(jnp.bfloat16)
            return (
                dot_nn(probs.astype(jnp.bfloat16), grad),
                dot_nn(grad_scores, queries),
                dot_nn(kt[:, there], grad_scores),
                there,
            )

        grad_v, grad_k, grad_q, there = one(block, True)
        dv[there, :] = grad_v
        dk[there, :] = grad_k

        def step(index, grad_q):
            grad_v, grad_k, term, there = one(index, False)
            dv[there, :] += grad_v
            dk[there, :] += grad_k
            return grad_q + term

        grad_q = lax.fori_loop(first_block(start, bound), block, step, grad_q)
        wide[here, :head_size] = (grad_q.T * scale).astype(jnp.bfloat16)

    wide[:, head_size : 2 * head_size] = dk[...].astype(jnp.bfloat16)
    wide[:, 2 * head_size :] = dv[...].astype(jnp.bfloat16)

    size = 3 * head_size

    @pl.loop(0, runs)
    def _(run):
        moved[rows_at(outloc[run], RUN), :] = wide[rows_at(run, RUN), :]

    @pl.loop(0, chips)
    def _(chip):
        send_out[chip, :size, :] = moved[rows_at(chip, span), :].astype(jnp.float32).T.astype(jnp.bfloat16)

    @pl.loop(0, runs)
    def _(run):
        moved[rows_at(inloc[run], RUN), :] = wide[rows_at(run, RUN), :]

    for copy in copies:
        copy.wait()
    raw[...] = jnp.zeros_like(raw)

    @pl.loop(0, tokens // BLOCK)
    def _(block):
        here = rows_at(block, BLOCK)
        turned = moved[here, :].astype(jnp.float32).T.astype(jnp.bfloat16)
        raw[...] += dot_nn(turned, normed[here, :])

    product = raw[...].T
    sums = jnp.sum(wide[...].astype(jnp.float32), axis=0, keepdims=True)
    high = sums.astype(jnp.bfloat16).astype(jnp.float32)
    tail = jnp.concatenate([high, sums - high, jnp.zeros((14, size), jnp.float32)], axis=0)
    for chip in range(chips):
        first = chip // 2 * 4 * share + chip % 2 * share
        rows = jnp.concatenate([product[first : first + share], product[first + 2 * share : first + 3 * share], tail], axis=0)
        rows = jnp.concatenate([rows, jnp.zeros((rows.shape[0], span - size), jnp.float32)], axis=1)
        send_out[chip, size:, :] = rows.astype(jnp.bfloat16)


def attend_backward(bound, inloc, outloc, grad_t, qs, ks, vs, attn_t, lse, pieces, share):
    tokens, head_size = qs.shape
    chips = grad_t.shape[0]
    width = pieces[0].shape[1]
    bf16 = jnp.bfloat16
    pairs = tokens * (tokens // 2)
    return pl.pallas_call(
        functools.partial(backward_kernel, head_size, len(pieces), share),
        out_shape=jax.ShapeDtypeStruct((chips, 3 * head_size + 2 * share + 16, tokens // chips), bf16),
        in_specs=[pl.BlockSpec(memory_space=SM)] * 3 + [pl.BlockSpec(memory_space=VM)] * 6
        + [pl.BlockSpec(memory_space=pltpu.HBM)] * len(pieces),
        out_specs=pl.BlockSpec(memory_space=VM),
        scratch_shapes=[
            VM((tokens, width), bf16),
            VM((3 * head_size, width), jnp.float32),
            VM((tokens, head_size), bf16),
            VM((head_size, tokens), bf16),
            VM((tokens, head_size), jnp.float32),
            VM((tokens, head_size), jnp.float32),
            VM((tokens, head_size), bf16),
            VM((tokens, 3 * head_size), bf16),
            VM((tokens, 3 * head_size), bf16),
            pltpu.SemaphoreType.DMA,
        ],
        compiler_params=pltpu.CompilerParams(vmem_limit_bytes=48 * 1024 * 1024),
        cost_estimate=pl.CostEstimate(flops=4 * 10 * pairs * head_size, bytes_accessed=tokens * 4096, transcendentals=pairs),
        name="attend_backward",
    )(bound, inloc, outloc, grad_t, qs, ks, vs, attn_t, lse, *pieces)


HALF_STEP = 512


def gelu_pair(values):
    cubic = values * values
    inner = 0.7978845608028654 * values * (1.0 + 0.044715 * cubic)
    bent = jnp.tanh(inner)
    slope = 0.7978845608028654 * (1.0 + 0.134145 * cubic)
    half = 0.5 * (1.0 + bent)
    return values * half, half + 0.5 * values * (1.0 - bent * bent) * slope


def load_rows(table, pieces, targets, sem, wait):
    slot = 0
    for piece in pieces:
        count = piece.shape[0]

        @pl.loop(0, count)
        def _(index, piece=piece, slot=slot):
            chip = table[0, slot + index]
            for rows, target in targets(chip):
                copy = pltpu.make_async_copy(piece.at[index, rows], target, sem)
                if wait:
                    copy.wait()
                else:
                    copy.start()

        slot += count


def project_kernel(count, table, got, *refs):
    pieces, (part_out, sent, attn_in, w_out, sem) = refs[:count], refs[count:]
    chips, size, span = got.shape
    share = w_out.shape[0] // chips
    rows = span // 2

    def targets(chip):
        return [(pl.ds(0, share), w_out.at[rows_at(chip, share)])]

    load_rows(table, pieces, targets, sem, False)
    for chip in range(chips):
        micro, head = divmod(chip, chips // 2)
        for rel in range(2):
            column = (rel * 2 + micro) * rows
            attn_in[head * size : (head + 1) * size, column : column + rows] = got[chip, :, rel * rows : (rel + 1) * rows]
    load_rows(table, pieces, targets, sem, True)
    left = attn_in[...].astype(jnp.float32).T.astype(jnp.bfloat16)
    part = dot_nn(left, w_out[...])
    part_out[...] = part
    sent[...] = part.astype(jnp.bfloat16)


def project(table, got, pieces, share):
    chips, size, span = got.shape
    width = pieces[0].shape[2]
    tokens = 2 * span
    bf16 = jnp.bfloat16
    return pl.pallas_call(
        functools.partial(project_kernel, len(pieces)),
        out_shape=(
            jax.ShapeDtypeStruct((tokens, width), jnp.float32),
            jax.ShapeDtypeStruct((tokens, width), bf16),
            jax.ShapeDtypeStruct((chips // 2 * size, tokens), bf16),
        ),
        in_specs=[pl.BlockSpec(memory_space=SM), pl.BlockSpec(memory_space=VM)]
        + [pl.BlockSpec(memory_space=pltpu.HBM)] * len(pieces),
        out_specs=[pl.BlockSpec(memory_space=VM)] * 3,
        scratch_shapes=[VM((chips * share, width), bf16), pltpu.SemaphoreType.DMA],
        compiler_params=pltpu.CompilerParams(vmem_limit_bytes=58 * 1024 * 1024),
        cost_estimate=pl.CostEstimate(
            flops=2 * tokens * chips * share * width, bytes_accessed=8 * tokens * width, transcendentals=0
        ),
        name="project",
    )(table, got, *pieces)


def middle_kernel(count, share, table, x_a, x_b, g_a, g_b, part, got_a, got_b, *refs):
    pieces = refs[:count]
    (resid, base, other, grad_act, grad_sent, fc_sums, vectors, terms) = refs[count : count + 8]
    (smalls, fc_bias, w_fc, w_proj, g_all, act, act_t, rest, proj_buf, fc_buf, small_sem, load_sem, proj_sem, fc_sem) = refs[count + 8 :]
    f32, bf16 = jnp.float32, jnp.bfloat16
    tokens, width = part.shape
    own = tokens // 2
    hidden = w_proj.shape[0]
    chips = terms.shape[0]
    each = hidden // chips
    folds = hidden // width
    fc_row = share + each

    def targets(chip):
        wanted = [(pl.ds(share, each), w_proj.at[rows_at(chip, each)])]
        for fold in range(folds):
            for core in range(2):
                first = fc_row + (fold * 2 + core) * share
                place = ((chip // 2) * 2 + core) * 2 + chip % 2
                wanted.append(
                    (pl.ds(first, share), w_fc.at[rows_at(place, share), pl.ds(fold * width, width)])
                )
        return wanted

    def small_targets(chip):
        return [(pl.ds(pieces[0].shape[1] - 16, 16), smalls.at[chip])]

    load_rows(table, pieces, small_targets, small_sem, False)
    load_rows(table, pieces, targets, load_sem, False)
    load_rows(table, pieces, small_targets, small_sem, True)
    small_sum = jnp.sum(smalls[...].astype(f32), axis=0)
    vectors[...] = small_sum[:8]
    for fold in range(folds):
        fc_bias[:, fold * width : (fold + 1) * width] = small_sum[8 + fold : 9 + fold]
    for half, (x_in, g_in, arrived) in enumerate(((x_a, g_a, got_a), (x_b, g_b, got_b))):
        here = slice(half * own, (half + 1) * own)
        g_all[here, :] = g_in[...]
        value = x_in[...].astype(f32) + part[here, :] + arrived[...].astype(f32) + vectors[2:3, :]
        resid[here, :] = value
        centred = value - jnp.mean(value, axis=-1, keepdims=True)
        inverse = lax.rsqrt(jnp.mean(centred * centred, axis=-1, keepdims=True) + 1e-05)
        rounded = (centred * inverse * vectors[0:1, :] + vectors[1:2, :]).astype(bf16)
        act[here, :] = rounded
        act_t[:, here] = rounded.astype(f32).T.astype(bf16)
    base[...] = resid[:own, :] + vectors[3:4, :]
    load_rows(table, pieces, targets, load_sem, True)

    per_step = HALF_STEP // each

    def copies(step, slot):
        made = []
        for index in range(per_step):
            made.append(
                pltpu.make_async_copy(
                    proj_buf.at[slot, pl.ds(index * each, each)],
                    terms.at[table[1, step * per_step + index], pl.ds(0, each)],
                    proj_sem.at[slot],
                )
            )
        fold = step // (width // HALF_STEP)
        column = pl.multiple_of(step % (width // HALF_STEP) * HALF_STEP, HALF_STEP)
        for chip in range(chips):
            for core in range(2):
                place = ((chip // 2) * 2 + core) * 2 + chip % 2
                made.append(
                    pltpu.make_async_copy(
                        fc_buf.at[slot, pl.ds(place * share, share)],
                        terms.at[
                            table[1, chip],
                            pl.ds(pl.multiple_of(each + share + (fold * 2 + core) * share, 16), share),
                            pl.ds(column, HALF_STEP),
                        ],
                        fc_sem.at[slot],
                    )
                )
        return made

    steps = hidden // HALF_STEP

    @pl.loop(0, steps)
    def _(step):
        slot = step % 2
        columns = pl.ds(pl.multiple_of(step * HALF_STEP, HALF_STEP), HALF_STEP)
        rows = rows_at(step, HALF_STEP)

        @pl.when(step >= 2)
        def _():
            for copy in copies(step - 2, slot):
                copy.wait()

        grads = g_all[...]
        value, slope = gelu_pair(dot_nn(act[...], w_fc[:, columns]) + fc_bias[:, columns])
        value = value.astype(bf16)
        proj_buf[slot] = dot_nn(value.astype(f32).T.astype(bf16), grads).astype(bf16)
        grad_pre = (dot_nt(grads, w_proj[rows, :]) * slope).astype(bf16)
        fc_sums[:, columns] = jnp.sum(grad_pre.astype(f32), axis=0, keepdims=True)
        fc_buf[slot] = dot_nn(act_t[...], grad_pre).astype(bf16)
        for copy in copies(step, slot):
            copy.start()
        projected = dot_nn(value, w_proj[rows, :])
        back = dot_nt(grad_pre, w_fc[:, columns])
        base[...] += projected[:own]

        @pl.when(step == 0)
        def _():
            grad_act[...] = back
            rest[...] = projected[own:]

        @pl.when(step > 0)
        def _():
            grad_act[...] += back
            rest[...] += projected[own:]

    other[...] = rest[...].astype(bf16)
    grad_sent[...] = grad_act[...].astype(bf16)
    for step in range(steps - 2, steps):
        for copy in copies(step, step % 2):
            copy.wait()


def middle(table, x_a, x_b, g_a, g_b, part, got_a, got_b, pieces, share, hidden):
    tokens, width = part.shape
    f32, bf16 = jnp.float32, jnp.bfloat16
    chips = table.shape[1]
    each = hidden // chips
    rows = share + each + 2 * share * (hidden // width)
    shape = jax.ShapeDtypeStruct
    return pl.pallas_call(
        functools.partial(middle_kernel, len(pieces), share),
        out_shape=(
            shape((tokens, width), f32),
            shape((tokens // 2, width), f32),
            shape((tokens // 2, width), bf16),
            shape((tokens, width), f32),
            shape((tokens, width), bf16),
            shape((1, hidden), f32),
            shape((8, width), f32),
            shape((chips, rows, width), bf16),
        ),
        in_specs=[pl.BlockSpec(memory_space=SM)]
        + [pl.BlockSpec(memory_space=VM)] * 7
        + [pl.BlockSpec(memory_space=pltpu.HBM)] * len(pieces),
        out_specs=[pl.BlockSpec(memory_space=VM)] * 7 + [pl.BlockSpec(memory_space=pltpu.HBM)],
        scratch_shapes=[
            VM((chips, 16, width), bf16),
            VM((1, hidden), f32),
            VM((width, hidden), bf16),
            VM((hidden, width), bf16),
            VM((tokens, width), bf16),
            VM((tokens, width), bf16),
            VM((width, tokens), bf16),
            VM((tokens // 2, width), f32),
            VM((2, HALF_STEP, width), bf16),
            VM((2, width, HALF_STEP), bf16),
            pltpu.SemaphoreType.DMA,
            pltpu.SemaphoreType.DMA,
            pltpu.SemaphoreType.DMA((2,)),
            pltpu.SemaphoreType.DMA((2,)),
        ],
        compiler_params=pltpu.CompilerParams(vmem_limit_bytes=56 * 1024 * 1024),
        cost_estimate=pl.CostEstimate(
            flops=12 * tokens * width * hidden, bytes_accessed=8 * width * hidden, transcendentals=tokens * hidden
        ),
        name="middle",
    )(table, x_a, x_b, g_a, g_b, part, got_a, got_b, *pieces)


def branch_kernel(share, row, table, resid, g_a, g_b, part, got_a, got_b, vectors, fc_sums, attn_in, given, grad_resid, branch, tails, terms, products, sem):
    f32, bf16 = jnp.float32, jnp.bfloat16
    tokens, width = resid.shape
    own = tokens // 2
    chips = tails.shape[0]
    gain_sum = jnp.zeros((1, width), f32)
    shift_sum = jnp.zeros((1, width), f32)
    bias_sum = jnp.zeros((1, width), f32)
    proj_sum = jnp.zeros((1, width), f32)
    for half, (g_in, arrived) in enumerate(((g_a, got_a), (g_b, got_b))):
        here = slice(half * own, (half + 1) * own)
        value = resid[here, :]
        centred = value - jnp.mean(value, axis=-1, keepdims=True)
        inverse = lax.rsqrt(jnp.mean(centred * centred, axis=-1, keepdims=True) + 1e-05)
        normed = centred * inverse
        grad = part[here, :] + arrived[...].astype(f32)
        gain_sum += jnp.sum(grad * normed, axis=0, keepdims=True)
        shift_sum += jnp.sum(grad, axis=0, keepdims=True)
        scaled = grad * vectors[0:1, :]
        given_grad = g_in[...].astype(f32)
        total = given_grad + inverse * (
            scaled
            - jnp.mean(scaled, axis=-1, keepdims=True)
            - normed * jnp.mean(scaled * normed, axis=-1, keepdims=True)
        )
        rounded = total.astype(bf16)
        bias_sum += jnp.sum(rounded.astype(f32), axis=0, keepdims=True)
        proj_sum += jnp.sum(given_grad, axis=0, keepdims=True)
        branch[here, :] = rounded
        if half == 0:
            grad_resid[...] = total
    group = width // (chips // 2)
    sums = jnp.concatenate([gain_sum, shift_sum, bias_sum, proj_sum], axis=0)
    each = fc_sums.shape[1] // chips
    for chip in range(chips):
        first = chip // 2 * group
        tail = jnp.concatenate(
            [
                sums[:, first : first + group],
                fc_sums[:, chip * each : (chip + 1) * each],
                jnp.zeros((3, group), f32),
            ],
            axis=0,
        )
        high = tail.astype(bf16)
        low = (tail - high.astype(f32)).astype(bf16)
        tails[chip] = jnp.concatenate([high, low], axis=1)
    products[...] = dot_nn(attn_in[...], branch[...]).astype(bf16)

    @pl.loop(0, chips)
    def _(chip):
        pltpu.make_async_copy(products.at[rows_at(chip, share)], terms.at[table[1, chip], pl.ds(row, share)], sem).start()

    @pl.loop(0, chips)
    def _(chip):
        pltpu.make_async_copy(products.at[rows_at(chip, share)], terms.at[table[1, chip], pl.ds(row, share)], sem).wait()


def branch_back(table, resid, g_a, g_b, part, got_a, got_b, vectors, fc_sums, attn_in, terms, share, row, span):
    tokens, width = resid.shape
    f32, bf16 = jnp.float32, jnp.bfloat16
    chips = table.shape[1]
    shape = jax.ShapeDtypeStruct
    return pl.pallas_call(
        functools.partial(branch_kernel, share, row),
        out_shape=(
            shape((tokens // 2, width), f32),
            shape((tokens, width), bf16),
            shape((chips, 8, span), bf16),
            shape(terms.shape, bf16),
        ),
        in_specs=[pl.BlockSpec(memory_space=SM)]
        + [pl.BlockSpec(memory_space=VM)] * 9
        + [pl.BlockSpec(memory_space=pltpu.HBM)],
        out_specs=[pl.BlockSpec(memory_space=VM)] * 3 + [pl.BlockSpec(memory_space=pltpu.HBM)],
        scratch_shapes=[VM((chips * share, width), bf16), pltpu.SemaphoreType.DMA],
        input_output_aliases={10: 3},
        compiler_params=pltpu.CompilerParams(vmem_limit_bytes=40 * 1024 * 1024),
        cost_estimate=pl.CostEstimate(
            flops=2 * tokens * chips * share * width, bytes_accessed=16 * tokens * width, transcendentals=0
        ),
        name="branch_back",
    )(table, resid, g_a, g_b, part, got_a, got_b, vectors, fc_sums, attn_in, terms)


def attention_back_kernel(count, table, branch, tails, *refs):
    pieces, (sent, w_out, sem) = refs[:count], refs[count:]
    chips, size, span = sent.shape
    size -= 8
    rows = span // 2
    share = w_out.shape[0] // chips

    def targets(chip):
        return [(pl.ds(0, share), w_out.at[rows_at(chip, share)])]

    load_rows(table, pieces, targets, sem, False)
    sent[:, size:, :] = tails[...]
    load_rows(table, pieces, targets, sem, True)
    grads = dot_nt(w_out[...], branch[...]).astype(jnp.bfloat16)
    for chip in range(chips):
        micro, head = divmod(chip, chips // 2)
        for rel in range(2):
            column = (rel * 2 + micro) * rows
            sent[chip, :size, rel * rows : (rel + 1) * rows] = grads[
                head * size : (head + 1) * size, column : column + rows
            ]


def attention_back(table, branch, tails, pieces, share, size):
    tokens, width = branch.shape
    chips, _, span = tails.shape
    bf16 = jnp.bfloat16
    return pl.pallas_call(
        functools.partial(attention_back_kernel, len(pieces)),
        out_shape=jax.ShapeDtypeStruct((chips, size + 8, span), bf16),
        in_specs=[pl.BlockSpec(memory_space=SM)]
        + [pl.BlockSpec(memory_space=VM)] * 2
        + [pl.BlockSpec(memory_space=pltpu.HBM)] * len(pieces),
        out_specs=pl.BlockSpec(memory_space=VM),
        scratch_shapes=[VM((chips * share, width), bf16), pltpu.SemaphoreType.DMA],
        compiler_params=pltpu.CompilerParams(vmem_limit_bytes=58 * 1024 * 1024),
        cost_estimate=pl.CostEstimate(
            flops=2 * tokens * chips * share * width, bytes_accessed=4 * tokens * width, transcendentals=0
        ),
        name="attention_back",
    )(table, branch, tails, *pieces)


def finish_kernel(order, got, weights, kept, sent, weight, grads, sem):
    chips, _, span = got.shape
    size = weight.shape[0] // len(order)
    rows = span // 2
    own = kept.shape[0]

    def copies():
        return [
            pltpu.make_async_copy(weights.at[slot], weight.at[pl.ds(head * size, size)], sem)
            for slot, head in enumerate(order)
        ]

    for copy in copies():
        copy.start()
    for chip in range(chips):
        micro, head = divmod(chip, chips // 2)
        turned = got[chip, :size, :].astype(jnp.float32).T.astype(jnp.bfloat16)
        for rel in range(2):
            row = (rel * 2 + micro) * rows
            grads[head, row : row + rows, :] = turned[rel * rows : (rel + 1) * rows]
    for copy in copies():
        copy.wait()
    left = jnp.concatenate([grads[head] for head in range(len(order))], axis=1)
    back = dot_nn(left, weight[...])
    kept[...] = back[:own]
    sent[...] = back[own:].astype(jnp.bfloat16)


def finish(got, weights, order):
    chips, _, span = got.shape
    heads, size, width = weights.shape
    bf16 = jnp.bfloat16
    return pl.pallas_call(
        functools.partial(finish_kernel, order),
        out_shape=(
            jax.ShapeDtypeStruct((span, width), jnp.float32),
            jax.ShapeDtypeStruct((span, width), bf16),
        ),
        in_specs=[pl.BlockSpec(memory_space=VM), pl.BlockSpec(memory_space=pltpu.HBM)],
        out_specs=[pl.BlockSpec(memory_space=VM)] * 2,
        scratch_shapes=[
            VM((heads * size, width), bf16),
            VM((heads, 2 * span, size), bf16),
            pltpu.SemaphoreType.DMA,
        ],
        compiler_params=pltpu.CompilerParams(vmem_limit_bytes=58 * 1024 * 1024),
        cost_estimate=pl.CostEstimate(
            flops=4 * span * width * heads * size,
            bytes_accessed=2 * width * heads * size + 8 * span * width,
            transcendentals=0,
        ),
        name="finish",
    )(got, weights)


PATHS = (("x", "z", "head"), ("head", "z", "x"))


PAIR = [(0, 1), (1, 0)]
NEAR = [(0, 1), (1, 0), (2, 3), (3, 2)]
FAR = [(0, 2), (2, 0), (1, 3), (3, 1)]


def swap(values, axis, pairs=PAIR):
    return lax.ppermute(values, axis, pairs)


def across(values, axis):
    return swap(values, axis, NEAR if axis == "z" else PAIR)


def in_order(mine, other, index, axis):
    first = jnp.where(index == 0, mine, other)
    second = jnp.where(index == 0, other, mine)
    return jnp.stack([first, second], axis=axis)


def split_float(values):
    high = values.astype(jnp.bfloat16)
    low = (values - high.astype(jnp.float32)).astype(jnp.bfloat16)
    return high, low


def run_table(order, pair_start):
    pairs = order.shape[0]
    runs = jnp.arange(2 * pairs, dtype=jnp.int32)[:, None]
    low = jnp.where(runs == order[None, :], pair_start[None, :], 0)
    high = jnp.where(runs == 2 * pairs - 1 - order[None, :], pair_start[None, :] + 1, 0)
    return jnp.sum(low + high, axis=1).astype(jnp.int32)


def ring_order(count, turn):
    half = [(z, (z + step + turn) % 2) for z in range(count) for step in range(2)]
    return [z * 4 + y for z, y in half] + [z * 4 + 2 + y for z, y in reversed(half)]


def core_groups(rings):
    return [[(chip // 2 * 2 + core) * 2 + chip % 2 for chip in ring] for core, ring in enumerate(rings)]


def cube_orders(depth):
    cycle = [0, 1, 3, 2, 6, 7, 5, 4]
    return [[chip + start for chip in cycle] for start in (0, 4 * depth)]


def fast_body(
    block_input,
    qkv_weight,
    q_bias,
    v_bias,
    out_weight,
    out_bias,
    norm1_gain,
    norm1_shift,
    norm2_gain,
    norm2_shift,
    fc_weight,
    fc_bias,
    proj_weight,
    proj_bias,
    out_grad,
    dealt,
    lengths,
):
    f32, bf16 = jnp.float32, jnp.bfloat16
    micro, rows, width = block_input.shape
    nz, nx = lax.axis_size("z"), lax.axis_size("x")
    iz, ix, ic, iy = (lax.axis_index(name) for name in ("z", "x", "core", "head"))
    zx = nz * nx
    every, chips = ("z", "x", "core", "head"), ("z", "x", "head")
    devices, chip_count = 4 * zx, 2 * zx
    heads = 2 * zx
    local = heads * DH // 2
    share = qkv_weight.shape[0]
    hidden_share = proj_weight.shape[0]
    hidden_half = hidden_share * chip_count

    inputs = block_input.astype(f32)
    normed_one, inverse_one = normalize(inputs)
    n1 = normed_one.astype(bf16)
    n1, qkv_weight, fc_weight, norm1_gain, norm2_gain = lax.optimization_barrier(
        (n1, qkv_weight, fc_weight, norm1_gain, norm2_gain)
    )
    gain_one = norm1_gain.astype(f32)
    shift_one = norm1_shift.astype(f32)
    raw_qkv = qkv_weight.astype(f32)
    scaled_qkv = (raw_qkv * gain_one[:, None]).astype(bf16)
    device = ((iz * nx + ix) * 2 + ic) * 2 + iy
    offset = jnp.sum(raw_qkv * shift_one[:, None], axis=0)
    zero = jnp.zeros((width,), f32)
    place = device * share
    offset = offset + jnp.concatenate(
        [
            lax.dynamic_update_slice(zero, q_bias.astype(f32), (place,)),
            zero,
            lax.dynamic_update_slice(zero, v_bias.astype(f32), (place,)),
        ]
    )
    high, low = split_float(offset)
    to_heads = jnp.concatenate([scaled_qkv, high[None], low[None], jnp.zeros((6, 3 * width), bf16)], axis=0)
    to_heads = to_heads.reshape(share + 8, 3, zx // 2, 2, 2, DH).transpose(2, 4, 3, 0, 1, 5)
    to_heads = to_heads.reshape(1, heads, share + 8, 3 * DH)
    to_heads = jnp.broadcast_to(to_heads, (2, heads, share + 8, 3 * DH)).reshape(devices, share + 8, 3 * DH)
    head_rows = lax.all_to_all(to_heads, every, split_axis=0, concat_axis=0, tiled=True)
    head_weight = head_rows[:, :share].reshape(width, 3 * DH)
    head_offset = jnp.sum(head_rows[:, share : share + 2].astype(f32), axis=(0, 1))

    mine = iz // 2
    near = lax.dynamic_index_in_dim(n1, mine, 0, keepdims=False)
    far = swap(lax.dynamic_index_in_dim(n1, 1 - mine, 0, keepdims=False), "z", FAR)
    paths = PATHS
    got = across(near, paths[0][0])
    far, got = lax.optimization_barrier((far, got))
    near = jnp.stack([near, got])
    near_got, far_got = across(near, paths[0][1]), across(far, paths[1][0])
    near_got, far_got = lax.optimization_barrier((near_got, far_got))
    near, far = jnp.stack([near, near_got]), jnp.stack([far, far_got])
    near_got, far_got = across(near, paths[0][2]), across(far, paths[1][1])
    far = jnp.stack([far, far_got])
    parts = [near, near_got, far, across(far, paths[1][2])]
    pieces, owners = [], []

    def add_all(flip):
        core = 1 - ic if flip else ic
        for index, part in enumerate(parts):
            pieces.append((swap(part, "core") if flip else part).reshape(-1, width))
            for second in range(2):
                for first in range(2):
                    flips = dict(zip(paths[index // 2], (first, second, index % 2)))
                    owners.append((iz ^ flips["z"] ^ (index // 2 * 2), ix ^ flips["x"], core, iy ^ flips["head"]))

    add_all(False)
    add_all(True)
    slot_device = jnp.stack([((z * nx + x) * 2 + core) * 2 + y for z, x, core, y in owners]).astype(jnp.int32)
    my_dealt = lax.dynamic_index_in_dim(dealt, mine, 0, keepdims=False)
    order = my_dealt.reshape(devices, rows)[:, 0] // RUN
    slot_of = jnp.sum(
        jnp.where(jnp.arange(devices)[:, None] == slot_device[None, :], jnp.arange(devices)[None, :], 0), axis=1
    )
    inloc = run_table(order, (slot_of * 2).astype(jnp.int32))
    ids = jnp.arange(devices, dtype=jnp.int32)
    id_y, id_c, id_zx = ids % 2, ids // 2 % 2, ids // 4
    send_pair = (id_zx * 2 + id_y) * 2 + (id_c ^ ic)
    outloc = run_table(order, (send_pair * 2).astype(jnp.int32))
    bound = lax.dynamic_index_in_dim(lengths, mine, 0, keepdims=False)[:1]

    fc_parts = fc_weight.reshape(share, zx, 2, 2, hidden_share)

    def core_columns(values, index):
        return lax.dynamic_index_in_dim(values, index, 2, keepdims=False)

    fc_mine = core_columns(fc_parts, ic).reshape(share, hidden_half)
    fc_other = swap(core_columns(fc_parts, 1 - ic).reshape(share, hidden_half), "core")
    fc_pair = in_order(fc_mine, fc_other, ic, 0).reshape(2 * share, hidden_half)
    small = jnp.stack([norm2_gain, norm2_shift, out_bias, proj_bias])
    small_rows = jnp.zeros((16, width), bf16)
    small_rows = lax.dynamic_update_slice(small_rows, small, (0, place))
    other_place = (((iz * nx + ix) * 2 + 1 - ic) * 2 + iy) * share
    small_rows = lax.dynamic_update_slice(small_rows, swap(small, "core"), (0, other_place))
    fc_place = ((iz * nx + ix) * 2 + iy) * hidden_share
    small_rows = lax.dynamic_update_slice(small_rows, fc_bias[None], (8 + fc_place // width, fc_place % width))
    folds = hidden_half // width
    fc_folded = fc_pair.reshape(2 * share, folds, width).transpose(1, 0, 2).reshape(-1, width)
    packed = jnp.concatenate([out_weight, proj_weight, fc_folded, small_rows], axis=0)
    rings = [ring_order(nz, turn) for turn in range(2)]
    places = [[ring.index(chip) for chip in range(chip_count)] for ring in rings]
    table = lax.dynamic_index_in_dim(
        jnp.array([[ring, place] for ring, place in zip(rings, places)], jnp.int32), ic, 0, keepdims=False
    )
    gathered = lax.all_gather(packed, every, axis=0, axis_index_groups=core_groups(rings))
    out_rows = share
    proj_rows = hidden_share
    fc_rows = 2 * share * folds

    mixed = [(product(piece, head_weight) + head_offset).astype(bf16) for piece in pieces]
    slots = jnp.concatenate(mixed, axis=0)
    attn_send, queries, keys, values, attn_t, lse = attend_forward(bound, inloc, outloc, slots, chip_count, DH)

    x_a, x_b = block_input.reshape(-1, width), swap(block_input, "core").reshape(-1, width)
    g_a, g_b = out_grad.reshape(-1, width), swap(out_grad, "core").reshape(-1, width)
    own = micro * rows
    attn_got = lax.all_to_all(attn_send, chips, split_axis=0, concat_axis=0, tiled=True)
    weight_turned, attn_got = lax.optimization_barrier((head_weight.T, attn_got))
    cubes = cube_orders(nz // 2)
    w_qkv = lax.all_gather(weight_turned, chips, axis=0, axis_index_groups=cubes)
    part, sent, attn_in = project(table, attn_got, [gathered], share)
    resid, base, project_other, grad_part, sent_back, fc_sums, vectors, terms = middle(
        table, x_a, x_b, g_a, g_b, part, swap(sent[own:], "core"), swap(sent[:own], "core"), [gathered], share, hidden_half
    )
    grad_resid, branch, tails, terms = branch_back(
        table,
        resid,
        g_a,
        g_b,
        grad_part,
        swap(sent_back[own:], "core"),
        swap(sent_back[:own], "core"),
        vectors,
        fc_sums,
        attn_in,
        terms,
        share,
        proj_rows,
        2 * rows,
    )
    grad_send = attention_back(table, branch, tails, [gathered], share, DH)
    output = (base + swap(project_other, "core").astype(f32)).astype(bf16)

    grad_got = lax.all_to_all(grad_send, chips, split_axis=0, concat_axis=0, tiled=True)
    vector_sums = jnp.sum(grad_got[:, DH:].astype(f32), axis=0)
    vector_sums = vector_sums[:, :rows] + vector_sums[:, rows:]
    final_vectors = lax.dynamic_slice(vector_sums, (0, (ic * 2 + iy) * share), (4, share))
    final_fc_b = vector_sums[4]

    summed = lax.psum_scatter(
        terms, every, scatter_dimension=0, tiled=True, axis_index_groups=core_groups(rings)
    )[0]
    final_proj_w = summed[:proj_rows].astype(f32)
    final_out_w = summed[proj_rows : proj_rows + out_rows].astype(f32)
    fc_sum = summed[proj_rows + out_rows :].reshape(folds, 2, share, width)
    fc_keep = lax.dynamic_index_in_dim(fc_sum, ic, 1, keepdims=False)
    fc_give = swap(lax.dynamic_index_in_dim(fc_sum, 1 - ic, 1, keepdims=False), "core")

    def by_owner(values):
        return values.transpose(1, 0, 2).reshape(share, zx, 2, hidden_share)

    final_fc_w = in_order(by_owner(fc_keep), by_owner(fc_give), ic, 2).reshape(share, 2 * hidden_half).astype(f32)

    send_grads = attend_backward(
        bound, inloc, outloc, grad_got, queries, keys, values, attn_t, lse, pieces, share
    )
    grads_got = lax.all_to_all(send_grads, chips, split_axis=0, concat_axis=0, tiled=True)
    back_own, back_other = finish(grads_got, w_qkv, cubes[0])
    raw_got = grads_got[:, 3 * DH :, : 3 * DH].astype(f32)
    raw_sum = jnp.sum(raw_got.reshape(2, zx, 2 * share + 16, 3 * DH), axis=0)
    raw_parts = raw_sum[:, : 2 * share].reshape(zx, 2, share, 3 * DH)
    sums_mine = raw_sum[:, 2 * share : 2 * share + 1] + raw_sum[:, 2 * share + 1 : 2 * share + 2]
    raw_keep = jnp.concatenate([lax.dynamic_index_in_dim(raw_parts, ic, 1, keepdims=False), sums_mine], axis=1)
    raw_give = jnp.concatenate([lax.dynamic_index_in_dim(raw_parts, 1 - ic, 1, keepdims=False), sums_mine], axis=1)
    raw_all = in_order(raw_keep, swap(raw_give, "core"), ic, 1).reshape(heads, share + 1, 3, DH)
    raw_all = raw_all.transpose(1, 2, 0, 3).reshape(share + 1, 3 * width)
    raw_grad, all_sums = raw_all[:share], raw_all[share]
    final_qkv_w = raw_grad * gain_one[:, None] + shift_one[:, None] * all_sums[None, :]
    final_gain_one = jnp.sum(raw_grad * raw_qkv, axis=1)
    final_shift_one = jnp.sum(raw_qkv * all_sums[None, :], axis=1)
    final_q_b = lax.dynamic_slice(all_sums, (place,), (share,))
    final_v_b = lax.dynamic_slice(all_sums, (2 * width + place,), (share,))

    back_own = back_own + swap(back_other, "core").astype(f32)
    back_own = back_own.reshape(micro, rows, width)
    input_grad = grad_resid.reshape(micro, rows, width) + norm_back(back_own, normed_one, inverse_one)

    return (
        output.reshape(micro, rows, width),
        input_grad.astype(bf16),
        final_qkv_w,
        final_q_b,
        final_v_b,
        final_out_w,
        final_vectors[2],
        final_gain_one,
        final_shift_one,
        final_vectors[0],
        final_vectors[1],
        final_fc_w,
        final_fc_b,
        final_proj_w,
        final_vectors[3],
    )


def specs(names):
    rows, vector, tokens = P(names, None), P(names), P(None, names, None)
    weights = (rows, vector, vector, rows, vector, vector, vector, vector, vector, rows, vector, rows, vector)
    return (tokens, *weights, tokens, P(), P()), (tokens, tokens, *weights)


def solution(mesh):
    sizes = dict(mesh.shape)
    if sizes["head"] == 2 and sizes["blk"] == 16:
        fine = Mesh(mesh.devices.reshape(2, 4, 2, 2), ("head", "z", "x", "core"))
        given, made = specs(("z", "x", "core", "head"))
        return jax.shard_map(fast_body, mesh=fine, in_specs=given, out_specs=made, check_vma=False)
    given, made = specs(("blk", "head"))
    return jax.shard_map(general_body, mesh=mesh, in_specs=given, out_specs=made, check_vma=False)
```

```python
import functools
import math

import jax
import jax.numpy as jnp
from jax import lax
from jax.experimental import pallas as pl
from jax.experimental.pallas import tpu as pltpu
from jax.sharding import Mesh
from jax.sharding import PartitionSpec as P

DH = 64


def gelu_tanh(values):
    inner = 0.7978845608028654 * (values + 0.044715 * values * values * values)
    return 0.5 * values * (1.0 + jnp.tanh(inner))


def normalize(values):
    centred = values - jnp.mean(values, axis=-1, keepdims=True)
    inverse = lax.rsqrt(jnp.mean(centred * centred, axis=-1, keepdims=True) + 1e-05)
    return (centred * inverse, inverse)


def norm_back(grad_normed, normed, inverse):
    return inverse * (
        grad_normed
        - jnp.mean(grad_normed, axis=-1, keepdims=True)
        - normed * jnp.mean(grad_normed * normed, axis=-1, keepdims=True)
    )


def product(left, right):
    return jnp.dot(left, right, preferred_element_type=jnp.float32)


def product_tn(left, right):
    return lax.dot_general(
        left, right, (((0,), (0,)), ((), ())), preferred_element_type=jnp.float32
    )


def product_nt(left, right):
    return lax.dot_general(
        left, right, (((1,), (1,)), ((), ())), preferred_element_type=jnp.float32
    )


def visible_pairs(query_pos, key_pos, boundary):
    same_side = (query_pos[:, None] >= boundary) == (key_pos[None, :] >= boundary)
    return same_side & (key_pos[None, :] <= query_pos[:, None])


def forward_tile(current, queries3, keys3, values3, visible, scale):
    running, total, accum = current
    scores = jnp.einsum("qhd,khd->hqk", queries3, keys3, preferred_element_type=jnp.float32) * scale
    scores = jnp.where(visible[None], scores, -1000000000.0)
    highest = jnp.maximum(running, jnp.max(scores, axis=-1))
    weights = jnp.where(visible[None], jnp.exp(scores - highest[..., None]), 0.0)
    factor = jnp.exp(running - highest)
    total = total * factor + jnp.sum(weights, axis=-1)
    accum = accum * factor[..., None] + jnp.einsum(
        "hqk,khd->hqd", weights.astype(jnp.bfloat16), values3, preferred_element_type=jnp.float32
    )
    return (highest, total, accum)


def general_forward(query_parts, pos_parts, positions, boundary, keys_group, values_group, key_span):
    heads_local, head_size = (query_parts[0].shape[1], query_parts[0].shape[2])
    scale = head_size ** (-0.5)

    def fold_keys(state, pieces, start):
        key_rows, value_rows = pieces
        count_rows = key_rows.shape[0]
        block_rows = math.gcd(count_rows, key_span)
        block_count = count_rows // block_rows

        def one_step(index, inner):
            offset = index * block_rows
            keys3 = lax.dynamic_slice_in_dim(key_rows, offset, block_rows).reshape(
                block_rows, heads_local, head_size
            )
            values3 = lax.dynamic_slice_in_dim(value_rows, offset, block_rows).reshape(
                block_rows, heads_local, head_size
            )
            key_pos = lax.dynamic_slice_in_dim(positions, offset, block_rows)
            part_queries = query_parts[0]
            visible = visible_pairs(pos_parts[0], key_pos, boundary)
            current = inner[0]
            result = forward_tile(current, part_queries, keys3, values3, visible, scale)
            updated = [result]
            return tuple(updated)

        return lax.fori_loop(0, block_count, one_step, state)

    initial = tuple(
        (
            (
                jnp.full((heads_local, part.shape[0]), -1000000000.0, jnp.float32),
                jnp.zeros((heads_local, part.shape[0]), jnp.float32),
                jnp.zeros((heads_local, part.shape[0], head_size), jnp.float32),
            )
            for part in query_parts
        )
    )
    return fold_keys(
        initial,
        (
            lax.all_gather(keys_group, "blk", axis=0, tiled=True),
            lax.all_gather(values_group, "blk", axis=0, tiled=True),
        ),
        jnp.int32(0),
    )


def backward_tile(current, queries3, grad3, log_total, delta, keys3, values3, visible, scale):
    grad_query, term = current
    scores = jnp.einsum("qhd,khd->hqk", queries3, keys3, preferred_element_type=jnp.float32) * scale
    scores = jnp.where(visible[None], scores, -1000000000.0)
    exact = jnp.where(visible[None], jnp.exp(scores - log_total[..., None]), 0.0)
    grad_probs = jnp.einsum("qhd,khd->hqk", grad3, values3, preferred_element_type=jnp.float32)
    grad_scores = (exact * (grad_probs - delta[..., None])).astype(jnp.bfloat16)
    grad_query = (
        grad_query
        + jnp.einsum("hqk,khd->hqd", grad_scores, keys3, preferred_element_type=jnp.float32) * scale
    )
    rounded = exact.astype(jnp.bfloat16)
    grad_values = jnp.einsum("hqk,qhd->khd", rounded, grad3, preferred_element_type=jnp.float32)
    grad_keys = (
        jnp.einsum("hqk,qhd->khd", grad_scores, queries3, preferred_element_type=jnp.float32)
        * scale
    )
    rows = keys3.shape[0]
    term = jnp.stack([grad_keys.reshape(rows, -1), grad_values.reshape(rows, -1)], axis=1)
    return (grad_query, term)


def general_backward(
    query_parts,
    grad_parts,
    total_parts,
    delta_parts,
    pos_parts,
    positions,
    boundary,
    keys_group,
    values_group,
    key_span,
    buffer_rows,
):
    heads_local, head_size = (query_parts[0].shape[1], query_parts[0].shape[2])
    scale = head_size ** (-0.5)

    def fold_keys(state, pieces, start):
        key_rows, value_rows = pieces
        count_rows = key_rows.shape[0]
        block_rows = math.gcd(count_rows, key_span)
        block_count = count_rows // block_rows

        def one_step(index, inner):
            offset = index * block_rows
            keys3 = lax.dynamic_slice_in_dim(key_rows, offset, block_rows).reshape(
                block_rows, heads_local, head_size
            )
            values3 = lax.dynamic_slice_in_dim(value_rows, offset, block_rows).reshape(
                block_rows, heads_local, head_size
            )
            key_pos = lax.dynamic_slice_in_dim(positions, offset, block_rows)
            grads_now, buffer = inner
            term = jnp.zeros((block_rows, 2, heads_local * head_size), jnp.float32)
            part_queries = query_parts[0]
            part_grads = grad_parts[0]
            part_total = total_parts[0]
            part_delta = delta_parts[0]
            visible = visible_pairs(pos_parts[0], key_pos, boundary)
            current = (grads_now[0], term)
            result = backward_tile(
                current,
                part_queries,
                part_grads,
                part_total,
                part_delta,
                keys3,
                values3,
                visible,
                scale,
            )
            updated = [result[0]]
            term = result[1]
            buffer = lax.dynamic_update_slice(buffer, term, (offset, 0, 0))
            return (tuple(updated), buffer)

        return lax.fori_loop(0, block_count, one_step, state)

    grads_init = tuple(
        (jnp.zeros((heads_local, part.shape[0], head_size), jnp.float32) for part in query_parts)
    )
    initial = (grads_init, jnp.zeros((buffer_rows, 2, heads_local * head_size), jnp.float32))
    return fold_keys(
        initial,
        (
            lax.all_gather(keys_group, "blk", axis=0, tiled=True),
            lax.all_gather(values_group, "blk", axis=0, tiled=True),
        ),
        jnp.int32(0),
    )


def general_body(
    block_input,
    qkv_weight,
    q_bias,
    v_bias,
    out_weight,
    out_bias,
    norm1_gain,
    norm1_shift,
    norm2_gain,
    norm2_shift,
    fc_weight,
    fc_bias,
    proj_weight,
    proj_bias,
    out_grad,
    dealt,
    lengths,
):
    micro_count, local_rows, width = block_input.shape
    head_devices = lax.axis_size("head")
    blk_devices = lax.axis_size("blk")
    group = local_rows * head_devices
    blk_index = lax.axis_index("blk")
    head_size = DH
    key_span = 1024
    part_count = group // group
    shards = (
        qkv_weight,
        q_bias,
        v_bias,
        out_weight,
        out_bias,
        norm1_gain,
        norm1_shift,
        norm2_gain,
        norm2_shift,
        fc_weight,
        fc_bias,
        proj_weight,
        proj_bias,
    )
    totals = [
        jnp.zeros((shard.shape[0] * blk_devices * head_devices,) + shard.shape[1:], jnp.float32)
        for shard in shards
    ]
    outputs = []
    input_grads = []
    for micro_index in range(micro_count):
        whole = (
            lax.all_gather(shards[0], ("blk", "head"), axis=0, tiled=True),
            lax.all_gather(shards[1], ("blk", "head"), axis=0, tiled=True),
            lax.all_gather(shards[2], ("blk", "head"), axis=0, tiled=True),
            lax.all_gather(shards[3], ("blk", "head"), axis=0, tiled=True),
            lax.all_gather(shards[4], ("blk", "head"), axis=0, tiled=True),
            lax.all_gather(shards[5], ("blk", "head"), axis=0, tiled=True),
            lax.all_gather(shards[6], ("blk", "head"), axis=0, tiled=True),
            lax.all_gather(shards[7], ("blk", "head"), axis=0, tiled=True),
            lax.all_gather(shards[8], ("blk", "head"), axis=0, tiled=True),
            lax.all_gather(shards[9], ("blk", "head"), axis=0, tiled=True),
            lax.all_gather(shards[10], ("blk", "head"), axis=0, tiled=True),
            lax.all_gather(shards[11], ("blk", "head"), axis=0, tiled=True),
            lax.all_gather(shards[12], ("blk", "head"), axis=0, tiled=True),
        )
        (
            w_qkv,
            b_query,
            b_value,
            w_out,
            b_out,
            gain_one,
            shift_one,
            gain_two,
            shift_two,
            w_fc,
            b_fc,
            w_proj,
            b_proj,
        ) = whole
        b_query = b_query.astype(jnp.float32)
        b_value = b_value.astype(jnp.float32)
        b_out = b_out.astype(jnp.float32)
        gain_one = gain_one.astype(jnp.float32)
        shift_one = shift_one.astype(jnp.float32)
        gain_two = gain_two.astype(jnp.float32)
        shift_two = shift_two.astype(jnp.float32)
        b_fc = b_fc.astype(jnp.float32)
        b_proj = b_proj.astype(jnp.float32)
        positions = dealt[micro_index]
        boundary = lengths[micro_index, 0]
        query_pos = lax.dynamic_slice_in_dim(positions, blk_index * group, group)
        inputs = block_input[micro_index].astype(jnp.float32)
        normed_one, inverse_one = normalize(inputs)
        act_one = (normed_one * gain_one + shift_one).astype(jnp.bfloat16)
        mixed = product(act_one, w_qkv)
        queries = (mixed[:, :width] + b_query).astype(jnp.bfloat16)
        keys = mixed[:, width : 2 * width].astype(jnp.bfloat16)
        values = (mixed[:, 2 * width :] + b_value).astype(jnp.bfloat16)
        heads_in = lax.all_to_all(
            jnp.stack([queries, keys, values], axis=1),
            "head",
            split_axis=2,
            concat_axis=0,
            tiled=True,
        )
        local_width = heads_in.shape[2]
        heads_local = local_width // head_size
        queries3 = heads_in[:, 0].reshape(group, heads_local, head_size)
        keys_group = heads_in[:, 1]
        values_group = heads_in[:, 2]
        query_parts = tuple((queries3 for index in range(part_count)))
        pos_parts = tuple((query_pos for index in range(part_count)))
        states = general_forward(
            query_parts, pos_parts, positions, boundary, keys_group, values_group, key_span
        )
        running = jnp.concatenate([state[0] for state in states], axis=1)
        total = jnp.concatenate([state[1] for state in states], axis=1)
        accum = jnp.concatenate([state[2] for state in states], axis=1)
        log_total = running + jnp.log(total)
        attn_heads = (
            (accum / total[..., None])
            .transpose(1, 0, 2)
            .reshape(group, local_width)
            .astype(jnp.bfloat16)
        )
        attended = lax.all_to_all(attn_heads, "head", split_axis=0, concat_axis=1, tiled=True)
        resid = inputs + product(attended, w_out) + b_out
        normed_two, inverse_two = normalize(resid)
        act_two = (normed_two * gain_two + shift_two).astype(jnp.bfloat16)
        pre = product(act_two, w_fc) + b_fc
        hidden = gelu_tanh(pre).astype(jnp.bfloat16)
        outputs.append((resid + product(hidden, w_proj) + b_proj).astype(jnp.bfloat16))
        cotangent = out_grad[micro_index]
        grad_proj_w = product_tn(hidden, cotangent)
        grad_proj_b = jnp.sum(cotangent.astype(jnp.float32), axis=0)
        grad_hidden = product_nt(cotangent, w_proj)
        grad_pre = jax.vjp(gelu_tanh, pre)[1](grad_hidden)[0].astype(jnp.bfloat16)
        grad_fc_w = product_tn(act_two, grad_pre)
        grad_fc_b = jnp.sum(grad_pre.astype(jnp.float32), axis=0)
        grad_act_two = product_nt(grad_pre, w_fc)
        grad_gain_two = jnp.sum(grad_act_two * normed_two, axis=0)
        grad_shift_two = jnp.sum(grad_act_two, axis=0)
        grad_resid = cotangent.astype(jnp.float32) + norm_back(
            grad_act_two * gain_two, normed_two, inverse_two
        )
        grad_branch = grad_resid.astype(jnp.bfloat16)
        grad_out_w = product_tn(attended, grad_branch)
        grad_out_b = jnp.sum(grad_branch.astype(jnp.float32), axis=0)
        grad_attn = product_nt(grad_branch, w_out).astype(jnp.bfloat16)
        grad_heads = lax.all_to_all(grad_attn, "head", split_axis=1, concat_axis=0, tiled=True)
        grad3 = grad_heads.reshape(group, heads_local, head_size)
        attn3 = attn_heads.reshape(group, heads_local, head_size)
        delta = jnp.sum(grad3.astype(jnp.float32) * attn3.astype(jnp.float32), axis=-1).T
        grad_parts = tuple((grad3 for index in range(part_count)))
        total_parts = tuple((log_total for index in range(part_count)))
        delta_parts = tuple((delta for index in range(part_count)))
        query_grads, buffer = general_backward(
            query_parts,
            grad_parts,
            total_parts,
            delta_parts,
            pos_parts,
            positions,
            boundary,
            keys_group,
            values_group,
            key_span,
            group * blk_devices,
        )
        kv_sums = lax.psum_scatter(buffer, "blk", scatter_dimension=0, tiled=True)
        grad_k_heads = kv_sums[:, 0].astype(jnp.bfloat16)
        grad_v_heads = kv_sums[:, 1].astype(jnp.bfloat16)
        grad_query = jnp.concatenate(list(query_grads), axis=1)
        grad_q_heads = (
            grad_query.transpose(1, 0, 2).reshape(group, local_width).astype(jnp.bfloat16)
        )
        grads_heads = jnp.stack([grad_q_heads, grad_k_heads, grad_v_heads], axis=1)
        back_tokens = lax.all_to_all(grads_heads, "head", split_axis=0, concat_axis=2, tiled=True)
        grad_mixed = back_tokens.reshape(local_rows, 3 * width)
        grad_qkv_w = product_tn(act_one, grad_mixed)
        grad_q_b = jnp.sum(back_tokens[:, 0].astype(jnp.float32), axis=0)
        grad_v_b = jnp.sum(back_tokens[:, 2].astype(jnp.float32), axis=0)
        grad_act_one = product_nt(grad_mixed, w_qkv)
        grad_gain_one = jnp.sum(grad_act_one * normed_one, axis=0)
        grad_shift_one = jnp.sum(grad_act_one, axis=0)
        input_grads.append(
            (grad_resid + norm_back(grad_act_one * gain_one, normed_one, inverse_one)).astype(
                jnp.bfloat16
            )
        )
        terms = (
            grad_qkv_w,
            grad_q_b,
            grad_v_b,
            grad_out_w,
            grad_out_b,
            grad_gain_one,
            grad_shift_one,
            grad_gain_two,
            grad_shift_two,
            grad_fc_w,
            grad_fc_b,
            grad_proj_w,
            grad_proj_b,
        )
        totals = [running_sum + term for running_sum, term in zip(totals, terms)]
    final = (
        lax.psum_scatter(totals[0], ("blk", "head"), scatter_dimension=0, tiled=True),
        lax.psum_scatter(totals[1], ("blk", "head"), scatter_dimension=0, tiled=True),
        lax.psum_scatter(totals[2], ("blk", "head"), scatter_dimension=0, tiled=True),
        lax.psum_scatter(totals[3], ("blk", "head"), scatter_dimension=0, tiled=True),
        lax.psum_scatter(totals[4], ("blk", "head"), scatter_dimension=0, tiled=True),
        lax.psum_scatter(totals[5], ("blk", "head"), scatter_dimension=0, tiled=True),
        lax.psum_scatter(totals[6], ("blk", "head"), scatter_dimension=0, tiled=True),
        lax.psum_scatter(totals[7], ("blk", "head"), scatter_dimension=0, tiled=True),
        lax.psum_scatter(totals[8], ("blk", "head"), scatter_dimension=0, tiled=True),
        lax.psum_scatter(totals[9], ("blk", "head"), scatter_dimension=0, tiled=True),
        lax.psum_scatter(totals[10], ("blk", "head"), scatter_dimension=0, tiled=True),
        lax.psum_scatter(totals[11], ("blk", "head"), scatter_dimension=0, tiled=True),
        lax.psum_scatter(totals[12], ("blk", "head"), scatter_dimension=0, tiled=True),
    )
    return (
        jnp.stack(outputs),
        jnp.stack(input_grads),
        final[0],
        final[1],
        final[2],
        final[3],
        final[4],
        final[5],
        final[6],
        final[7],
        final[8],
        final[9],
        final[10],
        final[11],
        final[12],
    )


RUN = 64
BLOCK = 512
NEG = -1000000000.0
VM = pltpu.VMEM
SM = pltpu.SMEM


def dot_nt(left, right):
    return lax.dot_general(left, right, (((1,), (1,)), ((), ())), preferred_element_type=jnp.float32)


def dot_nn(left, right):
    return lax.dot_general(left, right, (((1,), (0,)), ((), ())), preferred_element_type=jnp.float32)


def rows_at(index, size):
    return pl.ds(pl.multiple_of(index * size, size), size)


def first_block(start, bound):
    return jnp.where(start >= bound, bound // BLOCK, 0)


def forward_kernel(head_size, bound_ref, inloc, outloc, qkv, out, qs, ks, vs, attn_t, lse, vt, mixed):
    tokens = qkv.shape[0]
    runs = tokens // RUN
    scale = head_size ** (-0.5)
    bound = bound_ref[0]

    @pl.loop(0, runs, unroll=8)
    def _(run):
        rows = qkv[rows_at(inloc[run], RUN), :]
        here = rows_at(run, RUN)
        qs[here, :] = (rows[:, :head_size].astype(jnp.float32) * scale).astype(jnp.bfloat16)
        ks[here, :] = rows[:, head_size : 2 * head_size]
        vs[here, :] = rows[:, 2 * head_size :]

    @pl.loop(0, tokens // BLOCK, unroll=4)
    def _(block):
        here = rows_at(block, BLOCK)
        vt[:, here] = vs[here, :].astype(jnp.float32).T.astype(jnp.bfloat16)

    @pl.loop(0, tokens // BLOCK)
    def _(block):
        start = block * BLOCK
        here = rows_at(block, BLOCK)
        queries = qs[here, :]
        query_pos = start + lax.broadcasted_iota(jnp.int32, (1, BLOCK), 1)
        floor = jnp.where(query_pos >= bound, bound, 0)

        def scores_of(index, diagonal):
            keys = ks[rows_at(index, BLOCK), :]
            scores = dot_nt(keys, queries)
            key_pos = index * BLOCK + lax.broadcasted_iota(jnp.int32, (BLOCK, BLOCK), 0)
            visible = key_pos >= floor
            if diagonal:
                visible = visible & (key_pos <= query_pos)
            return jnp.where(visible, scores, NEG)

        scores = scores_of(block, True)
        highest = jnp.max(scores, axis=0, keepdims=True)
        weights = jnp.exp(scores - highest)
        total = jnp.sum(weights, axis=0, keepdims=True)
        accum = dot_nn(vt[:, here], weights.astype(jnp.bfloat16))

        def step(index, state):
            highest, total, accum = state
            scores = scores_of(index, False)
            higher = jnp.maximum(highest, jnp.max(scores, axis=0, keepdims=True))
            weights = jnp.exp(scores - higher)
            factor = jnp.exp(highest - higher)
            total = total * factor + jnp.sum(weights, axis=0, keepdims=True)
            accum = accum * factor + dot_nn(vt[:, rows_at(index, BLOCK)], weights.astype(jnp.bfloat16))
            return higher, total, accum

        highest, total, accum = lax.fori_loop(first_block(start, bound), block, step, (highest, total, accum))
        result = accum / total
        attn_t[:, here] = result.astype(jnp.bfloat16)
        lse[:, here] = highest + jnp.log(total)
        result = result.T.astype(jnp.bfloat16)
        for part in range(BLOCK // RUN):
            mixed[rows_at(outloc[block * (BLOCK // RUN) + part], RUN), :] = result[part * RUN : (part + 1) * RUN]

    chips, _, span = out.shape

    @pl.loop(0, chips, unroll=8)
    def _(chip):
        out[chip] = mixed[rows_at(chip, span), :].astype(jnp.float32).T.astype(jnp.bfloat16)


def attend_forward(bound, inloc, outloc, qkv, chips, head_size):
    tokens = qkv.shape[0]
    bf16 = jnp.bfloat16
    pairs = tokens * (tokens // 2)
    return pl.pallas_call(
        functools.partial(forward_kernel, head_size),
        out_shape=(
            jax.ShapeDtypeStruct((chips, head_size, tokens // chips), bf16),
            jax.ShapeDtypeStruct((tokens, head_size), bf16),
            jax.ShapeDtypeStruct((tokens, head_size), bf16),
            jax.ShapeDtypeStruct((tokens, head_size), bf16),
            jax.ShapeDtypeStruct((head_size, tokens), bf16),
            jax.ShapeDtypeStruct((1, tokens), jnp.float32),
        ),
        in_specs=[pl.BlockSpec(memory_space=SM)] * 3 + [pl.BlockSpec(memory_space=VM)],
        out_specs=[pl.BlockSpec(memory_space=VM)] * 6,
        scratch_shapes=[VM((head_size, tokens), bf16), VM((tokens, head_size), bf16)],
        compiler_params=pltpu.CompilerParams(vmem_limit_bytes=40 * 1024 * 1024),
        cost_estimate=pl.CostEstimate(flops=4 * 4 * pairs * head_size, bytes_accessed=tokens * 2048, transcendentals=pairs),
        name="attend_forward",
    )(bound, inloc, outloc, qkv)


def backward_kernel(
    head_size, count, share, bound_ref, inloc, outloc, grad_t, qs, ks, vs, attn_t, lse, *refs
):
    pieces = refs[:count]
    send_out, normed, raw, grads, kt, dk, dv, mixed, wide, moved, sem = refs[count:]
    tokens = qs.shape[0]
    runs = tokens // RUN
    scale = head_size ** (-0.5)
    bound = bound_ref[0]
    chips, _, span = grad_t.shape
    copies, filled = [], 0
    for piece in pieces:
        copies.append(pltpu.make_async_copy(piece, normed.at[pl.ds(filled, piece.shape[0])], sem))
        filled += piece.shape[0]
    for copy in copies:
        copy.start()

    @pl.loop(0, chips, unroll=8)
    def _(chip):
        mixed[rows_at(chip, span), :] = grad_t[chip, :head_size, :].astype(jnp.float32).T.astype(jnp.bfloat16)

    @pl.loop(0, runs, unroll=8)
    def _(run):
        grads[rows_at(run, RUN), :] = mixed[rows_at(outloc[run], RUN), :]

    @pl.loop(0, tokens // BLOCK, unroll=4)
    def _(block):
        here = rows_at(block, BLOCK)
        kt[:, here] = ks[here, :].astype(jnp.float32).T.astype(jnp.bfloat16)

    @pl.loop(0, tokens // BLOCK)
    def _(block):
        start = block * BLOCK
        here = rows_at(block, BLOCK)
        queries = qs[here, :]
        grad = grads[here, :]
        log_total = lse[:, here]
        delta = jnp.sum(grad.astype(jnp.float32).T * attn_t[:, here].astype(jnp.float32), axis=0, keepdims=True)
        query_pos = start + lax.broadcasted_iota(jnp.int32, (1, BLOCK), 1)
        floor = jnp.where(query_pos >= bound, bound, 0)

        def one(index, diagonal):
            there = rows_at(index, BLOCK)
            scores = dot_nt(ks[there, :], queries)
            key_pos = index * BLOCK + lax.broadcasted_iota(jnp.int32, (BLOCK, BLOCK), 0)
            visible = key_pos >= floor
            if diagonal:
                visible = visible & (key_pos <= query_pos)
            probs = jnp.where(visible, jnp.exp(scores - log_total), 0.0)
            grad_probs = dot_nt(vs[there, :], grad)
            grad_scores = (probs * (grad_probs - delta)).astype(jnp.bfloat16)
            return (
                dot_nn(probs.astype(jnp.bfloat16), grad),
                dot_nn(grad_scores, queries),
                dot_nn(kt[:, there], grad_scores),
                there,
            )

        grad_v, grad_k, grad_q, there = one(block, True)
        dv[there, :] = grad_v
        dk[there, :] = grad_k

        def step(index, grad_q):
            grad_v, grad_k, term, there = one(index, False)
            dv[there, :] += grad_v
            dk[there, :] += grad_k
            return grad_q + term

        grad_q = lax.fori_loop(first_block(start, bound), block, step, grad_q)
        wide[here, :head_size] = (grad_q.T * scale).astype(jnp.bfloat16)

    wide[:, head_size : 2 * head_size] = dk[...].astype(jnp.bfloat16)
    wide[:, 2 * head_size :] = dv[...].astype(jnp.bfloat16)

    size = 3 * head_size

    @pl.loop(0, runs, unroll=8)
    def _(run):
        moved[rows_at(outloc[run], RUN), :] = wide[rows_at(run, RUN), :]

    @pl.loop(0, chips, unroll=8)
    def _(chip):
        send_out[chip, :size, :] = moved[rows_at(chip, span), :].astype(jnp.float32).T.astype(jnp.bfloat16)

    @pl.loop(0, runs, unroll=8)
    def _(run):
        moved[rows_at(inloc[run], RUN), :] = wide[rows_at(run, RUN), :]

    for copy in copies:
        copy.wait()
    raw[...] = jnp.zeros_like(raw)

    @pl.loop(0, tokens // BLOCK, unroll=2)
    def _(block):
        here = rows_at(block, BLOCK)
        turned = moved[here, :].astype(jnp.float32).T.astype(jnp.bfloat16)
        raw[...] += dot_nn(turned, normed[here, :])

    product = raw[...].T
    sums = jnp.sum(wide[...].astype(jnp.float32), axis=0, keepdims=True)
    high = sums.astype(jnp.bfloat16).astype(jnp.float32)
    tail = jnp.concatenate([high, sums - high, jnp.zeros((14, size), jnp.float32)], axis=0)
    for chip in range(chips):
        first = chip // 2 * 4 * share + chip % 2 * share
        rows = jnp.concatenate([product[first : first + share], product[first + 2 * share : first + 3 * share], tail], axis=0)
        rows = jnp.concatenate([rows, jnp.zeros((rows.shape[0], span - size), jnp.float32)], axis=1)
        send_out[chip, size:, :] = rows.astype(jnp.bfloat16)


def attend_backward(bound, inloc, outloc, grad_t, qs, ks, vs, attn_t, lse, pieces, share):
    tokens, head_size = qs.shape
    chips = grad_t.shape[0]
    width = pieces[0].shape[1]
    bf16 = jnp.bfloat16
    pairs = tokens * (tokens // 2)
    return pl.pallas_call(
        functools.partial(backward_kernel, head_size, len(pieces), share),
        out_shape=jax.ShapeDtypeStruct((chips, 3 * head_size + 2 * share + 16, tokens // chips), bf16),
        in_specs=[pl.BlockSpec(memory_space=SM)] * 3 + [pl.BlockSpec(memory_space=VM)] * 6
        + [pl.BlockSpec(memory_space=pltpu.HBM)] * len(pieces),
        out_specs=pl.BlockSpec(memory_space=VM),
        scratch_shapes=[
            VM((tokens, width), bf16),
            VM((3 * head_size, width), jnp.float32),
            VM((tokens, head_size), bf16),
            VM((head_size, tokens), bf16),
            VM((tokens, head_size), jnp.float32),
            VM((tokens, head_size), jnp.float32),
            VM((tokens, head_size), bf16),
            VM((tokens, 3 * head_size), bf16),
            VM((tokens, 3 * head_size), bf16),
            pltpu.SemaphoreType.DMA,
        ],
        compiler_params=pltpu.CompilerParams(vmem_limit_bytes=48 * 1024 * 1024),
        cost_estimate=pl.CostEstimate(flops=4 * 10 * pairs * head_size, bytes_accessed=tokens * 4096, transcendentals=pairs),
        name="attend_backward",
    )(bound, inloc, outloc, grad_t, qs, ks, vs, attn_t, lse, *pieces)


HALF_STEP = 512


def gelu_pair(values):
    cubic = values * values
    inner = 0.7978845608028654 * values * (1.0 + 0.044715 * cubic)
    bent = jnp.tanh(inner)
    slope = 0.7978845608028654 * (1.0 + 0.134145 * cubic)
    half = 0.5 * (1.0 + bent)
    return values * half, half + 0.5 * values * (1.0 - bent * bent) * slope


def load_rows(table, pieces, targets, sem, wait):
    slot = 0
    for piece in pieces:
        count = piece.shape[0]

        @pl.loop(0, count)
        def _(index, piece=piece, slot=slot):
            chip = table[0, slot + index]
            for rows, target in targets(chip):
                copy = pltpu.make_async_copy(piece.at[index, rows], target, sem)
                if wait:
                    copy.wait()
                else:
                    copy.start()

        slot += count


def project_kernel(count, table, got, *refs):
    pieces, (part_out, sent, attn_in, w_out, sem) = refs[:count], refs[count:]
    chips, size, span = got.shape
    share = w_out.shape[0] // chips
    rows = span // 2

    def targets(chip):
        return [(pl.ds(0, share), w_out.at[rows_at(chip, share)])]

    load_rows(table, pieces, targets, sem, False)
    for chip in range(chips):
        micro, head = divmod(chip, chips // 2)
        for rel in range(2):
            column = (rel * 2 + micro) * rows
            attn_in[head * size : (head + 1) * size, column : column + rows] = got[chip, :, rel * rows : (rel + 1) * rows]
    load_rows(table, pieces, targets, sem, True)
    left = attn_in[...].astype(jnp.float32).T.astype(jnp.bfloat16)
    part = dot_nn(left, w_out[...])
    part_out[...] = part
    sent[...] = part.astype(jnp.bfloat16)


def project(table, got, pieces, share):
    chips, size, span = got.shape
    width = pieces[0].shape[2]
    tokens = 2 * span
    bf16 = jnp.bfloat16
    return pl.pallas_call(
        functools.partial(project_kernel, len(pieces)),
        out_shape=(
            jax.ShapeDtypeStruct((tokens, width), jnp.float32),
            jax.ShapeDtypeStruct((tokens, width), bf16),
            jax.ShapeDtypeStruct((chips // 2 * size, tokens), bf16),
        ),
        in_specs=[pl.BlockSpec(memory_space=SM), pl.BlockSpec(memory_space=VM)]
        + [pl.BlockSpec(memory_space=pltpu.HBM)] * len(pieces),
        out_specs=[pl.BlockSpec(memory_space=VM)] * 3,
        scratch_shapes=[VM((chips * share, width), bf16), pltpu.SemaphoreType.DMA],
        compiler_params=pltpu.CompilerParams(vmem_limit_bytes=58 * 1024 * 1024),
        cost_estimate=pl.CostEstimate(
            flops=2 * tokens * chips * share * width, bytes_accessed=8 * tokens * width, transcendentals=0
        ),
        name="project",
    )(table, got, *pieces)


def middle_kernel(count, share, table, x_a, x_b, g_a, g_b, part, got_a, got_b, *refs):
    pieces = refs[:count]
    (resid, base, other, grad_act, grad_sent, fc_sums, vectors, terms) = refs[count : count + 8]
    (smalls, fc_bias, w_fc, w_proj, g_all, act, act_t, rest, proj_buf, fc_buf, small_sem, load_sem, proj_sem, fc_sem) = refs[count + 8 :]
    f32, bf16 = jnp.float32, jnp.bfloat16
    tokens, width = part.shape
    own = tokens // 2
    hidden = w_proj.shape[0]
    chips = terms.shape[0]
    each = hidden // chips
    folds = hidden // width
    fc_row = share + each

    def targets(chip):
        wanted = [(pl.ds(share, each), w_proj.at[rows_at(chip, each)])]
        for fold in range(folds):
            for core in range(2):
                first = fc_row + (fold * 2 + core) * share
                place = ((chip // 2) * 2 + core) * 2 + chip % 2
                wanted.append(
                    (pl.ds(first, share), w_fc.at[rows_at(place, share), pl.ds(fold * width, width)])
                )
        return wanted

    def small_targets(chip):
        return [(pl.ds(pieces[0].shape[1] - 16, 16), smalls.at[chip])]

    load_rows(table, pieces, small_targets, small_sem, False)
    load_rows(table, pieces, targets, load_sem, False)
    load_rows(table, pieces, small_targets, small_sem, True)
    small_sum = jnp.sum(smalls[...].astype(f32), axis=0)
    vectors[...] = small_sum[:8]
    for fold in range(folds):
        fc_bias[:, fold * width : (fold + 1) * width] = small_sum[8 + fold : 9 + fold]
    for half, (x_in, g_in, arrived) in enumerate(((x_a, g_a, got_a), (x_b, g_b, got_b))):
        here = slice(half * own, (half + 1) * own)
        g_all[here, :] = g_in[...]
        value = x_in[...].astype(f32) + part[here, :] + arrived[...].astype(f32) + vectors[2:3, :]
        resid[here, :] = value
        centred = value - jnp.mean(value, axis=-1, keepdims=True)
        inverse = lax.rsqrt(jnp.mean(centred * centred, axis=-1, keepdims=True) + 1e-05)
        rounded = (centred * inverse * vectors[0:1, :] + vectors[1:2, :]).astype(bf16)
        act[here, :] = rounded
        act_t[:, here] = rounded.astype(f32).T.astype(bf16)
    base[...] = resid[:own, :] + vectors[3:4, :]
    load_rows(table, pieces, targets, load_sem, True)

    per_step = HALF_STEP // each

    def copies(step, slot):
        made = []
        for index in range(per_step):
            made.append(
                pltpu.make_async_copy(
                    proj_buf.at[slot, pl.ds(index * each, each)],
                    terms.at[table[1, step * per_step + index], pl.ds(0, each)],
                    proj_sem.at[slot],
                )
            )
        fold = step // (width // HALF_STEP)
        column = pl.multiple_of(step % (width // HALF_STEP) * HALF_STEP, HALF_STEP)
        for chip in range(chips):
            for core in range(2):
                place = ((chip // 2) * 2 + core) * 2 + chip % 2
                made.append(
                    pltpu.make_async_copy(
                        fc_buf.at[slot, pl.ds(place * share, share)],
                        terms.at[
                            table[1, chip],
                            pl.ds(pl.multiple_of(each + share + (fold * 2 + core) * share, 16), share),
                            pl.ds(column, HALF_STEP),
                        ],
                        fc_sem.at[slot],
                    )
                )
        return made

    steps = hidden // HALF_STEP

    @pl.loop(0, steps)
    def _(step):
        slot = step % 2
        columns = pl.ds(pl.multiple_of(step * HALF_STEP, HALF_STEP), HALF_STEP)
        rows = rows_at(step, HALF_STEP)

        @pl.when(step >= 2)
        def _():
            for copy in copies(step - 2, slot):
                copy.wait()

        grads = g_all[...]
        value, slope = gelu_pair(dot_nn(act[...], w_fc[:, columns]) + fc_bias[:, columns])
        value = value.astype(bf16)
        proj_buf[slot] = dot_nn(value.astype(f32).T.astype(bf16), grads).astype(bf16)
        grad_pre = (dot_nt(grads, w_proj[rows, :]) * slope).astype(bf16)
        fc_sums[:, columns] = jnp.sum(grad_pre.astype(f32), axis=0, keepdims=True)
        fc_buf[slot] = dot_nn(act_t[...], grad_pre).astype(bf16)
        for copy in copies(step, slot):
            copy.start()
        projected = dot_nn(value, w_proj[rows, :])
        back = dot_nt(grad_pre, w_fc[:, columns])
        base[...] += projected[:own]

        @pl.when(step == 0)
        def _():
            grad_act[...] = back
            rest[...] = projected[own:]

        @pl.when(step > 0)
        def _():
            grad_act[...] += back
            rest[...] += projected[own:]

    other[...] = rest[...].astype(bf16)
    grad_sent[...] = grad_act[...].astype(bf16)
    for step in range(steps - 2, steps):
        for copy in copies(step, step % 2):
            copy.wait()


def middle(table, x_a, x_b, g_a, g_b, part, got_a, got_b, pieces, share, hidden):
    tokens, width = part.shape
    f32, bf16 = jnp.float32, jnp.bfloat16
    chips = table.shape[1]
    each = hidden // chips
    rows = share + each + 2 * share * (hidden // width)
    shape = jax.ShapeDtypeStruct
    return pl.pallas_call(
        functools.partial(middle_kernel, len(pieces), share),
        out_shape=(
            shape((tokens, width), f32),
            shape((tokens // 2, width), f32),
            shape((tokens // 2, width), bf16),
            shape((tokens, width), f32),
            shape((tokens, width), bf16),
            shape((1, hidden), f32),
            shape((8, width), f32),
            shape((chips, rows, width), bf16),
        ),
        in_specs=[pl.BlockSpec(memory_space=SM)]
        + [pl.BlockSpec(memory_space=VM)] * 7
        + [pl.BlockSpec(memory_space=pltpu.HBM)] * len(pieces),
        out_specs=[pl.BlockSpec(memory_space=VM)] * 7 + [pl.BlockSpec(memory_space=pltpu.HBM)],
        scratch_shapes=[
            VM((chips, 16, width), bf16),
            VM((1, hidden), f32),
            VM((width, hidden), bf16),
            VM((hidden, width), bf16),
            VM((tokens, width), bf16),
            VM((tokens, width), bf16),
            VM((width, tokens), bf16),
            VM((tokens // 2, width), f32),
            VM((2, HALF_STEP, width), bf16),
            VM((2, width, HALF_STEP), bf16),
            pltpu.SemaphoreType.DMA,
            pltpu.SemaphoreType.DMA,
            pltpu.SemaphoreType.DMA((2,)),
            pltpu.SemaphoreType.DMA((2,)),
        ],
        compiler_params=pltpu.CompilerParams(vmem_limit_bytes=56 * 1024 * 1024),
        cost_estimate=pl.CostEstimate(
            flops=12 * tokens * width * hidden, bytes_accessed=8 * width * hidden, transcendentals=tokens * hidden
        ),
        name="middle",
    )(table, x_a, x_b, g_a, g_b, part, got_a, got_b, *pieces)


def branch_kernel(share, row, table, resid, g_a, g_b, part, got_a, got_b, vectors, fc_sums, attn_in, given, grad_resid, branch, tails, terms, products, sem):
    f32, bf16 = jnp.float32, jnp.bfloat16
    tokens, width = resid.shape
    own = tokens // 2
    chips = tails.shape[0]
    gain_sum = jnp.zeros((1, width), f32)
    shift_sum = jnp.zeros((1, width), f32)
    bias_sum = jnp.zeros((1, width), f32)
    proj_sum = jnp.zeros((1, width), f32)
    for half, (g_in, arrived) in enumerate(((g_a, got_a), (g_b, got_b))):
        here = slice(half * own, (half + 1) * own)
        value = resid[here, :]
        centred = value - jnp.mean(value, axis=-1, keepdims=True)
        inverse = lax.rsqrt(jnp.mean(centred * centred, axis=-1, keepdims=True) + 1e-05)
        normed = centred * inverse
        grad = part[here, :] + arrived[...].astype(f32)
        gain_sum += jnp.sum(grad * normed, axis=0, keepdims=True)
        shift_sum += jnp.sum(grad, axis=0, keepdims=True)
        scaled = grad * vectors[0:1, :]
        given_grad = g_in[...].astype(f32)
        total = given_grad + inverse * (
            scaled
            - jnp.mean(scaled, axis=-1, keepdims=True)
            - normed * jnp.mean(scaled * normed, axis=-1, keepdims=True)
        )
        rounded = total.astype(bf16)
        bias_sum += jnp.sum(rounded.astype(f32), axis=0, keepdims=True)
        proj_sum += jnp.sum(given_grad, axis=0, keepdims=True)
        branch[here, :] = rounded
        if half == 0:
            grad_resid[...] = total
    group = width // (chips // 2)
    sums = jnp.concatenate([gain_sum, shift_sum, bias_sum, proj_sum], axis=0)
    each = fc_sums.shape[1] // chips
    for chip in range(chips):
        first = chip // 2 * group
        tail = jnp.concatenate(
            [
                sums[:, first : first + group],
                fc_sums[:, chip * each : (chip + 1) * each],
                jnp.zeros((3, group), f32),
            ],
            axis=0,
        )
        high = tail.astype(bf16)
        low = (tail - high.astype(f32)).astype(bf16)
        tails[chip] = jnp.concatenate([high, low], axis=1)
    products[...] = dot_nn(attn_in[...], branch[...]).astype(bf16)

    @pl.loop(0, chips)
    def _(chip):
        pltpu.make_async_copy(products.at[rows_at(chip, share)], terms.at[table[1, chip], pl.ds(row, share)], sem).start()

    @pl.loop(0, chips)
    def _(chip):
        pltpu.make_async_copy(products.at[rows_at(chip, share)], terms.at[table[1, chip], pl.ds(row, share)], sem).wait()


def branch_back(table, resid, g_a, g_b, part, got_a, got_b, vectors, fc_sums, attn_in, terms, share, row, span):
    tokens, width = resid.shape
    f32, bf16 = jnp.float32, jnp.bfloat16
    chips = table.shape[1]
    shape = jax.ShapeDtypeStruct
    return pl.pallas_call(
        functools.partial(branch_kernel, share, row),
        out_shape=(
            shape((tokens // 2, width), f32),
            shape((tokens, width), bf16),
            shape((chips, 8, span), bf16),
            shape(terms.shape, bf16),
        ),
        in_specs=[pl.BlockSpec(memory_space=SM)]
        + [pl.BlockSpec(memory_space=VM)] * 9
        + [pl.BlockSpec(memory_space=pltpu.HBM)],
        out_specs=[pl.BlockSpec(memory_space=VM)] * 3 + [pl.BlockSpec(memory_space=pltpu.HBM)],
        scratch_shapes=[VM((chips * share, width), bf16), pltpu.SemaphoreType.DMA],
        input_output_aliases={10: 3},
        compiler_params=pltpu.CompilerParams(vmem_limit_bytes=40 * 1024 * 1024),
        cost_estimate=pl.CostEstimate(
            flops=2 * tokens * chips * share * width, bytes_accessed=16 * tokens * width, transcendentals=0
        ),
        name="branch_back",
    )(table, resid, g_a, g_b, part, got_a, got_b, vectors, fc_sums, attn_in, terms)


def attention_back_kernel(count, table, branch, tails, *refs):
    pieces, (sent, w_out, sem) = refs[:count], refs[count:]
    chips, size, span = sent.shape
    size -= 8
    rows = span // 2
    share = w_out.shape[0] // chips

    def targets(chip):
        return [(pl.ds(0, share), w_out.at[rows_at(chip, share)])]

    load_rows(table, pieces, targets, sem, False)
    sent[:, size:, :] = tails[...]
    load_rows(table, pieces, targets, sem, True)
    grads = dot_nt(w_out[...], branch[...]).astype(jnp.bfloat16)
    for chip in range(chips):
        micro, head = divmod(chip, chips // 2)
        for rel in range(2):
            column = (rel * 2 + micro) * rows
            sent[chip, :size, rel * rows : (rel + 1) * rows] = grads[
                head * size : (head + 1) * size, column : column + rows
            ]


def attention_back(table, branch, tails, pieces, share, size):
    tokens, width = branch.shape
    chips, _, span = tails.shape
    bf16 = jnp.bfloat16
    return pl.pallas_call(
        functools.partial(attention_back_kernel, len(pieces)),
        out_shape=jax.ShapeDtypeStruct((chips, size + 8, span), bf16),
        in_specs=[pl.BlockSpec(memory_space=SM)]
        + [pl.BlockSpec(memory_space=VM)] * 2
        + [pl.BlockSpec(memory_space=pltpu.HBM)] * len(pieces),
        out_specs=pl.BlockSpec(memory_space=VM),
        scratch_shapes=[VM((chips * share, width), bf16), pltpu.SemaphoreType.DMA],
        compiler_params=pltpu.CompilerParams(vmem_limit_bytes=58 * 1024 * 1024),
        cost_estimate=pl.CostEstimate(
            flops=2 * tokens * chips * share * width, bytes_accessed=4 * tokens * width, transcendentals=0
        ),
        name="attention_back",
    )(table, branch, tails, *pieces)


def finish_kernel(order, got, weights, kept, sent, weight, grads, sem):
    chips, _, span = got.shape
    size = weight.shape[0] // len(order)
    rows = span // 2
    own = kept.shape[0]

    def copies():
        return [
            pltpu.make_async_copy(weights.at[slot], weight.at[pl.ds(head * size, size)], sem)
            for slot, head in enumerate(order)
        ]

    for copy in copies():
        copy.start()
    for chip in range(chips):
        micro, head = divmod(chip, chips // 2)
        turned = got[chip, :size, :].astype(jnp.float32).T.astype(jnp.bfloat16)
        for rel in range(2):
            row = (rel * 2 + micro) * rows
            grads[head, row : row + rows, :] = turned[rel * rows : (rel + 1) * rows]
    for copy in copies():
        copy.wait()
    left = jnp.concatenate([grads[head] for head in range(len(order))], axis=1)
    back = dot_nn(left, weight[...])
    kept[...] = back[:own]
    sent[...] = back[own:].astype(jnp.bfloat16)


def finish(got, weights, order):
    chips, _, span = got.shape
    heads, size, width = weights.shape
    bf16 = jnp.bfloat16
    return pl.pallas_call(
        functools.partial(finish_kernel, order),
        out_shape=(
            jax.ShapeDtypeStruct((span, width), jnp.float32),
            jax.ShapeDtypeStruct((span, width), bf16),
        ),
        in_specs=[pl.BlockSpec(memory_space=VM), pl.BlockSpec(memory_space=pltpu.HBM)],
        out_specs=[pl.BlockSpec(memory_space=VM)] * 2,
        scratch_shapes=[
            VM((heads * size, width), bf16),
            VM((heads, 2 * span, size), bf16),
            pltpu.SemaphoreType.DMA,
        ],
        compiler_params=pltpu.CompilerParams(vmem_limit_bytes=58 * 1024 * 1024),
        cost_estimate=pl.CostEstimate(
            flops=4 * span * width * heads * size,
            bytes_accessed=2 * width * heads * size + 8 * span * width,
            transcendentals=0,
        ),
        name="finish",
    )(got, weights)


PATHS = (("x", "z", "head"), ("head", "z", "x"))


PAIR = [(0, 1), (1, 0)]
NEAR = [(0, 1), (1, 0), (2, 3), (3, 2)]
FAR = [(0, 2), (2, 0), (1, 3), (3, 1)]


def swap(values, axis, pairs=PAIR):
    return lax.ppermute(values, axis, pairs)


def across(values, axis):
    return swap(values, axis, NEAR if axis == "z" else PAIR)


def in_order(mine, other, index, axis):
    first = jnp.where(index == 0, mine, other)
    second = jnp.where(index == 0, other, mine)
    return jnp.stack([first, second], axis=axis)


def split_float(values):
    high = values.astype(jnp.bfloat16)
    low = (values - high.astype(jnp.float32)).astype(jnp.bfloat16)
    return high, low


def run_table(order, pair_start):
    pairs = order.shape[0]
    runs = jnp.arange(2 * pairs, dtype=jnp.int32)[:, None]
    low = jnp.where(runs == order[None, :], pair_start[None, :], 0)
    high = jnp.where(runs == 2 * pairs - 1 - order[None, :], pair_start[None, :] + 1, 0)
    return jnp.sum(low + high, axis=1).astype(jnp.int32)


def ring_order(count, turn):
    half = [(z, (z + step + turn) % 2) for z in range(count) for step in range(2)]
    return [z * 4 + y for z, y in half] + [z * 4 + 2 + y for z, y in reversed(half)]


def core_groups(rings):
    return [[(chip // 2 * 2 + core) * 2 + chip % 2 for chip in ring] for core, ring in enumerate(rings)]


def cube_orders(depth):
    cycle = [0, 1, 3, 2, 6, 7, 5, 4]
    return [[chip + start for chip in cycle] for start in (0, 4 * depth)]


def fast_body(
    block_input,
    qkv_weight,
    q_bias,
    v_bias,
    out_weight,
    out_bias,
    norm1_gain,
    norm1_shift,
    norm2_gain,
    norm2_shift,
    fc_weight,
    fc_bias,
    proj_weight,
    proj_bias,
    out_grad,
    dealt,
    lengths,
):
    f32, bf16 = jnp.float32, jnp.bfloat16
    micro, rows, width = block_input.shape
    nz, nx = lax.axis_size("z"), lax.axis_size("x")
    iz, ix, ic, iy = (lax.axis_index(name) for name in ("z", "x", "core", "head"))
    zx = nz * nx
    every, chips = ("z", "x", "core", "head"), ("z", "x", "head")
    devices, chip_count = 4 * zx, 2 * zx
    heads = 2 * zx
    local = heads * DH // 2
    share = qkv_weight.shape[0]
    hidden_share = proj_weight.shape[0]
    hidden_half = hidden_share * chip_count

    inputs = block_input.astype(f32)
    normed_one, inverse_one = normalize(inputs)
    n1 = normed_one.astype(bf16)
    n1, qkv_weight, fc_weight, norm1_gain, norm2_gain = lax.optimization_barrier(
        (n1, qkv_weight, fc_weight, norm1_gain, norm2_gain)
    )
    gain_one = norm1_gain.astype(f32)
    shift_one = norm1_shift.astype(f32)
    raw_qkv = qkv_weight.astype(f32)
    scaled_qkv = (raw_qkv * gain_one[:, None]).astype(bf16)
    device = ((iz * nx + ix) * 2 + ic) * 2 + iy
    offset = jnp.sum(raw_qkv * shift_one[:, None], axis=0)
    zero = jnp.zeros((width,), f32)
    place = device * share
    offset = offset + jnp.concatenate(
        [
            lax.dynamic_update_slice(zero, q_bias.astype(f32), (place,)),
            zero,
            lax.dynamic_update_slice(zero, v_bias.astype(f32), (place,)),
        ]
    )
    high, low = split_float(offset)
    to_heads = jnp.concatenate([scaled_qkv, high[None], low[None], jnp.zeros((6, 3 * width), bf16)], axis=0)
    to_heads = to_heads.reshape(share + 8, 3, zx // 2, 2, 2, DH).transpose(2, 4, 3, 0, 1, 5)
    to_heads = to_heads.reshape(1, heads, share + 8, 3 * DH)
    to_heads = jnp.broadcast_to(to_heads, (2, heads, share + 8, 3 * DH)).reshape(devices, share + 8, 3 * DH)
    head_rows = lax.all_to_all(to_heads, every, split_axis=0, concat_axis=0, tiled=True)
    head_weight = head_rows[:, :share].reshape(width, 3 * DH)
    head_offset = jnp.sum(head_rows[:, share : share + 2].astype(f32), axis=(0, 1))

    mine = iz // 2
    near = lax.dynamic_index_in_dim(n1, mine, 0, keepdims=False)
    far = swap(lax.dynamic_index_in_dim(n1, 1 - mine, 0, keepdims=False), "z", FAR)
    paths = PATHS
    got = across(near, paths[0][0])
    far, got = lax.optimization_barrier((far, got))
    near = jnp.stack([near, got])
    near_got, far_got = across(near, paths[0][1]), across(far, paths[1][0])
    near_got, far_got = lax.optimization_barrier((near_got, far_got))
    near, far = jnp.stack([near, near_got]), jnp.stack([far, far_got])
    near_got, far_got = across(near, paths[0][2]), across(far, paths[1][1])
    far = jnp.stack([far, far_got])
    parts = [near, near_got, far, across(far, paths[1][2])]
    pieces, owners = [], []

    def add_all(flip):
        core = 1 - ic if flip else ic
        for index, part in enumerate(parts):
            pieces.append((swap(part, "core") if flip else part).reshape(-1, width))
            for second in range(2):
                for first in range(2):
                    flips = dict(zip(paths[index // 2], (first, second, index % 2)))
                    owners.append((iz ^ flips["z"] ^ (index // 2 * 2), ix ^ flips["x"], core, iy ^ flips["head"]))

    add_all(False)
    add_all(True)
    slot_device = jnp.stack([((z * nx + x) * 2 + core) * 2 + y for z, x, core, y in owners]).astype(jnp.int32)
    my_dealt = lax.dynamic_index_in_dim(dealt, mine, 0, keepdims=False)
    order = my_dealt.reshape(devices, rows)[:, 0] // RUN
    slot_of = jnp.sum(
        jnp.where(jnp.arange(devices)[:, None] == slot_device[None, :], jnp.arange(devices)[None, :], 0), axis=1
    )
    inloc = run_table(order, (slot_of * 2).astype(jnp.int32))
    ids = jnp.arange(devices, dtype=jnp.int32)
    id_y, id_c, id_zx = ids % 2, ids // 2 % 2, ids // 4
    send_pair = (id_zx * 2 + id_y) * 2 + (id_c ^ ic)
    outloc = run_table(order, (send_pair * 2).astype(jnp.int32))
    bound = lax.dynamic_index_in_dim(lengths, mine, 0, keepdims=False)[:1]

    fc_parts = fc_weight.reshape(share, zx, 2, 2, hidden_share)

    def core_columns(values, index):
        return lax.dynamic_index_in_dim(values, index, 2, keepdims=False)

    fc_mine = core_columns(fc_parts, ic).reshape(share, hidden_half)
    fc_other = swap(core_columns(fc_parts, 1 - ic).reshape(share, hidden_half), "core")
    fc_pair = in_order(fc_mine, fc_other, ic, 0).reshape(2 * share, hidden_half)
    small = jnp.stack([norm2_gain, norm2_shift, out_bias, proj_bias])
    small_rows = jnp.zeros((16, width), bf16)
    small_rows = lax.dynamic_update_slice(small_rows, small, (0, place))
    other_place = (((iz * nx + ix) * 2 + 1 - ic) * 2 + iy) * share
    small_rows = lax.dynamic_update_slice(small_rows, swap(small, "core"), (0, other_place))
    fc_place = ((iz * nx + ix) * 2 + iy) * hidden_share
    small_rows = lax.dynamic_update_slice(small_rows, fc_bias[None], (8 + fc_place // width, fc_place % width))
    folds = hidden_half // width
    fc_folded = fc_pair.reshape(2 * share, folds, width).transpose(1, 0, 2).reshape(-1, width)
    packed = jnp.concatenate([out_weight, proj_weight, fc_folded, small_rows], axis=0)
    rings = [ring_order(nz, turn) for turn in range(2)]
    places = [[ring.index(chip) for chip in range(chip_count)] for ring in rings]
    table = lax.dynamic_index_in_dim(
        jnp.array([[ring, place] for ring, place in zip(rings, places)], jnp.int32), ic, 0, keepdims=False
    )
    gathered = lax.all_gather(packed, every, axis=0, axis_index_groups=core_groups(rings))
    out_rows = share
    proj_rows = hidden_share
    fc_rows = 2 * share * folds

    mixed = [(product(piece, head_weight) + head_offset).astype(bf16) for piece in pieces]
    slots = jnp.concatenate(mixed, axis=0)
    attn_send, queries, keys, values, attn_t, lse = attend_forward(bound, inloc, outloc, slots, chip_count, DH)

    x_a, x_b = block_input.reshape(-1, width), swap(block_input, "core").reshape(-1, width)
    g_a, g_b = out_grad.reshape(-1, width), swap(out_grad, "core").reshape(-1, width)
    own = micro * rows
    attn_got = lax.all_to_all(attn_send, chips, split_axis=0, concat_axis=0, tiled=True)
    weight_turned, attn_got = lax.optimization_barrier((head_weight.T, attn_got))
    cubes = cube_orders(nz // 2)
    w_qkv = lax.all_gather(weight_turned, chips, axis=0, axis_index_groups=cubes)
    part, sent, attn_in = project(table, attn_got, [gathered], share)
    resid, base, project_other, grad_part, sent_back, fc_sums, vectors, terms = middle(
        table, x_a, x_b, g_a, g_b, part, swap(sent[own:], "core"), swap(sent[:own], "core"), [gathered], share, hidden_half
    )
    grad_resid, branch, tails, terms = branch_back(
        table,
        resid,
        g_a,
        g_b,
        grad_part,
        swap(sent_back[own:], "core"),
        swap(sent_back[:own], "core"),
        vectors,
        fc_sums,
        attn_in,
        terms,
        share,
        proj_rows,
        2 * rows,
    )
    grad_send = attention_back(table, branch, tails, [gathered], share, DH)
    output = (base + swap(project_other, "core").astype(f32)).astype(bf16)

    grad_got = lax.all_to_all(grad_send, chips, split_axis=0, concat_axis=0, tiled=True)
    vector_sums = jnp.sum(grad_got[:, DH:].astype(f32), axis=0)
    vector_sums = vector_sums[:, :rows] + vector_sums[:, rows:]
    final_vectors = lax.dynamic_slice(vector_sums, (0, (ic * 2 + iy) * share), (4, share))
    final_fc_b = vector_sums[4]

    summed = lax.psum_scatter(
        terms, every, scatter_dimension=0, tiled=True, axis_index_groups=core_groups(rings)
    )[0]
    final_proj_w = summed[:proj_rows].astype(f32)
    final_out_w = summed[proj_rows : proj_rows + out_rows].astype(f32)
    fc_sum = summed[proj_rows + out_rows :].reshape(folds, 2, share, width)
    fc_keep = lax.dynamic_index_in_dim(fc_sum, ic, 1, keepdims=False)
    fc_give = swap(lax.dynamic_index_in_dim(fc_sum, 1 - ic, 1, keepdims=False), "core")

    def by_owner(values):
        return values.transpose(1, 0, 2).reshape(share, zx, 2, hidden_share)

    final_fc_w = in_order(by_owner(fc_keep), by_owner(fc_give), ic, 2).reshape(share, 2 * hidden_half).astype(f32)

    send_grads = attend_backward(
        bound, inloc, outloc, grad_got, queries, keys, values, attn_t, lse, pieces, share
    )
    grads_got = lax.all_to_all(send_grads, chips, split_axis=0, concat_axis=0, tiled=True)
    back_own, back_other = finish(grads_got, w_qkv, cubes[0])
    raw_got = grads_got[:, 3 * DH :, : 3 * DH].astype(f32)
    raw_sum = jnp.sum(raw_got.reshape(2, zx, 2 * share + 16, 3 * DH), axis=0)
    raw_parts = raw_sum[:, : 2 * share].reshape(zx, 2, share, 3 * DH)
    sums_mine = raw_sum[:, 2 * share : 2 * share + 1] + raw_sum[:, 2 * share + 1 : 2 * share + 2]
    raw_keep = jnp.concatenate([lax.dynamic_index_in_dim(raw_parts, ic, 1, keepdims=False), sums_mine], axis=1)
    raw_give = jnp.concatenate([lax.dynamic_index_in_dim(raw_parts, 1 - ic, 1, keepdims=False), sums_mine], axis=1)
    raw_all = in_order(raw_keep, swap(raw_give, "core"), ic, 1).reshape(heads, share + 1, 3, DH)
    raw_all = raw_all.transpose(1, 2, 0, 3).reshape(share + 1, 3 * width)
    raw_grad, all_sums = raw_all[:share], raw_all[share]
    final_qkv_w = raw_grad * gain_one[:, None] + shift_one[:, None] * all_sums[None, :]
    final_gain_one = jnp.sum(raw_grad * raw_qkv, axis=1)
    final_shift_one = jnp.sum(raw_qkv * all_sums[None, :], axis=1)
    final_q_b = lax.dynamic_slice(all_sums, (place,), (share,))
    final_v_b = lax.dynamic_slice(all_sums, (2 * width + place,), (share,))

    back_own = back_own + swap(back_other, "core").astype(f32)
    back_own = back_own.reshape(micro, rows, width)
    input_grad = grad_resid.reshape(micro, rows, width) + norm_back(back_own, normed_one, inverse_one)

    return (
        output.reshape(micro, rows, width),
        input_grad.astype(bf16),
        final_qkv_w,
        final_q_b,
        final_v_b,
        final_out_w,
        final_vectors[2],
        final_gain_one,
        final_shift_one,
        final_vectors[0],
        final_vectors[1],
        final_fc_w,
        final_fc_b,
        final_proj_w,
        final_vectors[3],
    )


def specs(names):
    rows, vector, tokens = P(names, None), P(names), P(None, names, None)
    weights = (rows, vector, vector, rows, vector, vector, vector, vector, vector, rows, vector, rows, vector)
    return (tokens, *weights, tokens, P(), P()), (tokens, tokens, *weights)


def solution(mesh):
    sizes = dict(mesh.shape)
    if sizes["head"] == 2 and sizes["blk"] == 16:
        fine = Mesh(mesh.devices.reshape(2, 4, 2, 2), ("head", "z", "x", "core"))
        given, made = specs(("z", "x", "core", "head"))
        return jax.shard_map(fast_body, mesh=fine, in_specs=given, out_specs=made, check_vma=False)
    given, made = specs(("blk", "head"))
    return jax.shard_map(general_body, mesh=mesh, in_specs=given, out_specs=made, check_vma=False)
```

```python
import functools
import math

import jax
import jax.numpy as jnp
from jax import lax
from jax.experimental import pallas as pl
from jax.experimental.pallas import tpu as pltpu
from jax.sharding import Mesh
from jax.sharding import PartitionSpec as P

DH = 64


def gelu_tanh(values):
    inner = 0.7978845608028654 * (values + 0.044715 * values * values * values)
    return 0.5 * values * (1.0 + jnp.tanh(inner))


def normalize(values):
    centred = values - jnp.mean(values, axis=-1, keepdims=True)
    inverse = lax.rsqrt(jnp.mean(centred * centred, axis=-1, keepdims=True) + 1e-05)
    return (centred * inverse, inverse)


def norm_back(grad_normed, normed, inverse):
    return inverse * (
        grad_normed
        - jnp.mean(grad_normed, axis=-1, keepdims=True)
        - normed * jnp.mean(grad_normed * normed, axis=-1, keepdims=True)
    )


def product(left, right):
    return jnp.dot(left, right, preferred_element_type=jnp.float32)


def product_tn(left, right):
    return lax.dot_general(
        left, right, (((0,), (0,)), ((), ())), preferred_element_type=jnp.float32
    )


def product_nt(left, right):
    return lax.dot_general(
        left, right, (((1,), (1,)), ((), ())), preferred_element_type=jnp.float32
    )


def visible_pairs(query_pos, key_pos, boundary):
    same_side = (query_pos[:, None] >= boundary) == (key_pos[None, :] >= boundary)
    return same_side & (key_pos[None, :] <= query_pos[:, None])


def forward_tile(current, queries3, keys3, values3, visible, scale):
    running, total, accum = current
    scores = jnp.einsum("qhd,khd->hqk", queries3, keys3, preferred_element_type=jnp.float32) * scale
    scores = jnp.where(visible[None], scores, -1000000000.0)
    highest = jnp.maximum(running, jnp.max(scores, axis=-1))
    weights = jnp.where(visible[None], jnp.exp(scores - highest[..., None]), 0.0)
    factor = jnp.exp(running - highest)
    total = total * factor + jnp.sum(weights, axis=-1)
    accum = accum * factor[..., None] + jnp.einsum(
        "hqk,khd->hqd", weights.astype(jnp.bfloat16), values3, preferred_element_type=jnp.float32
    )
    return (highest, total, accum)


def general_forward(query_parts, pos_parts, positions, boundary, keys_group, values_group, key_span):
    heads_local, head_size = (query_parts[0].shape[1], query_parts[0].shape[2])
    scale = head_size ** (-0.5)

    def fold_keys(state, pieces, start):
        key_rows, value_rows = pieces
        count_rows = key_rows.shape[0]
        block_rows = math.gcd(count_rows, key_span)
        block_count = count_rows // block_rows

        def one_step(index, inner):
            offset = index * block_rows
            keys3 = lax.dynamic_slice_in_dim(key_rows, offset, block_rows).reshape(
                block_rows, heads_local, head_size
            )
            values3 = lax.dynamic_slice_in_dim(value_rows, offset, block_rows).reshape(
                block_rows, heads_local, head_size
            )
            key_pos = lax.dynamic_slice_in_dim(positions, offset, block_rows)
            part_queries = query_parts[0]
            visible = visible_pairs(pos_parts[0], key_pos, boundary)
            current = inner[0]
            result = forward_tile(current, part_queries, keys3, values3, visible, scale)
            updated = [result]
            return tuple(updated)

        return lax.fori_loop(0, block_count, one_step, state)

    initial = tuple(
        (
            (
                jnp.full((heads_local, part.shape[0]), -1000000000.0, jnp.float32),
                jnp.zeros((heads_local, part.shape[0]), jnp.float32),
                jnp.zeros((heads_local, part.shape[0], head_size), jnp.float32),
            )
            for part in query_parts
        )
    )
    return fold_keys(
        initial,
        (
            lax.all_gather(keys_group, "blk", axis=0, tiled=True),
            lax.all_gather(values_group, "blk", axis=0, tiled=True),
        ),
        jnp.int32(0),
    )


def backward_tile(current, queries3, grad3, log_total, delta, keys3, values3, visible, scale):
    grad_query, term = current
    scores = jnp.einsum("qhd,khd->hqk", queries3, keys3, preferred_element_type=jnp.float32) * scale
    scores = jnp.where(visible[None], scores, -1000000000.0)
    exact = jnp.where(visible[None], jnp.exp(scores - log_total[..., None]), 0.0)
    grad_probs = jnp.einsum("qhd,khd->hqk", grad3, values3, preferred_element_type=jnp.float32)
    grad_scores = (exact * (grad_probs - delta[..., None])).astype(jnp.bfloat16)
    grad_query = (
        grad_query
        + jnp.einsum("hqk,khd->hqd", grad_scores, keys3, preferred_element_type=jnp.float32) * scale
    )
    rounded = exact.astype(jnp.bfloat16)
    grad_values = jnp.einsum("hqk,qhd->khd", rounded, grad3, preferred_element_type=jnp.float32)
    grad_keys = (
        jnp.einsum("hqk,qhd->khd", grad_scores, queries3, preferred_element_type=jnp.float32)
        * scale
    )
    rows = keys3.shape[0]
    term = jnp.stack([grad_keys.reshape(rows, -1), grad_values.reshape(rows, -1)], axis=1)
    return (grad_query, term)


def general_backward(
    query_parts,
    grad_parts,
    total_parts,
    delta_parts,
    pos_parts,
    positions,
    boundary,
    keys_group,
    values_group,
    key_span,
    buffer_rows,
):
    heads_local, head_size = (query_parts[0].shape[1], query_parts[0].shape[2])
    scale = head_size ** (-0.5)

    def fold_keys(state, pieces, start):
        key_rows, value_rows = pieces
        count_rows = key_rows.shape[0]
        block_rows = math.gcd(count_rows, key_span)
        block_count = count_rows // block_rows

        def one_step(index, inner):
            offset = index * block_rows
            keys3 = lax.dynamic_slice_in_dim(key_rows, offset, block_rows).reshape(
                block_rows, heads_local, head_size
            )
            values3 = lax.dynamic_slice_in_dim(value_rows, offset, block_rows).reshape(
                block_rows, heads_local, head_size
            )
            key_pos = lax.dynamic_slice_in_dim(positions, offset, block_rows)
            grads_now, buffer = inner
            term = jnp.zeros((block_rows, 2, heads_local * head_size), jnp.float32)
            part_queries = query_parts[0]
            part_grads = grad_parts[0]
            part_total = total_parts[0]
            part_delta = delta_parts[0]
            visible = visible_pairs(pos_parts[0], key_pos, boundary)
            current = (grads_now[0], term)
            result = backward_tile(
                current,
                part_queries,
                part_grads,
                part_total,
                part_delta,
                keys3,
                values3,
                visible,
                scale,
            )
            updated = [result[0]]
            term = result[1]
            buffer = lax.dynamic_update_slice(buffer, term, (offset, 0, 0))
            return (tuple(updated), buffer)

        return lax.fori_loop(0, block_count, one_step, state)

    grads_init = tuple(
        (jnp.zeros((heads_local, part.shape[0], head_size), jnp.float32) for part in query_parts)
    )
    initial = (grads_init, jnp.zeros((buffer_rows, 2, heads_local * head_size), jnp.float32))
    return fold_keys(
        initial,
        (
            lax.all_gather(keys_group, "blk", axis=0, tiled=True),
            lax.all_gather(values_group, "blk", axis=0, tiled=True),
        ),
        jnp.int32(0),
    )


def general_body(
    block_input,
    qkv_weight,
    q_bias,
    v_bias,
    out_weight,
    out_bias,
    norm1_gain,
    norm1_shift,
    norm2_gain,
    norm2_shift,
    fc_weight,
    fc_bias,
    proj_weight,
    proj_bias,
    out_grad,
    dealt,
    lengths,
):
    micro_count, local_rows, width = block_input.shape
    head_devices = lax.axis_size("head")
    blk_devices = lax.axis_size("blk")
    group = local_rows * head_devices
    blk_index = lax.axis_index("blk")
    head_size = DH
    key_span = 1024
    part_count = group // group
    shards = (
        qkv_weight,
        q_bias,
        v_bias,
        out_weight,
        out_bias,
        norm1_gain,
        norm1_shift,
        norm2_gain,
        norm2_shift,
        fc_weight,
        fc_bias,
        proj_weight,
        proj_bias,
    )
    totals = [
        jnp.zeros((shard.shape[0] * blk_devices * head_devices,) + shard.shape[1:], jnp.float32)
        for shard in shards
    ]
    outputs = []
    input_grads = []
    for micro_index in range(micro_count):
        whole = (
            lax.all_gather(shards[0], ("blk", "head"), axis=0, tiled=True),
            lax.all_gather(shards[1], ("blk", "head"), axis=0, tiled=True),
            lax.all_gather(shards[2], ("blk", "head"), axis=0, tiled=True),
            lax.all_gather(shards[3], ("blk", "head"), axis=0, tiled=True),
            lax.all_gather(shards[4], ("blk", "head"), axis=0, tiled=True),
            lax.all_gather(shards[5], ("blk", "head"), axis=0, tiled=True),
            lax.all_gather(shards[6], ("blk", "head"), axis=0, tiled=True),
            lax.all_gather(shards[7], ("blk", "head"), axis=0, tiled=True),
            lax.all_gather(shards[8], ("blk", "head"), axis=0, tiled=True),
            lax.all_gather(shards[9], ("blk", "head"), axis=0, tiled=True),
            lax.all_gather(shards[10], ("blk", "head"), axis=0, tiled=True),
            lax.all_gather(shards[11], ("blk", "head"), axis=0, tiled=True),
            lax.all_gather(shards[12], ("blk", "head"), axis=0, tiled=True),
        )
        (
            w_qkv,
            b_query,
            b_value,
            w_out,
            b_out,
            gain_one,
            shift_one,
            gain_two,
            shift_two,
            w_fc,
            b_fc,
            w_proj,
            b_proj,
        ) = whole
        b_query = b_query.astype(jnp.float32)
        b_value = b_value.astype(jnp.float32)
        b_out = b_out.astype(jnp.float32)
        gain_one = gain_one.astype(jnp.float32)
        shift_one = shift_one.astype(jnp.float32)
        gain_two = gain_two.astype(jnp.float32)
        shift_two = shift_two.astype(jnp.float32)
        b_fc = b_fc.astype(jnp.float32)
        b_proj = b_proj.astype(jnp.float32)
        positions = dealt[micro_index]
        boundary = lengths[micro_index, 0]
        query_pos = lax.dynamic_slice_in_dim(positions, blk_index * group, group)
        inputs = block_input[micro_index].astype(jnp.float32)
        normed_one, inverse_one = normalize(inputs)
        act_one = (normed_one * gain_one + shift_one).astype(jnp.bfloat16)
        mixed = product(act_one, w_qkv)
        queries = (mixed[:, :width] + b_query).astype(jnp.bfloat16)
        keys = mixed[:, width : 2 * width].astype(jnp.bfloat16)
        values = (mixed[:, 2 * width :] + b_value).astype(jnp.bfloat16)
        heads_in = lax.all_to_all(
            jnp.stack([queries, keys, values], axis=1),
            "head",
            split_axis=2,
            concat_axis=0,
            tiled=True,
        )
        local_width = heads_in.shape[2]
        heads_local = local_width // head_size
        queries3 = heads_in[:, 0].reshape(group, heads_local, head_size)
        keys_group = heads_in[:, 1]
        values_group = heads_in[:, 2]
        query_parts = tuple((queries3 for index in range(part_count)))
        pos_parts = tuple((query_pos for index in range(part_count)))
        states = general_forward(
            query_parts, pos_parts, positions, boundary, keys_group, values_group, key_span
        )
        running = jnp.concatenate([state[0] for state in states], axis=1)
        total = jnp.concatenate([state[1] for state in states], axis=1)
        accum = jnp.concatenate([state[2] for state in states], axis=1)
        log_total = running + jnp.log(total)
        attn_heads = (
            (accum / total[..., None])
            .transpose(1, 0, 2)
            .reshape(group, local_width)
            .astype(jnp.bfloat16)
        )
        attended = lax.all_to_all(attn_heads, "head", split_axis=0, concat_axis=1, tiled=True)
        resid = inputs + product(attended, w_out) + b_out
        normed_two, inverse_two = normalize(resid)
        act_two = (normed_two * gain_two + shift_two).astype(jnp.bfloat16)
        pre = product(act_two, w_fc) + b_fc
        hidden = gelu_tanh(pre).astype(jnp.bfloat16)
        outputs.append((resid + product(hidden, w_proj) + b_proj).astype(jnp.bfloat16))
        cotangent = out_grad[micro_index]
        grad_proj_w = product_tn(hidden, cotangent)
        grad_proj_b = jnp.sum(cotangent.astype(jnp.float32), axis=0)
        grad_hidden = product_nt(cotangent, w_proj)
        grad_pre = jax.vjp(gelu_tanh, pre)[1](grad_hidden)[0].astype(jnp.bfloat16)
        grad_fc_w = product_tn(act_two, grad_pre)
        grad_fc_b = jnp.sum(grad_pre.astype(jnp.float32), axis=0)
        grad_act_two = product_nt(grad_pre, w_fc)
        grad_gain_two = jnp.sum(grad_act_two * normed_two, axis=0)
        grad_shift_two = jnp.sum(grad_act_two, axis=0)
        grad_resid = cotangent.astype(jnp.float32) + norm_back(
            grad_act_two * gain_two, normed_two, inverse_two
        )
        grad_branch = grad_resid.astype(jnp.bfloat16)
        grad_out_w = product_tn(attended, grad_branch)
        grad_out_b = jnp.sum(grad_branch.astype(jnp.float32), axis=0)
        grad_attn = product_nt(grad_branch, w_out).astype(jnp.bfloat16)
        grad_heads = lax.all_to_all(grad_attn, "head", split_axis=1, concat_axis=0, tiled=True)
        grad3 = grad_heads.reshape(group, heads_local, head_size)
        attn3 = attn_heads.reshape(group, heads_local, head_size)
        delta = jnp.sum(grad3.astype(jnp.float32) * attn3.astype(jnp.float32), axis=-1).T
        grad_parts = tuple((grad3 for index in range(part_count)))
        total_parts = tuple((log_total for index in range(part_count)))
        delta_parts = tuple((delta for index in range(part_count)))
        query_grads, buffer = general_backward(
            query_parts,
            grad_parts,
            total_parts,
            delta_parts,
            pos_parts,
            positions,
            boundary,
            keys_group,
            values_group,
            key_span,
            group * blk_devices,
        )
        kv_sums = lax.psum_scatter(buffer, "blk", scatter_dimension=0, tiled=True)
        grad_k_heads = kv_sums[:, 0].astype(jnp.bfloat16)
        grad_v_heads = kv_sums[:, 1].astype(jnp.bfloat16)
        grad_query = jnp.concatenate(list(query_grads), axis=1)
        grad_q_heads = (
            grad_query.transpose(1, 0, 2).reshape(group, local_width).astype(jnp.bfloat16)
        )
        grads_heads = jnp.stack([grad_q_heads, grad_k_heads, grad_v_heads], axis=1)
        back_tokens = lax.all_to_all(grads_heads, "head", split_axis=0, concat_axis=2, tiled=True)
        grad_mixed = back_tokens.reshape(local_rows, 3 * width)
        grad_qkv_w = product_tn(act_one, grad_mixed)
        grad_q_b = jnp.sum(back_tokens[:, 0].astype(jnp.float32), axis=0)
        grad_v_b = jnp.sum(back_tokens[:, 2].astype(jnp.float32), axis=0)
        grad_act_one = product_nt(grad_mixed, w_qkv)
        grad_gain_one = jnp.sum(grad_act_one * normed_one, axis=0)
        grad_shift_one = jnp.sum(grad_act_one, axis=0)
        input_grads.append(
            (grad_resid + norm_back(grad_act_one * gain_one, normed_one, inverse_one)).astype(
                jnp.bfloat16
            )
        )
        terms = (
            grad_qkv_w,
            grad_q_b,
            grad_v_b,
            grad_out_w,
            grad_out_b,
            grad_gain_one,
            grad_shift_one,
            grad_gain_two,
            grad_shift_two,
            grad_fc_w,
            grad_fc_b,
            grad_proj_w,
            grad_proj_b,
        )
        totals = [running_sum + term for running_sum, term in zip(totals, terms)]
    final = (
        lax.psum_scatter(totals[0], ("blk", "head"), scatter_dimension=0, tiled=True),
        lax.psum_scatter(totals[1], ("blk", "head"), scatter_dimension=0, tiled=True),
        lax.psum_scatter(totals[2], ("blk", "head"), scatter_dimension=0, tiled=True),
        lax.psum_scatter(totals[3], ("blk", "head"), scatter_dimension=0, tiled=True),
        lax.psum_scatter(totals[4], ("blk", "head"), scatter_dimension=0, tiled=True),
        lax.psum_scatter(totals[5], ("blk", "head"), scatter_dimension=0, tiled=True),
        lax.psum_scatter(totals[6], ("blk", "head"), scatter_dimension=0, tiled=True),
        lax.psum_scatter(totals[7], ("blk", "head"), scatter_dimension=0, tiled=True),
        lax.psum_scatter(totals[8], ("blk", "head"), scatter_dimension=0, tiled=True),
        lax.psum_scatter(totals[9], ("blk", "head"), scatter_dimension=0, tiled=True),
        lax.psum_scatter(totals[10], ("blk", "head"), scatter_dimension=0, tiled=True),
        lax.psum_scatter(totals[11], ("blk", "head"), scatter_dimension=0, tiled=True),
        lax.psum_scatter(totals[12], ("blk", "head"), scatter_dimension=0, tiled=True),
    )
    return (
        jnp.stack(outputs),
        jnp.stack(input_grads),
        final[0],
        final[1],
        final[2],
        final[3],
        final[4],
        final[5],
        final[6],
        final[7],
        final[8],
        final[9],
        final[10],
        final[11],
        final[12],
    )


RUN = 64
BLOCK = 512
NEG = -1000000000.0
VM = pltpu.VMEM
SM = pltpu.SMEM


def dot_nt(left, right):
    return lax.dot_general(left, right, (((1,), (1,)), ((), ())), preferred_element_type=jnp.float32)


def dot_nn(left, right):
    return lax.dot_general(left, right, (((1,), (0,)), ((), ())), preferred_element_type=jnp.float32)


def rows_at(index, size):
    return pl.ds(pl.multiple_of(index * size, size), size)


def first_block(start, bound):
    return jnp.where(start >= bound, bound // BLOCK, 0)


def forward_kernel(head_size, bound_ref, inloc, outloc, qkv, out, qs, ks, vs, attn_t, lse, vt, mixed):
    tokens = qkv.shape[0]
    runs = tokens // RUN
    scale = head_size ** (-0.5)
    bound = bound_ref[0]

    @pl.loop(0, runs, unroll=8)
    def _(run):
        rows = qkv[rows_at(inloc[run], RUN), :]
        here = rows_at(run, RUN)
        qs[here, :] = (rows[:, :head_size].astype(jnp.float32) * scale).astype(jnp.bfloat16)
        ks[here, :] = rows[:, head_size : 2 * head_size]
        vs[here, :] = rows[:, 2 * head_size :]

    @pl.loop(0, tokens // BLOCK, unroll=4)
    def _(block):
        here = rows_at(block, BLOCK)
        vt[:, here] = vs[here, :].astype(jnp.float32).T.astype(jnp.bfloat16)

    @pl.loop(0, tokens // BLOCK)
    def _(block):
        start = block * BLOCK
        here = rows_at(block, BLOCK)
        queries = qs[here, :]
        query_pos = start + lax.broadcasted_iota(jnp.int32, (1, BLOCK), 1)
        floor = jnp.where(query_pos >= bound, bound, 0)

        def scores_of(index, diagonal):
            keys = ks[rows_at(index, BLOCK), :]
            scores = dot_nt(keys, queries)
            key_pos = index * BLOCK + lax.broadcasted_iota(jnp.int32, (BLOCK, BLOCK), 0)
            visible = key_pos >= floor
            if diagonal:
                visible = visible & (key_pos <= query_pos)
            return jnp.where(visible, scores, NEG)

        scores = scores_of(block, True)
        highest = jnp.max(scores, axis=0, keepdims=True)
        weights = jnp.exp(scores - highest)
        total = jnp.sum(weights, axis=0, keepdims=True)
        accum = dot_nn(vt[:, here], weights.astype(jnp.bfloat16))

        def step(index, state):
            highest, total, accum = state
            scores = scores_of(index, False)
            higher = jnp.maximum(highest, jnp.max(scores, axis=0, keepdims=True))
            weights = jnp.exp(scores - higher)
            factor = jnp.exp(highest - higher)
            total = total * factor + jnp.sum(weights, axis=0, keepdims=True)
            accum = accum * factor + dot_nn(vt[:, rows_at(index, BLOCK)], weights.astype(jnp.bfloat16))
            return higher, total, accum

        highest, total, accum = lax.fori_loop(first_block(start, bound), block, step, (highest, total, accum))
        result = accum / total
        attn_t[:, here] = result.astype(jnp.bfloat16)
        lse[:, here] = highest + jnp.log(total)
        result = result.T.astype(jnp.bfloat16)
        for part in range(BLOCK // RUN):
            mixed[rows_at(outloc[block * (BLOCK // RUN) + part], RUN), :] = result[part * RUN : (part + 1) * RUN]

    chips, _, span = out.shape

    @pl.loop(0, chips, unroll=8)
    def _(chip):
        out[chip] = mixed[rows_at(chip, span), :].astype(jnp.float32).T.astype(jnp.bfloat16)


def attend_forward(bound, inloc, outloc, qkv, chips, head_size):
    tokens = qkv.shape[0]
    bf16 = jnp.bfloat16
    pairs = tokens * (tokens // 2)
    return pl.pallas_call(
        functools.partial(forward_kernel, head_size),
        out_shape=(
            jax.ShapeDtypeStruct((chips, head_size, tokens // chips), bf16),
            jax.ShapeDtypeStruct((tokens, head_size), bf16),
            jax.ShapeDtypeStruct((tokens, head_size), bf16),
            jax.ShapeDtypeStruct((tokens, head_size), bf16),
            jax.ShapeDtypeStruct((head_size, tokens), bf16),
            jax.ShapeDtypeStruct((1, tokens), jnp.float32),
        ),
        in_specs=[pl.BlockSpec(memory_space=SM)] * 3 + [pl.BlockSpec(memory_space=VM)],
        out_specs=[pl.BlockSpec(memory_space=VM)] * 6,
        scratch_shapes=[VM((head_size, tokens), bf16), VM((tokens, head_size), bf16)],
        compiler_params=pltpu.CompilerParams(vmem_limit_bytes=40 * 1024 * 1024),
        cost_estimate=pl.CostEstimate(flops=4 * 4 * pairs * head_size, bytes_accessed=tokens * 2048, transcendentals=pairs),
        name="attend_forward",
    )(bound, inloc, outloc, qkv)


def backward_kernel(
    head_size, count, share, bound_ref, inloc, outloc, grad_t, qs, ks, vs, attn_t, lse, *refs
):
    pieces = refs[:count]
    send_out, normed, raw, grads, kt, dk, dv, mixed, wide, moved, sem = refs[count:]
    tokens = qs.shape[0]
    runs = tokens // RUN
    scale = head_size ** (-0.5)
    bound = bound_ref[0]
    chips, _, span = grad_t.shape
    copies, filled = [], 0
    for piece in pieces:
        copies.append(pltpu.make_async_copy(piece, normed.at[pl.ds(filled, piece.shape[0])], sem))
        filled += piece.shape[0]
    for copy in copies:
        copy.start()

    @pl.loop(0, chips, unroll=8)
    def _(chip):
        mixed[rows_at(chip, span), :] = grad_t[chip, :head_size, :].astype(jnp.float32).T.astype(jnp.bfloat16)

    @pl.loop(0, runs, unroll=8)
    def _(run):
        grads[rows_at(run, RUN), :] = mixed[rows_at(outloc[run], RUN), :]

    @pl.loop(0, tokens // BLOCK, unroll=4)
    def _(block):
        here = rows_at(block, BLOCK)
        kt[:, here] = ks[here, :].astype(jnp.float32).T.astype(jnp.bfloat16)

    @pl.loop(0, tokens // BLOCK)
    def _(block):
        start = block * BLOCK
        here = rows_at(block, BLOCK)
        queries = qs[here, :]
        grad = grads[here, :]
        log_total = lse[:, here]
        delta = jnp.sum(grad.astype(jnp.float32).T * attn_t[:, here].astype(jnp.float32), axis=0, keepdims=True)
        query_pos = start + lax.broadcasted_iota(jnp.int32, (1, BLOCK), 1)
        floor = jnp.where(query_pos >= bound, bound, 0)

        def one(index, diagonal):
            there = rows_at(index, BLOCK)
            scores = dot_nt(ks[there, :], queries)
            key_pos = index * BLOCK + lax.broadcasted_iota(jnp.int32, (BLOCK, BLOCK), 0)
            visible = key_pos >= floor
            if diagonal:
                visible = visible & (key_pos <= query_pos)
            probs = jnp.where(visible, jnp.exp(scores - log_total), 0.0)
            grad_probs = dot_nt(vs[there, :], grad)
            grad_scores = (probs * (grad_probs - delta)).astype(jnp.bfloat16)
            return (
                dot_nn(probs.astype(jnp.bfloat16), grad),
                dot_nn(grad_scores, queries),
                dot_nn(kt[:, there], grad_scores),
                there,
            )

        grad_v, grad_k, grad_q, there = one(block, True)
        dv[there, :] = grad_v
        dk[there, :] = grad_k

        def step(index, grad_q):
            grad_v, grad_k, term, there = one(index, False)
            dv[there, :] += grad_v
            dk[there, :] += grad_k
            return grad_q + term

        grad_q = lax.fori_loop(first_block(start, bound), block, step, grad_q)
        wide[here, :head_size] = (grad_q.T * scale).astype(jnp.bfloat16)

    wide[:, head_size : 2 * head_size] = dk[...].astype(jnp.bfloat16)
    wide[:, 2 * head_size :] = dv[...].astype(jnp.bfloat16)

    size = 3 * head_size

    @pl.loop(0, runs, unroll=8)
    def _(run):
        moved[rows_at(outloc[run], RUN), :] = wide[rows_at(run, RUN), :]

    @pl.loop(0, chips, unroll=8)
    def _(chip):
        send_out[chip, :size, :] = moved[rows_at(chip, span), :].astype(jnp.float32).T.astype(jnp.bfloat16)

    @pl.loop(0, runs, unroll=8)
    def _(run):
        moved[rows_at(inloc[run], RUN), :] = wide[rows_at(run, RUN), :]

    for copy in copies:
        copy.wait()
    raw[...] = jnp.zeros_like(raw)

    @pl.loop(0, tokens // BLOCK, unroll=2)
    def _(block):
        here = rows_at(block, BLOCK)
        turned = moved[here, :].astype(jnp.float32).T.astype(jnp.bfloat16)
        raw[...] += dot_nn(turned, normed[here, :])

    product = raw[...].T
    sums = jnp.sum(wide[...].astype(jnp.float32), axis=0, keepdims=True)
    high = sums.astype(jnp.bfloat16).astype(jnp.float32)
    tail = jnp.concatenate([high, sums - high, jnp.zeros((14, size), jnp.float32)], axis=0)
    for chip in range(chips):
        first = chip // 2 * 4 * share + chip % 2 * share
        rows = jnp.concatenate([product[first : first + share], product[first + 2 * share : first + 3 * share], tail], axis=0)
        rows = jnp.concatenate([rows, jnp.zeros((rows.shape[0], span - size), jnp.float32)], axis=1)
        send_out[chip, size:, :] = rows.astype(jnp.bfloat16)


def attend_backward(bound, inloc, outloc, grad_t, qs, ks, vs, attn_t, lse, pieces, share):
    tokens, head_size = qs.shape
    chips = grad_t.shape[0]
    width = pieces[0].shape[1]
    bf16 = jnp.bfloat16
    pairs = tokens * (tokens // 2)
    return pl.pallas_call(
        functools.partial(backward_kernel, head_size, len(pieces), share),
        out_shape=jax.ShapeDtypeStruct((chips, 3 * head_size + 2 * share + 16, tokens // chips), bf16),
        in_specs=[pl.BlockSpec(memory_space=SM)] * 3 + [pl.BlockSpec(memory_space=VM)] * 6
        + [pl.BlockSpec(memory_space=pltpu.HBM)] * len(pieces),
        out_specs=pl.BlockSpec(memory_space=VM),
        scratch_shapes=[
            VM((tokens, width), bf16),
            VM((3 * head_size, width), jnp.float32),
            VM((tokens, head_size), bf16),
            VM((head_size, tokens), bf16),
            VM((tokens, head_size), jnp.float32),
            VM((tokens, head_size), jnp.float32),
            VM((tokens, head_size), bf16),
            VM((tokens, 3 * head_size), bf16),
            VM((tokens, 3 * head_size), bf16),
            pltpu.SemaphoreType.DMA,
        ],
        compiler_params=pltpu.CompilerParams(vmem_limit_bytes=48 * 1024 * 1024),
        cost_estimate=pl.CostEstimate(flops=4 * 10 * pairs * head_size, bytes_accessed=tokens * 4096, transcendentals=pairs),
        name="attend_backward",
    )(bound, inloc, outloc, grad_t, qs, ks, vs, attn_t, lse, *pieces)


HALF_STEP = 512


def gelu_pair(values):
    cubic = values * values
    inner = 0.7978845608028654 * values * (1.0 + 0.044715 * cubic)
    bent = jnp.tanh(inner)
    slope = 0.7978845608028654 * (1.0 + 0.134145 * cubic)
    half = 0.5 * (1.0 + bent)
    return values * half, half + 0.5 * values * (1.0 - bent * bent) * slope


def load_rows(table, pieces, targets, sem, wait):
    slot = 0
    for piece in pieces:
        count = piece.shape[0]

        @pl.loop(0, count, unroll=4)
        def _(index, piece=piece, slot=slot):
            chip = table[0, slot + index]
            for rows, target in targets(chip):
                copy = pltpu.make_async_copy(piece.at[index, rows], target, sem)
                if wait:
                    copy.wait()
                else:
                    copy.start()

        slot += count


def project_kernel(count, table, got, *refs):
    pieces, (part_out, sent_a, sent_b, attn_in, w_out, sem) = refs[:count], refs[count:]
    chips, size, span = got.shape
    share = w_out.shape[0] // chips
    rows = span // 2

    def targets(chip):
        return [(pl.ds(0, share), w_out.at[rows_at(chip, share)])]

    load_rows(table, pieces, targets, sem, False)
    for chip in range(chips):
        micro, head = divmod(chip, chips // 2)
        for rel in range(2):
            column = (rel * 2 + micro) * rows
            attn_in[head * size : (head + 1) * size, column : column + rows] = got[chip, :, rel * rows : (rel + 1) * rows]
    load_rows(table, pieces, targets, sem, True)
    left = attn_in[...].astype(jnp.float32).T.astype(jnp.bfloat16)
    part = dot_nn(left, w_out[...])
    part_out[...] = part
    own = sent_a.shape[0]
    sent_a[...] = part[:own].astype(jnp.bfloat16)
    sent_b[...] = part[own:].astype(jnp.bfloat16)


def project(table, got, pieces, share):
    chips, size, span = got.shape
    width = pieces[0].shape[2]
    tokens = 2 * span
    bf16 = jnp.bfloat16
    return pl.pallas_call(
        functools.partial(project_kernel, len(pieces)),
        out_shape=(
            jax.ShapeDtypeStruct((tokens, width), jnp.float32),
            jax.ShapeDtypeStruct((tokens // 2, width), bf16),
            jax.ShapeDtypeStruct((tokens // 2, width), bf16),
            jax.ShapeDtypeStruct((chips // 2 * size, tokens), bf16),
        ),
        in_specs=[pl.BlockSpec(memory_space=SM), pl.BlockSpec(memory_space=VM)]
        + [pl.BlockSpec(memory_space=pltpu.HBM)] * len(pieces),
        out_specs=[pl.BlockSpec(memory_space=VM)] * 4,
        scratch_shapes=[VM((chips * share, width), bf16), pltpu.SemaphoreType.DMA],
        compiler_params=pltpu.CompilerParams(vmem_limit_bytes=58 * 1024 * 1024),
        cost_estimate=pl.CostEstimate(
            flops=2 * tokens * chips * share * width, bytes_accessed=8 * tokens * width, transcendentals=0
        ),
        name="project",
    )(table, got, *pieces)


def middle_kernel(count, share, table, x_a, x_b, g_a, g_b, part, got_a, got_b, *refs):
    pieces = refs[:count]
    (resid, base, other, grad_act, sent_a, sent_b, fc_sums, vectors, terms) = refs[count : count + 9]
    (smalls, fc_bias, w_fc, w_proj, g_all, act, act_t, rest, proj_buf, fc_buf, small_sem, load_sem, proj_sem, fc_sem) = refs[count + 9 :]
    f32, bf16 = jnp.float32, jnp.bfloat16
    tokens, width = part.shape
    own = tokens // 2
    hidden = w_proj.shape[0]
    chips = terms.shape[0]
    each = hidden // chips
    folds = hidden // width
    fc_row = share + each

    def targets(chip):
        wanted = [(pl.ds(share, each), w_proj.at[rows_at(chip, each)])]
        for fold in range(folds):
            for core in range(2):
                first = fc_row + (fold * 2 + core) * share
                place = ((chip // 2) * 2 + core) * 2 + chip % 2
                wanted.append(
                    (pl.ds(first, share), w_fc.at[rows_at(place, share), pl.ds(fold * width, width)])
                )
        return wanted

    def small_targets(chip):
        return [(pl.ds(pieces[0].shape[1] - 16, 16), smalls.at[chip])]

    load_rows(table, pieces, small_targets, small_sem, False)
    load_rows(table, pieces, targets, load_sem, False)
    load_rows(table, pieces, small_targets, small_sem, True)
    small_sum = jnp.sum(smalls[...].astype(f32), axis=0)
    vectors[...] = small_sum[:8]
    for fold in range(folds):
        fc_bias[:, fold * width : (fold + 1) * width] = small_sum[8 + fold : 9 + fold]
    for half, (x_in, g_in, arrived) in enumerate(((x_a, g_a, got_a), (x_b, g_b, got_b))):
        here = slice(half * own, (half + 1) * own)
        g_all[here, :] = g_in[...]
        value = x_in[...].astype(f32) + part[here, :] + arrived[...].astype(f32) + vectors[2:3, :]
        resid[here, :] = value
        centred = value - jnp.mean(value, axis=-1, keepdims=True)
        inverse = lax.rsqrt(jnp.mean(centred * centred, axis=-1, keepdims=True) + 1e-05)
        rounded = (centred * inverse * vectors[0:1, :] + vectors[1:2, :]).astype(bf16)
        act[here, :] = rounded
        act_t[:, here] = rounded.astype(f32).T.astype(bf16)
    base[...] = resid[:own, :] + vectors[3:4, :]
    load_rows(table, pieces, targets, load_sem, True)

    per_step = HALF_STEP // each

    def copies(step, slot):
        made = []
        for index in range(per_step):
            made.append(
                pltpu.make_async_copy(
                    proj_buf.at[slot, pl.ds(index * each, each)],
                    terms.at[table[1, step * per_step + index], pl.ds(0, each)],
                    proj_sem.at[slot],
                )
            )
        fold = step // (width // HALF_STEP)
        column = pl.multiple_of(step % (width // HALF_STEP) * HALF_STEP, HALF_STEP)
        for chip in range(chips):
            for core in range(2):
                place = ((chip // 2) * 2 + core) * 2 + chip % 2
                made.append(
                    pltpu.make_async_copy(
                        fc_buf.at[slot, pl.ds(place * share, share)],
                        terms.at[
                            table[1, chip],
                            pl.ds(pl.multiple_of(each + share + (fold * 2 + core) * share, 16), share),
                            pl.ds(column, HALF_STEP),
                        ],
                        fc_sem.at[slot],
                    )
                )
        return made

    steps = hidden // HALF_STEP

    @pl.loop(0, steps)
    def _(step):
        slot = step % 2
        columns = pl.ds(pl.multiple_of(step * HALF_STEP, HALF_STEP), HALF_STEP)
        rows = rows_at(step, HALF_STEP)

        @pl.when(step >= 2)
        def _():
            for copy in copies(step - 2, slot):
                copy.wait()

        grads = g_all[...]
        value, slope = gelu_pair(dot_nn(act[...], w_fc[:, columns]) + fc_bias[:, columns])
        value = value.astype(bf16)
        proj_buf[slot] = dot_nn(value.astype(f32).T.astype(bf16), grads).astype(bf16)
        grad_pre = (dot_nt(grads, w_proj[rows, :]) * slope).astype(bf16)
        fc_sums[:, columns] = jnp.sum(grad_pre.astype(f32), axis=0, keepdims=True)
        fc_buf[slot] = dot_nn(act_t[...], grad_pre).astype(bf16)
        for copy in copies(step, slot):
            copy.start()
        projected = dot_nn(value, w_proj[rows, :])
        back = dot_nt(grad_pre, w_fc[:, columns])
        base[...] += projected[:own]

        @pl.when(step == 0)
        def _():
            grad_act[...] = back
            rest[...] = projected[own:]

        @pl.when(step > 0)
        def _():
            grad_act[...] += back
            rest[...] += projected[own:]

    other[...] = rest[...].astype(bf16)
    sent_a[...] = grad_act[:own, :].astype(bf16)
    sent_b[...] = grad_act[own:, :].astype(bf16)
    for step in range(steps - 2, steps):
        for copy in copies(step, step % 2):
            copy.wait()


def middle(table, x_a, x_b, g_a, g_b, part, got_a, got_b, pieces, share, hidden):
    tokens, width = part.shape
    f32, bf16 = jnp.float32, jnp.bfloat16
    chips = table.shape[1]
    each = hidden // chips
    rows = share + each + 2 * share * (hidden // width)
    shape = jax.ShapeDtypeStruct
    return pl.pallas_call(
        functools.partial(middle_kernel, len(pieces), share),
        out_shape=(
            shape((tokens, width), f32),
            shape((tokens // 2, width), f32),
            shape((tokens // 2, width), bf16),
            shape((tokens, width), f32),
            shape((tokens // 2, width), bf16),
            shape((tokens // 2, width), bf16),
            shape((1, hidden), f32),
            shape((8, width), f32),
            shape((chips, rows, width), bf16),
        ),
        in_specs=[pl.BlockSpec(memory_space=SM)]
        + [pl.BlockSpec(memory_space=VM)] * 7
        + [pl.BlockSpec(memory_space=pltpu.HBM)] * len(pieces),
        out_specs=[pl.BlockSpec(memory_space=VM)] * 8 + [pl.BlockSpec(memory_space=pltpu.HBM)],
        scratch_shapes=[
            VM((chips, 16, width), bf16),
            VM((1, hidden), f32),
            VM((width, hidden), bf16),
            VM((hidden, width), bf16),
            VM((tokens, width), bf16),
            VM((tokens, width), bf16),
            VM((width, tokens), bf16),
            VM((tokens // 2, width), f32),
            VM((2, HALF_STEP, width), bf16),
            VM((2, width, HALF_STEP), bf16),
            pltpu.SemaphoreType.DMA,
            pltpu.SemaphoreType.DMA,
            pltpu.SemaphoreType.DMA((2,)),
            pltpu.SemaphoreType.DMA((2,)),
        ],
        compiler_params=pltpu.CompilerParams(vmem_limit_bytes=56 * 1024 * 1024),
        cost_estimate=pl.CostEstimate(
            flops=12 * tokens * width * hidden, bytes_accessed=8 * width * hidden, transcendentals=tokens * hidden
        ),
        name="middle",
    )(table, x_a, x_b, g_a, g_b, part, got_a, got_b, *pieces)


def branch_kernel(share, row, table, resid, g_a, g_b, part, got_a, got_b, vectors, fc_sums, attn_in, given, grad_resid, branch, tails, terms, products, sem):
    f32, bf16 = jnp.float32, jnp.bfloat16
    tokens, width = resid.shape
    own = tokens // 2
    chips = tails.shape[0]
    gain_sum = jnp.zeros((1, width), f32)
    shift_sum = jnp.zeros((1, width), f32)
    bias_sum = jnp.zeros((1, width), f32)
    proj_sum = jnp.zeros((1, width), f32)
    for half, (g_in, arrived) in enumerate(((g_a, got_a), (g_b, got_b))):
        here = slice(half * own, (half + 1) * own)
        value = resid[here, :]
        centred = value - jnp.mean(value, axis=-1, keepdims=True)
        inverse = lax.rsqrt(jnp.mean(centred * centred, axis=-1, keepdims=True) + 1e-05)
        normed = centred * inverse
        grad = part[here, :] + arrived[...].astype(f32)
        gain_sum += jnp.sum(grad * normed, axis=0, keepdims=True)
        shift_sum += jnp.sum(grad, axis=0, keepdims=True)
        scaled = grad * vectors[0:1, :]
        given_grad = g_in[...].astype(f32)
        total = given_grad + inverse * (
            scaled
            - jnp.mean(scaled, axis=-1, keepdims=True)
            - normed * jnp.mean(scaled * normed, axis=-1, keepdims=True)
        )
        rounded = total.astype(bf16)
        bias_sum += jnp.sum(rounded.astype(f32), axis=0, keepdims=True)
        proj_sum += jnp.sum(given_grad, axis=0, keepdims=True)
        branch[here, :] = rounded
        if half == 0:
            grad_resid[...] = total
    group = width // (chips // 2)
    sums = jnp.concatenate([gain_sum, shift_sum, bias_sum, proj_sum], axis=0)
    each = fc_sums.shape[1] // chips
    for chip in range(chips):
        first = chip // 2 * group
        tail = jnp.concatenate(
            [
                sums[:, first : first + group],
                fc_sums[:, chip * each : (chip + 1) * each],
                jnp.zeros((3, group), f32),
            ],
            axis=0,
        )
        high = tail.astype(bf16)
        low = (tail - high.astype(f32)).astype(bf16)
        tails[chip] = jnp.concatenate([high, low], axis=1)
    products[...] = dot_nn(attn_in[...], branch[...]).astype(bf16)

    @pl.loop(0, chips)
    def _(chip):
        pltpu.make_async_copy(products.at[rows_at(chip, share)], terms.at[table[1, chip], pl.ds(row, share)], sem).start()

    @pl.loop(0, chips)
    def _(chip):
        pltpu.make_async_copy(products.at[rows_at(chip, share)], terms.at[table[1, chip], pl.ds(row, share)], sem).wait()


def branch_back(table, resid, g_a, g_b, part, got_a, got_b, vectors, fc_sums, attn_in, terms, share, row, span):
    tokens, width = resid.shape
    f32, bf16 = jnp.float32, jnp.bfloat16
    chips = table.shape[1]
    shape = jax.ShapeDtypeStruct
    return pl.pallas_call(
        functools.partial(branch_kernel, share, row),
        out_shape=(
            shape((tokens // 2, width), f32),
            shape((tokens, width), bf16),
            shape((chips, 8, span), bf16),
            shape(terms.shape, bf16),
        ),
        in_specs=[pl.BlockSpec(memory_space=SM)]
        + [pl.BlockSpec(memory_space=VM)] * 9
        + [pl.BlockSpec(memory_space=pltpu.HBM)],
        out_specs=[pl.BlockSpec(memory_space=VM)] * 3 + [pl.BlockSpec(memory_space=pltpu.HBM)],
        scratch_shapes=[VM((chips * share, width), bf16), pltpu.SemaphoreType.DMA],
        input_output_aliases={10: 3},
        compiler_params=pltpu.CompilerParams(vmem_limit_bytes=40 * 1024 * 1024),
        cost_estimate=pl.CostEstimate(
            flops=2 * tokens * chips * share * width, bytes_accessed=16 * tokens * width, transcendentals=0
        ),
        name="branch_back",
    )(table, resid, g_a, g_b, part, got_a, got_b, vectors, fc_sums, attn_in, terms)


def attention_back_kernel(count, table, branch, tails, *refs):
    pieces, (sent, w_out, sem) = refs[:count], refs[count:]
    chips, size, span = sent.shape
    size -= 8
    rows = span // 2
    share = w_out.shape[0] // chips

    def targets(chip):
        return [(pl.ds(0, share), w_out.at[rows_at(chip, share)])]

    load_rows(table, pieces, targets, sem, False)
    sent[:, size:, :] = tails[...]
    load_rows(table, pieces, targets, sem, True)
    grads = dot_nt(w_out[...], branch[...]).astype(jnp.bfloat16)
    for chip in range(chips):
        micro, head = divmod(chip, chips // 2)
        for rel in range(2):
            column = (rel * 2 + micro) * rows
            sent[chip, :size, rel * rows : (rel + 1) * rows] = grads[
                head * size : (head + 1) * size, column : column + rows
            ]


def attention_back(table, branch, tails, pieces, share, size):
    tokens, width = branch.shape
    chips, _, span = tails.shape
    bf16 = jnp.bfloat16
    return pl.pallas_call(
        functools.partial(attention_back_kernel, len(pieces)),
        out_shape=jax.ShapeDtypeStruct((chips, size + 8, span), bf16),
        in_specs=[pl.BlockSpec(memory_space=SM)]
        + [pl.BlockSpec(memory_space=VM)] * 2
        + [pl.BlockSpec(memory_space=pltpu.HBM)] * len(pieces),
        out_specs=pl.BlockSpec(memory_space=VM),
        scratch_shapes=[VM((chips * share, width), bf16), pltpu.SemaphoreType.DMA],
        compiler_params=pltpu.CompilerParams(vmem_limit_bytes=58 * 1024 * 1024),
        cost_estimate=pl.CostEstimate(
            flops=2 * tokens * chips * share * width, bytes_accessed=4 * tokens * width, transcendentals=0
        ),
        name="attention_back",
    )(table, branch, tails, *pieces)


def finish_kernel(order, got, weights, kept, sent, weight, grads, sem):
    chips, _, span = got.shape
    size = weight.shape[0] // len(order)
    rows = span // 2
    own = kept.shape[0]

    def copies():
        return [
            pltpu.make_async_copy(weights.at[slot], weight.at[pl.ds(head * size, size)], sem)
            for slot, head in enumerate(order)
        ]

    for copy in copies():
        copy.start()
    for chip in range(chips):
        micro, head = divmod(chip, chips // 2)
        turned = got[chip, :size, :].astype(jnp.float32).T.astype(jnp.bfloat16)
        for rel in range(2):
            row = (rel * 2 + micro) * rows
            grads[head, row : row + rows, :] = turned[rel * rows : (rel + 1) * rows]
    for copy in copies():
        copy.wait()
    left = jnp.concatenate([grads[head] for head in range(len(order))], axis=1)
    back = dot_nn(left, weight[...])
    kept[...] = back[:own]
    sent[...] = back[own:].astype(jnp.bfloat16)


def finish(got, weights, order):
    chips, _, span = got.shape
    heads, size, width = weights.shape
    bf16 = jnp.bfloat16
    return pl.pallas_call(
        functools.partial(finish_kernel, order),
        out_shape=(
            jax.ShapeDtypeStruct((span, width), jnp.float32),
            jax.ShapeDtypeStruct((span, width), bf16),
        ),
        in_specs=[pl.BlockSpec(memory_space=VM), pl.BlockSpec(memory_space=pltpu.HBM)],
        out_specs=[pl.BlockSpec(memory_space=VM)] * 2,
        scratch_shapes=[
            VM((heads * size, width), bf16),
            VM((heads, 2 * span, size), bf16),
            pltpu.SemaphoreType.DMA,
        ],
        compiler_params=pltpu.CompilerParams(vmem_limit_bytes=58 * 1024 * 1024),
        cost_estimate=pl.CostEstimate(
            flops=4 * span * width * heads * size,
            bytes_accessed=2 * width * heads * size + 8 * span * width,
            transcendentals=0,
        ),
        name="finish",
    )(got, weights)


def unpack_kernel(share, core_ref, summed, given, proj, out, merged):
    f32 = jnp.float32
    core = core_ref[0]
    folds, _, width = given.shape
    each = proj.shape[0]
    proj[...] = summed[:each, :].astype(f32)
    out[...] = summed[each : each + share, :].astype(f32)
    group = each
    for fold in range(folds):
        first = pl.multiple_of(each + share + (fold * 2 + core) * share, share)
        for owner, rows in ((core, summed[pl.ds(first, share), :]), (1 - core, given[fold])):
            rows = rows.astype(f32)
            for index in range(width // group):
                number = fold * (width // group) + index
                place = ((number // 2 * 2 + owner) * 2 + number % 2) * group
                merged[:, pl.ds(pl.multiple_of(place, group), group)] = rows[:, index * group : (index + 1) * group]


def unpack(core, summed, given, share, each):
    folds, _, width = given.shape
    f32 = jnp.float32
    return pl.pallas_call(
        functools.partial(unpack_kernel, share),
        out_shape=(
            jax.ShapeDtypeStruct((each, width), f32),
            jax.ShapeDtypeStruct((share, width), f32),
            jax.ShapeDtypeStruct((share, 2 * folds * width), f32),
        ),
        in_specs=[pl.BlockSpec(memory_space=SM)] + [pl.BlockSpec(memory_space=VM)] * 2,
        out_specs=[pl.BlockSpec(memory_space=VM)] * 3,
        cost_estimate=pl.CostEstimate(flops=0, bytes_accessed=6 * summed.size, transcendentals=0),
        name="unpack",
    )(core, summed, given)


PATHS = (("x", "z", "head"), ("head", "z", "x"))


PAIR = [(0, 1), (1, 0)]
NEAR = [(0, 1), (1, 0), (2, 3), (3, 2)]
FAR = [(0, 2), (2, 0), (1, 3), (3, 1)]


def swap(values, axis, pairs=PAIR):
    return lax.ppermute(values, axis, pairs)


def across(values, axis):
    return swap(values, axis, NEAR if axis == "z" else PAIR)


def in_order(mine, other, index, axis):
    first = jnp.where(index == 0, mine, other)
    second = jnp.where(index == 0, other, mine)
    return jnp.stack([first, second], axis=axis)


def split_float(values):
    high = values.astype(jnp.bfloat16)
    low = (values - high.astype(jnp.float32)).astype(jnp.bfloat16)
    return high, low


def run_table(order, pair_start):
    pairs = order.shape[0]
    runs = jnp.arange(2 * pairs, dtype=jnp.int32)[:, None]
    low = jnp.where(runs == order[None, :], pair_start[None, :], 0)
    high = jnp.where(runs == 2 * pairs - 1 - order[None, :], pair_start[None, :] + 1, 0)
    return jnp.sum(low + high, axis=1).astype(jnp.int32)


def ring_order(count, turn):
    half = [(z, (z + step + turn) % 2) for z in range(count) for step in range(2)]
    return [z * 4 + y for z, y in half] + [z * 4 + 2 + y for z, y in reversed(half)]


def core_groups(rings):
    return [[(chip // 2 * 2 + core) * 2 + chip % 2 for chip in ring] for core, ring in enumerate(rings)]


def cube_orders(depth):
    cycle = [0, 1, 3, 2, 6, 7, 5, 4]
    return [[chip + start for chip in cycle] for start in (0, 4 * depth)]


def fast_body(
    block_input,
    qkv_weight,
    q_bias,
    v_bias,
    out_weight,
    out_bias,
    norm1_gain,
    norm1_shift,
    norm2_gain,
    norm2_shift,
    fc_weight,
    fc_bias,
    proj_weight,
    proj_bias,
    out_grad,
    dealt,
    lengths,
):
    f32, bf16 = jnp.float32, jnp.bfloat16
    micro, rows, width = block_input.shape
    nz, nx = lax.axis_size("z"), lax.axis_size("x")
    iz, ix, ic, iy = (lax.axis_index(name) for name in ("z", "x", "core", "head"))
    zx = nz * nx
    every, chips = ("z", "x", "core", "head"), ("z", "x", "head")
    devices, chip_count = 4 * zx, 2 * zx
    heads = 2 * zx
    local = heads * DH // 2
    share = qkv_weight.shape[0]
    hidden_share = proj_weight.shape[0]
    hidden_half = hidden_share * chip_count

    inputs = block_input.astype(f32)
    normed_one, inverse_one = normalize(inputs)
    n1 = normed_one.astype(bf16)
    n1, qkv_weight, fc_weight, norm1_gain, norm2_gain = lax.optimization_barrier(
        (n1, qkv_weight, fc_weight, norm1_gain, norm2_gain)
    )
    gain_one = norm1_gain.astype(f32)
    shift_one = norm1_shift.astype(f32)
    raw_qkv = qkv_weight.astype(f32)
    scaled_qkv = (raw_qkv * gain_one[:, None]).astype(bf16)
    device = ((iz * nx + ix) * 2 + ic) * 2 + iy
    offset = jnp.sum(raw_qkv * shift_one[:, None], axis=0)
    zero = jnp.zeros((width,), f32)
    place = device * share
    offset = offset + jnp.concatenate(
        [
            lax.dynamic_update_slice(zero, q_bias.astype(f32), (place,)),
            zero,
            lax.dynamic_update_slice(zero, v_bias.astype(f32), (place,)),
        ]
    )
    high, low = split_float(offset)
    to_heads = jnp.concatenate([scaled_qkv, high[None], low[None], jnp.zeros((6, 3 * width), bf16)], axis=0)
    to_heads = to_heads.reshape(share + 8, 3, zx // 2, 2, 2, DH).transpose(2, 4, 3, 0, 1, 5)
    to_heads = to_heads.reshape(1, heads, share + 8, 3 * DH)
    to_heads = jnp.broadcast_to(to_heads, (2, heads, share + 8, 3 * DH)).reshape(devices, share + 8, 3 * DH)
    head_rows = lax.all_to_all(to_heads, every, split_axis=0, concat_axis=0, tiled=True)
    head_weight = head_rows[:, :share].reshape(width, 3 * DH)
    head_offset = jnp.sum(head_rows[:, share : share + 2].astype(f32), axis=(0, 1))

    mine = iz // 2
    near = lax.dynamic_index_in_dim(n1, mine, 0, keepdims=False)
    far = swap(lax.dynamic_index_in_dim(n1, 1 - mine, 0, keepdims=False), "z", FAR)
    paths = PATHS
    got = across(near, paths[0][0])
    far, got = lax.optimization_barrier((far, got))
    near = jnp.stack([near, got])
    near_got, far_got = across(near, paths[0][1]), across(far, paths[1][0])
    near_got, far_got = lax.optimization_barrier((near_got, far_got))
    near, far = jnp.stack([near, near_got]), jnp.stack([far, far_got])
    near_got, far_got = across(near, paths[0][2]), across(far, paths[1][1])
    far = jnp.stack([far, far_got])
    parts = [near, near_got, far, across(far, paths[1][2])]
    pieces, owners = [], []

    def add_all(flip):
        core = 1 - ic if flip else ic
        for index, part in enumerate(parts):
            pieces.append((swap(part, "core") if flip else part).reshape(-1, width))
            for second in range(2):
                for first in range(2):
                    flips = dict(zip(paths[index // 2], (first, second, index % 2)))
                    owners.append((iz ^ flips["z"] ^ (index // 2 * 2), ix ^ flips["x"], core, iy ^ flips["head"]))

    add_all(False)
    add_all(True)
    slot_device = jnp.stack([((z * nx + x) * 2 + core) * 2 + y for z, x, core, y in owners]).astype(jnp.int32)
    my_dealt = lax.dynamic_index_in_dim(dealt, mine, 0, keepdims=False)
    order = my_dealt.reshape(devices, rows)[:, 0] // RUN
    slot_of = jnp.sum(
        jnp.where(jnp.arange(devices)[:, None] == slot_device[None, :], jnp.arange(devices)[None, :], 0), axis=1
    )
    inloc = run_table(order, (slot_of * 2).astype(jnp.int32))
    ids = jnp.arange(devices, dtype=jnp.int32)
    id_y, id_c, id_zx = ids % 2, ids // 2 % 2, ids // 4
    send_pair = (id_zx * 2 + id_y) * 2 + (id_c ^ ic)
    outloc = run_table(order, (send_pair * 2).astype(jnp.int32))
    bound = lax.dynamic_index_in_dim(lengths, mine, 0, keepdims=False)[:1]

    fc_parts = fc_weight.reshape(share, zx, 2, 2, hidden_share)

    def core_columns(values, index):
        return lax.dynamic_index_in_dim(values, index, 2, keepdims=False)

    fc_mine = core_columns(fc_parts, ic).reshape(share, hidden_half)
    fc_other = swap(core_columns(fc_parts, 1 - ic).reshape(share, hidden_half), "core")
    fc_pair = in_order(fc_mine, fc_other, ic, 0).reshape(2 * share, hidden_half)
    small = jnp.stack([norm2_gain, norm2_shift, out_bias, proj_bias])
    small_rows = jnp.zeros((16, width), bf16)
    small_rows = lax.dynamic_update_slice(small_rows, small, (0, place))
    other_place = (((iz * nx + ix) * 2 + 1 - ic) * 2 + iy) * share
    small_rows = lax.dynamic_update_slice(small_rows, swap(small, "core"), (0, other_place))
    fc_place = ((iz * nx + ix) * 2 + iy) * hidden_share
    small_rows = lax.dynamic_update_slice(small_rows, fc_bias[None], (8 + fc_place // width, fc_place % width))
    folds = hidden_half // width
    fc_folded = fc_pair.reshape(2 * share, folds, width).transpose(1, 0, 2).reshape(-1, width)
    packed = jnp.concatenate([out_weight, proj_weight, fc_folded, small_rows], axis=0)
    rings = [ring_order(nz, turn) for turn in range(2)]
    places = [[ring.index(chip) for chip in range(chip_count)] for ring in rings]
    table = lax.dynamic_index_in_dim(
        jnp.array([[ring, place] for ring, place in zip(rings, places)], jnp.int32), ic, 0, keepdims=False
    )
    gathered = lax.all_gather(packed, every, axis=0, axis_index_groups=core_groups(rings))
    out_rows = share
    proj_rows = hidden_share
    fc_rows = 2 * share * folds

    mixed = [(product(piece, head_weight) + head_offset).astype(bf16) for piece in pieces]
    slots = jnp.concatenate(mixed, axis=0)
    attn_send, queries, keys, values, attn_t, lse = attend_forward(bound, inloc, outloc, slots, chip_count, DH)

    x_a, x_b = block_input.reshape(-1, width), swap(block_input, "core").reshape(-1, width)
    g_a, g_b = out_grad.reshape(-1, width), swap(out_grad, "core").reshape(-1, width)
    attn_got = lax.all_to_all(attn_send, chips, split_axis=0, concat_axis=0, tiled=True)
    weight_turned, attn_got = lax.optimization_barrier((head_weight.T, attn_got))
    cubes = cube_orders(nz // 2)
    w_qkv = lax.all_gather(weight_turned, chips, axis=0, axis_index_groups=cubes)
    part, sent_a, sent_b, attn_in = project(table, attn_got, [gathered], share)
    resid, base, project_other, grad_part, back_a, back_b, fc_sums, vectors, terms = middle(
        table, x_a, x_b, g_a, g_b, part, swap(sent_b, "core"), swap(sent_a, "core"), [gathered], share, hidden_half
    )
    grad_resid, branch, tails, terms = branch_back(
        table,
        resid,
        g_a,
        g_b,
        grad_part,
        swap(back_b, "core"),
        swap(back_a, "core"),
        vectors,
        fc_sums,
        attn_in,
        terms,
        share,
        proj_rows,
        2 * rows,
    )
    grad_send = attention_back(table, branch, tails, [gathered], share, DH)
    output = (base + swap(project_other, "core").astype(f32)).astype(bf16)

    grad_got = lax.all_to_all(grad_send, chips, split_axis=0, concat_axis=0, tiled=True)
    vector_sums = jnp.sum(grad_got[:, DH:].astype(f32), axis=0)
    vector_sums = vector_sums[:, :rows] + vector_sums[:, rows:]
    final_vectors = lax.dynamic_slice(vector_sums, (0, (ic * 2 + iy) * share), (4, share))
    final_fc_b = vector_sums[4]

    summed = lax.psum_scatter(
        terms, every, scatter_dimension=0, tiled=True, axis_index_groups=core_groups(rings)
    )[0]
    fc_sum = summed[proj_rows + out_rows :].reshape(folds, 2, share, width)
    fc_give = swap(lax.dynamic_index_in_dim(fc_sum, 1 - ic, 1, keepdims=False), "core")
    final_proj_w, final_out_w, final_fc_w = unpack(
        ic.astype(jnp.int32).reshape(1), summed, fc_give, share, hidden_share
    )

    send_grads = attend_backward(
        bound, inloc, outloc, grad_got, queries, keys, values, attn_t, lse, pieces, share
    )
    grads_got = lax.all_to_all(send_grads, chips, split_axis=0, concat_axis=0, tiled=True)
    back_own, back_other = finish(grads_got, w_qkv, cubes[0])
    raw_got = grads_got[:, 3 * DH :, : 3 * DH].astype(f32)
    raw_sum = jnp.sum(raw_got.reshape(2, zx, 2 * share + 16, 3 * DH), axis=0)
    raw_parts = raw_sum[:, : 2 * share].reshape(zx, 2, share, 3 * DH)
    sums_mine = raw_sum[:, 2 * share : 2 * share + 1] + raw_sum[:, 2 * share + 1 : 2 * share + 2]
    raw_keep = jnp.concatenate([lax.dynamic_index_in_dim(raw_parts, ic, 1, keepdims=False), sums_mine], axis=1)
    raw_give = jnp.concatenate([lax.dynamic_index_in_dim(raw_parts, 1 - ic, 1, keepdims=False), sums_mine], axis=1)
    raw_all = in_order(raw_keep, swap(raw_give, "core"), ic, 1).reshape(heads, share + 1, 3, DH)
    raw_all = raw_all.transpose(1, 2, 0, 3).reshape(share + 1, 3 * width)
    raw_grad, all_sums = raw_all[:share], raw_all[share]
    final_qkv_w = raw_grad * gain_one[:, None] + shift_one[:, None] * all_sums[None, :]
    final_gain_one = jnp.sum(raw_grad * raw_qkv, axis=1)
    final_shift_one = jnp.sum(raw_qkv * all_sums[None, :], axis=1)
    final_q_b = lax.dynamic_slice(all_sums, (place,), (share,))
    final_v_b = lax.dynamic_slice(all_sums, (2 * width + place,), (share,))

    back_own = back_own + swap(back_other, "core").astype(f32)
    back_own = back_own.reshape(micro, rows, width)
    input_grad = grad_resid.reshape(micro, rows, width) + norm_back(back_own, normed_one, inverse_one)

    return (
        output.reshape(micro, rows, width),
        input_grad.astype(bf16),
        final_qkv_w,
        final_q_b,
        final_v_b,
        final_out_w,
        final_vectors[2],
        final_gain_one,
        final_shift_one,
        final_vectors[0],
        final_vectors[1],
        final_fc_w,
        final_fc_b,
        final_proj_w,
        final_vectors[3],
    )


def specs(names):
    rows, vector, tokens = P(names, None), P(names), P(None, names, None)
    weights = (rows, vector, vector, rows, vector, vector, vector, vector, vector, rows, vector, rows, vector)
    return (tokens, *weights, tokens, P(), P()), (tokens, tokens, *weights)


def solution(mesh):
    sizes = dict(mesh.shape)
    if sizes["head"] == 2 and sizes["blk"] == 16:
        fine = Mesh(mesh.devices.reshape(2, 4, 2, 2), ("head", "z", "x", "core"))
        given, made = specs(("z", "x", "core", "head"))
        return jax.shard_map(fast_body, mesh=fine, in_specs=given, out_specs=made, check_vma=False)
    given, made = specs(("blk", "head"))
    return jax.shard_map(general_body, mesh=mesh, in_specs=given, out_specs=made, check_vma=False)
```

```python
import functools
import math

import jax
import jax.numpy as jnp
from jax import lax
from jax.experimental import pallas as pl
from jax.experimental.pallas import tpu as pltpu
from jax.sharding import Mesh
from jax.sharding import PartitionSpec as P

DH = 64


def gelu_tanh(values):
    inner = 0.7978845608028654 * (values + 0.044715 * values * values * values)
    return 0.5 * values * (1.0 + jnp.tanh(inner))


def normalize(values):
    centred = values - jnp.mean(values, axis=-1, keepdims=True)
    inverse = lax.rsqrt(jnp.mean(centred * centred, axis=-1, keepdims=True) + 1e-05)
    return (centred * inverse, inverse)


def norm_back(grad_normed, normed, inverse):
    return inverse * (
        grad_normed
        - jnp.mean(grad_normed, axis=-1, keepdims=True)
        - normed * jnp.mean(grad_normed * normed, axis=-1, keepdims=True)
    )


def product(left, right):
    return jnp.dot(left, right, preferred_element_type=jnp.float32)


def product_tn(left, right):
    return lax.dot_general(
        left, right, (((0,), (0,)), ((), ())), preferred_element_type=jnp.float32
    )


def product_nt(left, right):
    return lax.dot_general(
        left, right, (((1,), (1,)), ((), ())), preferred_element_type=jnp.float32
    )


def visible_pairs(query_pos, key_pos, boundary):
    same_side = (query_pos[:, None] >= boundary) == (key_pos[None, :] >= boundary)
    return same_side & (key_pos[None, :] <= query_pos[:, None])


def forward_tile(current, queries3, keys3, values3, visible, scale):
    running, total, accum = current
    scores = jnp.einsum("qhd,khd->hqk", queries3, keys3, preferred_element_type=jnp.float32) * scale
    scores = jnp.where(visible[None], scores, -1000000000.0)
    highest = jnp.maximum(running, jnp.max(scores, axis=-1))
    weights = jnp.where(visible[None], jnp.exp(scores - highest[..., None]), 0.0)
    factor = jnp.exp(running - highest)
    total = total * factor + jnp.sum(weights, axis=-1)
    accum = accum * factor[..., None] + jnp.einsum(
        "hqk,khd->hqd", weights.astype(jnp.bfloat16), values3, preferred_element_type=jnp.float32
    )
    return (highest, total, accum)


def general_forward(query_parts, pos_parts, positions, boundary, keys_group, values_group, key_span):
    heads_local, head_size = (query_parts[0].shape[1], query_parts[0].shape[2])
    scale = head_size ** (-0.5)

    def fold_keys(state, pieces, start):
        key_rows, value_rows = pieces
        count_rows = key_rows.shape[0]
        block_rows = math.gcd(count_rows, key_span)
        block_count = count_rows // block_rows

        def one_step(index, inner):
            offset = index * block_rows
            keys3 = lax.dynamic_slice_in_dim(key_rows, offset, block_rows).reshape(
                block_rows, heads_local, head_size
            )
            values3 = lax.dynamic_slice_in_dim(value_rows, offset, block_rows).reshape(
                block_rows, heads_local, head_size
            )
            key_pos = lax.dynamic_slice_in_dim(positions, offset, block_rows)
            part_queries = query_parts[0]
            visible = visible_pairs(pos_parts[0], key_pos, boundary)
            current = inner[0]
            result = forward_tile(current, part_queries, keys3, values3, visible, scale)
            updated = [result]
            return tuple(updated)

        return lax.fori_loop(0, block_count, one_step, state)

    initial = tuple(
        (
            (
                jnp.full((heads_local, part.shape[0]), -1000000000.0, jnp.float32),
                jnp.zeros((heads_local, part.shape[0]), jnp.float32),
                jnp.zeros((heads_local, part.shape[0], head_size), jnp.float32),
            )
            for part in query_parts
        )
    )
    return fold_keys(
        initial,
        (
            lax.all_gather(keys_group, "blk", axis=0, tiled=True),
            lax.all_gather(values_group, "blk", axis=0, tiled=True),
        ),
        jnp.int32(0),
    )


def backward_tile(current, queries3, grad3, log_total, delta, keys3, values3, visible, scale):
    grad_query, term = current
    scores = jnp.einsum("qhd,khd->hqk", queries3, keys3, preferred_element_type=jnp.float32) * scale
    scores = jnp.where(visible[None], scores, -1000000000.0)
    exact = jnp.where(visible[None], jnp.exp(scores - log_total[..., None]), 0.0)
    grad_probs = jnp.einsum("qhd,khd->hqk", grad3, values3, preferred_element_type=jnp.float32)
    grad_scores = (exact * (grad_probs - delta[..., None])).astype(jnp.bfloat16)
    grad_query = (
        grad_query
        + jnp.einsum("hqk,khd->hqd", grad_scores, keys3, preferred_element_type=jnp.float32) * scale
    )
    rounded = exact.astype(jnp.bfloat16)
    grad_values = jnp.einsum("hqk,qhd->khd", rounded, grad3, preferred_element_type=jnp.float32)
    grad_keys = (
        jnp.einsum("hqk,qhd->khd", grad_scores, queries3, preferred_element_type=jnp.float32)
        * scale
    )
    rows = keys3.shape[0]
    term = jnp.stack([grad_keys.reshape(rows, -1), grad_values.reshape(rows, -1)], axis=1)
    return (grad_query, term)


def general_backward(
    query_parts,
    grad_parts,
    total_parts,
    delta_parts,
    pos_parts,
    positions,
    boundary,
    keys_group,
    values_group,
    key_span,
    buffer_rows,
):
    heads_local, head_size = (query_parts[0].shape[1], query_parts[0].shape[2])
    scale = head_size ** (-0.5)

    def fold_keys(state, pieces, start):
        key_rows, value_rows = pieces
        count_rows = key_rows.shape[0]
        block_rows = math.gcd(count_rows, key_span)
        block_count = count_rows // block_rows

        def one_step(index, inner):
            offset = index * block_rows
            keys3 = lax.dynamic_slice_in_dim(key_rows, offset, block_rows).reshape(
                block_rows, heads_local, head_size
            )
            values3 = lax.dynamic_slice_in_dim(value_rows, offset, block_rows).reshape(
                block_rows, heads_local, head_size
            )
            key_pos = lax.dynamic_slice_in_dim(positions, offset, block_rows)
            grads_now, buffer = inner
            term = jnp.zeros((block_rows, 2, heads_local * head_size), jnp.float32)
            part_queries = query_parts[0]
            part_grads = grad_parts[0]
            part_total = total_parts[0]
            part_delta = delta_parts[0]
            visible = visible_pairs(pos_parts[0], key_pos, boundary)
            current = (grads_now[0], term)
            result = backward_tile(
                current,
                part_queries,
                part_grads,
                part_total,
                part_delta,
                keys3,
                values3,
                visible,
                scale,
            )
            updated = [result[0]]
            term = result[1]
            buffer = lax.dynamic_update_slice(buffer, term, (offset, 0, 0))
            return (tuple(updated), buffer)

        return lax.fori_loop(0, block_count, one_step, state)

    grads_init = tuple(
        (jnp.zeros((heads_local, part.shape[0], head_size), jnp.float32) for part in query_parts)
    )
    initial = (grads_init, jnp.zeros((buffer_rows, 2, heads_local * head_size), jnp.float32))
    return fold_keys(
        initial,
        (
            lax.all_gather(keys_group, "blk", axis=0, tiled=True),
            lax.all_gather(values_group, "blk", axis=0, tiled=True),
        ),
        jnp.int32(0),
    )


def general_body(
    block_input,
    qkv_weight,
    q_bias,
    v_bias,
    out_weight,
    out_bias,
    norm1_gain,
    norm1_shift,
    norm2_gain,
    norm2_shift,
    fc_weight,
    fc_bias,
    proj_weight,
    proj_bias,
    out_grad,
    dealt,
    lengths,
):
    micro_count, local_rows, width = block_input.shape
    head_devices = lax.axis_size("head")
    blk_devices = lax.axis_size("blk")
    group = local_rows * head_devices
    blk_index = lax.axis_index("blk")
    head_size = DH
    key_span = 1024
    part_count = group // group
    shards = (
        qkv_weight,
        q_bias,
        v_bias,
        out_weight,
        out_bias,
        norm1_gain,
        norm1_shift,
        norm2_gain,
        norm2_shift,
        fc_weight,
        fc_bias,
        proj_weight,
        proj_bias,
    )
    totals = [
        jnp.zeros((shard.shape[0] * blk_devices * head_devices,) + shard.shape[1:], jnp.float32)
        for shard in shards
    ]
    outputs = []
    input_grads = []
    for micro_index in range(micro_count):
        whole = (
            lax.all_gather(shards[0], ("blk", "head"), axis=0, tiled=True),
            lax.all_gather(shards[1], ("blk", "head"), axis=0, tiled=True),
            lax.all_gather(shards[2], ("blk", "head"), axis=0, tiled=True),
            lax.all_gather(shards[3], ("blk", "head"), axis=0, tiled=True),
            lax.all_gather(shards[4], ("blk", "head"), axis=0, tiled=True),
            lax.all_gather(shards[5], ("blk", "head"), axis=0, tiled=True),
            lax.all_gather(shards[6], ("blk", "head"), axis=0, tiled=True),
            lax.all_gather(shards[7], ("blk", "head"), axis=0, tiled=True),
            lax.all_gather(shards[8], ("blk", "head"), axis=0, tiled=True),
            lax.all_gather(shards[9], ("blk", "head"), axis=0, tiled=True),
            lax.all_gather(shards[10], ("blk", "head"), axis=0, tiled=True),
            lax.all_gather(shards[11], ("blk", "head"), axis=0, tiled=True),
            lax.all_gather(shards[12], ("blk", "head"), axis=0, tiled=True),
        )
        (
            w_qkv,
            b_query,
            b_value,
            w_out,
            b_out,
            gain_one,
            shift_one,
            gain_two,
            shift_two,
            w_fc,
            b_fc,
            w_proj,
            b_proj,
        ) = whole
        b_query = b_query.astype(jnp.float32)
        b_value = b_value.astype(jnp.float32)
        b_out = b_out.astype(jnp.float32)
        gain_one = gain_one.astype(jnp.float32)
        shift_one = shift_one.astype(jnp.float32)
        gain_two = gain_two.astype(jnp.float32)
        shift_two = shift_two.astype(jnp.float32)
        b_fc = b_fc.astype(jnp.float32)
        b_proj = b_proj.astype(jnp.float32)
        positions = dealt[micro_index]
        boundary = lengths[micro_index, 0]
        query_pos = lax.dynamic_slice_in_dim(positions, blk_index * group, group)
        inputs = block_input[micro_index].astype(jnp.float32)
        normed_one, inverse_one = normalize(inputs)
        act_one = (normed_one * gain_one + shift_one).astype(jnp.bfloat16)
        mixed = product(act_one, w_qkv)
        queries = (mixed[:, :width] + b_query).astype(jnp.bfloat16)
        keys = mixed[:, width : 2 * width].astype(jnp.bfloat16)
        values = (mixed[:, 2 * width :] + b_value).astype(jnp.bfloat16)
        heads_in = lax.all_to_all(
            jnp.stack([queries, keys, values], axis=1),
            "head",
            split_axis=2,
            concat_axis=0,
            tiled=True,
        )
        local_width = heads_in.shape[2]
        heads_local = local_width // head_size
        queries3 = heads_in[:, 0].reshape(group, heads_local, head_size)
        keys_group = heads_in[:, 1]
        values_group = heads_in[:, 2]
        query_parts = tuple((queries3 for index in range(part_count)))
        pos_parts = tuple((query_pos for index in range(part_count)))
        states = general_forward(
            query_parts, pos_parts, positions, boundary, keys_group, values_group, key_span
        )
        running = jnp.concatenate([state[0] for state in states], axis=1)
        total = jnp.concatenate([state[1] for state in states], axis=1)
        accum = jnp.concatenate([state[2] for state in states], axis=1)
        log_total = running + jnp.log(total)
        attn_heads = (
            (accum / total[..., None])
            .transpose(1, 0, 2)
            .reshape(group, local_width)
            .astype(jnp.bfloat16)
        )
        attended = lax.all_to_all(attn_heads, "head", split_axis=0, concat_axis=1, tiled=True)
        resid = inputs + product(attended, w_out) + b_out
        normed_two, inverse_two = normalize(resid)
        act_two = (normed_two * gain_two + shift_two).astype(jnp.bfloat16)
        pre = product(act_two, w_fc) + b_fc
        hidden = gelu_tanh(pre).astype(jnp.bfloat16)
        outputs.append((resid + product(hidden, w_proj) + b_proj).astype(jnp.bfloat16))
        cotangent = out_grad[micro_index]
        grad_proj_w = product_tn(hidden, cotangent)
        grad_proj_b = jnp.sum(cotangent.astype(jnp.float32), axis=0)
        grad_hidden = product_nt(cotangent, w_proj)
        grad_pre = jax.vjp(gelu_tanh, pre)[1](grad_hidden)[0].astype(jnp.bfloat16)
        grad_fc_w = product_tn(act_two, grad_pre)
        grad_fc_b = jnp.sum(grad_pre.astype(jnp.float32), axis=0)
        grad_act_two = product_nt(grad_pre, w_fc)
        grad_gain_two = jnp.sum(grad_act_two * normed_two, axis=0)
        grad_shift_two = jnp.sum(grad_act_two, axis=0)
        grad_resid = cotangent.astype(jnp.float32) + norm_back(
            grad_act_two * gain_two, normed_two, inverse_two
        )
        grad_branch = grad_resid.astype(jnp.bfloat16)
        grad_out_w = product_tn(attended, grad_branch)
        grad_out_b = jnp.sum(grad_branch.astype(jnp.float32), axis=0)
        grad_attn = product_nt(grad_branch, w_out).astype(jnp.bfloat16)
        grad_heads = lax.all_to_all(grad_attn, "head", split_axis=1, concat_axis=0, tiled=True)
        grad3 = grad_heads.reshape(group, heads_local, head_size)
        attn3 = attn_heads.reshape(group, heads_local, head_size)
        delta = jnp.sum(grad3.astype(jnp.float32) * attn3.astype(jnp.float32), axis=-1).T
        grad_parts = tuple((grad3 for index in range(part_count)))
        total_parts = tuple((log_total for index in range(part_count)))
        delta_parts = tuple((delta for index in range(part_count)))
        query_grads, buffer = general_backward(
            query_parts,
            grad_parts,
            total_parts,
            delta_parts,
            pos_parts,
            positions,
            boundary,
            keys_group,
            values_group,
            key_span,
            group * blk_devices,
        )
        kv_sums = lax.psum_scatter(buffer, "blk", scatter_dimension=0, tiled=True)
        grad_k_heads = kv_sums[:, 0].astype(jnp.bfloat16)
        grad_v_heads = kv_sums[:, 1].astype(jnp.bfloat16)
        grad_query = jnp.concatenate(list(query_grads), axis=1)
        grad_q_heads = (
            grad_query.transpose(1, 0, 2).reshape(group, local_width).astype(jnp.bfloat16)
        )
        grads_heads = jnp.stack([grad_q_heads, grad_k_heads, grad_v_heads], axis=1)
        back_tokens = lax.all_to_all(grads_heads, "head", split_axis=0, concat_axis=2, tiled=True)
        grad_mixed = back_tokens.reshape(local_rows, 3 * width)
        grad_qkv_w = product_tn(act_one, grad_mixed)
        grad_q_b = jnp.sum(back_tokens[:, 0].astype(jnp.float32), axis=0)
        grad_v_b = jnp.sum(back_tokens[:, 2].astype(jnp.float32), axis=0)
        grad_act_one = product_nt(grad_mixed, w_qkv)
        grad_gain_one = jnp.sum(grad_act_one * normed_one, axis=0)
        grad_shift_one = jnp.sum(grad_act_one, axis=0)
        input_grads.append(
            (grad_resid + norm_back(grad_act_one * gain_one, normed_one, inverse_one)).astype(
                jnp.bfloat16
            )
        )
        terms = (
            grad_qkv_w,
            grad_q_b,
            grad_v_b,
            grad_out_w,
            grad_out_b,
            grad_gain_one,
            grad_shift_one,
            grad_gain_two,
            grad_shift_two,
            grad_fc_w,
            grad_fc_b,
            grad_proj_w,
            grad_proj_b,
        )
        totals = [running_sum + term for running_sum, term in zip(totals, terms)]
    final = (
        lax.psum_scatter(totals[0], ("blk", "head"), scatter_dimension=0, tiled=True),
        lax.psum_scatter(totals[1], ("blk", "head"), scatter_dimension=0, tiled=True),
        lax.psum_scatter(totals[2], ("blk", "head"), scatter_dimension=0, tiled=True),
        lax.psum_scatter(totals[3], ("blk", "head"), scatter_dimension=0, tiled=True),
        lax.psum_scatter(totals[4], ("blk", "head"), scatter_dimension=0, tiled=True),
        lax.psum_scatter(totals[5], ("blk", "head"), scatter_dimension=0, tiled=True),
        lax.psum_scatter(totals[6], ("blk", "head"), scatter_dimension=0, tiled=True),
        lax.psum_scatter(totals[7], ("blk", "head"), scatter_dimension=0, tiled=True),
        lax.psum_scatter(totals[8], ("blk", "head"), scatter_dimension=0, tiled=True),
        lax.psum_scatter(totals[9], ("blk", "head"), scatter_dimension=0, tiled=True),
        lax.psum_scatter(totals[10], ("blk", "head"), scatter_dimension=0, tiled=True),
        lax.psum_scatter(totals[11], ("blk", "head"), scatter_dimension=0, tiled=True),
        lax.psum_scatter(totals[12], ("blk", "head"), scatter_dimension=0, tiled=True),
    )
    return (
        jnp.stack(outputs),
        jnp.stack(input_grads),
        final[0],
        final[1],
        final[2],
        final[3],
        final[4],
        final[5],
        final[6],
        final[7],
        final[8],
        final[9],
        final[10],
        final[11],
        final[12],
    )


RUN = 64
BLOCK = 512
NEG = -1000000000.0
VM = pltpu.VMEM
SM = pltpu.SMEM


def dot_nt(left, right):
    return lax.dot_general(left, right, (((1,), (1,)), ((), ())), preferred_element_type=jnp.float32)


def dot_nn(left, right):
    return lax.dot_general(left, right, (((1,), (0,)), ((), ())), preferred_element_type=jnp.float32)


def rows_at(index, size):
    return pl.ds(pl.multiple_of(index * size, size), size)


def first_block(start, bound):
    return jnp.where(start >= bound, bound // BLOCK, 0)


def forward_kernel(head_size, bound_ref, inloc, outloc, qkv, out, qs, ks, vs, attn_t, lse, vt, mixed):
    tokens = qkv.shape[0]
    runs = tokens // RUN
    scale = head_size ** (-0.5)
    bound = bound_ref[0]

    @pl.loop(0, runs, unroll=8)
    def _(run):
        rows = qkv[rows_at(inloc[run], RUN), :]
        here = rows_at(run, RUN)
        qs[here, :] = (rows[:, :head_size].astype(jnp.float32) * scale).astype(jnp.bfloat16)
        ks[here, :] = rows[:, head_size : 2 * head_size]
        vs[here, :] = rows[:, 2 * head_size :]

    @pl.loop(0, tokens // BLOCK, unroll=4)
    def _(block):
        here = rows_at(block, BLOCK)
        vt[:, here] = vs[here, :].astype(jnp.float32).T.astype(jnp.bfloat16)

    @pl.loop(0, tokens // BLOCK)
    def _(block):
        start = block * BLOCK
        here = rows_at(block, BLOCK)
        queries = qs[here, :]
        query_pos = start + lax.broadcasted_iota(jnp.int32, (1, BLOCK), 1)
        floor = jnp.where(query_pos >= bound, bound, 0)

        def scores_of(index, diagonal):
            keys = ks[rows_at(index, BLOCK), :]
            scores = dot_nt(keys, queries)
            key_pos = index * BLOCK + lax.broadcasted_iota(jnp.int32, (BLOCK, BLOCK), 0)
            visible = key_pos >= floor
            if diagonal:
                visible = visible & (key_pos <= query_pos)
            return jnp.where(visible, scores, NEG)

        scores = scores_of(block, True)
        highest = jnp.max(scores, axis=0, keepdims=True)
        weights = jnp.exp(scores - highest)
        total = jnp.sum(weights, axis=0, keepdims=True)
        accum = dot_nn(vt[:, here], weights.astype(jnp.bfloat16))

        def step(index, state):
            highest, total, accum = state
            scores = scores_of(index, False)
            higher = jnp.maximum(highest, jnp.max(scores, axis=0, keepdims=True))
            weights = jnp.exp(scores - higher)
            factor = jnp.exp(highest - higher)
            total = total * factor + jnp.sum(weights, axis=0, keepdims=True)
            accum = accum * factor + dot_nn(vt[:, rows_at(index, BLOCK)], weights.astype(jnp.bfloat16))
            return higher, total, accum

        highest, total, accum = lax.fori_loop(first_block(start, bound), block, step, (highest, total, accum))
        result = accum / total
        attn_t[:, here] = result.astype(jnp.bfloat16)
        lse[:, here] = highest + jnp.log(total)
        result = result.T.astype(jnp.bfloat16)
        for part in range(BLOCK // RUN):
            mixed[rows_at(outloc[block * (BLOCK // RUN) + part], RUN), :] = result[part * RUN : (part + 1) * RUN]

    chips, _, span = out.shape

    @pl.loop(0, chips, unroll=8)
    def _(chip):
        out[chip] = mixed[rows_at(chip, span), :].astype(jnp.float32).T.astype(jnp.bfloat16)


def attend_forward(bound, inloc, outloc, qkv, chips, head_size):
    tokens = qkv.shape[0]
    bf16 = jnp.bfloat16
    pairs = tokens * (tokens // 2)
    return pl.pallas_call(
        functools.partial(forward_kernel, head_size),
        out_shape=(
            jax.ShapeDtypeStruct((chips, head_size, tokens // chips), bf16),
            jax.ShapeDtypeStruct((tokens, head_size), bf16),
            jax.ShapeDtypeStruct((tokens, head_size), bf16),
            jax.ShapeDtypeStruct((tokens, head_size), bf16),
            jax.ShapeDtypeStruct((head_size, tokens), bf16),
            jax.ShapeDtypeStruct((1, tokens), jnp.float32),
        ),
        in_specs=[pl.BlockSpec(memory_space=SM)] * 3 + [pl.BlockSpec(memory_space=VM)],
        out_specs=[pl.BlockSpec(memory_space=VM)] * 6,
        scratch_shapes=[VM((head_size, tokens), bf16), VM((tokens, head_size), bf16)],
        compiler_params=pltpu.CompilerParams(vmem_limit_bytes=40 * 1024 * 1024),
        cost_estimate=pl.CostEstimate(flops=4 * 4 * pairs * head_size, bytes_accessed=tokens * 2048, transcendentals=pairs),
        name="attend_forward",
    )(bound, inloc, outloc, qkv)


def backward_kernel(
    head_size, count, share, bound_ref, inloc, outloc, grad_t, qs, ks, vs, attn_t, lse, *refs
):
    pieces = refs[:count]
    send_out, normed, raw, grads, kt, dk, dv, mixed, wide, moved, sem = refs[count:]
    tokens = qs.shape[0]
    runs = tokens // RUN
    scale = head_size ** (-0.5)
    bound = bound_ref[0]
    chips, _, span = grad_t.shape
    copies, filled = [], 0
    for piece in pieces:
        copies.append(pltpu.make_async_copy(piece, normed.at[pl.ds(filled, piece.shape[0])], sem))
        filled += piece.shape[0]
    for copy in copies:
        copy.start()

    @pl.loop(0, chips, unroll=8)
    def _(chip):
        mixed[rows_at(chip, span), :] = grad_t[chip, :head_size, :].astype(jnp.float32).T.astype(jnp.bfloat16)

    @pl.loop(0, runs, unroll=8)
    def _(run):
        grads[rows_at(run, RUN), :] = mixed[rows_at(outloc[run], RUN), :]

    @pl.loop(0, tokens // BLOCK, unroll=4)
    def _(block):
        here = rows_at(block, BLOCK)
        kt[:, here] = ks[here, :].astype(jnp.float32).T.astype(jnp.bfloat16)

    @pl.loop(0, tokens // BLOCK)
    def _(block):
        start = block * BLOCK
        here = rows_at(block, BLOCK)
        queries = qs[here, :]
        grad = grads[here, :]
        log_total = lse[:, here]
        delta = jnp.sum(grad.astype(jnp.float32).T * attn_t[:, here].astype(jnp.float32), axis=0, keepdims=True)
        query_pos = start + lax.broadcasted_iota(jnp.int32, (1, BLOCK), 1)
        floor = jnp.where(query_pos >= bound, bound, 0)

        def one(index, diagonal):
            there = rows_at(index, BLOCK)
            scores = dot_nt(ks[there, :], queries)
            key_pos = index * BLOCK + lax.broadcasted_iota(jnp.int32, (BLOCK, BLOCK), 0)
            visible = key_pos >= floor
            if diagonal:
                visible = visible & (key_pos <= query_pos)
            probs = jnp.where(visible, jnp.exp(scores - log_total), 0.0)
            grad_probs = dot_nt(vs[there, :], grad)
            grad_scores = (probs * (grad_probs - delta)).astype(jnp.bfloat16)
            return (
                dot_nn(probs.astype(jnp.bfloat16), grad),
                dot_nn(grad_scores, queries),
                dot_nn(kt[:, there], grad_scores),
                there,
            )

        grad_v, grad_k, grad_q, there = one(block, True)
        dv[there, :] = grad_v
        dk[there, :] = grad_k

        def step(index, grad_q):
            grad_v, grad_k, term, there = one(index, False)
            dv[there, :] += grad_v
            dk[there, :] += grad_k
            return grad_q + term

        grad_q = lax.fori_loop(first_block(start, bound), block, step, grad_q)
        wide[here, :head_size] = (grad_q.T * scale).astype(jnp.bfloat16)

    wide[:, head_size : 2 * head_size] = dk[...].astype(jnp.bfloat16)
    wide[:, 2 * head_size :] = dv[...].astype(jnp.bfloat16)

    size = 3 * head_size

    @pl.loop(0, runs, unroll=8)
    def _(run):
        moved[rows_at(outloc[run], RUN), :] = wide[rows_at(run, RUN), :]

    @pl.loop(0, chips, unroll=8)
    def _(chip):
        send_out[chip, :size, :] = moved[rows_at(chip, span), :].astype(jnp.float32).T.astype(jnp.bfloat16)

    @pl.loop(0, runs, unroll=8)
    def _(run):
        moved[rows_at(inloc[run], RUN), :] = wide[rows_at(run, RUN), :]

    for copy in copies:
        copy.wait()
    raw[...] = jnp.zeros_like(raw)

    @pl.loop(0, tokens // BLOCK, unroll=2)
    def _(block):
        here = rows_at(block, BLOCK)
        turned = moved[here, :].astype(jnp.float32).T.astype(jnp.bfloat16)
        raw[...] += dot_nn(turned, normed[here, :])

    product = raw[...].T
    sums = jnp.sum(wide[...].astype(jnp.float32), axis=0, keepdims=True)
    high = sums.astype(jnp.bfloat16).astype(jnp.float32)
    tail = jnp.concatenate([high, sums - high, jnp.zeros((14, size), jnp.float32)], axis=0)
    for chip in range(chips):
        first = chip // 2 * 4 * share + chip % 2 * share
        rows = jnp.concatenate([product[first : first + share], product[first + 2 * share : first + 3 * share], tail], axis=0)
        rows = jnp.concatenate([rows, jnp.zeros((rows.shape[0], span - size), jnp.float32)], axis=1)
        send_out[chip, size:, :] = rows.astype(jnp.bfloat16)


def attend_backward(bound, inloc, outloc, grad_t, qs, ks, vs, attn_t, lse, pieces, share):
    tokens, head_size = qs.shape
    chips = grad_t.shape[0]
    width = pieces[0].shape[1]
    bf16 = jnp.bfloat16
    pairs = tokens * (tokens // 2)
    return pl.pallas_call(
        functools.partial(backward_kernel, head_size, len(pieces), share),
        out_shape=jax.ShapeDtypeStruct((chips, 3 * head_size + 2 * share + 16, tokens // chips), bf16),
        in_specs=[pl.BlockSpec(memory_space=SM)] * 3 + [pl.BlockSpec(memory_space=VM)] * 6
        + [pl.BlockSpec(memory_space=pltpu.HBM)] * len(pieces),
        out_specs=pl.BlockSpec(memory_space=VM),
        scratch_shapes=[
            VM((tokens, width), bf16),
            VM((3 * head_size, width), jnp.float32),
            VM((tokens, head_size), bf16),
            VM((head_size, tokens), bf16),
            VM((tokens, head_size), jnp.float32),
            VM((tokens, head_size), jnp.float32),
            VM((tokens, head_size), bf16),
            VM((tokens, 3 * head_size), bf16),
            VM((tokens, 3 * head_size), bf16),
            pltpu.SemaphoreType.DMA,
        ],
        compiler_params=pltpu.CompilerParams(vmem_limit_bytes=48 * 1024 * 1024),
        cost_estimate=pl.CostEstimate(flops=4 * 10 * pairs * head_size, bytes_accessed=tokens * 4096, transcendentals=pairs),
        name="attend_backward",
    )(bound, inloc, outloc, grad_t, qs, ks, vs, attn_t, lse, *pieces)


HALF_STEP = 1024


def gelu_pair(values):
    cubic = values * values
    inner = 0.7978845608028654 * values * (1.0 + 0.044715 * cubic)
    bent = jnp.tanh(inner)
    slope = 0.7978845608028654 * (1.0 + 0.134145 * cubic)
    half = 0.5 * (1.0 + bent)
    return values * half, half + 0.5 * values * (1.0 - bent * bent) * slope


def load_rows(table, pieces, targets, sem, wait):
    slot = 0
    for piece in pieces:
        count = piece.shape[0]

        @pl.loop(0, count, unroll=4)
        def _(index, piece=piece, slot=slot):
            chip = table[0, slot + index]
            for rows, target in targets(chip):
                copy = pltpu.make_async_copy(piece.at[index, rows], target, sem)
                if wait:
                    copy.wait()
                else:
                    copy.start()

        slot += count


def project_kernel(count, table, got, *refs):
    pieces, (part_out, sent_a, sent_b, attn_in, w_out, sem) = refs[:count], refs[count:]
    chips, size, span = got.shape
    share = w_out.shape[0] // chips
    rows = span // 2

    def targets(chip):
        return [(pl.ds(0, share), w_out.at[rows_at(chip, share)])]

    load_rows(table, pieces, targets, sem, False)
    for chip in range(chips):
        micro, head = divmod(chip, chips // 2)
        for rel in range(2):
            column = (rel * 2 + micro) * rows
            attn_in[head * size : (head + 1) * size, column : column + rows] = got[chip, :, rel * rows : (rel + 1) * rows]
    load_rows(table, pieces, targets, sem, True)
    left = attn_in[...].astype(jnp.float32).T.astype(jnp.bfloat16)
    part = dot_nn(left, w_out[...])
    part_out[...] = part
    own = sent_a.shape[0]
    sent_a[...] = part[:own].astype(jnp.bfloat16)
    sent_b[...] = part[own:].astype(jnp.bfloat16)


def project(table, got, pieces, share):
    chips, size, span = got.shape
    width = pieces[0].shape[2]
    tokens = 2 * span
    bf16 = jnp.bfloat16
    return pl.pallas_call(
        functools.partial(project_kernel, len(pieces)),
        out_shape=(
            jax.ShapeDtypeStruct((tokens, width), jnp.float32),
            jax.ShapeDtypeStruct((tokens // 2, width), bf16),
            jax.ShapeDtypeStruct((tokens // 2, width), bf16),
            jax.ShapeDtypeStruct((chips // 2 * size, tokens), bf16),
        ),
        in_specs=[pl.BlockSpec(memory_space=SM), pl.BlockSpec(memory_space=VM)]
        + [pl.BlockSpec(memory_space=pltpu.HBM)] * len(pieces),
        out_specs=[pl.BlockSpec(memory_space=VM)] * 4,
        scratch_shapes=[VM((chips * share, width), bf16), pltpu.SemaphoreType.DMA],
        compiler_params=pltpu.CompilerParams(vmem_limit_bytes=58 * 1024 * 1024),
        cost_estimate=pl.CostEstimate(
            flops=2 * tokens * chips * share * width, bytes_accessed=8 * tokens * width, transcendentals=0
        ),
        name="project",
    )(table, got, *pieces)


def middle_kernel(count, share, table, x_a, x_b, g_a, g_b, part, got_a, got_b, *refs):
    pieces = refs[:count]
    (resid, base, other, grad_act, sent_a, sent_b, fc_sums, vectors, terms) = refs[count : count + 9]
    (smalls, fc_bias, w_fc, w_proj, g_all, act, act_t, rest, proj_buf, fc_buf, small_sem, load_sem, proj_sem, fc_sem) = refs[count + 9 :]
    f32, bf16 = jnp.float32, jnp.bfloat16
    tokens, width = part.shape
    own = tokens // 2
    hidden = w_proj.shape[0]
    chips = terms.shape[0]
    each = hidden // chips
    folds = hidden // width
    fc_row = share + each

    def targets(chip):
        wanted = [(pl.ds(share, each), w_proj.at[rows_at(chip, each)])]
        for fold in range(folds):
            for core in range(2):
                first = fc_row + (fold * 2 + core) * share
                place = ((chip // 2) * 2 + core) * 2 + chip % 2
                wanted.append(
                    (pl.ds(first, share), w_fc.at[rows_at(place, share), pl.ds(fold * width, width)])
                )
        return wanted

    def small_targets(chip):
        return [(pl.ds(pieces[0].shape[1] - 16, 16), smalls.at[chip])]

    load_rows(table, pieces, small_targets, small_sem, False)
    load_rows(table, pieces, targets, load_sem, False)
    load_rows(table, pieces, small_targets, small_sem, True)
    small_sum = jnp.sum(smalls[...].astype(f32), axis=0)
    vectors[...] = small_sum[:8]
    for fold in range(folds):
        fc_bias[:, fold * width : (fold + 1) * width] = small_sum[8 + fold : 9 + fold]
    for half, (x_in, g_in, arrived) in enumerate(((x_a, g_a, got_a), (x_b, g_b, got_b))):
        here = slice(half * own, (half + 1) * own)
        g_all[here, :] = g_in[...]
        value = x_in[...].astype(f32) + part[here, :] + arrived[...].astype(f32) + vectors[2:3, :]
        resid[here, :] = value
        centred = value - jnp.mean(value, axis=-1, keepdims=True)
        inverse = lax.rsqrt(jnp.mean(centred * centred, axis=-1, keepdims=True) + 1e-05)
        rounded = (centred * inverse * vectors[0:1, :] + vectors[1:2, :]).astype(bf16)
        act[here, :] = rounded
        act_t[:, here] = rounded.astype(f32).T.astype(bf16)
    base[...] = resid[:own, :] + vectors[3:4, :]
    load_rows(table, pieces, targets, load_sem, True)

    per_step = HALF_STEP // each

    def copies(step, slot):
        made = []
        for index in range(per_step):
            made.append(
                pltpu.make_async_copy(
                    proj_buf.at[slot, pl.ds(index * each, each)],
                    terms.at[table[1, step * per_step + index], pl.ds(0, each)],
                    proj_sem.at[slot],
                )
            )
        fold = step // (width // HALF_STEP)
        column = pl.multiple_of(step % (width // HALF_STEP) * HALF_STEP, HALF_STEP)
        for chip in range(chips):
            for core in range(2):
                place = ((chip // 2) * 2 + core) * 2 + chip % 2
                made.append(
                    pltpu.make_async_copy(
                        fc_buf.at[slot, pl.ds(place * share, share)],
                        terms.at[
                            table[1, chip],
                            pl.ds(pl.multiple_of(each + share + (fold * 2 + core) * share, 16), share),
                            pl.ds(column, HALF_STEP),
                        ],
                        fc_sem.at[slot],
                    )
                )
        return made

    steps = hidden // HALF_STEP

    @pl.loop(0, steps)
    def _(step):
        slot = step % 2
        columns = pl.ds(pl.multiple_of(step * HALF_STEP, HALF_STEP), HALF_STEP)
        rows = rows_at(step, HALF_STEP)

        @pl.when(step >= 2)
        def _():
            for copy in copies(step - 2, slot):
                copy.wait()

        grads = g_all[...]
        value, slope = gelu_pair(dot_nn(act[...], w_fc[:, columns]) + fc_bias[:, columns])
        value = value.astype(bf16)
        proj_buf[slot] = dot_nn(value.astype(f32).T.astype(bf16), grads).astype(bf16)
        grad_pre = (dot_nt(grads, w_proj[rows, :]) * slope).astype(bf16)
        fc_sums[:, columns] = jnp.sum(grad_pre.astype(f32), axis=0, keepdims=True)
        fc_buf[slot] = dot_nn(act_t[...], grad_pre).astype(bf16)
        for copy in copies(step, slot):
            copy.start()
        projected = dot_nn(value, w_proj[rows, :])
        back = dot_nt(grad_pre, w_fc[:, columns])
        base[...] += projected[:own]

        @pl.when(step == 0)
        def _():
            grad_act[...] = back
            rest[...] = projected[own:]

        @pl.when(step > 0)
        def _():
            grad_act[...] += back
            rest[...] += projected[own:]

    other[...] = rest[...].astype(bf16)
    sent_a[...] = grad_act[:own, :].astype(bf16)
    sent_b[...] = grad_act[own:, :].astype(bf16)
    for step in range(steps - 2, steps):
        for copy in copies(step, step % 2):
            copy.wait()


def middle(table, x_a, x_b, g_a, g_b, part, got_a, got_b, pieces, share, hidden):
    tokens, width = part.shape
    f32, bf16 = jnp.float32, jnp.bfloat16
    chips = table.shape[1]
    each = hidden // chips
    rows = share + each + 2 * share * (hidden // width)
    shape = jax.ShapeDtypeStruct
    return pl.pallas_call(
        functools.partial(middle_kernel, len(pieces), share),
        out_shape=(
            shape((tokens, width), f32),
            shape((tokens // 2, width), f32),
            shape((tokens // 2, width), bf16),
            shape((tokens, width), f32),
            shape((tokens // 2, width), bf16),
            shape((tokens // 2, width), bf16),
            shape((1, hidden), f32),
            shape((8, width), f32),
            shape((chips, rows, width), bf16),
        ),
        in_specs=[pl.BlockSpec(memory_space=SM)]
        + [pl.BlockSpec(memory_space=VM)] * 7
        + [pl.BlockSpec(memory_space=pltpu.HBM)] * len(pieces),
        out_specs=[pl.BlockSpec(memory_space=VM)] * 8 + [pl.BlockSpec(memory_space=pltpu.HBM)],
        scratch_shapes=[
            VM((chips, 16, width), bf16),
            VM((1, hidden), f32),
            VM((width, hidden), bf16),
            VM((hidden, width), bf16),
            VM((tokens, width), bf16),
            VM((tokens, width), bf16),
            VM((width, tokens), bf16),
            VM((tokens // 2, width), f32),
            VM((2, HALF_STEP, width), bf16),
            VM((2, width, HALF_STEP), bf16),
            pltpu.SemaphoreType.DMA,
            pltpu.SemaphoreType.DMA,
            pltpu.SemaphoreType.DMA((2,)),
            pltpu.SemaphoreType.DMA((2,)),
        ],
        compiler_params=pltpu.CompilerParams(vmem_limit_bytes=56 * 1024 * 1024),
        cost_estimate=pl.CostEstimate(
            flops=12 * tokens * width * hidden, bytes_accessed=8 * width * hidden, transcendentals=tokens * hidden
        ),
        name="middle",
    )(table, x_a, x_b, g_a, g_b, part, got_a, got_b, *pieces)


def branch_kernel(share, row, table, resid, g_a, g_b, part, got_a, got_b, vectors, fc_sums, attn_in, given, grad_resid, branch, tails, terms, products, sem):
    f32, bf16 = jnp.float32, jnp.bfloat16
    tokens, width = resid.shape
    own = tokens // 2
    chips = tails.shape[0]
    gain_sum = jnp.zeros((1, width), f32)
    shift_sum = jnp.zeros((1, width), f32)
    bias_sum = jnp.zeros((1, width), f32)
    proj_sum = jnp.zeros((1, width), f32)
    for half, (g_in, arrived) in enumerate(((g_a, got_a), (g_b, got_b))):
        here = slice(half * own, (half + 1) * own)
        value = resid[here, :]
        centred = value - jnp.mean(value, axis=-1, keepdims=True)
        inverse = lax.rsqrt(jnp.mean(centred * centred, axis=-1, keepdims=True) + 1e-05)
        normed = centred * inverse
        grad = part[here, :] + arrived[...].astype(f32)
        gain_sum += jnp.sum(grad * normed, axis=0, keepdims=True)
        shift_sum += jnp.sum(grad, axis=0, keepdims=True)
        scaled = grad * vectors[0:1, :]
        given_grad = g_in[...].astype(f32)
        total = given_grad + inverse * (
            scaled
            - jnp.mean(scaled, axis=-1, keepdims=True)
            - normed * jnp.mean(scaled * normed, axis=-1, keepdims=True)
        )
        rounded = total.astype(bf16)
        bias_sum += jnp.sum(rounded.astype(f32), axis=0, keepdims=True)
        proj_sum += jnp.sum(given_grad, axis=0, keepdims=True)
        branch[here, :] = rounded
        if half == 0:
            grad_resid[...] = total
    group = width // (chips // 2)
    sums = jnp.concatenate([gain_sum, shift_sum, bias_sum, proj_sum], axis=0)
    each = fc_sums.shape[1] // chips
    for chip in range(chips):
        first = chip // 2 * group
        tail = jnp.concatenate(
            [
                sums[:, first : first + group],
                fc_sums[:, chip * each : (chip + 1) * each],
                jnp.zeros((3, group), f32),
            ],
            axis=0,
        )
        high = tail.astype(bf16)
        low = (tail - high.astype(f32)).astype(bf16)
        tails[chip] = jnp.concatenate([high, low], axis=1)
    products[...] = dot_nn(attn_in[...], branch[...]).astype(bf16)

    @pl.loop(0, chips)
    def _(chip):
        pltpu.make_async_copy(products.at[rows_at(chip, share)], terms.at[table[1, chip], pl.ds(row, share)], sem).start()

    @pl.loop(0, chips)
    def _(chip):
        pltpu.make_async_copy(products.at[rows_at(chip, share)], terms.at[table[1, chip], pl.ds(row, share)], sem).wait()


def branch_back(table, resid, g_a, g_b, part, got_a, got_b, vectors, fc_sums, attn_in, terms, share, row, span):
    tokens, width = resid.shape
    f32, bf16 = jnp.float32, jnp.bfloat16
    chips = table.shape[1]
    shape = jax.ShapeDtypeStruct
    return pl.pallas_call(
        functools.partial(branch_kernel, share, row),
        out_shape=(
            shape((tokens // 2, width), f32),
            shape((tokens, width), bf16),
            shape((chips, 8, span), bf16),
            shape(terms.shape, bf16),
        ),
        in_specs=[pl.BlockSpec(memory_space=SM)]
        + [pl.BlockSpec(memory_space=VM)] * 9
        + [pl.BlockSpec(memory_space=pltpu.HBM)],
        out_specs=[pl.BlockSpec(memory_space=VM)] * 3 + [pl.BlockSpec(memory_space=pltpu.HBM)],
        scratch_shapes=[VM((chips * share, width), bf16), pltpu.SemaphoreType.DMA],
        input_output_aliases={10: 3},
        compiler_params=pltpu.CompilerParams(vmem_limit_bytes=40 * 1024 * 1024),
        cost_estimate=pl.CostEstimate(
            flops=2 * tokens * chips * share * width, bytes_accessed=16 * tokens * width, transcendentals=0
        ),
        name="branch_back",
    )(table, resid, g_a, g_b, part, got_a, got_b, vectors, fc_sums, attn_in, terms)


def attention_back_kernel(count, table, branch, tails, *refs):
    pieces, (sent, w_out, sem) = refs[:count], refs[count:]
    chips, size, span = sent.shape
    size -= 8
    rows = span // 2
    share = w_out.shape[0] // chips

    def targets(chip):
        return [(pl.ds(0, share), w_out.at[rows_at(chip, share)])]

    load_rows(table, pieces, targets, sem, False)
    sent[:, size:, :] = tails[...]
    load_rows(table, pieces, targets, sem, True)
    grads = dot_nt(w_out[...], branch[...]).astype(jnp.bfloat16)
    for chip in range(chips):
        micro, head = divmod(chip, chips // 2)
        for rel in range(2):
            column = (rel * 2 + micro) * rows
            sent[chip, :size, rel * rows : (rel + 1) * rows] = grads[
                head * size : (head + 1) * size, column : column + rows
            ]


def attention_back(table, branch, tails, pieces, share, size):
    tokens, width = branch.shape
    chips, _, span = tails.shape
    bf16 = jnp.bfloat16
    return pl.pallas_call(
        functools.partial(attention_back_kernel, len(pieces)),
        out_shape=jax.ShapeDtypeStruct((chips, size + 8, span), bf16),
        in_specs=[pl.BlockSpec(memory_space=SM)]
        + [pl.BlockSpec(memory_space=VM)] * 2
        + [pl.BlockSpec(memory_space=pltpu.HBM)] * len(pieces),
        out_specs=pl.BlockSpec(memory_space=VM),
        scratch_shapes=[VM((chips * share, width), bf16), pltpu.SemaphoreType.DMA],
        compiler_params=pltpu.CompilerParams(vmem_limit_bytes=58 * 1024 * 1024),
        cost_estimate=pl.CostEstimate(
            flops=2 * tokens * chips * share * width, bytes_accessed=4 * tokens * width, transcendentals=0
        ),
        name="attention_back",
    )(table, branch, tails, *pieces)


def finish_kernel(order, got, weights, kept, sent, weight, grads, sem):
    chips, _, span = got.shape
    size = weight.shape[0] // len(order)
    rows = span // 2
    own = kept.shape[0]

    def copies():
        return [
            pltpu.make_async_copy(weights.at[slot], weight.at[pl.ds(head * size, size)], sem)
            for slot, head in enumerate(order)
        ]

    for copy in copies():
        copy.start()
    for chip in range(chips):
        micro, head = divmod(chip, chips // 2)
        turned = got[chip, :size, :].astype(jnp.float32).T.astype(jnp.bfloat16)
        for rel in range(2):
            row = (rel * 2 + micro) * rows
            grads[head, row : row + rows, :] = turned[rel * rows : (rel + 1) * rows]
    for copy in copies():
        copy.wait()
    left = jnp.concatenate([grads[head] for head in range(len(order))], axis=1)
    back = dot_nn(left, weight[...])
    kept[...] = back[:own]
    sent[...] = back[own:].astype(jnp.bfloat16)


def finish(got, weights, order):
    chips, _, span = got.shape
    heads, size, width = weights.shape
    bf16 = jnp.bfloat16
    return pl.pallas_call(
        functools.partial(finish_kernel, order),
        out_shape=(
            jax.ShapeDtypeStruct((span, width), jnp.float32),
            jax.ShapeDtypeStruct((span, width), bf16),
        ),
        in_specs=[pl.BlockSpec(memory_space=VM), pl.BlockSpec(memory_space=pltpu.HBM)],
        out_specs=[pl.BlockSpec(memory_space=VM)] * 2,
        scratch_shapes=[
            VM((heads * size, width), bf16),
            VM((heads, 2 * span, size), bf16),
            pltpu.SemaphoreType.DMA,
        ],
        compiler_params=pltpu.CompilerParams(vmem_limit_bytes=58 * 1024 * 1024),
        cost_estimate=pl.CostEstimate(
            flops=4 * span * width * heads * size,
            bytes_accessed=2 * width * heads * size + 8 * span * width,
            transcendentals=0,
        ),
        name="finish",
    )(got, weights)


def unpack_kernel(share, core_ref, summed, given, proj, out, merged):
    f32 = jnp.float32
    core = core_ref[0]
    folds, _, width = given.shape
    each = proj.shape[0]
    proj[...] = summed[:each, :].astype(f32)
    out[...] = summed[each : each + share, :].astype(f32)
    group = each
    for fold in range(folds):
        first = pl.multiple_of(each + share + (fold * 2 + core) * share, share)
        for owner, rows in ((core, summed[pl.ds(first, share), :]), (1 - core, given[fold])):
            rows = rows.astype(f32)
            for index in range(width // group):
                number = fold * (width // group) + index
                place = ((number // 2 * 2 + owner) * 2 + number % 2) * group
                merged[:, pl.ds(pl.multiple_of(place, group), group)] = rows[:, index * group : (index + 1) * group]


def unpack(core, summed, given, share, each):
    folds, _, width = given.shape
    f32 = jnp.float32
    return pl.pallas_call(
        functools.partial(unpack_kernel, share),
        out_shape=(
            jax.ShapeDtypeStruct((each, width), f32),
            jax.ShapeDtypeStruct((share, width), f32),
            jax.ShapeDtypeStruct((share, 2 * folds * width), f32),
        ),
        in_specs=[pl.BlockSpec(memory_space=SM)] + [pl.BlockSpec(memory_space=VM)] * 2,
        out_specs=[pl.BlockSpec(memory_space=VM)] * 3,
        cost_estimate=pl.CostEstimate(flops=0, bytes_accessed=6 * summed.size, transcendentals=0),
        name="unpack",
    )(core, summed, given)


PATHS = (("x", "z", "head"), ("head", "z", "x"))


PAIR = [(0, 1), (1, 0)]
NEAR = [(0, 1), (1, 0), (2, 3), (3, 2)]
FAR = [(0, 2), (2, 0), (1, 3), (3, 1)]


def swap(values, axis, pairs=PAIR):
    return lax.ppermute(values, axis, pairs)


def across(values, axis):
    return swap(values, axis, NEAR if axis == "z" else PAIR)


def in_order(mine, other, index, axis):
    first = jnp.where(index == 0, mine, other)
    second = jnp.where(index == 0, other, mine)
    return jnp.stack([first, second], axis=axis)


def split_float(values):
    high = values.astype(jnp.bfloat16)
    low = (values - high.astype(jnp.float32)).astype(jnp.bfloat16)
    return high, low


def run_table(order, pair_start):
    pairs = order.shape[0]
    runs = jnp.arange(2 * pairs, dtype=jnp.int32)[:, None]
    low = jnp.where(runs == order[None, :], pair_start[None, :], 0)
    high = jnp.where(runs == 2 * pairs - 1 - order[None, :], pair_start[None, :] + 1, 0)
    return jnp.sum(low + high, axis=1).astype(jnp.int32)


def ring_order(count, turn):
    half = [(z, (z + step + turn) % 2) for z in range(count) for step in range(2)]
    return [z * 4 + y for z, y in half] + [z * 4 + 2 + y for z, y in reversed(half)]


def core_groups(rings):
    return [[(chip // 2 * 2 + core) * 2 + chip % 2 for chip in ring] for core, ring in enumerate(rings)]


def cube_orders(depth):
    cycle = [0, 1, 3, 2, 6, 7, 5, 4]
    return [[chip + start for chip in cycle] for start in (0, 4 * depth)]


def fast_body(
    block_input,
    qkv_weight,
    q_bias,
    v_bias,
    out_weight,
    out_bias,
    norm1_gain,
    norm1_shift,
    norm2_gain,
    norm2_shift,
    fc_weight,
    fc_bias,
    proj_weight,
    proj_bias,
    out_grad,
    dealt,
    lengths,
):
    f32, bf16 = jnp.float32, jnp.bfloat16
    micro, rows, width = block_input.shape
    nz, nx = lax.axis_size("z"), lax.axis_size("x")
    iz, ix, ic, iy = (lax.axis_index(name) for name in ("z", "x", "core", "head"))
    zx = nz * nx
    every, chips = ("z", "x", "core", "head"), ("z", "x", "head")
    devices, chip_count = 4 * zx, 2 * zx
    heads = 2 * zx
    local = heads * DH // 2
    share = qkv_weight.shape[0]
    hidden_share = proj_weight.shape[0]
    hidden_half = hidden_share * chip_count

    inputs = block_input.astype(f32)
    normed_one, inverse_one = normalize(inputs)
    n1 = normed_one.astype(bf16)
    n1, qkv_weight, fc_weight, norm1_gain, norm2_gain = lax.optimization_barrier(
        (n1, qkv_weight, fc_weight, norm1_gain, norm2_gain)
    )
    gain_one = norm1_gain.astype(f32)
    shift_one = norm1_shift.astype(f32)
    raw_qkv = qkv_weight.astype(f32)
    scaled_qkv = (raw_qkv * gain_one[:, None]).astype(bf16)
    device = ((iz * nx + ix) * 2 + ic) * 2 + iy
    offset = jnp.sum(raw_qkv * shift_one[:, None], axis=0)
    zero = jnp.zeros((width,), f32)
    place = device * share
    offset = offset + jnp.concatenate(
        [
            lax.dynamic_update_slice(zero, q_bias.astype(f32), (place,)),
            zero,
            lax.dynamic_update_slice(zero, v_bias.astype(f32), (place,)),
        ]
    )
    high, low = split_float(offset)
    to_heads = jnp.concatenate([scaled_qkv, high[None], low[None], jnp.zeros((6, 3 * width), bf16)], axis=0)
    to_heads = to_heads.reshape(share + 8, 3, zx // 2, 2, 2, DH).transpose(2, 4, 3, 0, 1, 5)
    to_heads = to_heads.reshape(1, heads, share + 8, 3 * DH)
    to_heads = jnp.broadcast_to(to_heads, (2, heads, share + 8, 3 * DH)).reshape(devices, share + 8, 3 * DH)
    head_rows = lax.all_to_all(to_heads, every, split_axis=0, concat_axis=0, tiled=True)
    head_weight = head_rows[:, :share].reshape(width, 3 * DH)
    head_offset = jnp.sum(head_rows[:, share : share + 2].astype(f32), axis=(0, 1))

    mine = iz // 2
    near = lax.dynamic_index_in_dim(n1, mine, 0, keepdims=False)
    far = swap(lax.dynamic_index_in_dim(n1, 1 - mine, 0, keepdims=False), "z", FAR)
    paths = PATHS
    got = across(near, paths[0][0])
    far, got = lax.optimization_barrier((far, got))
    near = jnp.stack([near, got])
    near_got, far_got = across(near, paths[0][1]), across(far, paths[1][0])
    near_got, far_got = lax.optimization_barrier((near_got, far_got))
    near, far = jnp.stack([near, near_got]), jnp.stack([far, far_got])
    near_got, far_got = across(near, paths[0][2]), across(far, paths[1][1])
    far = jnp.stack([far, far_got])
    parts = [near, near_got, far, across(far, paths[1][2])]
    pieces, owners = [], []

    def add_all(flip):
        core = 1 - ic if flip else ic
        for index, part in enumerate(parts):
            pieces.append((swap(part, "core") if flip else part).reshape(-1, width))
            for second in range(2):
                for first in range(2):
                    flips = dict(zip(paths[index // 2], (first, second, index % 2)))
                    owners.append((iz ^ flips["z"] ^ (index // 2 * 2), ix ^ flips["x"], core, iy ^ flips["head"]))

    add_all(False)
    add_all(True)
    slot_device = jnp.stack([((z * nx + x) * 2 + core) * 2 + y for z, x, core, y in owners]).astype(jnp.int32)
    my_dealt = lax.dynamic_index_in_dim(dealt, mine, 0, keepdims=False)
    order = my_dealt.reshape(devices, rows)[:, 0] // RUN
    slot_of = jnp.sum(
        jnp.where(jnp.arange(devices)[:, None] == slot_device[None, :], jnp.arange(devices)[None, :], 0), axis=1
    )
    inloc = run_table(order, (slot_of * 2).astype(jnp.int32))
    ids = jnp.arange(devices, dtype=jnp.int32)
    id_y, id_c, id_zx = ids % 2, ids // 2 % 2, ids // 4
    send_pair = (id_zx * 2 + id_y) * 2 + (id_c ^ ic)
    outloc = run_table(order, (send_pair * 2).astype(jnp.int32))
    bound = lax.dynamic_index_in_dim(lengths, mine, 0, keepdims=False)[:1]

    fc_parts = fc_weight.reshape(share, zx, 2, 2, hidden_share)

    def core_columns(values, index):
        return lax.dynamic_index_in_dim(values, index, 2, keepdims=False)

    fc_mine = core_columns(fc_parts, ic).reshape(share, hidden_half)
    fc_other = swap(core_columns(fc_parts, 1 - ic).reshape(share, hidden_half), "core")
    fc_pair = in_order(fc_mine, fc_other, ic, 0).reshape(2 * share, hidden_half)
    small = jnp.stack([norm2_gain, norm2_shift, out_bias, proj_bias])
    small_rows = jnp.zeros((16, width), bf16)
    small_rows = lax.dynamic_update_slice(small_rows, small, (0, place))
    other_place = (((iz * nx + ix) * 2 + 1 - ic) * 2 + iy) * share
    small_rows = lax.dynamic_update_slice(small_rows, swap(small, "core"), (0, other_place))
    fc_place = ((iz * nx + ix) * 2 + iy) * hidden_share
    small_rows = lax.dynamic_update_slice(small_rows, fc_bias[None], (8 + fc_place // width, fc_place % width))
    folds = hidden_half // width
    fc_folded = fc_pair.reshape(2 * share, folds, width).transpose(1, 0, 2).reshape(-1, width)
    packed = jnp.concatenate([out_weight, proj_weight, fc_folded, small_rows], axis=0)
    rings = [ring_order(nz, turn) for turn in range(2)]
    places = [[ring.index(chip) for chip in range(chip_count)] for ring in rings]
    table = lax.dynamic_index_in_dim(
        jnp.array([[ring, place] for ring, place in zip(rings, places)], jnp.int32), ic, 0, keepdims=False
    )
    gathered = lax.all_gather(packed, every, axis=0, axis_index_groups=core_groups(rings))
    out_rows = share
    proj_rows = hidden_share
    fc_rows = 2 * share * folds

    mixed = [(product(piece, head_weight) + head_offset).astype(bf16) for piece in pieces]
    slots = jnp.concatenate(mixed, axis=0)
    attn_send, queries, keys, values, attn_t, lse = attend_forward(bound, inloc, outloc, slots, chip_count, DH)

    x_a, x_b = block_input.reshape(-1, width), swap(block_input, "core").reshape(-1, width)
    g_a, g_b = out_grad.reshape(-1, width), swap(out_grad, "core").reshape(-1, width)
    attn_got = lax.all_to_all(attn_send, chips, split_axis=0, concat_axis=0, tiled=True)
    weight_turned, attn_got = lax.optimization_barrier((head_weight.T, attn_got))
    cubes = cube_orders(nz // 2)
    w_qkv = lax.all_gather(weight_turned, chips, axis=0, axis_index_groups=cubes)
    part, sent_a, sent_b, attn_in = project(table, attn_got, [gathered], share)
    resid, base, project_other, grad_part, back_a, back_b, fc_sums, vectors, terms = middle(
        table, x_a, x_b, g_a, g_b, part, swap(sent_b, "core"), swap(sent_a, "core"), [gathered], share, hidden_half
    )
    grad_resid, branch, tails, terms = branch_back(
        table,
        resid,
        g_a,
        g_b,
        grad_part,
        swap(back_b, "core"),
        swap(back_a, "core"),
        vectors,
        fc_sums,
        attn_in,
        terms,
        share,
        proj_rows,
        2 * rows,
    )
    grad_send = attention_back(table, branch, tails, [gathered], share, DH)
    output = (base + swap(project_other, "core").astype(f32)).astype(bf16)

    grad_got = lax.all_to_all(grad_send, chips, split_axis=0, concat_axis=0, tiled=True)
    vector_sums = jnp.sum(grad_got[:, DH:].astype(f32), axis=0)
    vector_sums = vector_sums[:, :rows] + vector_sums[:, rows:]
    final_vectors = lax.dynamic_slice(vector_sums, (0, (ic * 2 + iy) * share), (4, share))
    final_fc_b = vector_sums[4]

    summed = lax.psum_scatter(
        terms, every, scatter_dimension=0, tiled=True, axis_index_groups=core_groups(rings)
    )[0]
    fc_sum = summed[proj_rows + out_rows :].reshape(folds, 2, share, width)
    fc_give = swap(lax.dynamic_index_in_dim(fc_sum, 1 - ic, 1, keepdims=False), "core")
    final_proj_w, final_out_w, final_fc_w = unpack(
        ic.astype(jnp.int32).reshape(1), summed, fc_give, share, hidden_share
    )

    send_grads = attend_backward(
        bound, inloc, outloc, grad_got, queries, keys, values, attn_t, lse, pieces, share
    )
    grads_got = lax.all_to_all(send_grads, chips, split_axis=0, concat_axis=0, tiled=True)
    back_own, back_other = finish(grads_got, w_qkv, cubes[0])
    raw_got = grads_got[:, 3 * DH :, : 3 * DH].astype(f32)
    raw_sum = jnp.sum(raw_got.reshape(2, zx, 2 * share + 16, 3 * DH), axis=0)
    raw_parts = raw_sum[:, : 2 * share].reshape(zx, 2, share, 3 * DH)
    sums_mine = raw_sum[:, 2 * share : 2 * share + 1] + raw_sum[:, 2 * share + 1 : 2 * share + 2]
    raw_keep = jnp.concatenate([lax.dynamic_index_in_dim(raw_parts, ic, 1, keepdims=False), sums_mine], axis=1)
    raw_give = jnp.concatenate([lax.dynamic_index_in_dim(raw_parts, 1 - ic, 1, keepdims=False), sums_mine], axis=1)
    raw_all = in_order(raw_keep, swap(raw_give, "core"), ic, 1).reshape(heads, share + 1, 3, DH)
    raw_all = raw_all.transpose(1, 2, 0, 3).reshape(share + 1, 3 * width)
    raw_grad, all_sums = raw_all[:share], raw_all[share]
    final_qkv_w = raw_grad * gain_one[:, None] + shift_one[:, None] * all_sums[None, :]
    final_gain_one = jnp.sum(raw_grad * raw_qkv, axis=1)
    final_shift_one = jnp.sum(raw_qkv * all_sums[None, :], axis=1)
    final_q_b = lax.dynamic_slice(all_sums, (place,), (share,))
    final_v_b = lax.dynamic_slice(all_sums, (2 * width + place,), (share,))

    back_own = back_own + swap(back_other, "core").astype(f32)
    back_own = back_own.reshape(micro, rows, width)
    input_grad = grad_resid.reshape(micro, rows, width) + norm_back(back_own, normed_one, inverse_one)

    return (
        output.reshape(micro, rows, width),
        input_grad.astype(bf16),
        final_qkv_w,
        final_q_b,
        final_v_b,
        final_out_w,
        final_vectors[2],
        final_gain_one,
        final_shift_one,
        final_vectors[0],
        final_vectors[1],
        final_fc_w,
        final_fc_b,
        final_proj_w,
        final_vectors[3],
    )


def specs(names):
    rows, vector, tokens = P(names, None), P(names), P(None, names, None)
    weights = (rows, vector, vector, rows, vector, vector, vector, vector, vector, rows, vector, rows, vector)
    return (tokens, *weights, tokens, P(), P()), (tokens, tokens, *weights)


def solution(mesh):
    sizes = dict(mesh.shape)
    if sizes["head"] == 2 and sizes["blk"] == 16:
        fine = Mesh(mesh.devices.reshape(2, 4, 2, 2), ("head", "z", "x", "core"))
        given, made = specs(("z", "x", "core", "head"))
        return jax.shard_map(fast_body, mesh=fine, in_specs=given, out_specs=made, check_vma=False)
    given, made = specs(("blk", "head"))
    return jax.shard_map(general_body, mesh=mesh, in_specs=given, out_specs=made, check_vma=False)
```

```python
import functools
import math

import jax
import jax.numpy as jnp
from jax import lax
from jax.experimental import pallas as pl
from jax.experimental.pallas import tpu as pltpu
from jax.sharding import Mesh
from jax.sharding import PartitionSpec as P

DH = 64


def gelu_tanh(values):
    inner = 0.7978845608028654 * (values + 0.044715 * values * values * values)
    return 0.5 * values * (1.0 + jnp.tanh(inner))


def normalize(values):
    centred = values - jnp.mean(values, axis=-1, keepdims=True)
    inverse = lax.rsqrt(jnp.mean(centred * centred, axis=-1, keepdims=True) + 1e-05)
    return (centred * inverse, inverse)


def norm_back(grad_normed, normed, inverse):
    return inverse * (
        grad_normed
        - jnp.mean(grad_normed, axis=-1, keepdims=True)
        - normed * jnp.mean(grad_normed * normed, axis=-1, keepdims=True)
    )


def product(left, right):
    return jnp.dot(left, right, preferred_element_type=jnp.float32)


def product_tn(left, right):
    return lax.dot_general(
        left, right, (((0,), (0,)), ((), ())), preferred_element_type=jnp.float32
    )


def product_nt(left, right):
    return lax.dot_general(
        left, right, (((1,), (1,)), ((), ())), preferred_element_type=jnp.float32
    )


def visible_pairs(query_pos, key_pos, boundary):
    same_side = (query_pos[:, None] >= boundary) == (key_pos[None, :] >= boundary)
    return same_side & (key_pos[None, :] <= query_pos[:, None])


def forward_tile(current, queries3, keys3, values3, visible, scale):
    running, total, accum = current
    scores = jnp.einsum("qhd,khd->hqk", queries3, keys3, preferred_element_type=jnp.float32) * scale
    scores = jnp.where(visible[None], scores, -1000000000.0)
    highest = jnp.maximum(running, jnp.max(scores, axis=-1))
    weights = jnp.where(visible[None], jnp.exp(scores - highest[..., None]), 0.0)
    factor = jnp.exp(running - highest)
    total = total * factor + jnp.sum(weights, axis=-1)
    accum = accum * factor[..., None] + jnp.einsum(
        "hqk,khd->hqd", weights.astype(jnp.bfloat16), values3, preferred_element_type=jnp.float32
    )
    return (highest, total, accum)


def general_forward(query_parts, pos_parts, positions, boundary, keys_group, values_group, key_span):
    heads_local, head_size = (query_parts[0].shape[1], query_parts[0].shape[2])
    scale = head_size ** (-0.5)

    def fold_keys(state, pieces, start):
        key_rows, value_rows = pieces
        count_rows = key_rows.shape[0]
        block_rows = math.gcd(count_rows, key_span)
        block_count = count_rows // block_rows

        def one_step(index, inner):
            offset = index * block_rows
            keys3 = lax.dynamic_slice_in_dim(key_rows, offset, block_rows).reshape(
                block_rows, heads_local, head_size
            )
            values3 = lax.dynamic_slice_in_dim(value_rows, offset, block_rows).reshape(
                block_rows, heads_local, head_size
            )
            key_pos = lax.dynamic_slice_in_dim(positions, offset, block_rows)
            part_queries = query_parts[0]
            visible = visible_pairs(pos_parts[0], key_pos, boundary)
            current = inner[0]
            result = forward_tile(current, part_queries, keys3, values3, visible, scale)
            updated = [result]
            return tuple(updated)

        return lax.fori_loop(0, block_count, one_step, state)

    initial = tuple(
        (
            (
                jnp.full((heads_local, part.shape[0]), -1000000000.0, jnp.float32),
                jnp.zeros((heads_local, part.shape[0]), jnp.float32),
                jnp.zeros((heads_local, part.shape[0], head_size), jnp.float32),
            )
            for part in query_parts
        )
    )
    return fold_keys(
        initial,
        (
            lax.all_gather(keys_group, "blk", axis=0, tiled=True),
            lax.all_gather(values_group, "blk", axis=0, tiled=True),
        ),
        jnp.int32(0),
    )


def backward_tile(current, queries3, grad3, log_total, delta, keys3, values3, visible, scale):
    grad_query, term = current
    scores = jnp.einsum("qhd,khd->hqk", queries3, keys3, preferred_element_type=jnp.float32) * scale
    scores = jnp.where(visible[None], scores, -1000000000.0)
    exact = jnp.where(visible[None], jnp.exp(scores - log_total[..., None]), 0.0)
    grad_probs = jnp.einsum("qhd,khd->hqk", grad3, values3, preferred_element_type=jnp.float32)
    grad_scores = (exact * (grad_probs - delta[..., None])).astype(jnp.bfloat16)
    grad_query = (
        grad_query
        + jnp.einsum("hqk,khd->hqd", grad_scores, keys3, preferred_element_type=jnp.float32) * scale
    )
    rounded = exact.astype(jnp.bfloat16)
    grad_values = jnp.einsum("hqk,qhd->khd", rounded, grad3, preferred_element_type=jnp.float32)
    grad_keys = (
        jnp.einsum("hqk,qhd->khd", grad_scores, queries3, preferred_element_type=jnp.float32)
        * scale
    )
    rows = keys3.shape[0]
    term = jnp.stack([grad_keys.reshape(rows, -1), grad_values.reshape(rows, -1)], axis=1)
    return (grad_query, term)


def general_backward(
    query_parts,
    grad_parts,
    total_parts,
    delta_parts,
    pos_parts,
    positions,
    boundary,
    keys_group,
    values_group,
    key_span,
    buffer_rows,
):
    heads_local, head_size = (query_parts[0].shape[1], query_parts[0].shape[2])
    scale = head_size ** (-0.5)

    def fold_keys(state, pieces, start):
        key_rows, value_rows = pieces
        count_rows = key_rows.shape[0]
        block_rows = math.gcd(count_rows, key_span)
        block_count = count_rows // block_rows

        def one_step(index, inner):
            offset = index * block_rows
            keys3 = lax.dynamic_slice_in_dim(key_rows, offset, block_rows).reshape(
                block_rows, heads_local, head_size
            )
            values3 = lax.dynamic_slice_in_dim(value_rows, offset, block_rows).reshape(
                block_rows, heads_local, head_size
            )
            key_pos = lax.dynamic_slice_in_dim(positions, offset, block_rows)
            grads_now, buffer = inner
            term = jnp.zeros((block_rows, 2, heads_local * head_size), jnp.float32)
            part_queries = query_parts[0]
            part_grads = grad_parts[0]
            part_total = total_parts[0]
            part_delta = delta_parts[0]
            visible = visible_pairs(pos_parts[0], key_pos, boundary)
            current = (grads_now[0], term)
            result = backward_tile(
                current,
                part_queries,
                part_grads,
                part_total,
                part_delta,
                keys3,
                values3,
                visible,
                scale,
            )
            updated = [result[0]]
            term = result[1]
            buffer = lax.dynamic_update_slice(buffer, term, (offset, 0, 0))
            return (tuple(updated), buffer)

        return lax.fori_loop(0, block_count, one_step, state)

    grads_init = tuple(
        (jnp.zeros((heads_local, part.shape[0], head_size), jnp.float32) for part in query_parts)
    )
    initial = (grads_init, jnp.zeros((buffer_rows, 2, heads_local * head_size), jnp.float32))
    return fold_keys(
        initial,
        (
            lax.all_gather(keys_group, "blk", axis=0, tiled=True),
            lax.all_gather(values_group, "blk", axis=0, tiled=True),
        ),
        jnp.int32(0),
    )


def general_body(
    block_input,
    qkv_weight,
    q_bias,
    v_bias,
    out_weight,
    out_bias,
    norm1_gain,
    norm1_shift,
    norm2_gain,
    norm2_shift,
    fc_weight,
    fc_bias,
    proj_weight,
    proj_bias,
    out_grad,
    dealt,
    lengths,
):
    micro_count, local_rows, width = block_input.shape
    head_devices = lax.axis_size("head")
    blk_devices = lax.axis_size("blk")
    group = local_rows * head_devices
    blk_index = lax.axis_index("blk")
    head_size = DH
    key_span = 1024
    part_count = group // group
    shards = (
        qkv_weight,
        q_bias,
        v_bias,
        out_weight,
        out_bias,
        norm1_gain,
        norm1_shift,
        norm2_gain,
        norm2_shift,
        fc_weight,
        fc_bias,
        proj_weight,
        proj_bias,
    )
    totals = [
        jnp.zeros((shard.shape[0] * blk_devices * head_devices,) + shard.shape[1:], jnp.float32)
        for shard in shards
    ]
    outputs = []
    input_grads = []
    for micro_index in range(micro_count):
        whole = (
            lax.all_gather(shards[0], ("blk", "head"), axis=0, tiled=True),
            lax.all_gather(shards[1], ("blk", "head"), axis=0, tiled=True),
            lax.all_gather(shards[2], ("blk", "head"), axis=0, tiled=True),
            lax.all_gather(shards[3], ("blk", "head"), axis=0, tiled=True),
            lax.all_gather(shards[4], ("blk", "head"), axis=0, tiled=True),
            lax.all_gather(shards[5], ("blk", "head"), axis=0, tiled=True),
            lax.all_gather(shards[6], ("blk", "head"), axis=0, tiled=True),
            lax.all_gather(shards[7], ("blk", "head"), axis=0, tiled=True),
            lax.all_gather(shards[8], ("blk", "head"), axis=0, tiled=True),
            lax.all_gather(shards[9], ("blk", "head"), axis=0, tiled=True),
            lax.all_gather(shards[10], ("blk", "head"), axis=0, tiled=True),
            lax.all_gather(shards[11], ("blk", "head"), axis=0, tiled=True),
            lax.all_gather(shards[12], ("blk", "head"), axis=0, tiled=True),
        )
        (
            w_qkv,
            b_query,
            b_value,
            w_out,
            b_out,
            gain_one,
            shift_one,
            gain_two,
            shift_two,
            w_fc,
            b_fc,
            w_proj,
            b_proj,
        ) = whole
        b_query = b_query.astype(jnp.float32)
        b_value = b_value.astype(jnp.float32)
        b_out = b_out.astype(jnp.float32)
        gain_one = gain_one.astype(jnp.float32)
        shift_one = shift_one.astype(jnp.float32)
        gain_two = gain_two.astype(jnp.float32)
        shift_two = shift_two.astype(jnp.float32)
        b_fc = b_fc.astype(jnp.float32)
        b_proj = b_proj.astype(jnp.float32)
        positions = dealt[micro_index]
        boundary = lengths[micro_index, 0]
        query_pos = lax.dynamic_slice_in_dim(positions, blk_index * group, group)
        inputs = block_input[micro_index].astype(jnp.float32)
        normed_one, inverse_one = normalize(inputs)
        act_one = (normed_one * gain_one + shift_one).astype(jnp.bfloat16)
        mixed = product(act_one, w_qkv)
        queries = (mixed[:, :width] + b_query).astype(jnp.bfloat16)
        keys = mixed[:, width : 2 * width].astype(jnp.bfloat16)
        values = (mixed[:, 2 * width :] + b_value).astype(jnp.bfloat16)
        heads_in = lax.all_to_all(
            jnp.stack([queries, keys, values], axis=1),
            "head",
            split_axis=2,
            concat_axis=0,
            tiled=True,
        )
        local_width = heads_in.shape[2]
        heads_local = local_width // head_size
        queries3 = heads_in[:, 0].reshape(group, heads_local, head_size)
        keys_group = heads_in[:, 1]
        values_group = heads_in[:, 2]
        query_parts = tuple((queries3 for index in range(part_count)))
        pos_parts = tuple((query_pos for index in range(part_count)))
        states = general_forward(
            query_parts, pos_parts, positions, boundary, keys_group, values_group, key_span
        )
        running = jnp.concatenate([state[0] for state in states], axis=1)
        total = jnp.concatenate([state[1] for state in states], axis=1)
        accum = jnp.concatenate([state[2] for state in states], axis=1)
        log_total = running + jnp.log(total)
        attn_heads = (
            (accum / total[..., None])
            .transpose(1, 0, 2)
            .reshape(group, local_width)
            .astype(jnp.bfloat16)
        )
        attended = lax.all_to_all(attn_heads, "head", split_axis=0, concat_axis=1, tiled=True)
        resid = inputs + product(attended, w_out) + b_out
        normed_two, inverse_two = normalize(resid)
        act_two = (normed_two * gain_two + shift_two).astype(jnp.bfloat16)
        pre = product(act_two, w_fc) + b_fc
        hidden = gelu_tanh(pre).astype(jnp.bfloat16)
        outputs.append((resid + product(hidden, w_proj) + b_proj).astype(jnp.bfloat16))
        cotangent = out_grad[micro_index]
        grad_proj_w = product_tn(hidden, cotangent)
        grad_proj_b = jnp.sum(cotangent.astype(jnp.float32), axis=0)
        grad_hidden = product_nt(cotangent, w_proj)
        grad_pre = jax.vjp(gelu_tanh, pre)[1](grad_hidden)[0].astype(jnp.bfloat16)
        grad_fc_w = product_tn(act_two, grad_pre)
        grad_fc_b = jnp.sum(grad_pre.astype(jnp.float32), axis=0)
        grad_act_two = product_nt(grad_pre, w_fc)
        grad_gain_two = jnp.sum(grad_act_two * normed_two, axis=0)
        grad_shift_two = jnp.sum(grad_act_two, axis=0)
        grad_resid = cotangent.astype(jnp.float32) + norm_back(
            grad_act_two * gain_two, normed_two, inverse_two
        )
        grad_branch = grad_resid.astype(jnp.bfloat16)
        grad_out_w = product_tn(attended, grad_branch)
        grad_out_b = jnp.sum(grad_branch.astype(jnp.float32), axis=0)
        grad_attn = product_nt(grad_branch, w_out).astype(jnp.bfloat16)
        grad_heads = lax.all_to_all(grad_attn, "head", split_axis=1, concat_axis=0, tiled=True)
        grad3 = grad_heads.reshape(group, heads_local, head_size)
        attn3 = attn_heads.reshape(group, heads_local, head_size)
        delta = jnp.sum(grad3.astype(jnp.float32) * attn3.astype(jnp.float32), axis=-1).T
        grad_parts = tuple((grad3 for index in range(part_count)))
        total_parts = tuple((log_total for index in range(part_count)))
        delta_parts = tuple((delta for index in range(part_count)))
        query_grads, buffer = general_backward(
            query_parts,
            grad_parts,
            total_parts,
            delta_parts,
            pos_parts,
            positions,
            boundary,
            keys_group,
            values_group,
            key_span,
            group * blk_devices,
        )
        kv_sums = lax.psum_scatter(buffer, "blk", scatter_dimension=0, tiled=True)
        grad_k_heads = kv_sums[:, 0].astype(jnp.bfloat16)
        grad_v_heads = kv_sums[:, 1].astype(jnp.bfloat16)
        grad_query = jnp.concatenate(list(query_grads), axis=1)
        grad_q_heads = (
            grad_query.transpose(1, 0, 2).reshape(group, local_width).astype(jnp.bfloat16)
        )
        grads_heads = jnp.stack([grad_q_heads, grad_k_heads, grad_v_heads], axis=1)
        back_tokens = lax.all_to_all(grads_heads, "head", split_axis=0, concat_axis=2, tiled=True)
        grad_mixed = back_tokens.reshape(local_rows, 3 * width)
        grad_qkv_w = product_tn(act_one, grad_mixed)
        grad_q_b = jnp.sum(back_tokens[:, 0].astype(jnp.float32), axis=0)
        grad_v_b = jnp.sum(back_tokens[:, 2].astype(jnp.float32), axis=0)
        grad_act_one = product_nt(grad_mixed, w_qkv)
        grad_gain_one = jnp.sum(grad_act_one * normed_one, axis=0)
        grad_shift_one = jnp.sum(grad_act_one, axis=0)
        input_grads.append(
            (grad_resid + norm_back(grad_act_one * gain_one, normed_one, inverse_one)).astype(
                jnp.bfloat16
            )
        )
        terms = (
            grad_qkv_w,
            grad_q_b,
            grad_v_b,
            grad_out_w,
            grad_out_b,
            grad_gain_one,
            grad_shift_one,
            grad_gain_two,
            grad_shift_two,
            grad_fc_w,
            grad_fc_b,
            grad_proj_w,
            grad_proj_b,
        )
        totals = [running_sum + term for running_sum, term in zip(totals, terms)]
    final = (
        lax.psum_scatter(totals[0], ("blk", "head"), scatter_dimension=0, tiled=True),
        lax.psum_scatter(totals[1], ("blk", "head"), scatter_dimension=0, tiled=True),
        lax.psum_scatter(totals[2], ("blk", "head"), scatter_dimension=0, tiled=True),
        lax.psum_scatter(totals[3], ("blk", "head"), scatter_dimension=0, tiled=True),
        lax.psum_scatter(totals[4], ("blk", "head"), scatter_dimension=0, tiled=True),
        lax.psum_scatter(totals[5], ("blk", "head"), scatter_dimension=0, tiled=True),
        lax.psum_scatter(totals[6], ("blk", "head"), scatter_dimension=0, tiled=True),
        lax.psum_scatter(totals[7], ("blk", "head"), scatter_dimension=0, tiled=True),
        lax.psum_scatter(totals[8], ("blk", "head"), scatter_dimension=0, tiled=True),
        lax.psum_scatter(totals[9], ("blk", "head"), scatter_dimension=0, tiled=True),
        lax.psum_scatter(totals[10], ("blk", "head"), scatter_dimension=0, tiled=True),
        lax.psum_scatter(totals[11], ("blk", "head"), scatter_dimension=0, tiled=True),
        lax.psum_scatter(totals[12], ("blk", "head"), scatter_dimension=0, tiled=True),
    )
    return (
        jnp.stack(outputs),
        jnp.stack(input_grads),
        final[0],
        final[1],
        final[2],
        final[3],
        final[4],
        final[5],
        final[6],
        final[7],
        final[8],
        final[9],
        final[10],
        final[11],
        final[12],
    )


RUN = 64
BLOCK = 1024
NEG = -1000000000.0
VM = pltpu.VMEM
SM = pltpu.SMEM


def dot_nt(left, right):
    return lax.dot_general(left, right, (((1,), (1,)), ((), ())), preferred_element_type=jnp.float32)


def dot_nn(left, right):
    return lax.dot_general(left, right, (((1,), (0,)), ((), ())), preferred_element_type=jnp.float32)


def rows_at(index, size):
    return pl.ds(pl.multiple_of(index * size, size), size)


def first_block(start, bound):
    return jnp.where(start >= bound, bound // BLOCK, 0)


def clear_block(block, bound):
    last = (block + 1) * BLOCK - 1
    return jnp.where(last >= bound, jnp.minimum((bound + BLOCK - 1) // BLOCK, block), 0)


def forward_kernel(head_size, bound_ref, inloc, outloc, qkv, out, qs, ks, vs, attn_t, lse, vt, mixed):
    tokens = qkv.shape[0]
    runs = tokens // RUN
    scale = head_size ** (-0.5)
    bound = bound_ref[0]

    @pl.loop(0, runs, unroll=8)
    def _(run):
        rows = qkv[rows_at(inloc[run], RUN), :]
        here = rows_at(run, RUN)
        qs[here, :] = (rows[:, :head_size].astype(jnp.float32) * scale).astype(jnp.bfloat16)
        ks[here, :] = rows[:, head_size : 2 * head_size]
        vs[here, :] = rows[:, 2 * head_size :]

    @pl.loop(0, tokens // BLOCK, unroll=4)
    def _(block):
        here = rows_at(block, BLOCK)
        vt[:, here] = vs[here, :].astype(jnp.float32).T.astype(jnp.bfloat16)

    @pl.loop(0, tokens // BLOCK)
    def _(block):
        start = block * BLOCK
        here = rows_at(block, BLOCK)
        queries = qs[here, :]
        query_pos = start + lax.broadcasted_iota(jnp.int32, (1, BLOCK), 1)
        floor = jnp.where(query_pos >= bound, bound, 0)

        def scores_of(index, diagonal, bounded=True):
            keys = ks[rows_at(index, BLOCK), :]
            scores = dot_nt(keys, queries)
            if not bounded:
                return scores
            key_pos = index * BLOCK + lax.broadcasted_iota(jnp.int32, (BLOCK, BLOCK), 0)
            visible = key_pos >= floor
            if diagonal:
                visible = visible & (key_pos <= query_pos)
            return jnp.where(visible, scores, NEG)

        scores = scores_of(block, True)
        highest = jnp.max(scores, axis=0, keepdims=True)
        weights = jnp.exp(scores - highest)
        total = jnp.sum(weights, axis=0, keepdims=True)
        accum = dot_nn(vt[:, here], weights.astype(jnp.bfloat16))

        def step(bounded, index, state):
            highest, total, accum = state
            scores = scores_of(index, False, bounded)
            higher = jnp.maximum(highest, jnp.max(scores, axis=0, keepdims=True))
            weights = jnp.exp(scores - higher)
            factor = jnp.exp(highest - higher)
            total = total * factor + jnp.sum(weights, axis=0, keepdims=True)
            accum = accum * factor + dot_nn(vt[:, rows_at(index, BLOCK)], weights.astype(jnp.bfloat16))
            return higher, total, accum

        first, clear = first_block(start, bound), clear_block(block, bound)
        state = lax.fori_loop(first, clear, functools.partial(step, True), (highest, total, accum))
        highest, total, accum = lax.fori_loop(clear, block, functools.partial(step, False), state)
        result = accum / total
        attn_t[:, here] = result.astype(jnp.bfloat16)
        lse[:, here] = highest + jnp.log(total)
        result = result.T.astype(jnp.bfloat16)
        for part in range(BLOCK // RUN):
            mixed[rows_at(outloc[block * (BLOCK // RUN) + part], RUN), :] = result[part * RUN : (part + 1) * RUN]

    chips, _, span = out.shape

    @pl.loop(0, chips, unroll=8)
    def _(chip):
        out[chip] = mixed[rows_at(chip, span), :].astype(jnp.float32).T.astype(jnp.bfloat16)


def attend_forward(bound, inloc, outloc, qkv, chips, head_size):
    tokens = qkv.shape[0]
    bf16 = jnp.bfloat16
    pairs = tokens * (tokens // 2)
    return pl.pallas_call(
        functools.partial(forward_kernel, head_size),
        out_shape=(
            jax.ShapeDtypeStruct((chips, head_size, tokens // chips), bf16),
            jax.ShapeDtypeStruct((tokens, head_size), bf16),
            jax.ShapeDtypeStruct((tokens, head_size), bf16),
            jax.ShapeDtypeStruct((tokens, head_size), bf16),
            jax.ShapeDtypeStruct((head_size, tokens), bf16),
            jax.ShapeDtypeStruct((1, tokens), jnp.float32),
        ),
        in_specs=[pl.BlockSpec(memory_space=SM)] * 3 + [pl.BlockSpec(memory_space=VM)],
        out_specs=[pl.BlockSpec(memory_space=VM)] * 6,
        scratch_shapes=[VM((head_size, tokens), bf16), VM((tokens, head_size), bf16)],
        compiler_params=pltpu.CompilerParams(vmem_limit_bytes=40 * 1024 * 1024),
        cost_estimate=pl.CostEstimate(flops=4 * 4 * pairs * head_size, bytes_accessed=tokens * 2048, transcendentals=pairs),
        name="attend_forward",
    )(bound, inloc, outloc, qkv)


def backward_kernel(
    head_size, count, share, bound_ref, inloc, outloc, grad_t, qs, ks, vs, attn_t, lse, *refs
):
    pieces = refs[:count]
    send_out, normed, raw, grads, kt, dk, dv, mixed, wide, moved, sem = refs[count:]
    tokens = qs.shape[0]
    runs = tokens // RUN
    scale = head_size ** (-0.5)
    bound = bound_ref[0]
    chips, _, span = grad_t.shape
    copies, filled = [], 0
    for piece in pieces:
        copies.append(pltpu.make_async_copy(piece, normed.at[pl.ds(filled, piece.shape[0])], sem))
        filled += piece.shape[0]
    for copy in copies:
        copy.start()

    @pl.loop(0, chips, unroll=8)
    def _(chip):
        mixed[rows_at(chip, span), :] = grad_t[chip, :head_size, :].astype(jnp.float32).T.astype(jnp.bfloat16)

    @pl.loop(0, runs, unroll=8)
    def _(run):
        grads[rows_at(run, RUN), :] = mixed[rows_at(outloc[run], RUN), :]

    @pl.loop(0, tokens // BLOCK, unroll=4)
    def _(block):
        here = rows_at(block, BLOCK)
        kt[:, here] = ks[here, :].astype(jnp.float32).T.astype(jnp.bfloat16)

    @pl.loop(0, tokens // BLOCK)
    def _(block):
        start = block * BLOCK
        here = rows_at(block, BLOCK)
        queries = qs[here, :]
        grad = grads[here, :]
        log_total = lse[:, here]
        delta = jnp.sum(grad.astype(jnp.float32).T * attn_t[:, here].astype(jnp.float32), axis=0, keepdims=True)
        query_pos = start + lax.broadcasted_iota(jnp.int32, (1, BLOCK), 1)
        floor = jnp.where(query_pos >= bound, bound, 0)

        def one(index, diagonal, bounded=True):
            there = rows_at(index, BLOCK)
            scores = dot_nt(ks[there, :], queries)
            probs = jnp.exp(scores - log_total)
            if bounded:
                key_pos = index * BLOCK + lax.broadcasted_iota(jnp.int32, (BLOCK, BLOCK), 0)
                visible = key_pos >= floor
                if diagonal:
                    visible = visible & (key_pos <= query_pos)
                probs = jnp.where(visible, probs, 0.0)
            grad_probs = dot_nt(vs[there, :], grad)
            grad_scores = (probs * (grad_probs - delta)).astype(jnp.bfloat16)
            return (
                dot_nn(probs.astype(jnp.bfloat16), grad),
                dot_nn(grad_scores, queries),
                dot_nn(kt[:, there], grad_scores),
                there,
            )

        grad_v, grad_k, grad_q, there = one(block, True)
        dv[there, :] = grad_v
        dk[there, :] = grad_k

        def step(bounded, index, grad_q):
            grad_v, grad_k, term, there = one(index, False, bounded)
            dv[there, :] += grad_v
            dk[there, :] += grad_k
            return grad_q + term

        first, clear = first_block(start, bound), clear_block(block, bound)
        grad_q = lax.fori_loop(first, clear, functools.partial(step, True), grad_q)
        grad_q = lax.fori_loop(clear, block, functools.partial(step, False), grad_q)
        wide[here, :head_size] = (grad_q.T * scale).astype(jnp.bfloat16)

    wide[:, head_size : 2 * head_size] = dk[...].astype(jnp.bfloat16)
    wide[:, 2 * head_size :] = dv[...].astype(jnp.bfloat16)

    size = 3 * head_size

    @pl.loop(0, runs, unroll=8)
    def _(run):
        moved[rows_at(outloc[run], RUN), :] = wide[rows_at(run, RUN), :]

    @pl.loop(0, chips, unroll=8)
    def _(chip):
        send_out[chip, :size, :] = moved[rows_at(chip, span), :].astype(jnp.float32).T.astype(jnp.bfloat16)

    @pl.loop(0, runs, unroll=8)
    def _(run):
        moved[rows_at(inloc[run], RUN), :] = wide[rows_at(run, RUN), :]

    for copy in copies:
        copy.wait()
    raw[...] = jnp.zeros_like(raw)

    @pl.loop(0, tokens // BLOCK)
    def _(block):
        here = rows_at(block, BLOCK)
        turned = moved[here, :].astype(jnp.float32).T.astype(jnp.bfloat16)
        raw[...] += dot_nn(turned, normed[here, :])

    product = raw[...].T
    sums = jnp.sum(wide[...].astype(jnp.float32), axis=0, keepdims=True)
    high = sums.astype(jnp.bfloat16).astype(jnp.float32)
    tail = jnp.concatenate([high, sums - high, jnp.zeros((14, size), jnp.float32)], axis=0)
    for chip in range(chips):
        first = chip // 2 * 4 * share + chip % 2 * share
        rows = jnp.concatenate([product[first : first + share], product[first + 2 * share : first + 3 * share], tail], axis=0)
        rows = jnp.concatenate([rows, jnp.zeros((rows.shape[0], span - size), jnp.float32)], axis=1)
        send_out[chip, size:, :] = rows.astype(jnp.bfloat16)


def attend_backward(bound, inloc, outloc, grad_t, qs, ks, vs, attn_t, lse, pieces, share):
    tokens, head_size = qs.shape
    chips = grad_t.shape[0]
    width = pieces[0].shape[1]
    bf16 = jnp.bfloat16
    pairs = tokens * (tokens // 2)
    return pl.pallas_call(
        functools.partial(backward_kernel, head_size, len(pieces), share),
        out_shape=jax.ShapeDtypeStruct((chips, 3 * head_size + 2 * share + 16, tokens // chips), bf16),
        in_specs=[pl.BlockSpec(memory_space=SM)] * 3 + [pl.BlockSpec(memory_space=VM)] * 6
        + [pl.BlockSpec(memory_space=pltpu.HBM)] * len(pieces),
        out_specs=pl.BlockSpec(memory_space=VM),
        scratch_shapes=[
            VM((tokens, width), bf16),
            VM((3 * head_size, width), jnp.float32),
            VM((tokens, head_size), bf16),
            VM((head_size, tokens), bf16),
            VM((tokens, head_size), jnp.float32),
            VM((tokens, head_size), jnp.float32),
            VM((tokens, head_size), bf16),
            VM((tokens, 3 * head_size), bf16),
            VM((tokens, 3 * head_size), bf16),
            pltpu.SemaphoreType.DMA,
        ],
        compiler_params=pltpu.CompilerParams(vmem_limit_bytes=48 * 1024 * 1024),
        cost_estimate=pl.CostEstimate(flops=4 * 10 * pairs * head_size, bytes_accessed=tokens * 4096, transcendentals=pairs),
        name="attend_backward",
    )(bound, inloc, outloc, grad_t, qs, ks, vs, attn_t, lse, *pieces)


HALF_STEP = 1024


def gelu_pair(values):
    cubic = values * values
    inner = 0.7978845608028654 * values * (1.0 + 0.044715 * cubic)
    bent = jnp.tanh(inner)
    slope = 0.7978845608028654 * (1.0 + 0.134145 * cubic)
    half = 0.5 * (1.0 + bent)
    return values * half, half + 0.5 * values * (1.0 - bent * bent) * slope


def load_rows(table, pieces, targets, sem, wait):
    slot = 0
    for piece in pieces:
        count = piece.shape[0]

        @pl.loop(0, count, unroll=4)
        def _(index, piece=piece, slot=slot):
            chip = table[0, slot + index]
            for rows, target in targets(chip):
                copy = pltpu.make_async_copy(piece.at[index, rows], target, sem)
                if wait:
                    copy.wait()
                else:
                    copy.start()

        slot += count


def project_kernel(count, table, got, *refs):
    pieces, (part_out, sent_a, sent_b, attn_in, w_out, sem) = refs[:count], refs[count:]
    chips, size, span = got.shape
    share = w_out.shape[0] // chips
    rows = span // 2

    def targets(chip):
        return [(pl.ds(0, share), w_out.at[rows_at(chip, share)])]

    load_rows(table, pieces, targets, sem, False)
    for chip in range(chips):
        micro, head = divmod(chip, chips // 2)
        for rel in range(2):
            column = (rel * 2 + micro) * rows
            attn_in[head * size : (head + 1) * size, column : column + rows] = got[chip, :, rel * rows : (rel + 1) * rows]
    load_rows(table, pieces, targets, sem, True)
    left = attn_in[...].astype(jnp.float32).T.astype(jnp.bfloat16)
    part = dot_nn(left, w_out[...])
    part_out[...] = part
    own = sent_a.shape[0]
    sent_a[...] = part[:own].astype(jnp.bfloat16)
    sent_b[...] = part[own:].astype(jnp.bfloat16)


def project(table, got, pieces, share):
    chips, size, span = got.shape
    width = pieces[0].shape[2]
    tokens = 2 * span
    bf16 = jnp.bfloat16
    return pl.pallas_call(
        functools.partial(project_kernel, len(pieces)),
        out_shape=(
            jax.ShapeDtypeStruct((tokens, width), jnp.float32),
            jax.ShapeDtypeStruct((tokens // 2, width), bf16),
            jax.ShapeDtypeStruct((tokens // 2, width), bf16),
            jax.ShapeDtypeStruct((chips // 2 * size, tokens), bf16),
        ),
        in_specs=[pl.BlockSpec(memory_space=SM), pl.BlockSpec(memory_space=VM)]
        + [pl.BlockSpec(memory_space=pltpu.HBM)] * len(pieces),
        out_specs=[pl.BlockSpec(memory_space=VM)] * 4,
        scratch_shapes=[VM((chips * share, width), bf16), pltpu.SemaphoreType.DMA],
        compiler_params=pltpu.CompilerParams(vmem_limit_bytes=58 * 1024 * 1024),
        cost_estimate=pl.CostEstimate(
            flops=2 * tokens * chips * share * width, bytes_accessed=8 * tokens * width, transcendentals=0
        ),
        name="project",
    )(table, got, *pieces)


def middle_kernel(count, share, table, x_a, x_b, g_a, g_b, part, got_a, got_b, *refs):
    pieces = refs[:count]
    (resid, base, other, grad_act, sent_a, sent_b, fc_sums, vectors, terms) = refs[count : count + 9]
    (smalls, fc_bias, w_fc, w_proj, g_all, act, act_t, rest, proj_buf, fc_buf, small_sem, load_sem, proj_sem, fc_sem) = refs[count + 9 :]
    f32, bf16 = jnp.float32, jnp.bfloat16
    tokens, width = part.shape
    own = tokens // 2
    hidden = w_proj.shape[0]
    chips = terms.shape[0]
    each = hidden // chips
    folds = hidden // width
    fc_row = share + each

    def targets(chip):
        wanted = [(pl.ds(share, each), w_proj.at[rows_at(chip, each)])]
        for fold in range(folds):
            for core in range(2):
                first = fc_row + (fold * 2 + core) * share
                place = ((chip // 2) * 2 + core) * 2 + chip % 2
                wanted.append(
                    (pl.ds(first, share), w_fc.at[rows_at(place, share), pl.ds(fold * width, width)])
                )
        return wanted

    def small_targets(chip):
        return [(pl.ds(pieces[0].shape[1] - 16, 16), smalls.at[chip])]

    load_rows(table, pieces, small_targets, small_sem, False)
    load_rows(table, pieces, targets, load_sem, False)
    load_rows(table, pieces, small_targets, small_sem, True)
    small_sum = jnp.sum(smalls[...].astype(f32), axis=0)
    vectors[...] = small_sum[:8]
    for fold in range(folds):
        fc_bias[:, fold * width : (fold + 1) * width] = small_sum[8 + fold : 9 + fold]
    for half, (x_in, g_in, arrived) in enumerate(((x_a, g_a, got_a), (x_b, g_b, got_b))):
        here = slice(half * own, (half + 1) * own)
        g_all[here, :] = g_in[...]
        value = x_in[...].astype(f32) + part[here, :] + arrived[...].astype(f32) + vectors[2:3, :]
        resid[here, :] = value
        centred = value - jnp.mean(value, axis=-1, keepdims=True)
        inverse = lax.rsqrt(jnp.mean(centred * centred, axis=-1, keepdims=True) + 1e-05)
        rounded = (centred * inverse * vectors[0:1, :] + vectors[1:2, :]).astype(bf16)
        act[here, :] = rounded
        act_t[:, here] = rounded.astype(f32).T.astype(bf16)
    base[...] = resid[:own, :] + vectors[3:4, :]
    load_rows(table, pieces, targets, load_sem, True)

    per_step = HALF_STEP // each

    def copies(step, slot):
        made = []
        for index in range(per_step):
            made.append(
                pltpu.make_async_copy(
                    proj_buf.at[slot, pl.ds(index * each, each)],
                    terms.at[table[1, step * per_step + index], pl.ds(0, each)],
                    proj_sem.at[slot],
                )
            )
        fold = step // (width // HALF_STEP)
        column = pl.multiple_of(step % (width // HALF_STEP) * HALF_STEP, HALF_STEP)
        for chip in range(chips):
            for core in range(2):
                place = ((chip // 2) * 2 + core) * 2 + chip % 2
                made.append(
                    pltpu.make_async_copy(
                        fc_buf.at[slot, pl.ds(place * share, share)],
                        terms.at[
                            table[1, chip],
                            pl.ds(pl.multiple_of(each + share + (fold * 2 + core) * share, 16), share),
                            pl.ds(column, HALF_STEP),
                        ],
                        fc_sem.at[slot],
                    )
                )
        return made

    steps = hidden // HALF_STEP

    @pl.loop(0, steps)
    def _(step):
        slot = step % 2
        columns = pl.ds(pl.multiple_of(step * HALF_STEP, HALF_STEP), HALF_STEP)
        rows = rows_at(step, HALF_STEP)

        @pl.when(step >= 2)
        def _():
            for copy in copies(step - 2, slot):
                copy.wait()

        grads = g_all[...]
        value, slope = gelu_pair(dot_nn(act[...], w_fc[:, columns]) + fc_bias[:, columns])
        value = value.astype(bf16)
        proj_buf[slot] = dot_nn(value.astype(f32).T.astype(bf16), grads).astype(bf16)
        grad_pre = (dot_nt(grads, w_proj[rows, :]) * slope).astype(bf16)
        fc_sums[:, columns] = jnp.sum(grad_pre.astype(f32), axis=0, keepdims=True)
        fc_buf[slot] = dot_nn(act_t[...], grad_pre).astype(bf16)
        for copy in copies(step, slot):
            copy.start()
        projected = dot_nn(value, w_proj[rows, :])
        back = dot_nt(grad_pre, w_fc[:, columns])
        base[...] += projected[:own]

        @pl.when(step == 0)
        def _():
            grad_act[...] = back
            rest[...] = projected[own:]

        @pl.when(step > 0)
        def _():
            grad_act[...] += back
            rest[...] += projected[own:]

    other[...] = rest[...].astype(bf16)
    sent_a[...] = grad_act[:own, :].astype(bf16)
    sent_b[...] = grad_act[own:, :].astype(bf16)
    for step in range(steps - 2, steps):
        for copy in copies(step, step % 2):
            copy.wait()


def middle(table, x_a, x_b, g_a, g_b, part, got_a, got_b, pieces, share, hidden):
    tokens, width = part.shape
    f32, bf16 = jnp.float32, jnp.bfloat16
    chips = table.shape[1]
    each = hidden // chips
    rows = share + each + 2 * share * (hidden // width)
    shape = jax.ShapeDtypeStruct
    return pl.pallas_call(
        functools.partial(middle_kernel, len(pieces), share),
        out_shape=(
            shape((tokens, width), f32),
            shape((tokens // 2, width), f32),
            shape((tokens // 2, width), bf16),
            shape((tokens, width), f32),
            shape((tokens // 2, width), bf16),
            shape((tokens // 2, width), bf16),
            shape((1, hidden), f32),
            shape((8, width), f32),
            shape((chips, rows, width), bf16),
        ),
        in_specs=[pl.BlockSpec(memory_space=SM)]
        + [pl.BlockSpec(memory_space=VM)] * 7
        + [pl.BlockSpec(memory_space=pltpu.HBM)] * len(pieces),
        out_specs=[pl.BlockSpec(memory_space=VM)] * 8 + [pl.BlockSpec(memory_space=pltpu.HBM)],
        scratch_shapes=[
            VM((chips, 16, width), bf16),
            VM((1, hidden), f32),
            VM((width, hidden), bf16),
            VM((hidden, width), bf16),
            VM((tokens, width), bf16),
            VM((tokens, width), bf16),
            VM((width, tokens), bf16),
            VM((tokens // 2, width), f32),
            VM((2, HALF_STEP, width), bf16),
            VM((2, width, HALF_STEP), bf16),
            pltpu.SemaphoreType.DMA,
            pltpu.SemaphoreType.DMA,
            pltpu.SemaphoreType.DMA((2,)),
            pltpu.SemaphoreType.DMA((2,)),
        ],
        compiler_params=pltpu.CompilerParams(vmem_limit_bytes=56 * 1024 * 1024),
        cost_estimate=pl.CostEstimate(
            flops=12 * tokens * width * hidden, bytes_accessed=8 * width * hidden, transcendentals=tokens * hidden
        ),
        name="middle",
    )(table, x_a, x_b, g_a, g_b, part, got_a, got_b, *pieces)


def branch_kernel(share, row, table, resid, g_a, g_b, part, got_a, got_b, vectors, fc_sums, attn_in, given, grad_resid, branch, tails, terms, products, sem):
    f32, bf16 = jnp.float32, jnp.bfloat16
    tokens, width = resid.shape
    own = tokens // 2
    chips = tails.shape[0]
    gain_sum = jnp.zeros((1, width), f32)
    shift_sum = jnp.zeros((1, width), f32)
    bias_sum = jnp.zeros((1, width), f32)
    proj_sum = jnp.zeros((1, width), f32)
    for half, (g_in, arrived) in enumerate(((g_a, got_a), (g_b, got_b))):
        here = slice(half * own, (half + 1) * own)
        value = resid[here, :]
        centred = value - jnp.mean(value, axis=-1, keepdims=True)
        inverse = lax.rsqrt(jnp.mean(centred * centred, axis=-1, keepdims=True) + 1e-05)
        normed = centred * inverse
        grad = part[here, :] + arrived[...].astype(f32)
        gain_sum += jnp.sum(grad * normed, axis=0, keepdims=True)
        shift_sum += jnp.sum(grad, axis=0, keepdims=True)
        scaled = grad * vectors[0:1, :]
        given_grad = g_in[...].astype(f32)
        total = given_grad + inverse * (
            scaled
            - jnp.mean(scaled, axis=-1, keepdims=True)
            - normed * jnp.mean(scaled * normed, axis=-1, keepdims=True)
        )
        rounded = total.astype(bf16)
        bias_sum += jnp.sum(rounded.astype(f32), axis=0, keepdims=True)
        proj_sum += jnp.sum(given_grad, axis=0, keepdims=True)
        branch[here, :] = rounded
        if half == 0:
            grad_resid[...] = total
    group = width // (chips // 2)
    sums = jnp.concatenate([gain_sum, shift_sum, bias_sum, proj_sum], axis=0)
    each = fc_sums.shape[1] // chips
    for chip in range(chips):
        first = chip // 2 * group
        tail = jnp.concatenate(
            [
                sums[:, first : first + group],
                fc_sums[:, chip * each : (chip + 1) * each],
                jnp.zeros((3, group), f32),
            ],
            axis=0,
        )
        high = tail.astype(bf16)
        low = (tail - high.astype(f32)).astype(bf16)
        tails[chip] = jnp.concatenate([high, low], axis=1)
    products[...] = dot_nn(attn_in[...], branch[...]).astype(bf16)

    @pl.loop(0, chips)
    def _(chip):
        pltpu.make_async_copy(products.at[rows_at(chip, share)], terms.at[table[1, chip], pl.ds(row, share)], sem).start()

    @pl.loop(0, chips)
    def _(chip):
        pltpu.make_async_copy(products.at[rows_at(chip, share)], terms.at[table[1, chip], pl.ds(row, share)], sem).wait()


def branch_back(table, resid, g_a, g_b, part, got_a, got_b, vectors, fc_sums, attn_in, terms, share, row, span):
    tokens, width = resid.shape
    f32, bf16 = jnp.float32, jnp.bfloat16
    chips = table.shape[1]
    shape = jax.ShapeDtypeStruct
    return pl.pallas_call(
        functools.partial(branch_kernel, share, row),
        out_shape=(
            shape((tokens // 2, width), f32),
            shape((tokens, width), bf16),
            shape((chips, 8, span), bf16),
            shape(terms.shape, bf16),
        ),
        in_specs=[pl.BlockSpec(memory_space=SM)]
        + [pl.BlockSpec(memory_space=VM)] * 9
        + [pl.BlockSpec(memory_space=pltpu.HBM)],
        out_specs=[pl.BlockSpec(memory_space=VM)] * 3 + [pl.BlockSpec(memory_space=pltpu.HBM)],
        scratch_shapes=[VM((chips * share, width), bf16), pltpu.SemaphoreType.DMA],
        input_output_aliases={10: 3},
        compiler_params=pltpu.CompilerParams(vmem_limit_bytes=40 * 1024 * 1024),
        cost_estimate=pl.CostEstimate(
            flops=2 * tokens * chips * share * width, bytes_accessed=16 * tokens * width, transcendentals=0
        ),
        name="branch_back",
    )(table, resid, g_a, g_b, part, got_a, got_b, vectors, fc_sums, attn_in, terms)


def attention_back_kernel(count, table, branch, tails, *refs):
    pieces, (sent, w_out, sem) = refs[:count], refs[count:]
    chips, size, span = sent.shape
    size -= 8
    rows = span // 2
    share = w_out.shape[0] // chips

    def targets(chip):
        return [(pl.ds(0, share), w_out.at[rows_at(chip, share)])]

    load_rows(table, pieces, targets, sem, False)
    sent[:, size:, :] = tails[...]
    load_rows(table, pieces, targets, sem, True)
    grads = dot_nt(w_out[...], branch[...]).astype(jnp.bfloat16)
    for chip in range(chips):
        micro, head = divmod(chip, chips // 2)
        for rel in range(2):
            column = (rel * 2 + micro) * rows
            sent[chip, :size, rel * rows : (rel + 1) * rows] = grads[
                head * size : (head + 1) * size, column : column + rows
            ]


def attention_back(table, branch, tails, pieces, share, size):
    tokens, width = branch.shape
    chips, _, span = tails.shape
    bf16 = jnp.bfloat16
    return pl.pallas_call(
        functools.partial(attention_back_kernel, len(pieces)),
        out_shape=jax.ShapeDtypeStruct((chips, size + 8, span), bf16),
        in_specs=[pl.BlockSpec(memory_space=SM)]
        + [pl.BlockSpec(memory_space=VM)] * 2
        + [pl.BlockSpec(memory_space=pltpu.HBM)] * len(pieces),
        out_specs=pl.BlockSpec(memory_space=VM),
        scratch_shapes=[VM((chips * share, width), bf16), pltpu.SemaphoreType.DMA],
        compiler_params=pltpu.CompilerParams(vmem_limit_bytes=58 * 1024 * 1024),
        cost_estimate=pl.CostEstimate(
            flops=2 * tokens * chips * share * width, bytes_accessed=4 * tokens * width, transcendentals=0
        ),
        name="attention_back",
    )(table, branch, tails, *pieces)


def finish_kernel(order, got, weights, kept, sent, weight, grads, sem):
    chips, _, span = got.shape
    size = weight.shape[0] // len(order)
    rows = span // 2
    own = kept.shape[0]

    def copies():
        return [
            pltpu.make_async_copy(weights.at[slot], weight.at[pl.ds(head * size, size)], sem)
            for slot, head in enumerate(order)
        ]

    for copy in copies():
        copy.start()
    for chip in range(chips):
        micro, head = divmod(chip, chips // 2)
        turned = got[chip, :size, :].astype(jnp.float32).T.astype(jnp.bfloat16)
        for rel in range(2):
            row = (rel * 2 + micro) * rows
            grads[head, row : row + rows, :] = turned[rel * rows : (rel + 1) * rows]
    for copy in copies():
        copy.wait()
    left = jnp.concatenate([grads[head] for head in range(len(order))], axis=1)
    back = dot_nn(left, weight[...])
    kept[...] = back[:own]
    sent[...] = back[own:].astype(jnp.bfloat16)


def finish(got, weights, order):
    chips, _, span = got.shape
    heads, size, width = weights.shape
    bf16 = jnp.bfloat16
    return pl.pallas_call(
        functools.partial(finish_kernel, order),
        out_shape=(
            jax.ShapeDtypeStruct((span, width), jnp.float32),
            jax.ShapeDtypeStruct((span, width), bf16),
        ),
        in_specs=[pl.BlockSpec(memory_space=VM), pl.BlockSpec(memory_space=pltpu.HBM)],
        out_specs=[pl.BlockSpec(memory_space=VM)] * 2,
        scratch_shapes=[
            VM((heads * size, width), bf16),
            VM((heads, 2 * span, size), bf16),
            pltpu.SemaphoreType.DMA,
        ],
        compiler_params=pltpu.CompilerParams(vmem_limit_bytes=58 * 1024 * 1024),
        cost_estimate=pl.CostEstimate(
            flops=4 * span * width * heads * size,
            bytes_accessed=2 * width * heads * size + 8 * span * width,
            transcendentals=0,
        ),
        name="finish",
    )(got, weights)


def unpack_kernel(share, core_ref, summed, given, proj, out, merged):
    f32 = jnp.float32
    core = core_ref[0]
    folds, _, width = given.shape
    each = proj.shape[0]
    proj[...] = summed[:each, :].astype(f32)
    out[...] = summed[each : each + share, :].astype(f32)
    group = each
    for fold in range(folds):
        first = pl.multiple_of(each + share + (fold * 2 + core) * share, share)
        for owner, rows in ((core, summed[pl.ds(first, share), :]), (1 - core, given[fold])):
            rows = rows.astype(f32)
            for index in range(width // group):
                number = fold * (width // group) + index
                place = ((number // 2 * 2 + owner) * 2 + number % 2) * group
                merged[:, pl.ds(pl.multiple_of(place, group), group)] = rows[:, index * group : (index + 1) * group]


def unpack(core, summed, given, share, each):
    folds, _, width = given.shape
    f32 = jnp.float32
    return pl.pallas_call(
        functools.partial(unpack_kernel, share),
        out_shape=(
            jax.ShapeDtypeStruct((each, width), f32),
            jax.ShapeDtypeStruct((share, width), f32),
            jax.ShapeDtypeStruct((share, 2 * folds * width), f32),
        ),
        in_specs=[pl.BlockSpec(memory_space=SM)] + [pl.BlockSpec(memory_space=VM)] * 2,
        out_specs=[pl.BlockSpec(memory_space=VM)] * 3,
        cost_estimate=pl.CostEstimate(flops=0, bytes_accessed=6 * summed.size, transcendentals=0),
        name="unpack",
    )(core, summed, given)


PATHS = (("x", "z", "head"), ("head", "z", "x"))


PAIR = [(0, 1), (1, 0)]
NEAR = [(0, 1), (1, 0), (2, 3), (3, 2)]
FAR = [(0, 2), (2, 0), (1, 3), (3, 1)]


def swap(values, axis, pairs=PAIR):
    return lax.ppermute(values, axis, pairs)


def across(values, axis):
    return swap(values, axis, NEAR if axis == "z" else PAIR)


def in_order(mine, other, index, axis):
    first = jnp.where(index == 0, mine, other)
    second = jnp.where(index == 0, other, mine)
    return jnp.stack([first, second], axis=axis)


def split_float(values):
    high = values.astype(jnp.bfloat16)
    low = (values - high.astype(jnp.float32)).astype(jnp.bfloat16)
    return high, low


def run_table(order, pair_start):
    pairs = order.shape[0]
    runs = jnp.arange(2 * pairs, dtype=jnp.int32)[:, None]
    low = jnp.where(runs == order[None, :], pair_start[None, :], 0)
    high = jnp.where(runs == 2 * pairs - 1 - order[None, :], pair_start[None, :] + 1, 0)
    return jnp.sum(low + high, axis=1).astype(jnp.int32)


def ring_order(count, turn):
    half = [(z, (z + step + turn) % 2) for z in range(count) for step in range(2)]
    return [z * 4 + y for z, y in half] + [z * 4 + 2 + y for z, y in reversed(half)]


def core_groups(rings):
    return [[(chip // 2 * 2 + core) * 2 + chip % 2 for chip in ring] for core, ring in enumerate(rings)]


def cube_orders(depth):
    cycle = [0, 1, 3, 2, 6, 7, 5, 4]
    return [[chip + start for chip in cycle] for start in (0, 4 * depth)]


def fast_body(
    block_input,
    qkv_weight,
    q_bias,
    v_bias,
    out_weight,
    out_bias,
    norm1_gain,
    norm1_shift,
    norm2_gain,
    norm2_shift,
    fc_weight,
    fc_bias,
    proj_weight,
    proj_bias,
    out_grad,
    dealt,
    lengths,
):
    f32, bf16 = jnp.float32, jnp.bfloat16
    micro, rows, width = block_input.shape
    nz, nx = lax.axis_size("z"), lax.axis_size("x")
    iz, ix, ic, iy = (lax.axis_index(name) for name in ("z", "x", "core", "head"))
    zx = nz * nx
    every, chips = ("z", "x", "core", "head"), ("z", "x", "head")
    devices, chip_count = 4 * zx, 2 * zx
    heads = 2 * zx
    local = heads * DH // 2
    share = qkv_weight.shape[0]
    hidden_share = proj_weight.shape[0]
    hidden_half = hidden_share * chip_count

    inputs = block_input.astype(f32)
    normed_one, inverse_one = normalize(inputs)
    n1 = normed_one.astype(bf16)
    n1, qkv_weight, fc_weight, norm1_gain, norm2_gain = lax.optimization_barrier(
        (n1, qkv_weight, fc_weight, norm1_gain, norm2_gain)
    )
    gain_one = norm1_gain.astype(f32)
    shift_one = norm1_shift.astype(f32)
    raw_qkv = qkv_weight.astype(f32)
    scaled_qkv = (raw_qkv * gain_one[:, None]).astype(bf16)
    device = ((iz * nx + ix) * 2 + ic) * 2 + iy
    offset = jnp.sum(raw_qkv * shift_one[:, None], axis=0)
    zero = jnp.zeros((width,), f32)
    place = device * share
    offset = offset + jnp.concatenate(
        [
            lax.dynamic_update_slice(zero, q_bias.astype(f32), (place,)),
            zero,
            lax.dynamic_update_slice(zero, v_bias.astype(f32), (place,)),
        ]
    )
    high, low = split_float(offset)
    to_heads = jnp.concatenate([scaled_qkv, high[None], low[None], jnp.zeros((6, 3 * width), bf16)], axis=0)
    to_heads = to_heads.reshape(share + 8, 3, zx // 2, 2, 2, DH).transpose(2, 4, 3, 0, 1, 5)
    to_heads = to_heads.reshape(1, heads, share + 8, 3 * DH)
    to_heads = jnp.broadcast_to(to_heads, (2, heads, share + 8, 3 * DH)).reshape(devices, share + 8, 3 * DH)
    head_rows = lax.all_to_all(to_heads, every, split_axis=0, concat_axis=0, tiled=True)
    head_weight = head_rows[:, :share].reshape(width, 3 * DH)
    head_offset = jnp.sum(head_rows[:, share : share + 2].astype(f32), axis=(0, 1))

    mine = iz // 2
    near = lax.dynamic_index_in_dim(n1, mine, 0, keepdims=False)
    far = swap(lax.dynamic_index_in_dim(n1, 1 - mine, 0, keepdims=False), "z", FAR)
    paths = PATHS
    got = across(near, paths[0][0])
    far, got = lax.optimization_barrier((far, got))
    near = jnp.stack([near, got])
    near_got, far_got = across(near, paths[0][1]), across(far, paths[1][0])
    near_got, far_got = lax.optimization_barrier((near_got, far_got))
    near, far = jnp.stack([near, near_got]), jnp.stack([far, far_got])
    near_got, far_got = across(near, paths[0][2]), across(far, paths[1][1])
    far = jnp.stack([far, far_got])
    parts = [near, near_got, far, across(far, paths[1][2])]
    pieces, owners = [], []

    def add_all(flip):
        core = 1 - ic if flip else ic
        for index, part in enumerate(parts):
            pieces.append((swap(part, "core") if flip else part).reshape(-1, width))
            for second in range(2):
                for first in range(2):
                    flips = dict(zip(paths[index // 2], (first, second, index % 2)))
                    owners.append((iz ^ flips["z"] ^ (index // 2 * 2), ix ^ flips["x"], core, iy ^ flips["head"]))

    add_all(False)
    add_all(True)
    slot_device = jnp.stack([((z * nx + x) * 2 + core) * 2 + y for z, x, core, y in owners]).astype(jnp.int32)
    my_dealt = lax.dynamic_index_in_dim(dealt, mine, 0, keepdims=False)
    order = my_dealt.reshape(devices, rows)[:, 0] // RUN
    slot_of = jnp.sum(
        jnp.where(jnp.arange(devices)[:, None] == slot_device[None, :], jnp.arange(devices)[None, :], 0), axis=1
    )
    inloc = run_table(order, (slot_of * 2).astype(jnp.int32))
    ids = jnp.arange(devices, dtype=jnp.int32)
    id_y, id_c, id_zx = ids % 2, ids // 2 % 2, ids // 4
    send_pair = (id_zx * 2 + id_y) * 2 + (id_c ^ ic)
    outloc = run_table(order, (send_pair * 2).astype(jnp.int32))
    bound = lax.dynamic_index_in_dim(lengths, mine, 0, keepdims=False)[:1]

    fc_parts = fc_weight.reshape(share, zx, 2, 2, hidden_share)

    def core_columns(values, index):
        return lax.dynamic_index_in_dim(values, index, 2, keepdims=False)

    fc_mine = core_columns(fc_parts, ic).reshape(share, hidden_half)
    fc_other = swap(core_columns(fc_parts, 1 - ic).reshape(share, hidden_half), "core")
    fc_pair = in_order(fc_mine, fc_other, ic, 0).reshape(2 * share, hidden_half)
    small = jnp.stack([norm2_gain, norm2_shift, out_bias, proj_bias])
    small_rows = jnp.zeros((16, width), bf16)
    small_rows = lax.dynamic_update_slice(small_rows, small, (0, place))
    other_place = (((iz * nx + ix) * 2 + 1 - ic) * 2 + iy) * share
    small_rows = lax.dynamic_update_slice(small_rows, swap(small, "core"), (0, other_place))
    fc_place = ((iz * nx + ix) * 2 + iy) * hidden_share
    small_rows = lax.dynamic_update_slice(small_rows, fc_bias[None], (8 + fc_place // width, fc_place % width))
    folds = hidden_half // width
    fc_folded = fc_pair.reshape(2 * share, folds, width).transpose(1, 0, 2).reshape(-1, width)
    packed = jnp.concatenate([out_weight, proj_weight, fc_folded, small_rows], axis=0)
    rings = [ring_order(nz, turn) for turn in range(2)]
    places = [[ring.index(chip) for chip in range(chip_count)] for ring in rings]
    table = lax.dynamic_index_in_dim(
        jnp.array([[ring, place] for ring, place in zip(rings, places)], jnp.int32), ic, 0, keepdims=False
    )
    gathered = lax.all_gather(packed, every, axis=0, axis_index_groups=core_groups(rings))
    out_rows = share
    proj_rows = hidden_share
    fc_rows = 2 * share * folds

    mixed = [(product(piece, head_weight) + head_offset).astype(bf16) for piece in pieces]
    slots = jnp.concatenate(mixed, axis=0)
    attn_send, queries, keys, values, attn_t, lse = attend_forward(bound, inloc, outloc, slots, chip_count, DH)

    x_a, x_b = block_input.reshape(-1, width), swap(block_input, "core").reshape(-1, width)
    g_a, g_b = out_grad.reshape(-1, width), swap(out_grad, "core").reshape(-1, width)
    attn_got = lax.all_to_all(attn_send, chips, split_axis=0, concat_axis=0, tiled=True)
    weight_turned, attn_got = lax.optimization_barrier((head_weight.T, attn_got))
    cubes = cube_orders(nz // 2)
    w_qkv = lax.all_gather(weight_turned, chips, axis=0, axis_index_groups=cubes)
    part, sent_a, sent_b, attn_in = project(table, attn_got, [gathered], share)
    resid, base, project_other, grad_part, back_a, back_b, fc_sums, vectors, terms = middle(
        table, x_a, x_b, g_a, g_b, part, swap(sent_b, "core"), swap(sent_a, "core"), [gathered], share, hidden_half
    )
    grad_resid, branch, tails, terms = branch_back(
        table,
        resid,
        g_a,
        g_b,
        grad_part,
        swap(back_b, "core"),
        swap(back_a, "core"),
        vectors,
        fc_sums,
        attn_in,
        terms,
        share,
        proj_rows,
        2 * rows,
    )
    grad_send = attention_back(table, branch, tails, [gathered], share, DH)
    output = (base + swap(project_other, "core").astype(f32)).astype(bf16)

    grad_got = lax.all_to_all(grad_send, chips, split_axis=0, concat_axis=0, tiled=True)
    vector_sums = jnp.sum(grad_got[:, DH:].astype(f32), axis=0)
    vector_sums = vector_sums[:, :rows] + vector_sums[:, rows:]
    final_vectors = lax.dynamic_slice(vector_sums, (0, (ic * 2 + iy) * share), (4, share))
    final_fc_b = vector_sums[4]

    summed = lax.psum_scatter(
        terms, every, scatter_dimension=0, tiled=True, axis_index_groups=core_groups(rings)
    )[0]
    fc_sum = summed[proj_rows + out_rows :].reshape(folds, 2, share, width)
    fc_give = swap(lax.dynamic_index_in_dim(fc_sum, 1 - ic, 1, keepdims=False), "core")
    final_proj_w, final_out_w, final_fc_w = unpack(
        ic.astype(jnp.int32).reshape(1), summed, fc_give, share, hidden_share
    )

    send_grads = attend_backward(
        bound, inloc, outloc, grad_got, queries, keys, values, attn_t, lse, pieces, share
    )
    grads_got = lax.all_to_all(send_grads, chips, split_axis=0, concat_axis=0, tiled=True)
    back_own, back_other = finish(grads_got, w_qkv, cubes[0])
    raw_got = grads_got[:, 3 * DH :, : 3 * DH].astype(f32)
    raw_sum = jnp.sum(raw_got.reshape(2, zx, 2 * share + 16, 3 * DH), axis=0)
    raw_parts = raw_sum[:, : 2 * share].reshape(zx, 2, share, 3 * DH)
    sums_mine = raw_sum[:, 2 * share : 2 * share + 1] + raw_sum[:, 2 * share + 1 : 2 * share + 2]
    raw_keep = jnp.concatenate([lax.dynamic_index_in_dim(raw_parts, ic, 1, keepdims=False), sums_mine], axis=1)
    raw_give = jnp.concatenate([lax.dynamic_index_in_dim(raw_parts, 1 - ic, 1, keepdims=False), sums_mine], axis=1)
    raw_all = in_order(raw_keep, swap(raw_give, "core"), ic, 1).reshape(heads, share + 1, 3, DH)
    raw_all = raw_all.transpose(1, 2, 0, 3).reshape(share + 1, 3 * width)
    raw_grad, all_sums = raw_all[:share], raw_all[share]
    final_qkv_w = raw_grad * gain_one[:, None] + shift_one[:, None] * all_sums[None, :]
    final_gain_one = jnp.sum(raw_grad * raw_qkv, axis=1)
    final_shift_one = jnp.sum(raw_qkv * all_sums[None, :], axis=1)
    final_q_b = lax.dynamic_slice(all_sums, (place,), (share,))
    final_v_b = lax.dynamic_slice(all_sums, (2 * width + place,), (share,))

    back_own = back_own + swap(back_other, "core").astype(f32)
    back_own = back_own.reshape(micro, rows, width)
    input_grad = grad_resid.reshape(micro, rows, width) + norm_back(back_own, normed_one, inverse_one)

    return (
        output.reshape(micro, rows, width),
        input_grad.astype(bf16),
        final_qkv_w,
        final_q_b,
        final_v_b,
        final_out_w,
        final_vectors[2],
        final_gain_one,
        final_shift_one,
        final_vectors[0],
        final_vectors[1],
        final_fc_w,
        final_fc_b,
        final_proj_w,
        final_vectors[3],
    )


def specs(names):
    rows, vector, tokens = P(names, None), P(names), P(None, names, None)
    weights = (rows, vector, vector, rows, vector, vector, vector, vector, vector, rows, vector, rows, vector)
    return (tokens, *weights, tokens, P(), P()), (tokens, tokens, *weights)


def solution(mesh):
    sizes = dict(mesh.shape)
    if sizes["head"] == 2 and sizes["blk"] == 16:
        fine = Mesh(mesh.devices.reshape(2, 4, 2, 2), ("head", "z", "x", "core"))
        given, made = specs(("z", "x", "core", "head"))
        return jax.shard_map(fast_body, mesh=fine, in_specs=given, out_specs=made, check_vma=False)
    given, made = specs(("blk", "head"))
    return jax.shard_map(general_body, mesh=mesh, in_specs=given, out_specs=made, check_vma=False)
```
